32 devices in a mesh: event: 2 (over x), pack: 4 (over z), tensor: 4 (over y, core).
Axes of the slice: x: 2, y: 2, z: 4, core: 2. Of those that a mesh axis runs over, the one named last changes fastest.
Arguments:
- features: bfloat16 [4096, 1024], P(('event', 'pack', 'tensor')), may hold values from -6 to 6
- dest_owner: int32 [4096], P(('event', 'pack', 'tensor')), may hold values from 0 to 7, as said below
- dest_slot: int32 [4096], P(('event', 'pack', 'tensor')), may hold values from 0 to 127, as said below
- doc_ids: int32 [8, 512], P(('event', 'pack')), may hold values from 0 to 7, never falling along the last dimension, each value on 1 to 128 neighbouring positions
- enc_weight: bfloat16 [2, 1024, 1024], replicated, may hold values from -0.1875 to 0.1875
- attn_in: bfloat16 [4, 1024, 1024], P(None, None, 'tensor'), may hold values from -0.1875 to 0.1875
- attn_out: bfloat16 [1024, 1024], P('tensor'), may hold values from -0.1875 to 0.1875
- ffn_in: bfloat16 [2, 1024, 2048], P(None, None, 'tensor'), may hold values from -0.1875 to 0.1875
- ffn_out: bfloat16 [2048, 1024], P('tensor'), may hold values from -0.125 to 0.125
- out_grad: bfloat16 [8, 512, 1024], P(('event', 'pack'), 'tensor'), may hold values from -6 to 6
Outputs:
- packed_out: bfloat16 [8, 512, 1024], P(('event', 'pack'), 'tensor')
- row_grad: bfloat16 [4096, 1024], P(('event', 'pack', 'tensor'))
- enc_grad: float32 [2, 1024, 1024], P(None, ('event', 'pack'), 'tensor')
The draws below stay inside these ranges and needn't reach their ends.
Inputs may be any that keep to these rules, and one draw needn't show every extreme that they name: `dest_owner`: the sequence of each event, numbered over event and pack with event slowest. From the devices of one tensor index every sequence receives exactly 128 events; from one device at most 24 events go to one sequence, every device sends exactly 24 to some sequence, and every sequence receives exactly 24 from some device. `dest_slot`: events of one tensor index that go to one sequence have distinct slots, so they fill that sequence's positions tix * 128 to tix * 128 + 127. `doc_ids`: document numbers never fall along a sequence; a document holds 1 to 128 positions.
All inputs are finite; a program needn't handle non-finite values.
Results may differ from the reference program's by a relative error of at most 0.023.
Values may be sent and summed in bfloat16 or wider, within the bound.
No kernel may reach another device: no remote copies, remote signals or barrier semaphores. Data moves between devices by JAX's collectives and lax.ppermute only.
A program may use at most 128 MiB of HBM per device.

```python
import math
import jax
import jax.numpy as jnp
import numpy as np
from jax import lax

D = 1024
HEADS = 16
FF = 2048
ENC_LAYERS = 2
ROWS_DEV = 128
SEQS = 8
LEN = 512
EVENTS = 4096
DOCS = 8
DOC_MOST = 128
N_TENSOR = 4


def route_plan(key):
    base = jax.random.fold_in(key, 11)

    def one_slice(slice_key):
        subkeys = jax.random.split(slice_key, 6)
        mean_load = ROWS_DEV // SEQS
        half_load = mean_load // 2
        spread = jax.random.randint(subkeys[0], (SEQS // 2,), 0, half_load + 1)
        spread = spread.at[0].set(half_load)
        pattern = jnp.concatenate([mean_load + spread, mean_load - spread]).astype(jnp.int32)
        pattern = pattern[jax.random.permutation(subkeys[1], SEQS)]
        shift_dst = jax.random.permutation(subkeys[2], SEQS)
        shift_src = jax.random.permutation(subkeys[3], SEQS)
        counts = pattern[(shift_dst[None, :] - shift_src[:, None]) % SEQS]
        bounds = jnp.cumsum(counts, axis=1)
        begins = bounds - counts
        ordinal = jnp.arange(ROWS_DEV, dtype=jnp.int32)
        owner_sorted = jnp.sum((ordinal[None, :, None] >= bounds[:, None, :]).astype(jnp.int32), axis=2)
        rank_sorted = ordinal[None, :] - jnp.take_along_axis(begins, owner_sorted, axis=1)
        arrive = jnp.cumsum(counts, axis=0) - counts
        position = jnp.take_along_axis(arrive, owner_sorted, axis=1) + rank_sorted
        slot_keys = jax.random.split(subkeys[4], SEQS)
        slot_perm = jax.vmap(lambda item: jax.random.permutation(item, ROWS_DEV))(slot_keys)
        slot_sorted = slot_perm[owner_sorted, position]
        row_keys = jax.random.split(subkeys[5], SEQS)
        row_perm = jax.vmap(lambda item: jax.random.permutation(item, ROWS_DEV))(row_keys)
        inverse = jnp.argsort(row_perm, axis=1)
        owners = jnp.take_along_axis(owner_sorted, inverse, axis=1)
        slots = jnp.take_along_axis(slot_sorted, inverse, axis=1)
        return (owners, slots)
    owners, slots = jax.vmap(one_slice)(jax.random.split(base, N_TENSOR))
    owners = owners.transpose(1, 0, 2).reshape(-1).astype(jnp.int32)
    slots = slots.transpose(1, 0, 2).reshape(-1).astype(jnp.int32)
    return (owners, slots)


def draw_dest_owner(key, part):
    return route_plan(key)[0]


def draw_dest_slot(key, part):
    return route_plan(key)[1]


def spiked(result, rng, source, target, shards_of, factor):
    def block_of(axis_at):
        return (jnp.arange(result.shape[axis_at]) // (result.shape[axis_at] // shards_of)).reshape((-1,) + (1,) * (result.ndim - 1 - axis_at))

    one_side = jax.random.permutation(rng, shards_of)[block_of(target)]
    far = (block_of(target) + shards_of // 2) % shards_of
    return jnp.where((block_of(source) == one_side) | (block_of(source) == far), factor * result, result)


def levels(rng, extent, pieces, smallest, largest):
    loudness, own = 1.0, jax.random.fold_in(rng, 6)
    for dim, blocks in pieces:
        steps = jnp.exp(jax.random.uniform(jax.random.fold_in(own, dim), (blocks,), jnp.float32, smallest / len(pieces), largest / len(pieces)))
        loudness = loudness * jnp.repeat(steps, extent[dim] // blocks).reshape([-1 if axis == dim else 1 for axis in range(len(extent))])
    return loudness


def split_up(amount, total, bound, skew):
    loads = [(1 << 20) // math.isqrt(standing ** skew) + 1 for standing in range(2, amount + 1)]
    spare, given = total - bound - (amount - 1), [1] * (amount - 1)
    while spare > 0:
        free = [i for i in range(amount - 1) if given[i] < bound]
        mass, left = sum([loads[i] for i in free]), spare
        for i in free:
            addition = min(bound - given[i], max(1, left * loads[i] // mass), spare)
            given[i] = given[i] + addition
            spare = spare - addition
    return np.array([bound] + given)


def ragged(own_key, amount, total, bound, slope):
    if amount == 2:
        one = jax.random.randint(own_key, (), max(1, total - bound), min(bound, total - 1) + 1)
        return jnp.stack([one, total - one])
    sizes = jnp.asarray(split_up(amount, total, bound, slope), jnp.int32)
    twos = (amount - 1) // 2
    donor, sink = sizes[1:1 + 2 * twos:2], sizes[2:2 + 2 * twos:2]
    room = jnp.minimum(donor - 1, bound - sink)
    passed = jax.random.randint(jax.random.fold_in(own_key, 1), (twos,), 0, 1 << 20) % (room + 1)
    sizes = sizes.at[1:1 + 2 * twos:2].set(donor - passed).at[2:2 + 2 * twos:2].set(sink + passed)
    return sizes[jax.random.permutation(jax.random.fold_in(own_key, 2), amount)]


def centred(key, dims, scale, reach, shards=(), held_as=jnp.bfloat16):
    gain = levels(key, dims, shards, -0.22, 0.18) if shards else 1.0
    drawn = jax.random.normal(key, dims, jnp.float32) * scale * gain
    return jnp.minimum(jnp.maximum(drawn, -reach), reach).astype(held_as)


def gaussian_with(stream_key, extent, scale, most, cuts, heavy, held_as=jnp.bfloat16):
    drawn = scale * jax.random.normal(stream_key, extent, jnp.float32)
    if cuts:
        drawn = drawn * levels(stream_key, extent, cuts, -0.22, 0.18)
    return jnp.clip(spiked(drawn, jax.random.fold_in(stream_key, 3), *heavy), -most, most).astype(held_as)


def setup_inputs(seed: int = 0) -> dict:
    seeds = jax.random.split(jax.random.key(seed), 11)
    features = gaussian_with(seeds[0], (EVENTS, D), 1.0, 6.0, ((0, 32),), (0, 1, 32, 2.75))
    dest_owner = draw_dest_owner(jax.random.fold_in(seeds[10], 71), 0)
    dest_slot = draw_dest_slot(jax.random.fold_in(seeds[10], 71), 0)
    doc_ids = jax.vmap(lambda own: jnp.searchsorted(jnp.cumsum(ragged(own, DOCS, LEN, DOC_MOST, 1)), jnp.arange(LEN), side="right"))(jax.random.split(seeds[3], SEQS)).reshape((SEQS, LEN)).astype(jnp.int32)
    enc_weight = centred(seeds[4], (ENC_LAYERS, D, D), D ** -0.5, 0.1875)
    attn_in = centred(seeds[5], (4, D, D), D ** -0.5, 0.1875, ((2, 4),))
    attn_out = centred(seeds[6], (D, D), D ** -0.5, 0.1875, ((0, 4),))
    ffn_in = centred(seeds[7], (2, D, FF), D ** -0.5, 0.1875, ((2, 4),))
    ffn_out = centred(seeds[8], (FF, D), FF ** -0.5, 0.125, ((0, 4),))
    out_grad = centred(seeds[9], (SEQS, LEN, D), 1.0, 6.0, ((0, 8), (1, 4)))
    return {"features": features, "dest_owner": dest_owner, "dest_slot": dest_slot, "doc_ids": doc_ids, "enc_weight": enc_weight, "attn_in": attn_in, "attn_out": attn_out, "ffn_in": ffn_in, "ffn_out": ffn_out, "out_grad": out_grad}


EPS = 1e-06

def silu_grad(value):
    sigma = jax.nn.sigmoid(value)
    return sigma * (1.0 + value * (1.0 - sigma))

def norm_rows(rows):
    wide = rows.astype(jnp.float32)
    factor = lax.rsqrt(lax.optimization_barrier(jnp.mean(wide * wide, axis=-1, keepdims=True)) + EPS)
    return (wide * factor, factor)

def norm_back(grad, normed, factor):
    return factor * (grad - normed * lax.optimization_barrier(jnp.mean(grad * normed, axis=-1, keepdims=True)))

def rounded(value):
    return lax.optimization_barrier(value.astype(jnp.bfloat16)).astype(jnp.float32)

def doc_counts(documents):
    length = documents.shape[0]
    places = jnp.arange(length, dtype=jnp.int32)
    change = jnp.concatenate([jnp.ones((1,), bool), documents[1:] != documents[:-1]])
    first = lax.cummax(jnp.where(change, places, 0), axis=0)
    return (places - first + 1).astype(jnp.float32)

def group_terms(left, right, spec):
    group_width = left.shape[-1] // N_TENSOR
    total = None
    for group in range(N_TENSOR):
        lower = group * group_width
        term = jnp.einsum(spec, left[..., lower:lower + group_width].astype(jnp.float32), right[..., lower:lower + group_width].astype(jnp.float32))
        total = rounded(term) if total is None else total + rounded(term)
    return total

def split_heads(value):
    return value.reshape(value.shape[0], HEADS, D // HEADS).transpose(1, 0, 2)

def join_heads(value):
    return value.transpose(1, 0, 2).reshape(value.shape[1], D)

def sequence_step(packed, documents, d_out, attn_in, attn_out, ffn_in, ffn_out):
    head_scale = (D // HEADS) ** (-0.5)
    counts = doc_counts(documents)
    root = jnp.sqrt(counts)[:, None]
    places = jnp.arange(LEN, dtype=jnp.int32)
    allowed = (documents[:, None] == documents[None, :]) & (places[None, :] <= places[:, None])
    normed_f, factor1 = norm_rows(packed)
    normed = normed_f.astype(jnp.bfloat16)
    projected = jnp.einsum('rd,kdc->krc', normed.astype(jnp.float32), attn_in.astype(jnp.float32)).astype(jnp.bfloat16)
    query = split_heads(projected[0]).astype(jnp.float32)
    keys = split_heads(projected[1]).astype(jnp.float32)
    values = split_heads(projected[2]).astype(jnp.float32)
    gate_raw = projected[3].astype(jnp.float32)
    scores = jnp.einsum('hqd,hkd->hqk', query, keys) * head_scale
    weights = jnp.where(allowed[None], jax.nn.silu(scores), 0.0).astype(jnp.bfloat16)
    attended = join_heads(jnp.einsum('hqk,hkd->hqd', weights.astype(jnp.float32), values)) / root
    gated = (attended * jax.nn.silu(gate_raw)).astype(jnp.bfloat16)
    attn_sum = group_terms(gated, attn_out.T, 'rc,dc->rd')
    resid = (packed.astype(jnp.float32) + attn_sum).astype(jnp.bfloat16)
    normed2_f, factor2 = norm_rows(resid)
    normed2 = normed2_f.astype(jnp.bfloat16)
    gate_up = jnp.einsum('rd,kdf->krf', normed2.astype(jnp.float32), ffn_in.astype(jnp.float32))
    gate, upper = (gate_up[0], gate_up[1])
    hidden = (jax.nn.silu(gate) * upper).astype(jnp.bfloat16)
    ffn_sum = group_terms(hidden, ffn_out.T, 'rf,df->rd')
    packed_out = (resid.astype(jnp.float32) + ffn_sum).astype(jnp.bfloat16)
    d_hidden = jnp.dot(d_out, ffn_out.T, preferred_element_type=jnp.float32)
    d_gate = (d_hidden * upper * silu_grad(gate)).astype(jnp.bfloat16)
    d_upper = (d_hidden * jax.nn.silu(gate)).astype(jnp.bfloat16)
    d_normed2 = group_terms(jnp.stack([d_gate, d_upper]), ffn_in, 'krf,kdf->rd')
    d_resid = (d_out.astype(jnp.float32) + norm_back(d_normed2, normed2_f, factor2)).astype(jnp.bfloat16)
    d_gated = jnp.dot(d_resid, attn_out.T, preferred_element_type=jnp.float32)
    d_attended = (d_gated * jax.nn.silu(gate_raw) / root).astype(jnp.bfloat16)
    d_gate_proj = (d_gated * attended * silu_grad(gate_raw)).astype(jnp.bfloat16)
    d_att_heads = split_heads(d_attended).astype(jnp.float32)
    d_weights = jnp.einsum('hqd,hkd->hqk', d_att_heads, values)
    d_scores = jnp.where(allowed[None], d_weights * silu_grad(scores), 0.0).astype(jnp.bfloat16).astype(jnp.float32)
    d_query = (jnp.einsum('hqk,hkd->hqd', d_scores, keys) * head_scale).astype(jnp.bfloat16)
    d_keys = (jnp.einsum('hqk,hqd->hkd', d_scores, query) * head_scale).astype(jnp.bfloat16)
    d_values = jnp.einsum('hqk,hqd->hkd', weights.astype(jnp.float32), d_att_heads).astype(jnp.bfloat16)
    d_projected = jnp.stack([join_heads(d_query), join_heads(d_keys), join_heads(d_values), d_gate_proj])
    d_normed = group_terms(d_projected, attn_in, 'krc,kdc->rd')
    d_packed = (d_resid.astype(jnp.float32) + norm_back(d_normed, normed_f, factor1)).astype(jnp.bfloat16)
    return (packed_out, d_packed)

def reference(features, dest_owner, dest_slot, doc_ids, enc_weight, attn_in, attn_out, ffn_in, ffn_out, out_grad):
    activations = [features]
    pre_acts = []
    for layer in range(ENC_LAYERS - 1):
        preact = jnp.dot(activations[-1], enc_weight[layer], preferred_element_type=jnp.float32)
        pre_acts.append(preact)
        activations.append(jax.nn.silu(preact).astype(jnp.bfloat16))
    encoded = jnp.dot(activations[-1], enc_weight[ENC_LAYERS - 1], preferred_element_type=jnp.float32).astype(jnp.bfloat16)
    device_of = jnp.arange(EVENTS, dtype=jnp.int32) // ROWS_DEV
    position = device_of % N_TENSOR * ROWS_DEV + dest_slot
    packed = jnp.zeros((SEQS, LEN, D), jnp.bfloat16).at[dest_owner, position].set(encoded)

    def one_sequence(inputs):
        return sequence_step(inputs[0], inputs[1], inputs[2], attn_in, attn_out, ffn_in, ffn_out)
    packed_out, d_packed = lax.map(one_sequence, (packed, doc_ids, out_grad))
    row_grad = d_packed[dest_owner, position]
    cotangent = row_grad
    grads = []
    for layer in reversed(range(ENC_LAYERS)):
        grads.append(lax.dot_general(activations[layer], cotangent, (((0,), (0,)), ((), ())), preferred_element_type=jnp.float32))
        if layer > 0:
            back = lax.dot_general(cotangent, enc_weight[layer], (((1,), (1,)), ((), ())), preferred_element_type=jnp.float32)
            cotangent = (back * silu_grad(pre_acts[layer - 1])).astype(jnp.bfloat16)
    enc_grad = jnp.stack(grads[::-1])
    return (packed_out, row_grad, enc_grad)
```

```python
import jax
import jax.numpy as jnp
from jax import lax
from jax.sharding import PartitionSpec as P

D = 1024
HEADS = 16
EPS = 1e-06
SLOT_LANES = 128


def silu_grad(value):
    sigma = jax.nn.sigmoid(value)
    return sigma * (1.0 + value * (1.0 - sigma))


def norm_rows(rows):
    wide = rows.astype(jnp.float32)
    factor = lax.rsqrt(jnp.mean(wide * wide, axis=-1, keepdims=True) + EPS)
    return (wide * factor, factor)


def norm_back(grad, normed, factor):
    return factor * (grad - normed * jnp.mean(grad * normed, axis=-1, keepdims=True))


def dot(left, right, dims=((1,), (0,))):
    return lax.dot_general(left, right, (dims, ((), ())), preferred_element_type=jnp.float32)


def bf16(value):
    return value.astype(jnp.bfloat16)


def near(value):
    count = lax.axis_size("tensor")
    return lax.ppermute(value, "tensor", [(i, i ^ 1) for i in range(count)])


def far(value):
    count = lax.axis_size("tensor")
    return lax.ppermute(value, "tensor", [(i, i ^ 2) for i in range(count)])


def doc_counts(documents):
    length = documents.shape[0]
    places = jnp.arange(length, dtype=jnp.int32)
    same = (documents[:, None] == documents[None, :]) & (places[None, :] <= places[:, None])
    return jnp.sum(same.astype(jnp.float32), axis=1)


def bucket_index(dest_owner, groups, capacity):
    onehot = (dest_owner[:, None] == jnp.arange(groups, dtype=jnp.int32)[None, :]).astype(jnp.int32)
    rows = dest_owner.shape[0]
    order = jnp.arange(rows, dtype=jnp.int32)
    earlier = (dest_owner[:, None] == dest_owner[None, :]) & (order[None, :] < order[:, None])
    rank = jnp.sum(earlier.astype(jnp.int32), axis=1)
    return dest_owner * capacity + rank


def scatter_sum(value, axis):
    count = lax.axis_size(axis)
    me = lax.axis_index(axis)
    total = lax.dynamic_index_in_dim(value, me, 0, keepdims=False)
    for step in range(1, count):
        target = lax.rem(me + step, count)
        block = bf16(lax.dynamic_index_in_dim(value, target, 0, keepdims=False))
        total = total + lax.ppermute(
            block, axis, [(i, (i + step) % count) for i in range(count)]
        ).astype(jnp.float32)
    return total


def shards(
    features,
    dest_owner,
    dest_slot,
    doc_ids,
    enc_weight,
    attn_in,
    attn_out,
    ffn_in,
    ffn_out,
    out_grad,
):
    rows_dev, width = features.shape
    groups = lax.axis_size(("event", "pack"))
    tensor_count = lax.axis_size("tensor")
    t = lax.axis_index("tensor")
    d_out = out_grad[0]
    documents = doc_ids[0]
    length = documents.shape[0]

    mean_load = rows_dev // groups
    capacity = mean_load + mean_load // 2
    place = bucket_index(dest_owner, groups, capacity)
    spots = jnp.arange(groups * capacity, dtype=jnp.int32)
    send_hot = spots[:, None] == place[None, :]
    with_slot = jnp.concatenate(
        [features, jnp.broadcast_to(bf16(dest_slot + 1)[:, None], (rows_dev, SLOT_LANES))], axis=1
    )
    send = bf16(dot(bf16(send_hot), with_slot)).reshape(groups, capacity, width + SLOT_LANES)
    got = lax.all_to_all(send, ("event", "pack"), split_axis=0, concat_axis=0, tiled=True)
    got = got.reshape(groups * capacity, width + SLOT_LANES)
    got_slots = got[:, width].astype(jnp.int32) - 1
    recv_hot = bf16(jnp.arange(rows_dev, dtype=jnp.int32)[:, None] == got_slots[None, :])
    mine = bf16(dot(recv_hot, got[:, :width]))

    d_out_far = far(d_out)
    ffn_in_near = near(ffn_in)
    ffn_out_near = near(ffn_out)
    attn_out_near = near(attn_out)

    mine_near = near(mine)
    mine_far = far(mine)
    mine_both = near(mine_far)

    def encode(rows):
        pre = dot(rows, enc_weight[0])
        act = bf16(jax.nn.silu(pre))
        packed = bf16(dot(act, enc_weight[1]))
        normed_f, factor = norm_rows(packed)
        proj = bf16(
            jnp.einsum("rd,kdc->krc", bf16(normed_f), attn_in, preferred_element_type=jnp.float32)
        )
        return pre, act, packed, proj

    pair_a = jnp.concatenate([mine, mine_near], axis=0)
    pair_b = jnp.concatenate([mine_far, mine_both], axis=0)
    pre_a, act_a, packed_a, proj_a = encode(pair_a)
    pre_b, act_b, packed_b, proj_b = encode(pair_b)
    proj_rel = [proj_a[:, :rows_dev], proj_a[:, rows_dev:], proj_b[:, :rows_dev], proj_b[:, rows_dev:]]
    packed = packed_a[:rows_dev]

    def reorder(blocks, axis):
        stacked = jnp.stack(blocks)
        return jnp.concatenate(
            [lax.dynamic_index_in_dim(stacked, t ^ b, 0, keepdims=False) for b in range(tensor_count)],
            axis=axis,
        )

    projected = reorder(proj_rel, 1)
    local_cols = projected.shape[2]
    head_dim = D // HEADS
    local_heads = local_cols // head_dim
    head_scale = head_dim ** (-0.5)

    def split_heads(value):
        return value.reshape(length, local_heads, head_dim).transpose(1, 0, 2)

    def join_heads(value):
        return value.transpose(1, 0, 2).reshape(length, local_cols)

    query = split_heads(projected[0])
    keys = split_heads(projected[1])
    values = split_heads(projected[2])
    gate_raw = projected[3].astype(jnp.float32)
    root = jnp.sqrt(doc_counts(documents))[:, None]
    places = jnp.arange(length, dtype=jnp.int32)
    saved = []
    parts = []
    for b in range(tensor_count):
        lower, upper = b * rows_dev, (b + 1) * rows_dev
        first = max(lower - rows_dev, 0)
        allowed = (documents[lower:upper, None] == documents[None, first:upper]) & (
            places[None, first:upper] <= places[lower:upper, None]
        )
        scores = (
            jnp.einsum(
                "hqd,hkd->hqk",
                query[:, lower:upper],
                keys[:, first:upper],
                preferred_element_type=jnp.float32,
            )
            * head_scale
        )
        weights = bf16(jnp.where(allowed[None], jax.nn.silu(scores), 0.0))
        parts.append(
            jnp.einsum(
                "hqk,hkd->hqd", weights, values[:, first:upper], preferred_element_type=jnp.float32
            )
        )
        saved.append((lower, upper, first, allowed, scores, weights))
    attended = join_heads(jnp.concatenate(parts, axis=1)) / root
    gated = bf16(attended * jax.nn.silu(gate_raw))

    def block(value, index):
        return lax.dynamic_slice_in_dim(value, index * rows_dev, rows_dev, axis=0)

    give = jnp.concatenate([block(gated, t ^ 3), block(gated, t ^ 1)], axis=0)
    keep = jnp.concatenate([block(gated, t ^ 2), block(gated, t)], axis=0)
    take = near(give)
    attn_part = dot(keep, attn_out) + dot(take, attn_out_near)
    attn_sum = attn_part[rows_dev:] + far(bf16(attn_part[:rows_dev])).astype(jnp.float32)
    resid = bf16(packed.astype(jnp.float32) + attn_sum)
    normed2_f, factor2 = norm_rows(resid)
    normed2 = bf16(normed2_f)
    normed2_far = far(normed2)

    def ffn(rows, cotangent):
        out = 0.0
        back = 0.0
        for w_in, w_out in ((ffn_in, ffn_out), (ffn_in_near, ffn_out_near)):
            d_hidden = dot(cotangent, w_out, ((1,), (1,)))
            gate = dot(rows, w_in[0])
            upper = dot(rows, w_in[1])
            sigma = jax.nn.sigmoid(gate)
            silu = gate * sigma
            hidden = bf16(silu * upper)
            d_gate = bf16(d_hidden * upper * (sigma * (1.0 + gate * (1.0 - sigma))))
            d_upper = bf16(d_hidden * silu)
            out = out + dot(hidden, w_out)
            back = (
                back + dot(d_gate, w_in[0], ((1,), (1,))) + dot(d_upper, w_in[1], ((1,), (1,)))
            )
        return out, back

    out_own, back_own = ffn(normed2, d_out)
    out_far, back_far = ffn(normed2_far, d_out_far)
    d_normed2 = back_own + far(bf16(back_far)).astype(jnp.float32)
    ffn_sum = out_own + far(bf16(out_far)).astype(jnp.float32)
    packed_out = bf16(resid.astype(jnp.float32) + ffn_sum)
    d_resid = bf16(d_out.astype(jnp.float32) + norm_back(d_normed2, normed2_f, factor2))

    d_resid_near = near(d_resid)
    d_resid_far = far(d_resid)
    d_resid_both = near(d_resid_far)
    d_resid_all = reorder([d_resid, d_resid_near, d_resid_far, d_resid_both], 0)
    d_gated = dot(d_resid_all, attn_out, ((1,), (1,)))
    d_attended = bf16(d_gated * jax.nn.silu(gate_raw) / root)
    d_gate_proj = bf16(d_gated * attended * silu_grad(gate_raw))
    d_heads = split_heads(d_attended)
    d_query_parts = []
    d_keys = jnp.zeros(keys.shape, jnp.float32)
    d_values = jnp.zeros(keys.shape, jnp.float32)
    for lower, upper, first, allowed, scores, weights in saved:
        d_block = d_heads[:, lower:upper]
        d_weights = jnp.einsum(
            "hqd,hkd->hqk", d_block, values[:, first:upper], preferred_element_type=jnp.float32
        )
        d_scores = bf16(jnp.where(allowed[None], d_weights * silu_grad(scores), 0.0))
        d_query_parts.append(
            jnp.einsum(
                "hqk,hkd->hqd", d_scores, keys[:, first:upper], preferred_element_type=jnp.float32
            )
        )
        d_keys = d_keys.at[:, first:upper].add(
            jnp.einsum(
                "hqk,hqd->hkd", d_scores, query[:, lower:upper], preferred_element_type=jnp.float32
            )
        )
        d_values = d_values.at[:, first:upper].add(
            jnp.einsum("hqk,hqd->hkd", weights, d_block, preferred_element_type=jnp.float32)
        )
    d_query = jnp.concatenate(d_query_parts, axis=1) * head_scale
    d_projected = jnp.stack(
        [
            bf16(join_heads(d_query)),
            bf16(join_heads(d_keys * head_scale)),
            bf16(join_heads(d_values)),
            d_gate_proj,
        ]
    )
    d_norm_part = jnp.einsum(
        "krc,kdc->rd", d_projected, attn_in, preferred_element_type=jnp.float32
    )
    give = bf16(jnp.concatenate([block(d_norm_part, t ^ 3), block(d_norm_part, t ^ 1)], axis=0))
    take = near(give).astype(jnp.float32)
    sum_far = block(d_norm_part, t ^ 2) + take[:rows_dev]
    d_normed = block(d_norm_part, t) + take[rows_dev:] + far(bf16(sum_far)).astype(jnp.float32)
    normed_f, factor1 = norm_rows(packed)
    d_packed = bf16(d_resid.astype(jnp.float32) + norm_back(d_normed, normed_f, factor1))

    back_rows = bf16(dot(recv_hot, d_packed, ((0,), (0,)))).reshape(groups, capacity, width)
    returned = lax.all_to_all(back_rows, ("event", "pack"), split_axis=0, concat_axis=0, tiled=True)
    returned = returned.reshape(groups * capacity, width)
    row_grad = bf16(dot(bf16(send_hot), returned, ((0,), (0,))))

    cot_near = near(d_packed)
    cot_far = far(d_packed)
    cot_both = near(cot_far)
    cot1 = jnp.concatenate([d_packed, cot_near, cot_far, cot_both], axis=0)
    cols = width // tensor_count

    def columns(value):
        return lax.dynamic_slice_in_dim(value, t * cols, cols, axis=1)

    act0 = jnp.concatenate([pair_a, pair_b], axis=0)
    act1 = jnp.concatenate([act_a, act_b], axis=0)
    pre0 = jnp.concatenate([columns(pre_a), columns(pre_b)], axis=0)
    w1_rows = lax.dynamic_slice_in_dim(enc_weight[1], t * cols, cols, axis=0)
    cot0 = bf16(dot(cot1, w1_rows, ((1,), (1,))) * silu_grad(pre0))
    event_count = lax.axis_size("event")
    pack_count = lax.axis_size("pack")

    def reduce_layer(act, cot):
        part = dot(act, cot, ((0,), (0,)))
        part = part.reshape(event_count, width // event_count, cols)
        part = scatter_sum(part, "event")
        part = part.reshape(pack_count, width // event_count // pack_count, cols)
        return scatter_sum(part, "pack")

    grad1 = reduce_layer(act1, columns(cot1))
    grad0 = reduce_layer(act0, cot0)
    return (packed_out[None], row_grad, jnp.stack([grad0, grad1]))


def solution(mesh):
    placed = (
        P(("event", "pack", "tensor"), None),
        P(("event", "pack", "tensor")),
        P(("event", "pack", "tensor")),
        P(("event", "pack"), None),
        P(),
        P(None, None, "tensor"),
        P("tensor", None),
        P(None, None, "tensor"),
        P("tensor", None),
        P(("event", "pack"), "tensor", None),
    )
    return jax.shard_map(
        shards,
        mesh=mesh,
        in_specs=placed,
        out_specs=(
            P(("event", "pack"), "tensor", None),
            P(("event", "pack", "tensor"), None),
            P(None, ("event", "pack"), "tensor"),
        ),
        check_vma=False,
    )
```

```python
import functools

import jax
import jax.numpy as jnp
from jax import lax
from jax.experimental import pallas as pl
from jax.experimental.pallas import tpu as pltpu
from jax.sharding import PartitionSpec as P

D = 1024
HEADS = 16
HEAD = D // HEADS
EPS = 1e-06
F32 = jnp.float32
BF16 = jnp.bfloat16
MIB = 1 << 20
CHUNK = 256


def dot(left, right, dims=((1,), (0,))):
    return lax.dot_general(left, right, (dims, ((), ())), preferred_element_type=F32)


NT = ((1,), (1,))
TN = ((0,), (0,))


def bf16(value):
    return value.astype(BF16)


def silu_grad(value, sigma):
    return sigma * (1.0 + value * (1.0 - sigma))


def norm_factor(wide):
    return lax.rsqrt(jnp.mean(wide * wide, axis=-1, keepdims=True) + EPS)


def norm_back(grad, normed, factor):
    return factor * (grad - normed * jnp.mean(grad * normed, axis=-1, keepdims=True))


def turned(row, rows):
    return jnp.broadcast_to(row.astype(F32), (rows, rows)).T


def like(shape, dtype):
    return jax.ShapeDtypeStruct(shape, dtype)


def run(body, outs, scalars, args, weights=(), scratch=(), flops=0, moved=0, name=None):
    specs = []
    operands = []
    if scalars is not None:
        specs.append(pl.BlockSpec(memory_space=pltpu.SMEM))
        operands.append(scalars)
    specs += [pl.BlockSpec(memory_space=pltpu.VMEM)] * len(args)
    specs += [pl.BlockSpec(memory_space=pl.ANY)] * len(weights)
    operands += list(args) + list(weights)
    total = sum(a.size * a.dtype.itemsize for a in list(args) + list(weights) + list(outs))
    buffers = [pltpu.VMEM(w.shape, w.dtype) for w in weights]
    if weights:
        buffers.append(pltpu.SemaphoreType.DMA((16,)))
    return pl.pallas_call(
        body,
        out_shape=list(outs),
        in_specs=specs,
        out_specs=[pl.BlockSpec(memory_space=pltpu.VMEM)] * len(outs),
        scratch_shapes=buffers + list(scratch),
        compiler_params=pltpu.CompilerParams(vmem_limit_bytes=40 * MIB),
        cost_estimate=pl.CostEstimate(flops=flops, bytes_accessed=total, transcendentals=0),
        name=name,
    )(*operands)


def load(sources, targets, sems, cuts):
    started = []
    index = 0
    for source, target, pieces in zip(sources, targets, cuts):
        mine = []
        for piece in pieces:
            copy = pltpu.make_async_copy(source.at[piece], target.at[piece], sems.at[index])
            copy.start()
            mine.append(copy)
            index += 1
        started.append(mine)
    return started


def route_send(capacity, where, owner, slot, features, *outs):
    sends, place_ref = outs[:-1], outs[-1]
    groups = len(sends)
    rows, width = features.shape
    o_row = owner[...]
    o_col = turned(o_row, rows)
    i = lax.broadcasted_iota(jnp.int32, (rows, rows), 0)
    j = lax.broadcasted_iota(jnp.int32, (rows, rows), 1)
    earlier = jnp.where((o_col == o_row.astype(F32)) & (i < j), 1.0, 0.0)
    rank = jnp.sum(earlier, axis=0, keepdims=True).astype(jnp.int32)
    rel = o_row - where[0]
    rel = jnp.where(rel < 0, rel + groups, rel)
    place = rel * capacity + rank
    place_ref[...] = place
    spots = lax.broadcasted_iota(jnp.int32, (groups * capacity, rows), 0)
    hot = jnp.where(spots == place, 1.0, 0.0).astype(BF16)
    big = dot(hot, features[...])
    tags = dot(hot, bf16(turned(slot[...] + 1, rows)))
    for k in range(groups):
        part = slice(k * capacity, (k + 1) * capacity)
        sends[k][:, :width] = bf16(big[part])
        sends[k][:, width:] = bf16(tags[part])


def route_recv(*refs):
    gots, (rows_ref, hot_ref) = refs[:-2], refs[-2:]
    rows, width = rows_ref.shape
    got = jnp.concatenate([g[...].astype(F32) for g in gots], axis=0)
    lanes = lax.broadcasted_iota(jnp.int32, (got.shape[0], rows), 1) + 1
    hot = jnp.where(got[:, width:] == lanes.astype(F32), 1.0, 0.0).astype(BF16)
    hot_ref[...] = hot
    rows_ref[...] = bf16(dot(hot, bf16(got[:, :width]), TN))


def back_send(hot, d_packed, *sends):
    groups = len(sends)
    capacity = hot.shape[0] // groups
    big = dot(hot[...], d_packed[...])
    for k in range(groups):
        sends[k][...] = bf16(big[k * capacity : (k + 1) * capacity])


def back_recv(place, *refs):
    gots, out = refs[:-1], refs[-1]
    got = bf16(jnp.concatenate([g[...].astype(F32) for g in gots], axis=0))
    spots = lax.broadcasted_iota(jnp.int32, (got.shape[0], out.shape[0]), 0)
    hot = jnp.where(spots == place[...], 1.0, 0.0).astype(BF16)
    out[...] = bf16(dot(hot, got, TN))


def encode(where, rows, weights, loads, pre_all, pre_ref, act_ref, packed_ref, store):
    w0, w1, w_in = weights
    load0, load1, load_in = loads
    width = rows.shape[1]
    cols = pre_ref.shape[1]
    for n in range(width // CHUNK):
        part = slice(n * CHUNK, (n + 1) * CHUNK)
        load0[n].wait()
        pre = dot(rows, w0[:, part])
        pre_all[:, part] = pre
        act_ref[:, part] = bf16(pre * jax.nn.sigmoid(pre))
    pre_ref[...] = pre_all[:, pl.ds(pl.multiple_of(where[1] * cols, cols), cols)]
    act = act_ref[...]
    pieces = []
    for n in range(width // CHUNK):
        load1[n].wait()
        pieces.append(bf16(dot(act, w1[:, n * CHUNK : (n + 1) * CHUNK])))
    packed = jnp.concatenate(pieces, axis=1)
    if packed_ref is not None:
        packed_ref[...] = packed[: packed_ref.shape[0]]
    wide = packed.astype(F32)
    normed = bf16(wide * norm_factor(wide))
    for c in range(w_in.shape[0]):
        load_in[c].wait()
        store(c, bf16(dot(normed, w_in[c])))


def enc_cuts(width, comps):
    whole = slice(None)
    columns = [(whole, slice(n * CHUNK, (n + 1) * CHUNK)) for n in range(width // CHUNK)]
    return [
        [(0,) + c for c in columns],
        [(1,) + c for c in columns],
        [(c,) for c in range(comps)],
    ]


def start_encoder(enc, w_in, enc_v, w_in_v, sems):
    cuts = enc_cuts(enc.shape[2], w_in.shape[0])
    return load((enc, enc, w_in), (enc_v, enc_v, w_in_v), sems, cuts)


def encode_first(
    where, first, second, enc, w_in, pre_ref, act_ref, packed_ref, proj_ref, enc_v, w_in_v, sems, pre_all
):
    loads = start_encoder(enc, w_in, enc_v, w_in_v, sems)
    rows = jnp.concatenate([first[...], second[...]], axis=0)
    half = first.shape[0]

    def store(c, value):
        proj_ref[c, 0] = value[:half]
        proj_ref[c, 1] = value[half:]

    encode(
        where, rows, (enc_v.at[0], enc_v.at[1], w_in_v), loads, pre_all, pre_ref, act_ref, packed_ref, store
    )


def window(where, docs, r, rows):
    t = where[1]
    b = t ^ r
    ahead = jnp.where(b > 0, (b - 1) ^ t, r)
    doc_q = turned(docs[b], rows)
    doc_own = docs[b].astype(F32)
    doc_ahead = docs[jnp.maximum(b - 1, 0)].astype(F32)
    i = lax.broadcasted_iota(jnp.int32, (rows, rows), 0)
    j = lax.broadcasted_iota(jnp.int32, (rows, rows), 1)
    own = jnp.where((doc_q == doc_own) & (j <= i), 1.0, 0.0)
    prior = jnp.where(doc_q == doc_ahead, 1.0, 0.0) * jnp.where(b > 0, 1.0, 0.0)
    allowed = jnp.concatenate([prior, own], axis=1)
    root_inv = lax.rsqrt(jnp.sum(allowed, axis=1, keepdims=True))
    return ahead, allowed, root_inv


def head_masks(cols):
    lane = lax.broadcasted_iota(jnp.int32, (1, cols), 1) // HEAD
    return [jnp.where(lane == h, 1.0, 0.0) for h in range(cols // HEAD)]


def spread(value, masks):
    return jnp.concatenate([value * bf16(m) for m in masks], axis=0)


def collect(value, masks):
    rows = value.shape[0] // len(masks)
    total = None
    for h, m in enumerate(masks):
        part = value[h * rows : (h + 1) * rows] * m
        total = part if total is None else total + part
    return total


def attend_first(
    where, docs, third, fourth, proj_a, enc, w_in,
    pre_ref, act_ref, proj_ref, att_ref, give_ref, keep_ref,
    enc_v, w_in_v, sems, pre_all,
):
    loads = start_encoder(enc, w_in, enc_v, w_in_v, sems)
    rows = jnp.concatenate([third[...], fourth[...]], axis=0)
    half = third.shape[0]
    cols = proj_a.shape[-1]
    proj_ref[:, 0:2] = proj_a[...]

    def store(c, value):
        proj_ref[c, 2] = value[:half]
        proj_ref[c, 3] = value[half:]

    encode(where, rows, (enc_v.at[0], enc_v.at[1], w_in_v), loads, pre_all, pre_ref, act_ref, None, store)
    masks = head_masks(cols)
    for r, (target, place) in enumerate(((keep_ref, 1), (give_ref, 1), (keep_ref, 0), (give_ref, 0))):
        ahead, allowed, root_inv = window(where, docs, r, half)
        keys = jnp.concatenate([proj_ref[1, ahead], proj_ref[1, r]], axis=0)
        values = jnp.concatenate([proj_ref[2, ahead], proj_ref[2, r]], axis=0)
        many = jnp.concatenate([allowed] * len(masks), axis=0)
        scores = dot(spread(proj_ref[0, r], masks), keys, NT) * HEAD ** (-0.5)
        weights = bf16(scores * jax.nn.sigmoid(scores) * many)
        attended = collect(dot(weights, values), masks) * root_inv
        gate = proj_ref[3, r].astype(F32)
        att_ref[r] = attended
        target[place * half : (place + 1) * half, :] = bf16(attended * gate * jax.nn.sigmoid(gate))


def out_part(give_rows, half_index, keep, take, w_own, w_near):
    part = slice(half_index * give_rows, (half_index + 1) * give_rows)
    return dot(keep[part, :], w_own[...]) + dot(take[part, :], w_near[...])


def attn_out_far(keep, take, w_own, w_near, out):
    out[...] = bf16(out_part(out.shape[0], 0, keep, take, w_own, w_near))


def attn_out_own(keep, take, w_own, w_near, packed, out):
    out[...] = out_part(out.shape[0], 1, keep, take, w_own, w_near) + packed[...].astype(F32)


def residual(part, got, resid_ref, normed_ref):
    resid = bf16(part[...] + got[...].astype(F32))
    resid_ref[...] = resid
    wide = resid.astype(F32)
    normed_ref[...] = bf16(wide * norm_factor(wide))


def ffn(rows_ref, d_out_ref, in_a, in_b, out_a, out_b, hidden_ref, back_ref, in_av, in_bv, out_av, out_bv, sems):
    whole = (slice(None),)
    loads = load(
        (out_a, in_a, out_b, in_b), (out_av, in_av, out_bv, in_bv), sems,
        [[whole], [(0,), (1,)], [whole], [(0,), (1,)]],
    )
    rows = rows_ref[...]
    cotangent = d_out_ref[...]
    units = out_a.shape[0]
    back = None
    for index, (w_in, w_out) in enumerate(((in_av, out_av), (in_bv, out_bv))):
        load_out, load_in = loads[2 * index], loads[2 * index + 1]
        load_out[0].wait()
        load_in[0].wait()
        load_in[1].wait()
        for n in range(units // CHUNK):
            part = slice(n * CHUNK, (n + 1) * CHUNK)
            d_hidden = dot(cotangent, w_out[part, :], NT)
            gate = dot(rows, w_in[0, :, part])
            upper = dot(rows, w_in[1, :, part])
            sigma = jax.nn.sigmoid(gate)
            silu = gate * sigma
            hidden_ref[:, index * units + n * CHUNK : index * units + (n + 1) * CHUNK] = bf16(silu * upper)
            d_gate = bf16(d_hidden * upper * silu_grad(gate, sigma))
            d_upper = bf16(d_hidden * silu)
            term = dot(d_gate, w_in[0, :, part], NT) + dot(d_upper, w_in[1, :, part], NT)
            back = term if back is None else back + term
    back_ref[...] = back.astype(back_ref.dtype)


def ffn_out_far(hidden, w_a, w_b, out):
    units = w_a.shape[0]
    out[...] = bf16(dot(hidden[:, :units], w_a[...]) + dot(hidden[:, units:], w_b[...]))


def ffn_out_own(hidden, w_a, w_b, resid, got, out):
    units = w_a.shape[0]
    total = dot(hidden[:, :units], w_a[...]) + dot(hidden[:, units:], w_b[...])
    out[...] = bf16(resid[...].astype(F32) + total + got[...].astype(F32))


def resid_back(back, got, resid, d_out, out):
    wide = resid[...].astype(F32)
    factor = norm_factor(wide)
    grad = back[...] + got[...].astype(F32)
    out[...] = bf16(d_out[...].astype(F32) + norm_back(grad, wide * factor, factor))


def attend_back(where, docs, d_resid, r, proj_ref, att_ref, w_out, masks, d_q, d_k, d_v, d_g):
    half = d_resid.shape[0]
    scale = HEAD ** (-0.5)
    ahead, allowed, root_inv = window(where, docs, r, half)
    gate = proj_ref[3, r].astype(F32)
    sigma_g = jax.nn.sigmoid(gate)
    d_gated = dot(d_resid, w_out, NT)
    d_att = bf16(d_gated * (gate * sigma_g) * root_inv)
    d_g[r] = bf16(d_gated * att_ref[r] * silu_grad(gate, sigma_g))
    keys = jnp.concatenate([proj_ref[1, ahead], proj_ref[1, r]], axis=0)
    values = jnp.concatenate([proj_ref[2, ahead], proj_ref[2, r]], axis=0)
    many = jnp.concatenate([allowed] * len(masks), axis=0)
    query = spread(proj_ref[0, r], masks)
    d_att_m = spread(d_att, masks)
    scores = dot(query, keys, NT) * scale
    sigma = jax.nn.sigmoid(scores)
    weights = bf16(scores * sigma * many)
    d_weights = dot(d_att_m, values, NT)
    d_scores = bf16(d_weights * silu_grad(scores, sigma) * many)
    d_q[r] = bf16(collect(dot(d_scores, keys), masks) * scale)
    d_keys = dot(d_scores, query, TN) * scale
    d_values = dot(weights, d_att_m, TN)
    d_k[ahead] += d_keys[:half]
    d_k[r] += d_keys[half:]
    d_v[ahead] += d_values[:half]
    d_v[r] += d_values[half:]


def attn_back_first(where, docs, first, second, proj, att, w_out, d_q, d_k, d_v, d_g):
    masks = head_masks(w_out.shape[0])
    d_k[...] = jnp.zeros_like(d_k)
    d_v[...] = jnp.zeros_like(d_v)
    for r, rows in enumerate((first, second)):
        attend_back(where, docs, rows[...], r, proj, att, w_out[...], masks, d_q, d_k, d_v, d_g)


def attn_back_second(
    where, docs, third, fourth, proj, att, w_out, d_q_a, d_k_a, d_v_a, d_g_a, w_in,
    give_ref, keep_ref, w_in_v, sems, d_q, d_k, d_v, d_g,
):
    comps = w_in.shape[0]
    loads = load((w_in,), (w_in_v,), sems, [[(c,) for c in range(comps)]])[0]
    masks = head_masks(w_out.shape[0])
    half = third.shape[0]
    d_q[0:2] = d_q_a[...]
    d_g[0:2] = d_g_a[...]
    d_k[...] = d_k_a[...]
    d_v[...] = d_v_a[...]
    for r, rows in ((2, third), (3, fourth)):
        attend_back(where, docs, rows[...], r, proj, att, w_out[...], masks, d_q, d_k, d_v, d_g)
    for copy in loads:
        copy.wait()
    for first, second, target in ((3, 1, give_ref), (2, 0, keep_ref)):
        total = None
        for c, grads in enumerate((d_q, d_k, d_v, d_g)):
            left = jnp.concatenate([bf16(grads[first]), bf16(grads[second])], axis=0)
            term = dot(left, w_in_v[c], NT)
            total = term if total is None else total + term
        target[...] = total.astype(target.dtype)


def add_far(keep, take, out):
    half = out.shape[0]
    out[...] = bf16(keep[:half, :] + take[:half, :].astype(F32))


def packed_back(keep, take, got, packed, d_resid, out):
    half = out.shape[0]
    wide = packed[...].astype(F32)
    factor = norm_factor(wide)
    grad = keep[half:, :] + take[half:, :].astype(F32) + got[...].astype(F32)
    out[...] = bf16(d_resid[...].astype(F32) + norm_back(grad, wide * factor, factor))


def column_of(ref, index, cols):
    return ref[:, pl.ds(pl.multiple_of(index * cols, cols), cols)]


def enc_grads_first(where, cot_a, cot_b, act0_a, act0_b, act1, pre, w1_rows, part1, part0):
    cols = pre.shape[1]
    half = cot_a.shape[0]
    cot = jnp.concatenate([cot_a[...], cot_b[...]], axis=0)
    cot_cols = jnp.concatenate(
        [column_of(cot_a, where[1], cols), column_of(cot_b, where[1], cols)], axis=0
    )
    part1[...] = dot(act1[...], cot_cols, TN)
    value = pre[...]
    back = dot(cot, w1_rows[...], NT)
    cot0 = bf16(back * silu_grad(value, jax.nn.sigmoid(value)))
    act0 = jnp.concatenate([act0_a[...], act0_b[...]], axis=0)
    part0[...] = dot(act0, cot0, TN)


def split_events(where, part, total, keep, sends):
    count = len(sends) + 1
    total[...] = total[...] + part[...]
    size = keep.shape[0]
    for k in range(count):
        index = where[2] + k
        index = jnp.where(index >= count, index - count, index)
        rows = total[pl.ds(pl.multiple_of(index * size, size), size), :]
        if k == 0:
            keep[...] = rows
        else:
            sends[k - 1][...] = bf16(rows)


def enc_grad1_second(where, cot_a, cot_b, act1, part1, *rest):
    outs, total = rest[:-1], rest[-1]
    cols = part1.shape[1]
    cot_cols = jnp.concatenate(
        [column_of(cot_a, where[1], cols), column_of(cot_b, where[1], cols)], axis=0
    )
    total[...] = dot(act1[...], cot_cols, TN)
    split_events(where, part1, total, outs[0], outs[1:])


def enc_grad0_second(where, cot_a, cot_b, act0_a, act0_b, pre, w1_rows, part0, *rest):
    outs, total = rest[:-1], rest[-1]
    cot = jnp.concatenate([cot_a[...], cot_b[...]], axis=0)
    value = pre[...]
    back = dot(cot, w1_rows[...], NT)
    cot0 = bf16(back * silu_grad(value, jax.nn.sigmoid(value)))
    act0 = jnp.concatenate([act0_a[...], act0_b[...]], axis=0)
    total[...] = dot(act0, cot0, TN)
    split_events(where, part0, total, outs[0], outs[1:])


def split_packs(where, keep, *refs):
    packs = refs[-1]
    gots, outs, total = refs[: -1 - packs - 1], refs[-1 - packs - 1 : -2], refs[-2]
    value = keep[...]
    for got in gots:
        value = value + got[...].astype(F32)
    total[...] = value
    size = outs[0].shape[0]
    for k in range(packs):
        index = where[3] + k
        index = jnp.where(index >= packs, index - packs, index)
        rows = total[pl.ds(pl.multiple_of(index * size, size), size), :]
        outs[k][...] = rows.astype(outs[k].dtype)


def shards(
    features,
    dest_owner,
    dest_slot,
    doc_ids,
    enc_weight,
    attn_in,
    attn_out,
    ffn_in,
    ffn_out,
    out_grad,
):
    rows_dev, width = features.shape
    group_axes = ("event", "pack")
    groups = lax.axis_size(group_axes)
    events = lax.axis_size("event")
    packs = lax.axis_size("pack")
    tensors = lax.axis_size("tensor")
    cols = attn_in.shape[2]
    comps = attn_in.shape[0]
    units = ffn_out.shape[0]
    where = jnp.stack(
        [lax.axis_index(group_axes), lax.axis_index("tensor"), lax.axis_index("event"), lax.axis_index("pack")]
    ).astype(jnp.int32)
    d_out = out_grad[0]
    docs = doc_ids.reshape(tensors, 1, rows_dev)

    def near(value):
        return lax.ppermute(value, "tensor", [(i, i ^ 1) for i in range(tensors)])

    def far(value):
        return lax.ppermute(value, "tensor", [(i, i ^ 2) for i in range(tensors)])

    def shifted(value, axes, count, step):
        return lax.ppermute(value, axes, [(i, (i + step) % count) for i in range(count)])

    row_b = like((rows_dev, width), BF16)
    row_f = like((rows_dev, width), F32)

    mean_load = rows_dev // groups
    capacity = -(-(mean_load + mean_load // 2) // 8) * 8
    *sends, place = run(
        functools.partial(route_send, capacity),
        [like((capacity, width + rows_dev), BF16)] * groups + [like((1, rows_dev), jnp.int32)],
        where,
        [dest_owner.reshape(1, rows_dev), dest_slot.reshape(1, rows_dev), features],
        flops=2 * groups * capacity * rows_dev * width,
        name="route_send",
    )
    gots = [sends[0]] + [shifted(sends[k], group_axes, groups, k) for k in range(1, groups)]
    mine, hot = run(
        route_recv,
        [row_b, like((groups * capacity, rows_dev), BF16)],
        None,
        gots,
        flops=2 * groups * capacity * rows_dev * width,
        name="route_recv",
    )

    mine_near = near(mine)
    mine_far = far(mine)
    mine_both = near(mine_far)
    d_out_far = far(d_out)
    ffn_in_near = near(ffn_in)
    ffn_out_near = near(ffn_out)
    attn_out_near = near(attn_out)

    pair = 2 * rows_dev
    enc_flops = 2 * pair * width * (2 * width + comps * cols)
    pre_a, act_a, packed, proj_a = run(
        encode_first,
        [
            like((pair, cols), F32),
            like((pair, width), BF16),
            row_b,
            like((comps, 2, rows_dev, cols), BF16),
        ],
        where,
        [mine, mine_near],
        [enc_weight, attn_in],
        [pltpu.VMEM((pair, width), F32)],
        flops=enc_flops,
        name="encode_first",
    )
    pre_b, act_b, proj, attended, give, keep = run(
        attend_first,
        [
            like((pair, cols), F32),
            like((pair, width), BF16),
            like((comps, tensors, rows_dev, cols), BF16),
            like((tensors, rows_dev, cols), F32),
            like((pair, cols), BF16),
            like((pair, cols), BF16),
        ],
        where,
        [docs, mine_far, mine_both, proj_a],
        [enc_weight, attn_in],
        [pltpu.VMEM((pair, width), F32)],
        flops=2 * enc_flops,
        name="attend_first",
    )
    take = near(give)
    out_flops = 2 * rows_dev * width * 2 * cols
    (part_far,) = run(
        attn_out_far, [row_b], None, [keep, take, attn_out, attn_out_near], flops=out_flops, name="attn_out_far"
    )
    got_part = far(part_far)
    (part_own,) = run(
        attn_out_own, [row_f], None, [keep, take, attn_out, attn_out_near, packed], flops=out_flops, name="attn_out_own"
    )
    resid, normed2 = run(residual, [row_b, row_b], None, [part_own, got_part], name="residual")
    normed2_far = far(normed2)

    def feed(rows, cotangent, back_type, name):
        return run(
            ffn,
            [like((rows_dev, 2 * units), BF16), like((rows_dev, width), back_type)],
            None,
            [rows, cotangent],
            [ffn_in, ffn_in_near, ffn_out, ffn_out_near],
            flops=2 * rows_dev * width * 2 * units * 5,
            name=name,
        )

    hidden_own, back_own = feed(normed2, d_out, F32, "ffn_own")
    hidden_far, back_far = feed(normed2_far, d_out_far, BF16, "ffn_far")
    got_back = far(back_far)
    (d_resid,) = run(resid_back, [row_b], None, [back_own, got_back, resid, d_out], name="resid_back")
    ffn_flops = 2 * rows_dev * width * 2 * units
    (out_far,) = run(
        ffn_out_far, [row_b], None, [hidden_far, ffn_out, ffn_out_near], flops=ffn_flops, name="ffn_out_far"
    )
    got_out = far(out_far)
    (packed_out,) = run(
        ffn_out_own, [row_b], None, [hidden_own, ffn_out, ffn_out_near, resid, got_out], flops=ffn_flops, name="ffn_out_own"
    )

    d_resid_near = near(d_resid)
    d_resid_far = far(d_resid)
    d_resid_both = near(d_resid_far)
    att_flops = 2 * rows_dev * 2 * cols * (width + 6 * rows_dev * 4)
    block_f = like((tensors, rows_dev, cols), F32)
    two_b = like((2, rows_dev, cols), BF16)
    d_q, d_k, d_v, d_g = run(
        attn_back_first,
        [two_b, block_f, block_f, two_b],
        where,
        [docs, d_resid, d_resid_near, proj, attended, attn_out],
        flops=att_flops,
        name="attn_back_first",
    )
    four_b = pltpu.VMEM((tensors, rows_dev, cols), BF16)
    four_f = pltpu.VMEM((tensors, rows_dev, cols), F32)
    give, keep = run(
        attn_back_second,
        [like((pair, width), BF16), like((pair, width), F32)],
        where,
        [docs, d_resid_far, d_resid_both, proj, attended, attn_out, d_q, d_k, d_v, d_g],
        [attn_in],
        [four_b, four_f, four_f, four_b],
        flops=att_flops + 2 * 2 * pair * comps * cols * width,
        name="attn_back_second",
    )
    take = near(give)
    (sum_far,) = run(add_far, [row_b], None, [keep, take], name="add_far")
    got_sum = far(sum_far)
    (d_packed,) = run(packed_back, [row_b], None, [keep, take, got_sum, packed, d_resid], name="packed_back")

    cot_near = near(d_packed)
    cot_far = far(d_packed)
    cot_both = near(cot_far)
    w1_rows = lax.dynamic_slice_in_dim(enc_weight[1], lax.axis_index("tensor") * cols, cols, axis=0)
    grad_flops = 2 * pair * width * cols
    part_f = like((width, cols), F32)
    part1, part0 = run(
        enc_grads_first,
        [part_f, part_f],
        where,
        [d_packed, cot_near, mine, mine_near, act_a, pre_a, w1_rows],
        flops=3 * grad_flops,
        name="enc_grads_first",
    )
    event_rows = width // events
    event_outs = [like((event_rows, cols), F32)] + [like((event_rows, cols), BF16)] * (events - 1)
    total = [pltpu.VMEM((width, cols), F32)]
    keep1, *sends1 = run(
        enc_grad1_second, event_outs, where, [cot_far, cot_both, act_b, part1], (), total, flops=grad_flops, name="enc_grad1_second"
    )
    keep0, *sends0 = run(
        enc_grad0_second,
        event_outs,
        where,
        [cot_far, cot_both, mine_far, mine_both, pre_b, w1_rows, part0],
        (),
        total,
        flops=2 * grad_flops,
        name="enc_grad0_second",
    )
    pack_rows = event_rows // packs
    pack_outs = [like((pack_rows, cols), F32)] + [like((pack_rows, cols), BF16)] * (packs - 1)

    def over_events(keep, sends, name):
        gots = [shifted(s, "event", events, k + 1) for k, s in enumerate(sends)]
        return run(
            lambda *refs: split_packs(*refs, packs),
            pack_outs,
            where,
            [keep] + gots,
            (),
            [pltpu.VMEM((event_rows, cols), F32)],
            name=name,
        )

    keep1, *sends1 = over_events(keep1, sends1, "split_packs1")
    keep0, *sends0 = over_events(keep0, sends0, "split_packs0")
    gots1 = [shifted(s, "pack", packs, k + 1) for k, s in enumerate(sends1)]
    gots0 = [shifted(s, "pack", packs, k + 1) for k, s in enumerate(sends0)]

    backs = run(
        back_send,
        [like((capacity, width), BF16)] * groups,
        None,
        [hot, d_packed],
        flops=2 * groups * capacity * rows_dev * width,
        name="back_send",
    )
    returned = [backs[0]] + [
        shifted(backs[k], group_axes, groups, groups - k) for k in range(1, groups)
    ]
    (row_grad,) = run(
        back_recv,
        [row_b],
        None,
        [place] + returned,
        flops=2 * groups * capacity * rows_dev * width,
        name="back_recv",
    )

    def finish(refs, out):
        count = packs
        for layer in range(2):
            group = refs[layer * count : (layer + 1) * count]
            value = group[0][...]
            for got in group[1:]:
                value = value + got[...].astype(F32)
            out[layer] = value

    (enc_grad,) = run(
        lambda *refs: finish(refs[:-1], refs[-1]),
        [like((2, pack_rows, cols), F32)],
        None,
        [keep0] + gots0 + [keep1] + gots1,
        name="finish",
    )
    return (packed_out[None], row_grad, enc_grad)


def solution(mesh):
    placed = (
        P(("event", "pack", "tensor"), None),
        P(("event", "pack", "tensor")),
        P(("event", "pack", "tensor")),
        P(("event", "pack"), None),
        P(),
        P(None, None, "tensor"),
        P("tensor", None),
        P(None, None, "tensor"),
        P("tensor", None),
        P(("event", "pack"), "tensor", None),
    )
    return jax.shard_map(
        shards,
        mesh=mesh,
        in_specs=placed,
        out_specs=(
            P(("event", "pack"), "tensor", None),
            P(("event", "pack", "tensor"), None),
            P(None, ("event", "pack"), "tensor"),
        ),
        check_vma=False,
    )
```

```python
import functools

import jax
import jax.numpy as jnp
from jax import lax
from jax.experimental import pallas as pl
from jax.experimental.pallas import tpu as pltpu
from jax.sharding import PartitionSpec as P

D = 1024
HEADS = 16
HEAD = D // HEADS
EPS = 1e-06
F32 = jnp.float32
BF16 = jnp.bfloat16
MIB = 1 << 20
CHUNK = 256


def dot(left, right, dims=((1,), (0,))):
    return lax.dot_general(left, right, (dims, ((), ())), preferred_element_type=F32)


NT = ((1,), (1,))
TN = ((0,), (0,))


def bf16(value):
    return value.astype(BF16)


def silu_grad(value, sigma):
    return sigma * (1.0 + value * (1.0 - sigma))


def norm_factor(wide):
    return lax.rsqrt(jnp.mean(wide * wide, axis=-1, keepdims=True) + EPS)


def norm_back(grad, normed, factor):
    return factor * (grad - normed * jnp.mean(grad * normed, axis=-1, keepdims=True))


def turned(row, rows):
    return jnp.broadcast_to(row.astype(F32), (rows, rows)).T


def like(shape, dtype):
    return jax.ShapeDtypeStruct(shape, dtype)


def run(body, outs, scalars, args, scratch=(), flops=0, name=None, limit=16, space=pltpu.VMEM):
    specs = [pl.BlockSpec(memory_space=space)] * len(args)
    operands = list(args)
    if scalars is not None:
        specs = [pl.BlockSpec(memory_space=pltpu.SMEM)] + specs
        operands = [scalars] + operands
    total = sum(a.size * a.dtype.itemsize for a in list(args) + list(outs))
    return pl.pallas_call(
        body,
        out_shape=list(outs),
        in_specs=specs,
        out_specs=[pl.BlockSpec(memory_space=pltpu.VMEM)] * len(outs),
        scratch_shapes=list(scratch),
        compiler_params=pltpu.CompilerParams(vmem_limit_bytes=limit * MIB),
        cost_estimate=pl.CostEstimate(flops=flops, bytes_accessed=total, transcendentals=0),
        name=name,
    )(*operands)


def tie(*values):
    return lax.optimization_barrier(values)


def route_send(capacity, where, owner_hbm, slot_hbm, features_hbm, *refs):
    outs, (owner, slot, features, sems) = refs[:-4], refs[-4:]
    sends, place_ref = outs[:-1], outs[-1]
    copies = [
        pltpu.make_async_copy(source, target, sems.at[n])
        for n, (source, target) in enumerate(
            ((owner_hbm, owner), (slot_hbm, slot), (features_hbm, features))
        )
    ]
    for copy in copies:
        copy.start()
    for copy in copies:
        copy.wait()
    groups = len(sends)
    rows, width = features.shape
    o_row = owner[...]
    o_col = turned(o_row, rows)
    i = lax.broadcasted_iota(jnp.int32, (rows, rows), 0)
    j = lax.broadcasted_iota(jnp.int32, (rows, rows), 1)
    earlier = jnp.where((o_col == o_row.astype(F32)) & (i < j), 1.0, 0.0)
    rank = jnp.sum(earlier, axis=0, keepdims=True).astype(jnp.int32)
    place = (o_row ^ where[0]) * capacity + rank
    place_ref[...] = place
    spots = lax.broadcasted_iota(jnp.int32, (groups * capacity, rows), 0)
    hot = jnp.where(spots == place, 1.0, 0.0).astype(BF16)
    big = dot(hot, features[...])
    tags = dot(hot, bf16(turned(slot[...] + 1, rows)))
    for k in range(groups):
        part = slice(k * capacity, (k + 1) * capacity)
        sends[k][:, :width] = bf16(big[part])
        sends[k][:, width:] = bf16(tags[part])


def route_recv(*refs):
    gots, (rows_ref, hot_ref) = refs[:-2], refs[-2:]
    rows, width = rows_ref.shape
    got = jnp.concatenate([g[...].astype(F32) for g in gots], axis=0)
    lanes = lax.broadcasted_iota(jnp.int32, (got.shape[0], rows), 1) + 1
    hot = jnp.where(got[:, width:] == lanes.astype(F32), 1.0, 0.0).astype(BF16)
    hot_ref[...] = hot
    rows_ref[...] = bf16(dot(hot, bf16(got[:, :width]), TN))


def back_send(hot, d_packed, *sends):
    groups = len(sends)
    capacity = hot.shape[0] // groups
    big = dot(hot[...], d_packed[...])
    for k in range(groups):
        sends[k][...] = bf16(big[k * capacity : (k + 1) * capacity])


def back_recv(place, *refs):
    gots, out = refs[:-1], refs[-1]
    got = bf16(jnp.concatenate([g[...].astype(F32) for g in gots], axis=0))
    spots = lax.broadcasted_iota(jnp.int32, (got.shape[0], out.shape[0]), 0)
    hot = jnp.where(spots == place[...], 1.0, 0.0).astype(BF16)
    out[...] = bf16(dot(hot, got, TN))


def encode(where, rows, enc, w_in, pre_all, pre_ref, act_ref, packed_ref, store):
    width = rows.shape[1]
    cols = pre_ref.shape[1]
    for n in range(width // CHUNK):
        part = slice(n * CHUNK, (n + 1) * CHUNK)
        pre = dot(rows, enc[0, :, part])
        pre_all[:, part] = pre
        act_ref[:, part] = bf16(pre * jax.nn.sigmoid(pre))
    pre_ref[...] = pre_all[:, pl.ds(pl.multiple_of(where[1] * cols, cols), cols)]
    packed = bf16(dot(act_ref[...], enc[1]))
    if packed_ref is not None:
        packed_ref[...] = packed[: packed_ref.shape[0]]
    wide = packed.astype(F32)
    normed = bf16(wide * norm_factor(wide))
    for c in range(w_in.shape[0]):
        store(c, bf16(dot(normed, w_in[c])))


def encode_first(where, first, second, enc, w_in, pre_ref, act_ref, packed_ref, proj_ref, pre_all):
    rows = jnp.concatenate([first[...], second[...]], axis=0)
    half = first.shape[0]

    def store(c, value):
        proj_ref[c, 0] = value[:half]
        proj_ref[c, 1] = value[half:]

    encode(where, rows, enc, w_in, pre_all, pre_ref, act_ref, packed_ref, store)


def window(where, docs, r, rows):
    t = where[1]
    b = t ^ r
    ahead = jnp.where(b > 0, (b - 1) ^ t, r)
    doc_q = turned(docs[b], rows)
    doc_own = docs[b].astype(F32)
    doc_ahead = docs[jnp.maximum(b - 1, 0)].astype(F32)
    i = lax.broadcasted_iota(jnp.int32, (rows, rows), 0)
    j = lax.broadcasted_iota(jnp.int32, (rows, rows), 1)
    own = jnp.where((doc_q == doc_own) & (j <= i), 1.0, 0.0)
    prior = jnp.where(doc_q == doc_ahead, 1.0, 0.0) * jnp.where(b > 0, 1.0, 0.0)
    allowed = jnp.concatenate([prior, own], axis=1)
    root_inv = lax.rsqrt(jnp.sum(allowed, axis=1, keepdims=True))
    return ahead, allowed, root_inv


def head_masks(cols):
    lane = lax.broadcasted_iota(jnp.int32, (1, cols), 1) // HEAD
    return [jnp.where(lane == h, 1.0, 0.0) for h in range(cols // HEAD)]


def spread(value, masks):
    return jnp.concatenate([value * bf16(m) for m in masks], axis=0)


def collect(value, masks):
    rows = value.shape[0] // len(masks)
    total = None
    for h, m in enumerate(masks):
        part = value[h * rows : (h + 1) * rows] * m
        total = part if total is None else total + part
    return total


def attend_first(
    where, docs, third, fourth, proj_a, enc, w_in,
    pre_ref, act_ref, proj_ref, att_ref, give_ref, keep_ref, pre_all,
):
    rows = jnp.concatenate([third[...], fourth[...]], axis=0)
    half = third.shape[0]
    cols = proj_a.shape[-1]
    proj_ref[:, 0:2] = proj_a[...]

    def store(c, value):
        proj_ref[c, 2] = value[:half]
        proj_ref[c, 3] = value[half:]

    encode(where, rows, enc, w_in, pre_all, pre_ref, act_ref, None, store)
    masks = head_masks(cols)
    for r, (target, place) in enumerate(((keep_ref, 1), (give_ref, 1), (keep_ref, 0), (give_ref, 0))):
        ahead, allowed, root_inv = window(where, docs, r, half)
        keys = jnp.concatenate([proj_ref[1, ahead], proj_ref[1, r]], axis=0)
        values = jnp.concatenate([proj_ref[2, ahead], proj_ref[2, r]], axis=0)
        many = jnp.concatenate([allowed] * len(masks), axis=0)
        scores = dot(spread(proj_ref[0, r], masks), keys, NT) * HEAD ** (-0.5)
        weights = bf16(scores * jax.nn.sigmoid(scores) * many)
        attended = collect(dot(weights, values), masks) * root_inv
        gate = proj_ref[3, r].astype(F32)
        att_ref[r] = attended
        target[place * half : (place + 1) * half, :] = bf16(attended * gate * jax.nn.sigmoid(gate))


def out_part(give_rows, half_index, keep, take, w_own, w_near):
    part = slice(half_index * give_rows, (half_index + 1) * give_rows)
    return dot(keep[part, :], w_own[...]) + dot(take[part, :], w_near[...])


def attn_out_far(keep, take, w_own, w_near, out):
    out[...] = bf16(out_part(out.shape[0], 0, keep, take, w_own, w_near))


def attn_out_own(keep, take, w_own, w_near, packed, out):
    out[...] = out_part(out.shape[0], 1, keep, take, w_own, w_near) + packed[...].astype(F32)


def residual(part, got, resid_ref, normed_ref):
    resid = bf16(part[...] + got[...].astype(F32))
    resid_ref[...] = resid
    wide = resid.astype(F32)
    normed_ref[...] = bf16(wide * norm_factor(wide))


def ffn(rows_ref, d_out_ref, in_a, in_b, out_a, out_b, hidden_ref, back_ref):
    rows = rows_ref[...]
    cotangent = d_out_ref[...]
    units = out_a.shape[0]
    back = None
    for index, (w_in, w_out) in enumerate(((in_a, out_a), (in_b, out_b))):
        for n in range(units // CHUNK):
            part = slice(n * CHUNK, (n + 1) * CHUNK)
            d_hidden = dot(cotangent, w_out[part, :], NT)
            gate = dot(rows, w_in[0, :, part])
            upper = dot(rows, w_in[1, :, part])
            sigma = jax.nn.sigmoid(gate)
            silu = gate * sigma
            hidden_ref[:, index * units + n * CHUNK : index * units + (n + 1) * CHUNK] = bf16(silu * upper)
            d_gate = bf16(d_hidden * upper * silu_grad(gate, sigma))
            d_upper = bf16(d_hidden * silu)
            term = dot(d_gate, w_in[0, :, part], NT) + dot(d_upper, w_in[1, :, part], NT)
            back = term if back is None else back + term
    back_ref[...] = back.astype(back_ref.dtype)


def ffn_out_far(hidden, w_a, w_b, out):
    units = w_a.shape[0]
    out[...] = bf16(dot(hidden[:, :units], w_a[...]) + dot(hidden[:, units:], w_b[...]))


def ffn_out_own(hidden, w_a, w_b, resid, got, out):
    units = w_a.shape[0]
    total = dot(hidden[:, :units], w_a[...]) + dot(hidden[:, units:], w_b[...])
    out[...] = bf16(resid[...].astype(F32) + total + got[...].astype(F32))


def resid_back(back, got, resid, d_out, out):
    wide = resid[...].astype(F32)
    factor = norm_factor(wide)
    grad = back[...] + got[...].astype(F32)
    out[...] = bf16(d_out[...].astype(F32) + norm_back(grad, wide * factor, factor))


def attend_back(where, docs, d_resid, r, proj_ref, att_ref, w_out, masks, d_q, d_k, d_v, d_g):
    half = d_resid.shape[0]
    scale = HEAD ** (-0.5)
    ahead, allowed, root_inv = window(where, docs, r, half)
    gate = proj_ref[3, r].astype(F32)
    sigma_g = jax.nn.sigmoid(gate)
    d_gated = dot(d_resid, w_out, NT)
    d_att = bf16(d_gated * (gate * sigma_g) * root_inv)
    d_g[r] = bf16(d_gated * att_ref[r] * silu_grad(gate, sigma_g))
    keys = jnp.concatenate([proj_ref[1, ahead], proj_ref[1, r]], axis=0)
    values = jnp.concatenate([proj_ref[2, ahead], proj_ref[2, r]], axis=0)
    many = jnp.concatenate([allowed] * len(masks), axis=0)
    query = spread(proj_ref[0, r], masks)
    d_att_m = spread(d_att, masks)
    scores = dot(query, keys, NT) * scale
    sigma = jax.nn.sigmoid(scores)
    weights = bf16(scores * sigma * many)
    d_weights = dot(d_att_m, values, NT)
    d_scores = bf16(d_weights * silu_grad(scores, sigma) * many)
    d_q[r] = bf16(collect(dot(d_scores, keys), masks) * scale)
    d_keys = dot(d_scores, query, TN) * scale
    d_values = dot(weights, d_att_m, TN)
    d_k[ahead] += d_keys[:half]
    d_k[r] += d_keys[half:]
    d_v[ahead] += d_values[:half]
    d_v[r] += d_values[half:]


def attn_back_first(where, docs, first, second, proj, att, w_out, d_q, d_k, d_v, d_g):
    masks = head_masks(w_out.shape[0])
    d_k[...] = jnp.zeros_like(d_k)
    d_v[...] = jnp.zeros_like(d_v)
    for r, rows in enumerate((first, second)):
        attend_back(where, docs, rows[...], r, proj, att, w_out[...], masks, d_q, d_k, d_v, d_g)


def attn_back_second(
    where, docs, third, fourth, proj, att, w_out, d_q_a, d_k_a, d_v_a, d_g_a, w_in,
    give_ref, keep_ref, d_q, d_k, d_v, d_g,
):
    masks = head_masks(w_out.shape[0])
    half = third.shape[0]
    d_q[0:2] = d_q_a[...]
    d_g[0:2] = d_g_a[...]
    d_k[...] = d_k_a[...]
    d_v[...] = d_v_a[...]
    for r, rows in ((2, third), (3, fourth)):
        attend_back(where, docs, rows[...], r, proj, att, w_out[...], masks, d_q, d_k, d_v, d_g)
    for first, second, target in ((3, 1, give_ref), (2, 0, keep_ref)):
        total = None
        for c, grads in enumerate((d_q, d_k, d_v, d_g)):
            left = jnp.concatenate([bf16(grads[first]), bf16(grads[second])], axis=0)
            term = dot(left, w_in[c], NT)
            total = term if total is None else total + term
        target[...] = total.astype(target.dtype)


def add_far(keep, take, out):
    half = out.shape[0]
    out[...] = bf16(keep[:half, :] + take[:half, :].astype(F32))


def packed_back(keep, take, got, packed, d_resid, out):
    half = out.shape[0]
    wide = packed[...].astype(F32)
    factor = norm_factor(wide)
    grad = keep[half:, :] + take[half:, :].astype(F32) + got[...].astype(F32)
    out[...] = bf16(d_resid[...].astype(F32) + norm_back(grad, wide * factor, factor))


def column_of(ref, index, cols):
    return ref[:, pl.ds(pl.multiple_of(index * cols, cols), cols)]


def rows_term(act_refs, cot):
    return dot(jnp.concatenate([a[...] for a in act_refs], axis=0), cot, TN)


def first_cot(where, cot_a, cot_b, pre, enc):
    cols = pre.shape[1]
    cot = jnp.concatenate([cot_a[...], cot_b[...]], axis=0)
    value = pre[...]
    w1_rows = enc[1, pl.ds(pl.multiple_of(where[1] * cols, cols), cols), :]
    return bf16(dot(cot, w1_rows, NT) * silu_grad(value, jax.nn.sigmoid(value)))


def cot_columns(where, cot_a, cot_b, cols):
    return jnp.concatenate(
        [column_of(cot_a, where[1], cols), column_of(cot_b, where[1], cols)], axis=0
    )


def enc_grads_first(where, cot_a, cot_b, act0_a, act0_b, act1, pre, enc, part1, part0):
    cols = pre.shape[1]
    part1[...] = rows_term([act1], cot_columns(where, cot_a, cot_b, cols))
    part0[...] = rows_term([act0_a, act0_b], first_cot(where, cot_a, cot_b, pre, enc))


def halve(where, bits, bit, total, keep, send):
    place = bits.index(bit)
    count, size, _ = keep.shape
    mine = (where[0] >> bit) & 1
    for j in range(count):
        low = j & ((1 << place) - 1)
        base = ((j >> place) << (place + 1)) | low
        for target, value in ((keep, mine), (send, 1 - mine)):
            index = base + (value << place)
            rows = total[pl.ds(pl.multiple_of(index * size, size), size), :]
            target[j] = rows.astype(target.dtype)


def enc_grad1_second(bits, bit, where, cot_a, cot_b, act1, part1, keep, send, total):
    total[...] = rows_term([act1], cot_columns(where, cot_a, cot_b, part1.shape[1])) + part1[...]
    halve(where, bits, bit, total, keep, send)


def enc_grad0_second(bits, bit, where, cot_a, cot_b, act0_a, act0_b, pre, enc, part0, keep, send, total):
    total[...] = rows_term([act0_a, act0_b], first_cot(where, cot_a, cot_b, pre, enc)) + part0[...]
    halve(where, bits, bit, total, keep, send)


def halve_again(bits, bit, where, kept, got, keep, send, total):
    count, size, _ = kept.shape
    for j in range(count):
        total[j * size : (j + 1) * size, :] = kept[j] + got[j].astype(F32)
    halve(where, bits, bit, total, keep, send)


def finish(kept0, got0, kept1, got1, out):
    out[0] = kept0[0] + got0[0].astype(F32)
    out[1] = kept1[0] + got1[0].astype(F32)


def shards(
    features,
    dest_owner,
    dest_slot,
    doc_ids,
    enc_weight,
    attn_in,
    attn_out,
    ffn_in,
    ffn_out,
    out_grad,
):
    rows_dev, width = features.shape
    group_axes = ("event", "pack")
    groups = lax.axis_size(group_axes)
    packs = lax.axis_size("pack")
    tensors = lax.axis_size("tensor")
    cols = attn_in.shape[2]
    comps = attn_in.shape[0]
    units = ffn_out.shape[0]
    where = jnp.stack([lax.axis_index(group_axes), lax.axis_index("tensor")]).astype(jnp.int32)
    d_out = out_grad[0]
    docs = doc_ids.reshape(tensors, 1, rows_dev)

    def near(value):
        return lax.ppermute(value, "tensor", [(i, i ^ 1) for i in range(tensors)])

    def far(value):
        return lax.ppermute(value, "tensor", [(i, i ^ 2) for i in range(tensors)])

    def crossed(value, k):
        return lax.ppermute(value, group_axes, [(i, i ^ k) for i in range(groups)])

    row_b = like((rows_dev, width), BF16)
    row_f = like((rows_dev, width), F32)

    mean_load = rows_dev // groups
    capacity = -(-(mean_load + mean_load // 2) // 8) * 8
    *sends, place = run(
        functools.partial(route_send, capacity),
        [like((capacity, width + rows_dev), BF16)] * groups + [like((1, rows_dev), jnp.int32)],
        where,
        [dest_owner.reshape(1, rows_dev), dest_slot.reshape(1, rows_dev), features],
        [
            pltpu.VMEM((1, rows_dev), jnp.int32),
            pltpu.VMEM((1, rows_dev), jnp.int32),
            pltpu.VMEM((rows_dev, width), BF16),
            pltpu.SemaphoreType.DMA((3,)),
        ],
        space=pltpu.HBM,
        flops=2 * groups * capacity * rows_dev * width,
        name="route_send",
    )
    order = sorted(range(1, groups), key=lambda k: (-(k % packs), k))

    def exchange(parts):
        got = {k: crossed(parts[k], k) for k in order}
        return [parts[0]] + [got[k] for k in range(1, groups)]

    gots = exchange(sends)
    d_out_far = far(d_out)
    ffn_in_near = near(ffn_in)
    ffn_out_near = near(ffn_out)
    attn_out_near = near(attn_out)
    d_out_far, ffn_in_near, ffn_out_near, attn_out_near, *gots = tie(
        d_out_far, ffn_in_near, ffn_out_near, attn_out_near, *gots
    )
    mine, hot = run(
        route_recv,
        [row_b, like((groups * capacity, rows_dev), BF16)],
        None,
        gots,
        flops=2 * groups * capacity * rows_dev * width,
        name="route_recv",
    )

    mine_near = near(mine)
    mine_far = far(mine)

    pair = 2 * rows_dev
    enc_flops = 2 * pair * width * (2 * width + comps * cols)
    pre_a, act_a, packed, proj_a = run(
        encode_first,
        [
            like((pair, cols), F32),
            like((pair, width), BF16),
            row_b,
            like((comps, 2, rows_dev, cols), BF16),
        ],
        where,
        [mine, mine_near, enc_weight, attn_in],
        [pltpu.VMEM((pair, width), F32)],
        flops=enc_flops,
        name="encode_first",
    )
    mine_far, proj_a = tie(mine_far, proj_a)
    mine_both = near(mine_far)
    pre_b, act_b, proj, attended, give, keep = run(
        attend_first,
        [
            like((pair, cols), F32),
            like((pair, width), BF16),
            like((comps, tensors, rows_dev, cols), BF16),
            like((tensors, rows_dev, cols), F32),
            like((pair, cols), BF16),
            like((pair, cols), BF16),
        ],
        where,
        [docs, mine_far, mine_both, proj_a, enc_weight, attn_in],
        [pltpu.VMEM((pair, width), F32)],
        flops=2 * enc_flops,
        name="attend_first",
    )
    take = near(give)
    out_flops = 2 * rows_dev * width * 2 * cols
    (part_far,) = run(
        attn_out_far, [row_b], None, [keep, take, attn_out, attn_out_near], flops=out_flops, name="attn_out_far"
    )
    got_part = far(part_far)
    (part_own,) = run(
        attn_out_own, [row_f], None, [keep, take, attn_out, attn_out_near, packed], flops=out_flops, name="attn_out_own"
    )
    resid, normed2 = run(residual, [row_b, row_b], None, [part_own, got_part], name="residual")
    normed2_far = far(normed2)

    def feed(rows, cotangent, back_type, name):
        return run(
            ffn,
            [like((rows_dev, 2 * units), BF16), like((rows_dev, width), back_type)],
            None,
            [rows, cotangent, ffn_in, ffn_in_near, ffn_out, ffn_out_near],
            flops=2 * rows_dev * width * 2 * units * 5,
            name=name,
        )

    hidden_own, back_own = feed(normed2, d_out, F32, "ffn_own")
    normed2_far, back_own = tie(normed2_far, back_own)
    hidden_far, back_far = feed(normed2_far, d_out_far, BF16, "ffn_far")
    got_back = far(back_far)
    (d_resid,) = run(resid_back, [row_b], None, [back_own, got_back, resid, d_out], name="resid_back")
    ffn_flops = 2 * rows_dev * width * 2 * units
    (out_far,) = run(
        ffn_out_far, [row_b], None, [hidden_far, ffn_out, ffn_out_near], flops=ffn_flops, name="ffn_out_far"
    )
    d_resid_near = near(d_resid)
    d_resid_far = far(d_resid)
    att_flops = 2 * rows_dev * 2 * cols * (width + 6 * rows_dev * 4)
    block_f = like((tensors, rows_dev, cols), F32)
    two_b = like((2, rows_dev, cols), BF16)
    d_q, d_k, d_v, d_g = run(
        attn_back_first,
        [two_b, block_f, block_f, two_b],
        where,
        [docs, d_resid, d_resid_near, proj, attended, attn_out],
        flops=att_flops,
        name="attn_back_first",
    )
    d_resid_far, d_k = tie(d_resid_far, d_k)
    d_resid_both = near(d_resid_far)
    d_resid_both, out_far = tie(d_resid_both, out_far)
    got_out = far(out_far)
    four_b = pltpu.VMEM((tensors, rows_dev, cols), BF16)
    four_f = pltpu.VMEM((tensors, rows_dev, cols), F32)
    give, keep = run(
        attn_back_second,
        [like((pair, width), BF16), like((pair, width), F32)],
        where,
        [docs, d_resid_far, d_resid_both, proj, attended, attn_out, d_q, d_k, d_v, d_g, attn_in],
        [four_b, four_f, four_f, four_b],
        flops=att_flops + 2 * 2 * pair * comps * cols * width,
        name="attn_back_second",
    )
    take = near(give)
    (sum_far,) = run(add_far, [row_b], None, [keep, take], name="add_far")
    sum_far, got_out = tie(sum_far, got_out)
    got_sum = far(sum_far)
    (packed_out,) = run(
        ffn_out_own, [row_b], None, [hidden_own, ffn_out, ffn_out_near, resid, got_out], flops=ffn_flops, name="ffn_out_own"
    )

    got_sum, packed_out = tie(got_sum, packed_out)
    (d_packed,) = run(packed_back, [row_b], None, [keep, take, got_sum, packed, d_resid], name="packed_back")

    cot_far = far(d_packed)
    cot_near = near(d_packed)
    backs = run(
        back_send,
        [like((capacity, width), BF16)] * groups,
        None,
        [hot, d_packed],
        flops=2 * groups * capacity * rows_dev * width,
        name="back_send",
    )
    returned = exchange(backs)
    grad_flops = 2 * pair * width * cols
    part_f = like((width, cols), F32)
    part1, part0 = run(
        enc_grads_first,
        [part_f, part_f],
        where,
        [d_packed, cot_near, mine, mine_near, act_a, pre_a, enc_weight],
        flops=3 * grad_flops,
        name="enc_grads_first",
    )
    cot_far, part1, part0 = tie(cot_far, part1, part0)
    cot_both = near(cot_far)

    bits = list(range(groups.bit_length() - 1))
    pack_bits = bits[: packs.bit_length() - 1]
    event_bits = bits[len(pack_bits) :]
    size = width // groups
    total = [pltpu.VMEM((width, cols), F32)]

    def halves(remaining):
        shape = (2 ** (len(remaining) - 1), size, cols)
        return [like(shape, F32), like(shape, BF16)]

    def reduce_over(stages, start, name):
        remaining = list(bits)
        kept, send = start((tuple(remaining), stages[0]))
        got = crossed(send, 1 << stages[0])
        remaining.remove(stages[0])
        for bit in stages[1:]:
            kept, send = run(
                functools.partial(halve_again, tuple(remaining), bit),
                halves(remaining),
                where,
                [kept, got],
                [pltpu.VMEM((kept.shape[0] * size, cols), F32)],
                name=name + str(bit),
            )
            got = crossed(send, 1 << bit)
            remaining.remove(bit)
        return kept, got

    def start1(setting):
        return run(
            functools.partial(enc_grad1_second, *setting),
            halves(bits),
            where,
            [cot_far, cot_both, act_b, part1],
            total,
            flops=grad_flops,
            name="enc_grad1_second",
        )

    def start0(setting):
        return run(
            functools.partial(enc_grad0_second, *setting),
            halves(bits),
            where,
            [cot_far, cot_both, mine_far, mine_both, pre_b, enc_weight, part0],
            total,
            flops=2 * grad_flops,
            name="enc_grad0_second",
        )

    kept1, got1 = reduce_over(event_bits + pack_bits, start1, "halve1_")
    kept0, got0 = reduce_over(pack_bits[:1] + event_bits + pack_bits[1:], start0, "halve0_")
    (row_grad,) = run(
        back_recv,
        [row_b],
        None,
        [place] + returned,
        flops=2 * groups * capacity * rows_dev * width,
        name="back_recv",
    )
    (enc_grad,) = run(finish, [like((2, size, cols), F32)], None, [kept0, got0, kept1, got1], name="finish")
    return (packed_out[None], row_grad, enc_grad)


def solution(mesh):
    placed = (
        P(("event", "pack", "tensor"), None),
        P(("event", "pack", "tensor")),
        P(("event", "pack", "tensor")),
        P(("event", "pack"), None),
        P(),
        P(None, None, "tensor"),
        P("tensor", None),
        P(None, None, "tensor"),
        P("tensor", None),
        P(("event", "pack"), "tensor", None),
    )
    return jax.shard_map(
        shards,
        mesh=mesh,
        in_specs=placed,
        out_specs=(
            P(("event", "pack"), "tensor", None),
            P(("event", "pack", "tensor"), None),
            P(None, ("event", "pack"), "tensor"),
        ),
        check_vma=False,
    )
```

```python
import functools

import jax
import jax.numpy as jnp
from jax import lax
from jax.experimental import pallas as pl
from jax.experimental.pallas import tpu as pltpu
from jax.sharding import PartitionSpec as P

D = 1024
HEADS = 16
HEAD = D // HEADS
EPS = 1e-06
F32 = jnp.float32
BF16 = jnp.bfloat16
MIB = 1 << 20
CHUNK = 256


def dot(left, right, dims=((1,), (0,))):
    return lax.dot_general(left, right, (dims, ((), ())), preferred_element_type=F32)


NT = ((1,), (1,))
TN = ((0,), (0,))


def bf16(value):
    return value.astype(BF16)


def silu_grad(value, sigma):
    return sigma * (1.0 + value * (1.0 - sigma))


def norm_factor(wide):
    return lax.rsqrt(jnp.mean(wide * wide, axis=-1, keepdims=True) + EPS)


def norm_back(grad, normed, factor):
    return factor * (grad - normed * jnp.mean(grad * normed, axis=-1, keepdims=True))


def turned(row, rows):
    return jnp.broadcast_to(row.astype(F32), (rows, rows)).T


def like(shape, dtype):
    return jax.ShapeDtypeStruct(shape, dtype)


def run(body, outs, scalars, args, scratch=(), flops=0, name=None, limit=16, space=pltpu.VMEM):
    specs = [pl.BlockSpec(memory_space=space)] * len(args)
    operands = list(args)
    if scalars is not None:
        specs = [pl.BlockSpec(memory_space=pltpu.SMEM)] + specs
        operands = [scalars] + operands
    return pl.pallas_call(
        body,
        out_shape=list(outs),
        in_specs=specs,
        out_specs=[pl.BlockSpec(memory_space=pltpu.VMEM)] * len(outs),
        scratch_shapes=list(scratch),
        compiler_params=pltpu.CompilerParams(vmem_limit_bytes=limit * MIB),
        cost_estimate=pl.CostEstimate(flops=flops, bytes_accessed=0, transcendentals=0),
        name=name,
    )(*operands)


def tie(*values):
    return lax.optimization_barrier(values)


def route_send(capacity, where, code, features, *outs):
    sends, place_ref = outs[:-1], outs[-1]
    groups = len(sends)
    rows, width = features.shape
    shift = rows.bit_length() - 1
    o_row = code[...] >> shift
    slot = code[...] & (rows - 1)
    o_col = turned(o_row, rows)
    i = lax.broadcasted_iota(jnp.int32, (rows, rows), 0)
    j = lax.broadcasted_iota(jnp.int32, (rows, rows), 1)
    earlier = jnp.where((o_col == o_row.astype(F32)) & (i < j), 1.0, 0.0)
    rank = jnp.sum(earlier, axis=0, keepdims=True).astype(jnp.int32)
    place = (o_row ^ where[0]) * capacity + rank
    place_ref[...] = place
    spots = lax.broadcasted_iota(jnp.int32, (groups * capacity, rows), 0)
    hot = jnp.where(spots == place, 1.0, 0.0).astype(BF16)
    big = dot(hot, features[...])
    tags = dot(hot, bf16(turned(slot + 1, rows)))
    for k in range(groups):
        part = slice(k * capacity, (k + 1) * capacity)
        sends[k][:, :width] = bf16(big[part])
        sends[k][:, width:] = bf16(tags[part])


def route_recv(*refs):
    gots, (rows_ref, hot_ref) = refs[:-2], refs[-2:]
    rows, width = rows_ref.shape
    got = jnp.concatenate([g[...].astype(F32) for g in gots], axis=0)
    lanes = lax.broadcasted_iota(jnp.int32, (got.shape[0], rows), 1) + 1
    hot = jnp.where(got[:, width:] == lanes.astype(F32), 1.0, 0.0).astype(BF16)
    hot_ref[...] = hot
    rows_ref[...] = bf16(dot(hot, bf16(got[:, :width]), TN))


def back_send(events, hot, d_packed, *sends):
    packs = len(sends)
    capacity = hot.shape[0] // (events * packs)
    big = dot(hot[...], d_packed[...])
    for b in range(packs):
        parts = [
            big[(a * packs + b) * capacity : (a * packs + b + 1) * capacity] for a in range(events)
        ]
        sends[b][...] = bf16(jnp.concatenate(parts, axis=0))


def back_turn(*refs):
    events = refs[-1]
    refs = refs[:-1]
    packs = len(refs) - (events - 1) - 1
    gots, own, sends = refs[:packs], refs[packs], refs[packs + 1 :]
    wide = [g[...].astype(F32) for g in gots]
    capacity = wide[0].shape[0] // events
    for a, target in enumerate((own, *sends)):
        parts = [w[a * capacity : (a + 1) * capacity] for w in wide]
        target[...] = bf16(jnp.concatenate(parts, axis=0))


def back_recv(place, *refs):
    gots, out = refs[:-1], refs[-1]
    got = jnp.concatenate([g[...] for g in gots], axis=0)
    spots = lax.broadcasted_iota(jnp.int32, (got.shape[0], out.shape[0]), 0)
    hot = jnp.where(spots == place[...], 1.0, 0.0).astype(BF16)
    out[...] = bf16(dot(hot, got, TN))


def encode(where, rows, enc, w_in, pre_all, pre_ref, act_ref, packed_ref, store):
    width = rows.shape[1]
    cols = pre_ref.shape[1]
    for n in range(width // CHUNK):
        part = slice(n * CHUNK, (n + 1) * CHUNK)
        pre = dot(rows, enc[0, :, part])
        pre_all[:, part] = pre
        act_ref[:, part] = bf16(pre * jax.nn.sigmoid(pre))
    pre_ref[...] = pre_all[:, pl.ds(pl.multiple_of(where[1] * cols, cols), cols)]
    packed = bf16(dot(act_ref[...], enc[1]))
    packed_ref[...] = packed[: packed_ref.shape[0]]
    wide = packed.astype(F32)
    normed = bf16(wide * norm_factor(wide))
    for c in range(w_in.shape[0]):
        store(c, bf16(dot(normed, w_in[c])))


def encode_first(where, first, second, enc, w_in, pre_ref, act_ref, packed_ref, proj_ref, pre_all):
    rows = jnp.concatenate([first[...], second[...]], axis=0)
    half = first.shape[0]

    def store(c, value):
        proj_ref[c, 0] = value[:half]
        proj_ref[c, 1] = value[half:]

    encode(where, rows, enc, w_in, pre_all, pre_ref, act_ref, packed_ref, store)


def window(where, docs, r, rows):
    t = where[1]
    b = t ^ r
    ahead = jnp.where(b > 0, (b - 1) ^ t, r)
    doc_q = turned(docs[b], rows)
    doc_own = docs[b].astype(F32)
    doc_ahead = docs[jnp.maximum(b - 1, 0)].astype(F32)
    i = lax.broadcasted_iota(jnp.int32, (rows, rows), 0)
    j = lax.broadcasted_iota(jnp.int32, (rows, rows), 1)
    own = jnp.where((doc_q == doc_own) & (j <= i), 1.0, 0.0)
    prior = jnp.where(doc_q == doc_ahead, 1.0, 0.0) * jnp.where(b > 0, 1.0, 0.0)
    allowed = jnp.concatenate([prior, own], axis=1)
    root_inv = lax.rsqrt(jnp.sum(allowed, axis=1, keepdims=True))
    return ahead, allowed, root_inv


def head_masks(cols):
    lane = lax.broadcasted_iota(jnp.int32, (1, cols), 1) // HEAD
    return [jnp.where(lane == h, 1.0, 0.0) for h in range(cols // HEAD)]


def spread(value, masks):
    return jnp.concatenate([value * bf16(m) for m in masks], axis=0)


def collect(value, masks):
    rows = value.shape[0] // len(masks)
    total = None
    for h, m in enumerate(masks):
        part = value[h * rows : (h + 1) * rows] * m
        total = part if total is None else total + part
    return total


def attend_first(
    where, docs, third, fourth, proj_a, enc, w_in,
    pre_ref, act_ref, packed_ref, proj_ref, att_ref, give_ref, keep_ref, pre_all,
):
    rows = jnp.concatenate([third[...], fourth[...]], axis=0)
    half = third.shape[0]
    cols = proj_a.shape[-1]
    proj_ref[:, 0:2] = proj_a[...]

    def store(c, value):
        proj_ref[c, 2] = value[:half]
        proj_ref[c, 3] = value[half:]

    encode(where, rows, enc, w_in, pre_all, pre_ref, act_ref, packed_ref, store)
    masks = head_masks(cols)
    for r, (target, place) in enumerate(((keep_ref, 1), (give_ref, 1), (keep_ref, 0), (give_ref, 0))):
        ahead, allowed, root_inv = window(where, docs, r, half)
        keys = jnp.concatenate([proj_ref[1, ahead], proj_ref[1, r]], axis=0)
        values = jnp.concatenate([proj_ref[2, ahead], proj_ref[2, r]], axis=0)
        many = jnp.concatenate([allowed] * len(masks), axis=0)
        scores = dot(spread(proj_ref[0, r], masks), keys, NT) * HEAD ** (-0.5)
        weights = bf16(scores * jax.nn.sigmoid(scores) * many)
        attended = collect(dot(weights, values), masks) * root_inv
        gate = proj_ref[3, r].astype(F32)
        att_ref[r] = attended
        target[place * half : (place + 1) * half, :] = bf16(attended * gate * jax.nn.sigmoid(gate))


def attn_out_part(index, keep, take, w_own, w_near, out):
    rows = out.shape[0]
    part = slice(index * rows, (index + 1) * rows)
    out[...] = bf16(dot(keep[part, :], w_own[...]) + dot(take[part, :], w_near[...]))


def residual(packed, part, got, resid_ref, normed_ref):
    resid = bf16(packed[...].astype(F32) + (part[...].astype(F32) + got[...].astype(F32)))
    resid_ref[...] = resid
    wide = resid.astype(F32)
    normed_ref[...] = bf16(wide * norm_factor(wide))


def ffn(rows_ref, d_out_ref, in_a, in_b, out_a, out_b, hidden_ref, back_ref):
    rows = rows_ref[...]
    cotangent = d_out_ref[...]
    units = out_a.shape[0]
    back = None
    for index, (w_in, w_out) in enumerate(((in_a, out_a), (in_b, out_b))):
        for n in range(units // CHUNK):
            part = slice(n * CHUNK, (n + 1) * CHUNK)
            d_hidden = dot(cotangent, w_out[part, :], NT)
            gate = dot(rows, w_in[0, :, part])
            upper = dot(rows, w_in[1, :, part])
            sigma = jax.nn.sigmoid(gate)
            silu = gate * sigma
            hidden_ref[:, index * units + n * CHUNK : index * units + (n + 1) * CHUNK] = bf16(silu * upper)
            d_gate = bf16(d_hidden * upper * silu_grad(gate, sigma))
            d_upper = bf16(d_hidden * silu)
            term = dot(d_gate, w_in[0, :, part], NT) + dot(d_upper, w_in[1, :, part], NT)
            back = term if back is None else back + term
    back_ref[...] = back.astype(back_ref.dtype)


def ffn_out_far(hidden, w_a, w_b, out):
    units = w_a.shape[0]
    out[...] = bf16(dot(hidden[:, :units], w_a[...]) + dot(hidden[:, units:], w_b[...]))


def ffn_out_own(hidden, w_a, w_b, resid, got, out):
    units = w_a.shape[0]
    total = dot(hidden[:, :units], w_a[...]) + dot(hidden[:, units:], w_b[...])
    out[...] = bf16(resid[...].astype(F32) + total + got[...].astype(F32))


def resid_back(back, got, resid, d_out, out):
    wide = resid[...].astype(F32)
    factor = norm_factor(wide)
    grad = back[...].astype(F32) + got[...].astype(F32)
    out[...] = bf16(d_out[...].astype(F32) + norm_back(grad, wide * factor, factor))


def attend_back(where, docs, d_resid, r, proj_ref, att_ref, w_out, masks, d_q, d_k, d_v, d_g):
    half = d_resid.shape[0]
    scale = HEAD ** (-0.5)
    ahead, allowed, root_inv = window(where, docs, r, half)
    gate = proj_ref[3, r].astype(F32)
    sigma_g = jax.nn.sigmoid(gate)
    d_gated = dot(d_resid, w_out, NT)
    d_att = bf16(d_gated * (gate * sigma_g) * root_inv)
    d_g[r] = bf16(d_gated * att_ref[r] * silu_grad(gate, sigma_g))
    keys = jnp.concatenate([proj_ref[1, ahead], proj_ref[1, r]], axis=0)
    values = jnp.concatenate([proj_ref[2, ahead], proj_ref[2, r]], axis=0)
    many = jnp.concatenate([allowed] * len(masks), axis=0)
    query = spread(proj_ref[0, r], masks)
    d_att_m = spread(d_att, masks)
    scores = dot(query, keys, NT) * scale
    sigma = jax.nn.sigmoid(scores)
    weights = bf16(scores * sigma * many)
    d_weights = dot(d_att_m, values, NT)
    d_scores = bf16(d_weights * silu_grad(scores, sigma) * many)
    d_q[r] = bf16(collect(dot(d_scores, keys), masks) * scale)
    d_keys = dot(d_scores, query, TN) * scale
    d_values = dot(weights, d_att_m, TN)
    d_k[ahead] += d_keys[:half]
    d_k[r] += d_keys[half:]
    d_v[ahead] += d_values[:half]
    d_v[r] += d_values[half:]


def attn_back_first(where, docs, third, fourth, proj, att, w_out, d_q, d_k, d_v, d_g):
    masks = head_masks(w_out.shape[0])
    d_k[...] = jnp.zeros_like(d_k)
    d_v[...] = jnp.zeros_like(d_v)
    for r, rows in ((2, third), (3, fourth)):
        attend_back(where, docs, rows[...], r, proj, att, w_out[...], masks, d_q, d_k, d_v, d_g)


def back_norm(grads, w_in, first, second):
    total = None
    for c, grad in enumerate(grads):
        left = jnp.concatenate([grad[first], grad[second]], axis=0)
        term = dot(left, w_in[c], NT)
        total = term if total is None else total + term
    return total


def attn_back_second(
    where, docs, first, second, proj, att, w_out, d_q_far, d_k_far, d_v_far, d_g_far, w_in,
    give_ref, d_q, d_k, d_v, d_g, sum_k, sum_v,
):
    masks = head_masks(w_out.shape[0])
    d_q[2:4] = d_q_far[2:4]
    d_g[2:4] = d_g_far[2:4]
    sum_k[...] = d_k_far[...]
    sum_v[...] = d_v_far[...]
    for r, rows in ((0, first), (1, second)):
        attend_back(where, docs, rows[...], r, proj, att, w_out[...], masks, d_q, sum_k, sum_v, d_g)
    d_k[...] = bf16(sum_k[...])
    d_v[...] = bf16(sum_v[...])
    give_ref[...] = bf16(back_norm((d_q, d_k, d_v, d_g), w_in, 3, 1))


def attn_back_keep(d_q, d_k, d_v, d_g, w_in, keep_ref):
    keep_ref[...] = back_norm((d_q, d_k, d_v, d_g), w_in, 2, 0)


def add_near(keep, take, out_far, out_own):
    half = out_far.shape[0]
    out_far[...] = bf16(keep[:half, :] + take[:half, :].astype(F32))
    out_own[...] = bf16(keep[half:, :] + take[half:, :].astype(F32))


def packed_back(part, got, packed, d_resid, out):
    wide = packed[...].astype(F32)
    factor = norm_factor(wide)
    grad = part[...].astype(F32) + got[...].astype(F32)
    out[...] = bf16(d_resid[...].astype(F32) + norm_back(grad, wide * factor, factor))


def column_of(ref, index, cols):
    return ref[:, pl.ds(pl.multiple_of(index * cols, cols), cols)]


def rows_term(act_refs, cot):
    return dot(jnp.concatenate([a[...] for a in act_refs], axis=0), cot, TN)


def first_cot(where, cot_a, cot_b, pre, enc):
    cols = pre.shape[1]
    cot = jnp.concatenate([cot_a[...], cot_b[...]], axis=0)
    value = pre[...]
    w1_rows = enc[1, pl.ds(pl.multiple_of(where[1] * cols, cols), cols), :]
    return bf16(dot(cot, w1_rows, NT) * silu_grad(value, jax.nn.sigmoid(value)))


def cot_columns(where, cot_a, cot_b, cols):
    return jnp.concatenate(
        [column_of(cot_a, where[1], cols), column_of(cot_b, where[1], cols)], axis=0
    )


def enc_grads_first(where, cot_a, cot_b, act0_a, act0_b, act1, pre, enc, part1, part0):
    cols = pre.shape[1]
    part1[...] = rows_term([act1], cot_columns(where, cot_a, cot_b, cols))
    part0[...] = rows_term([act0_a, act0_b], first_cot(where, cot_a, cot_b, pre, enc))


def halve(where, bits, bit, total, keep, send):
    place = bits.index(bit)
    count, size, _ = keep.shape
    mine = (where[0] >> bit) & 1
    for j in range(count):
        low = j & ((1 << place) - 1)
        base = ((j >> place) << (place + 1)) | low
        for target, value in ((keep, mine), (send, 1 - mine)):
            index = base + (value << place)
            rows = total[pl.ds(pl.multiple_of(index * size, size), size), :]
            target[j] = rows.astype(target.dtype)


def enc_grad1_second(bits, bit, where, cot_a, cot_b, act1, part1, keep, send, total):
    total[...] = rows_term([act1], cot_columns(where, cot_a, cot_b, part1.shape[1])) + part1[...]
    halve(where, bits, bit, total, keep, send)


def enc_grad0_second(bits, bit, where, cot_a, cot_b, act0_a, act0_b, pre, enc, part0, keep, send, total):
    total[...] = rows_term([act0_a, act0_b], first_cot(where, cot_a, cot_b, pre, enc)) + part0[...]
    halve(where, bits, bit, total, keep, send)


def halve_again(bits, bit, where, kept, got, keep, send):
    place = bits.index(bit)
    mine = (where[0] >> bit) & 1
    for j in range(keep.shape[0]):
        low = j & ((1 << place) - 1)
        base = ((j >> place) << (place + 1)) | low
        for target, value in ((keep, mine), (send, 1 - mine)):
            index = base + (value << place)
            target[j] = (kept[index] + got[index].astype(F32)).astype(target.dtype)


def finish(kept0, got0, kept1, got1, out):
    out[0] = kept0[0] + got0[0].astype(F32)
    out[1] = kept1[0] + got1[0].astype(F32)


def shards(
    features,
    dest_owner,
    dest_slot,
    doc_ids,
    enc_weight,
    attn_in,
    attn_out,
    ffn_in,
    ffn_out,
    out_grad,
):
    rows_dev, width = features.shape
    group_axes = ("event", "pack")
    groups = lax.axis_size(group_axes)
    events = lax.axis_size("event")
    packs = lax.axis_size("pack")
    tensors = lax.axis_size("tensor")
    cols = attn_in.shape[2]
    comps = attn_in.shape[0]
    units = ffn_out.shape[0]
    where = jnp.stack([lax.axis_index(group_axes), lax.axis_index("tensor")]).astype(jnp.int32)
    d_out = out_grad[0]
    docs = doc_ids.reshape(tensors, 1, rows_dev)

    def near(value):
        return lax.ppermute(value, "tensor", [(i, i ^ 1) for i in range(tensors)])

    def far(value):
        return lax.ppermute(value, "tensor", [(i, i ^ 2) for i in range(tensors)])

    def crossed(value, k):
        return lax.ppermute(value, group_axes, [(i, i ^ k) for i in range(groups)])

    row_b = like((rows_dev, width), BF16)
    row_f = like((rows_dev, width), F32)

    mean_load = rows_dev // groups
    capacity = -(-(mean_load + mean_load // 2) // 8) * 8
    code = (dest_owner * rows_dev + dest_slot).reshape(1, rows_dev)
    *sends, place = run(
        functools.partial(route_send, capacity),
        [like((capacity, width + rows_dev), BF16)] * groups + [like((1, rows_dev), jnp.int32)],
        where,
        [code, features],
        flops=4 * 10**9,
        name="route_send",
    )
    order = sorted(range(1, groups), key=lambda k: (-(k % packs), k))
    ffn_in_near, ffn_out_near, attn_out_near = near(ffn_in), near(ffn_out), near(attn_out)
    early = {k: crossed(sends[k], k) for k in order[:2]}
    ffn_in_near, ffn_out_near, attn_out_near, *sends = tie(
        ffn_in_near, ffn_out_near, attn_out_near, *sends
    )
    crossing = early | {k: crossed(sends[k], k) for k in order[2:]}
    gots = [sends[0]] + [crossing[k] for k in range(1, groups)]
    mine, hot = run(
        route_recv,
        [row_b, like((groups * capacity, rows_dev), BF16)],
        None,
        gots,
        name="route_recv",
    )

    mine_far = far(mine)
    mine_near = near(mine)

    pair = 2 * rows_dev
    pre_a, act_a, packed, proj_a = run(
        encode_first,
        [
            like((pair, cols), F32),
            like((pair, width), BF16),
            row_b,
            like((comps, 2, rows_dev, cols), BF16),
        ],
        where,
        [mine, mine_near, enc_weight, attn_in],
        [pltpu.VMEM((pair, width), F32)],
        name="encode_first",
    )
    mine_far, proj_a = tie(mine_far, proj_a)
    mine_far, d_out_late = tie(mine_far, d_out)
    mine_both = near(mine_far)
    d_out_far = far(d_out_late)
    pre_b, act_b, packed_far, proj, attended, give, keep = run(
        attend_first,
        [
            like((pair, cols), F32),
            like((pair, width), BF16),
            row_b,
            like((comps, tensors, rows_dev, cols), BF16),
            like((tensors, rows_dev, cols), F32),
            like((pair, cols), BF16),
            like((pair, cols), BF16),
        ],
        where,
        [docs, mine_far, mine_both, proj_a, enc_weight, attn_in],
        [pltpu.VMEM((pair, width), F32)],
        name="attend_first",
    )
    take = near(give)
    take, d_out_far = tie(take, d_out_far)


    def out_part(index, name):
        return run(
            functools.partial(attn_out_part, index),
            [row_b],
            None,
            [keep, take, attn_out, attn_out_near],
            name=name,
        )[0]

    part_far = out_part(0, "attn_out_far")
    got_own = far(part_far)
    part_own = out_part(1, "attn_out_own")
    got_far = far(part_own)

    def feed(rows, cotangent, name):
        return run(
            ffn,
            [like((rows_dev, 2 * units), BF16), row_b],
            None,
            [rows, cotangent, ffn_in, ffn_in_near, ffn_out, ffn_out_near],
            name=name,
        )

    resid, normed2 = run(residual, [row_b, row_b], None, [packed, part_own, got_own], name="residual")
    hidden_own, back_own = feed(normed2, d_out, "ffn_own")
    got_far, back_own = tie(got_far, back_own)
    got_back_far = far(back_own)
    resid_far, normed2_far = run(
        residual, [row_b, row_b], None, [packed_far, part_far, got_far], name="residual_far"
    )
    hidden_far, back_far = feed(normed2_far, d_out_far, "ffn_far")
    got_back_own = far(back_far)

    (d_resid_far,) = run(
        resid_back, [row_b], None, [back_far, got_back_far, resid_far, d_out_far], name="resid_back_far"
    )
    d_resid_both = near(d_resid_far)
    block_f = like((tensors, rows_dev, cols), F32)
    block_b = like((tensors, rows_dev, cols), BF16)
    d_q, d_k, d_v, d_g = run(
        attn_back_first,
        [block_b, block_f, block_f, block_b],
        where,
        [docs, d_resid_far, d_resid_both, proj, attended, attn_out],
        name="attn_back_first",
    )
    got_back_own, d_q = tie(got_back_own, d_q)
    (d_resid,) = run(resid_back, [row_b], None, [back_own, got_back_own, resid, d_out], name="resid_back")
    d_resid_near = near(d_resid)
    give, *d_projected = run(
        attn_back_second,
        [like((pair, width), BF16)] + [block_b] * 4,
        where,
        [docs, d_resid, d_resid_near, proj, attended, attn_out, d_q, d_k, d_v, d_g, attn_in],
        [pltpu.VMEM((tensors, rows_dev, cols), F32)] * 2,
        name="attn_back_second",
    )
    take = near(give)
    (keep,) = run(
        attn_back_keep,
        [like((pair, width), F32)],
        None,
        [*d_projected, attn_in],
        name="attn_back_keep",
    )
    sum_far, sum_own = run(add_near, [row_b, row_b], None, [keep, take], name="add_near")
    got_own = far(sum_far)
    got_far = far(sum_own)
    (d_packed,) = run(packed_back, [row_b], None, [sum_own, got_own, packed, d_resid], name="packed_back")

    cot_near = near(d_packed)
    backs = run(
        functools.partial(back_send, events),
        [like((events * capacity, width), BF16)] * packs,
        None,
        [hot, d_packed],
        name="back_send",
    )
    over_pack = [backs[0]] + [crossed(backs[b], b) for b in range(1, packs)]
    part_f = like((width, cols), F32)
    part1, part0 = run(
        enc_grads_first,
        [part_f, part_f],
        where,
        [d_packed, cot_near, mine, mine_near, act_a, pre_a, enc_weight],
        name="enc_grads_first",
    )
    got_far, part1, part0 = tie(got_far, part1, part0)
    (cot_far,) = run(
        packed_back, [row_b], None, [sum_far, got_far, packed_far, d_resid_far], name="packed_back_far"
    )
    cot_both = near(cot_far)
    cot_both, *over_pack = tie(cot_both, *over_pack)
    back_own, *back_sends = run(
        lambda *refs: back_turn(*refs, events),
        [like((packs * capacity, width), BF16)] * events,
        None,
        over_pack,
        name="back_turn",
    )
    over_event = [back_own] + [crossed(v, (a + 1) * packs) for a, v in enumerate(back_sends)]

    cot_far, hidden_far = tie(cot_far, hidden_far)
    (out_far,) = run(
        ffn_out_far, [row_b], None, [hidden_far, ffn_out, ffn_out_near], name="ffn_out_far"
    )
    got_out = far(out_far)
    (packed_out,) = run(
        ffn_out_own, [row_b], None, [hidden_own, ffn_out, ffn_out_near, resid, got_out], name="ffn_out_own"
    )

    bits = list(range(groups.bit_length() - 1))
    pack_bits = bits[: packs.bit_length() - 1]
    event_bits = bits[len(pack_bits) :]
    size = width // groups
    total = [pltpu.VMEM((width, cols), F32)]

    def halves(remaining):
        shape = (2 ** (len(remaining) - 1), size, cols)
        return [like(shape, F32), like(shape, BF16)]

    def reduce_over(stages, start, name):
        remaining = list(bits)
        kept, send = start((tuple(remaining), stages[0]))
        got = crossed(send, 1 << stages[0])
        remaining.remove(stages[0])
        for bit in stages[1:]:
            kept, send = run(
                functools.partial(halve_again, tuple(remaining), bit),
                halves(remaining),
                where,
                [kept, got],
                name=name + str(bit),
            )
            got = crossed(send, 1 << bit)
            remaining.remove(bit)
        return kept, got

    def start1(setting):
        return run(
            functools.partial(enc_grad1_second, *setting),
            halves(bits),
            where,
            [cot_far, cot_both, act_b, part1],
            total,
            name="enc_grad1_second",
        )

    def start0(setting):
        return run(
            functools.partial(enc_grad0_second, *setting),
            halves(bits),
            where,
            [cot_far, cot_both, mine_far, mine_both, pre_b, enc_weight, part0],
            total,
            name="enc_grad0_second",
        )

    kept1, got1 = reduce_over(event_bits + pack_bits, start1, "halve1_")
    kept0, got0 = reduce_over(pack_bits[:1] + event_bits + pack_bits[1:], start0, "halve0_")
    (row_grad,) = run(
        back_recv,
        [row_b],
        None,
        [place] + over_event,
        name="back_recv",
    )
    (enc_grad,) = run(finish, [like((2, size, cols), F32)], None, [kept0, got0, kept1, got1], name="finish")
    return (packed_out[None], row_grad, enc_grad)


def solution(mesh):
    placed = (
        P(("event", "pack", "tensor"), None),
        P(("event", "pack", "tensor")),
        P(("event", "pack", "tensor")),
        P(("event", "pack"), None),
        P(),
        P(None, None, "tensor"),
        P("tensor", None),
        P(None, None, "tensor"),
        P("tensor", None),
        P(("event", "pack"), "tensor", None),
    )
    return jax.shard_map(
        shards,
        mesh=mesh,
        in_specs=placed,
        out_specs=(
            P(("event", "pack"), "tensor", None),
            P(("event", "pack", "tensor"), None),
            P(None, ("event", "pack"), "tensor"),
        ),
        check_vma=False,
    )
```

```python
import functools

import jax
import jax.numpy as jnp
from jax import lax
from jax.experimental import pallas as pl
from jax.experimental.pallas import tpu as pltpu
from jax.sharding import PartitionSpec as P

D = 1024
HEADS = 16
HEAD = D // HEADS
EPS = 1e-06
F32 = jnp.float32
BF16 = jnp.bfloat16
MIB = 1 << 20
CHUNK = 256


def dot(left, right, dims=((1,), (0,))):
    return lax.dot_general(left, right, (dims, ((), ())), preferred_element_type=F32)


NT = ((1,), (1,))
TN = ((0,), (0,))


def bf16(value):
    return value.astype(BF16)


def silu_grad(value, sigma):
    return sigma * (1.0 + value * (1.0 - sigma))


def norm_factor(wide):
    return lax.rsqrt(jnp.mean(wide * wide, axis=-1, keepdims=True) + EPS)


def norm_back(grad, normed, factor):
    return factor * (grad - normed * jnp.mean(grad * normed, axis=-1, keepdims=True))


def turned(row, rows):
    return jnp.broadcast_to(row.astype(F32), (rows, rows)).T


def like(shape, dtype):
    return jax.ShapeDtypeStruct(shape, dtype)


def run(body, outs, scalars, args, scratch=(), flops=0, name=None, limit=16, space=pltpu.VMEM):
    specs = [pl.BlockSpec(memory_space=space)] * len(args)
    operands = list(args)
    if scalars is not None:
        specs = [pl.BlockSpec(memory_space=pltpu.SMEM)] + specs
        operands = [scalars] + operands
    return pl.pallas_call(
        body,
        out_shape=list(outs),
        in_specs=specs,
        out_specs=[pl.BlockSpec(memory_space=pltpu.VMEM)] * len(outs),
        scratch_shapes=list(scratch),
        compiler_params=pltpu.CompilerParams(vmem_limit_bytes=limit * MIB),
        cost_estimate=pl.CostEstimate(flops=flops, bytes_accessed=0, transcendentals=0),
        name=name,
    )(*operands)


def tie(*values):
    return lax.optimization_barrier(values)


def route_send(capacity, where, code, features, *outs):
    sends, place_ref = outs[:-1], outs[-1]
    groups = len(sends)
    rows, width = features.shape
    shift = rows.bit_length() - 1
    o_row = code[...] >> shift
    slot = code[...] & (rows - 1)
    o_col = turned(o_row, rows)
    i = lax.broadcasted_iota(jnp.int32, (rows, rows), 0)
    j = lax.broadcasted_iota(jnp.int32, (rows, rows), 1)
    earlier = jnp.where((o_col == o_row.astype(F32)) & (i < j), 1.0, 0.0)
    rank = jnp.sum(earlier, axis=0, keepdims=True).astype(jnp.int32)
    place = (o_row ^ where[0]) * capacity + rank
    place_ref[...] = place
    spots = lax.broadcasted_iota(jnp.int32, (groups * capacity, rows), 0)
    hot = jnp.where(spots == place, 1.0, 0.0).astype(BF16)
    big = dot(hot, features[...])
    tags = dot(hot, bf16(turned(slot + 1, rows)))
    for k in range(groups):
        part = slice(k * capacity, (k + 1) * capacity)
        sends[k][:, :width] = bf16(big[part])
        sends[k][:, width:] = bf16(tags[part])


def route_recv(*refs):
    gots, (rows_ref, hot_ref) = refs[:-2], refs[-2:]
    rows, width = rows_ref.shape
    got = jnp.concatenate([g[...].astype(F32) for g in gots], axis=0)
    lanes = lax.broadcasted_iota(jnp.int32, (got.shape[0], rows), 1) + 1
    hot = jnp.where(got[:, width:] == lanes.astype(F32), 1.0, 0.0).astype(BF16)
    hot_ref[...] = hot
    rows_ref[...] = bf16(dot(hot, bf16(got[:, :width]), TN))


def back_send(events, hot, d_packed, *sends):
    packs = len(sends)
    capacity = hot.shape[0] // (events * packs)
    big = dot(hot[...], d_packed[...])
    for b in range(packs):
        parts = [
            big[(a * packs + b) * capacity : (a * packs + b + 1) * capacity] for a in range(events)
        ]
        sends[b][...] = bf16(jnp.concatenate(parts, axis=0))


def back_turn(*refs):
    events = refs[-1]
    refs = refs[:-1]
    packs = len(refs) - (events - 1) - 1
    gots, own, sends = refs[:packs], refs[packs], refs[packs + 1 :]
    wide = [g[...].astype(F32) for g in gots]
    capacity = wide[0].shape[0] // events
    for a, target in enumerate((own, *sends)):
        parts = [w[a * capacity : (a + 1) * capacity] for w in wide]
        target[...] = bf16(jnp.concatenate(parts, axis=0))


def back_recv(place, *refs):
    gots, out = refs[:-1], refs[-1]
    got = jnp.concatenate([g[...] for g in gots], axis=0)
    spots = lax.broadcasted_iota(jnp.int32, (got.shape[0], out.shape[0]), 0)
    hot = jnp.where(spots == place[...], 1.0, 0.0).astype(BF16)
    out[...] = bf16(dot(hot, got, TN))


def encode(where, rows, enc, w_in, pre_all, pre_ref, act_ref, packed_ref, store):
    width = rows.shape[1]
    cols = pre_ref.shape[1]
    for n in range(width // CHUNK):
        part = slice(n * CHUNK, (n + 1) * CHUNK)
        pre = dot(rows, enc[0, :, part])
        pre_all[:, part] = pre
        act_ref[:, part] = bf16(pre * jax.nn.sigmoid(pre))
    pre_ref[...] = pre_all[:, pl.ds(pl.multiple_of(where[1] * cols, cols), cols)]
    packed = bf16(dot(act_ref[...], enc[1]))
    packed_ref[...] = packed[: packed_ref.shape[0]]
    wide = packed.astype(F32)
    normed = bf16(wide * norm_factor(wide))
    for c in range(w_in.shape[0]):
        store(c, bf16(dot(normed, w_in[c])))


def encode_first(where, first, second, enc, w_in, pre_ref, act_ref, packed_ref, proj_ref, pre_all):
    rows = jnp.concatenate([first[...], second[...]], axis=0)
    half = first.shape[0]

    def store(c, value):
        proj_ref[c, 0] = value[:half]
        proj_ref[c, 1] = value[half:]

    encode(where, rows, enc, w_in, pre_all, pre_ref, act_ref, packed_ref, store)


def window(where, docs, r, rows):
    t = where[1]
    b = t ^ r
    ahead = jnp.where(b > 0, (b - 1) ^ t, r)
    doc_q = turned(docs[b], rows)
    doc_own = docs[b].astype(F32)
    doc_ahead = docs[jnp.maximum(b - 1, 0)].astype(F32)
    i = lax.broadcasted_iota(jnp.int32, (rows, rows), 0)
    j = lax.broadcasted_iota(jnp.int32, (rows, rows), 1)
    own = jnp.where((doc_q == doc_own) & (j <= i), 1.0, 0.0)
    prior = jnp.where(doc_q == doc_ahead, 1.0, 0.0) * jnp.where(b > 0, 1.0, 0.0)
    allowed = jnp.concatenate([prior, own], axis=1)
    root_inv = lax.rsqrt(jnp.sum(allowed, axis=1, keepdims=True))
    return ahead, allowed, root_inv


def head_masks(cols):
    lane = lax.broadcasted_iota(jnp.int32, (1, cols), 1) // HEAD
    return [jnp.where(lane == h, 1.0, 0.0) for h in range(cols // HEAD)]


def spread(value, masks):
    return jnp.concatenate([value * bf16(m) for m in masks], axis=0)


def collect(value, masks):
    rows = value.shape[0] // len(masks)
    total = None
    for h, m in enumerate(masks):
        part = value[h * rows : (h + 1) * rows] * m
        total = part if total is None else total + part
    return total


def attend_first(
    where, docs, third, fourth, proj_a, enc, w_in,
    pre_ref, act_ref, packed_ref, proj_ref, att_ref, give_ref, keep_ref, pre_all,
):
    rows = jnp.concatenate([third[...], fourth[...]], axis=0)
    half = third.shape[0]
    cols = proj_a.shape[-1]
    proj_ref[:, 0:2] = proj_a[...]

    def store(c, value):
        proj_ref[c, 2] = value[:half]
        proj_ref[c, 3] = value[half:]

    encode(where, rows, enc, w_in, pre_all, pre_ref, act_ref, packed_ref, store)
    masks = head_masks(cols)
    for r, (target, place) in enumerate(((keep_ref, 1), (give_ref, 1), (keep_ref, 0), (give_ref, 0))):
        ahead, allowed, root_inv = window(where, docs, r, half)
        keys = jnp.concatenate([proj_ref[1, ahead], proj_ref[1, r]], axis=0)
        values = jnp.concatenate([proj_ref[2, ahead], proj_ref[2, r]], axis=0)
        many = jnp.concatenate([allowed] * len(masks), axis=0)
        scores = dot(spread(proj_ref[0, r], masks), keys, NT) * HEAD ** (-0.5)
        weights = bf16(scores * jax.nn.sigmoid(scores) * many)
        attended = collect(dot(weights, values), masks) * root_inv
        gate = proj_ref[3, r].astype(F32)
        att_ref[r] = attended
        target[place * half : (place + 1) * half, :] = bf16(attended * gate * jax.nn.sigmoid(gate))


def attn_out_part(index, keep, take, w_own, w_near, out):
    rows = out.shape[0]
    part = slice(index * rows, (index + 1) * rows)
    out[...] = bf16(dot(keep[part, :], w_own[...]) + dot(take[part, :], w_near[...]))


def residual(packed, part, got, resid_ref, normed_ref):
    resid = bf16(packed[...].astype(F32) + (part[...].astype(F32) + got[...].astype(F32)))
    resid_ref[...] = resid
    wide = resid.astype(F32)
    normed_ref[...] = bf16(wide * norm_factor(wide))


def ffn(rows_ref, d_out_ref, in_a, in_b, out_a, out_b, hidden_ref, back_ref):
    rows = rows_ref[...]
    cotangent = d_out_ref[...]
    units = out_a.shape[0]
    back = None
    for index, (w_in, w_out) in enumerate(((in_a, out_a), (in_b, out_b))):
        for n in range(units // CHUNK):
            part = slice(n * CHUNK, (n + 1) * CHUNK)
            d_hidden = dot(cotangent, w_out[part, :], NT)
            gate = dot(rows, w_in[0, :, part])
            upper = dot(rows, w_in[1, :, part])
            sigma = jax.nn.sigmoid(gate)
            silu = gate * sigma
            hidden_ref[:, index * units + n * CHUNK : index * units + (n + 1) * CHUNK] = bf16(silu * upper)
            d_gate = bf16(d_hidden * upper * silu_grad(gate, sigma))
            d_upper = bf16(d_hidden * silu)
            term = dot(d_gate, w_in[0, :, part], NT) + dot(d_upper, w_in[1, :, part], NT)
            back = term if back is None else back + term
    back_ref[...] = back.astype(back_ref.dtype)


def ffn_out_far(hidden, w_a, w_b, out):
    units = w_a.shape[0]
    out[...] = bf16(dot(hidden[:, :units], w_a[...]) + dot(hidden[:, units:], w_b[...]))


def ffn_out_own(hidden, w_a, w_b, resid, got, out):
    units = w_a.shape[0]
    total = dot(hidden[:, :units], w_a[...]) + dot(hidden[:, units:], w_b[...])
    out[...] = bf16(resid[...].astype(F32) + total + got[...].astype(F32))


def store_halves(value, out, halves):
    out[...] = value
    rows = value.shape[0] // max(len(halves), 1)
    for n, target in enumerate(halves):
        target[...] = value[n * rows : (n + 1) * rows]


def resid_back(back, got, resid, d_out, out, *halves):
    wide = resid[...].astype(F32)
    factor = norm_factor(wide)
    grad = back[...].astype(F32) + got[...].astype(F32)
    store_halves(bf16(d_out[...].astype(F32) + norm_back(grad, wide * factor, factor)), out, halves)


def attend_back(where, docs, d_resid, r, proj_ref, att_ref, w_out, masks, d_q, d_k, d_v, d_g):
    half = d_resid.shape[0]
    scale = HEAD ** (-0.5)
    ahead, allowed, root_inv = window(where, docs, r, half)
    gate = proj_ref[3, r].astype(F32)
    sigma_g = jax.nn.sigmoid(gate)
    d_gated = dot(d_resid, w_out, NT)
    d_att = bf16(d_gated * (gate * sigma_g) * root_inv)
    d_g[r] = bf16(d_gated * att_ref[r] * silu_grad(gate, sigma_g))
    keys = jnp.concatenate([proj_ref[1, ahead], proj_ref[1, r]], axis=0)
    values = jnp.concatenate([proj_ref[2, ahead], proj_ref[2, r]], axis=0)
    many = jnp.concatenate([allowed] * len(masks), axis=0)
    query = spread(proj_ref[0, r], masks)
    d_att_m = spread(d_att, masks)
    scores = dot(query, keys, NT) * scale
    sigma = jax.nn.sigmoid(scores)
    weights = bf16(scores * sigma * many)
    d_weights = dot(d_att_m, values, NT)
    d_scores = bf16(d_weights * silu_grad(scores, sigma) * many)
    d_q[r] = bf16(collect(dot(d_scores, keys), masks) * scale)
    d_keys = dot(d_scores, query, TN) * scale
    d_values = dot(weights, d_att_m, TN)
    d_k[ahead] += d_keys[:half]
    d_k[r] += d_keys[half:]
    d_v[ahead] += d_values[:half]
    d_v[r] += d_values[half:]


def joined(refs):
    return jnp.concatenate([r[...] for r in refs], axis=0)


def attn_back_first(where, docs, third, fourth_a, fourth_b, proj, att, w_out, d_q, d_k, d_v, d_g):
    masks = head_masks(w_out.shape[0])
    d_k[...] = jnp.zeros_like(d_k)
    d_v[...] = jnp.zeros_like(d_v)
    for r, rows in ((2, [third]), (3, [fourth_a, fourth_b])):
        attend_back(where, docs, joined(rows), r, proj, att, w_out[...], masks, d_q, d_k, d_v, d_g)


def back_norm(grads, w_in, first, second):
    total = None
    for c, grad in enumerate(grads):
        left = jnp.concatenate([grad[first], grad[second]], axis=0)
        term = dot(left, w_in[c], NT)
        total = term if total is None else total + term
    return total


def attn_back_second(
    where, docs, first, second, proj, att, w_out, d_q_far, d_k_far, d_v_far, d_g_far, w_in,
    give_ref, d_q, d_k, d_v, d_g, sum_k, sum_v,
):
    masks = head_masks(w_out.shape[0])
    d_q[2:4] = d_q_far[2:4]
    d_g[2:4] = d_g_far[2:4]
    sum_k[...] = d_k_far[...]
    sum_v[...] = d_v_far[...]
    for r, rows in ((0, first), (1, second)):
        attend_back(where, docs, rows[...], r, proj, att, w_out[...], masks, d_q, sum_k, sum_v, d_g)
    d_k[...] = bf16(sum_k[...])
    d_v[...] = bf16(sum_v[...])
    give_ref[...] = bf16(back_norm((d_q, d_k, d_v, d_g), w_in, 3, 1))


def attn_back_keep(d_q, d_k, d_v, d_g, w_in, keep_ref):
    keep_ref[...] = back_norm((d_q, d_k, d_v, d_g), w_in, 2, 0)


def add_near(keep, take, out_far, out_own):
    half = out_far.shape[0]
    out_far[...] = bf16(keep[:half, :] + take[:half, :].astype(F32))
    out_own[...] = bf16(keep[half:, :] + take[half:, :].astype(F32))


def packed_back(part, got, packed, d_resid, out, *halves):
    wide = packed[...].astype(F32)
    factor = norm_factor(wide)
    grad = part[...].astype(F32) + got[...].astype(F32)
    store_halves(bf16(d_resid[...].astype(F32) + norm_back(grad, wide * factor, factor)), out, halves)


def column_of(ref, index, cols):
    return ref[:, pl.ds(pl.multiple_of(index * cols, cols), cols)]


def rows_term(act_refs, cot):
    return dot(jnp.concatenate([a[...] for a in act_refs], axis=0), cot, TN)


def first_cot(where, cots, pre, enc):
    cols = pre.shape[1]
    cot = joined(cots)
    value = pre[...]
    w1_rows = enc[1, pl.ds(pl.multiple_of(where[1] * cols, cols), cols), :]
    return bf16(dot(cot, w1_rows, NT) * silu_grad(value, jax.nn.sigmoid(value)))


def cot_columns(where, cots, cols):
    return jnp.concatenate([column_of(c, where[1], cols) for c in cots], axis=0)


def enc_grads_first(where, *refs):
    cots, (act0_a, act0_b, act1, pre, enc, part1, part0) = refs[:-7], refs[-7:]
    cols = pre.shape[1]
    part1[...] = rows_term([act1], cot_columns(where, cots, cols))
    part0[...] = rows_term([act0_a, act0_b], first_cot(where, cots, pre, enc))


def halve(where, bits, bit, total, keep, send):
    place = bits.index(bit)
    count, size, _ = keep.shape
    mine = (where[0] >> bit) & 1
    for j in range(count):
        low = j & ((1 << place) - 1)
        base = ((j >> place) << (place + 1)) | low
        for target, value in ((keep, mine), (send, 1 - mine)):
            index = base + (value << place)
            rows = total[pl.ds(pl.multiple_of(index * size, size), size), :]
            target[j] = rows.astype(target.dtype)


def enc_grad1_second(bits, bit, where, *refs):
    cots, (act1, part1, keep, send, total) = refs[:-5], refs[-5:]
    total[...] = rows_term([act1], cot_columns(where, cots, part1.shape[1])) + part1[...]
    halve(where, bits, bit, total, keep, send)


def enc_grad0_second(bits, bit, where, *refs):
    cots, (act0_a, act0_b, pre, enc, part0, keep, send, total) = refs[:-8], refs[-8:]
    total[...] = rows_term([act0_a, act0_b], first_cot(where, cots, pre, enc)) + part0[...]
    halve(where, bits, bit, total, keep, send)


def halve_again(bits, bit, where, kept, got, keep, send):
    place = bits.index(bit)
    mine = (where[0] >> bit) & 1
    for j in range(keep.shape[0]):
        low = j & ((1 << place) - 1)
        base = ((j >> place) << (place + 1)) | low
        for target, value in ((keep, mine), (send, 1 - mine)):
            index = base + (value << place)
            target[j] = (kept[index] + got[index].astype(F32)).astype(target.dtype)


def finish(kept0, got0, kept1, got1, out):
    out[0] = kept0[0] + got0[0].astype(F32)
    out[1] = kept1[0] + got1[0].astype(F32)


def shards(
    features,
    dest_owner,
    dest_slot,
    doc_ids,
    enc_weight,
    attn_in,
    attn_out,
    ffn_in,
    ffn_out,
    out_grad,
):
    rows_dev, width = features.shape
    group_axes = ("event", "pack")
    groups = lax.axis_size(group_axes)
    events = lax.axis_size("event")
    packs = lax.axis_size("pack")
    tensors = lax.axis_size("tensor")
    cols = attn_in.shape[2]
    comps = attn_in.shape[0]
    units = ffn_out.shape[0]
    where = jnp.stack([lax.axis_index(group_axes), lax.axis_index("tensor")]).astype(jnp.int32)
    d_out = out_grad[0]
    docs = doc_ids.reshape(tensors, 1, rows_dev)

    def near(value):
        return lax.ppermute(value, "tensor", [(i, i ^ 1) for i in range(tensors)])

    def far(value):
        return lax.ppermute(value, "tensor", [(i, i ^ 2) for i in range(tensors)])

    def crossed(value, k):
        return lax.ppermute(value, group_axes, [(i, i ^ k) for i in range(groups)])

    row_b = like((rows_dev, width), BF16)
    row_f = like((rows_dev, width), F32)

    mean_load = rows_dev // groups
    capacity = -(-(mean_load + mean_load // 2) // 8) * 8
    code = (dest_owner * rows_dev + dest_slot).reshape(1, rows_dev)
    *sends, place = run(
        functools.partial(route_send, capacity),
        [like((capacity, width + rows_dev), BF16)] * groups + [like((1, rows_dev), jnp.int32)],
        where,
        [code, features],
        flops=4 * 10**9,
        name="route_send",
    )
    order = sorted(range(1, groups), key=lambda k: (-(k % packs), k))
    ffn_in_near, ffn_out_near, d_out_far = near(ffn_in), near(ffn_out), far(d_out)
    early = {k: crossed(sends[k], k) for k in order[:2]}
    ffn_in_near, ffn_out_near, *sends = tie(ffn_in_near, ffn_out_near, *sends)
    crossing = early | {k: crossed(sends[k], k) for k in order[2:]}
    gots = [sends[0]] + [crossing[k] for k in range(1, groups)]
    d_out_far, *gots = tie(d_out_far, *gots)
    mine, hot = run(
        route_recv,
        [row_b, like((groups * capacity, rows_dev), BF16)],
        None,
        gots,
        name="route_recv",
    )

    mine_far = far(mine)
    mine_near = near(mine)

    pair = 2 * rows_dev
    pre_a, act_a, packed, proj_a = run(
        encode_first,
        [
            like((pair, cols), F32),
            like((pair, width), BF16),
            row_b,
            like((comps, 2, rows_dev, cols), BF16),
        ],
        where,
        [mine, mine_near, enc_weight, attn_in],
        [pltpu.VMEM((pair, width), F32)],
        name="encode_first",
    )
    mine_far, proj_a = tie(mine_far, proj_a)
    mine_far, attn_out_late = tie(mine_far, attn_out)
    mine_both = near(mine_far)
    attn_out_near = near(attn_out_late)
    pre_b, act_b, packed_far, proj, attended, give, keep = run(
        attend_first,
        [
            like((pair, cols), F32),
            like((pair, width), BF16),
            row_b,
            like((comps, tensors, rows_dev, cols), BF16),
            like((tensors, rows_dev, cols), F32),
            like((pair, cols), BF16),
            like((pair, cols), BF16),
        ],
        where,
        [docs, mine_far, mine_both, proj_a, enc_weight, attn_in],
        [pltpu.VMEM((pair, width), F32)],
        name="attend_first",
    )
    take = near(give)


    def out_part(index, name):
        return run(
            functools.partial(attn_out_part, index),
            [row_b],
            None,
            [keep, take, attn_out, attn_out_near],
            name=name,
        )[0]

    part_far = out_part(0, "attn_out_far")
    got_own = far(part_far)
    part_own = out_part(1, "attn_out_own")
    got_far = far(part_own)

    def feed(rows, cotangent, name):
        return run(
            ffn,
            [like((rows_dev, 2 * units), BF16), row_b],
            None,
            [rows, cotangent, ffn_in, ffn_in_near, ffn_out, ffn_out_near],
            name=name,
        )

    resid, normed2 = run(residual, [row_b, row_b], None, [packed, part_own, got_own], name="residual")
    hidden_own, back_own = feed(normed2, d_out, "ffn_own")
    got_far, back_own = tie(got_far, back_own)
    got_back_far = far(back_own)
    resid_far, normed2_far = run(
        residual, [row_b, row_b], None, [packed_far, part_far, got_far], name="residual_far"
    )
    hidden_far, back_far = feed(normed2_far, d_out_far, "ffn_far")
    got_back_own = far(back_far)

    pieces = 2
    piece_b = like((rows_dev // pieces, width), BF16)
    d_resid_far, *halves = run(
        resid_back,
        [row_b] + [piece_b] * pieces,
        None,
        [back_far, got_back_far, resid_far, d_out_far],
        name="resid_back_far",
    )
    d_resid_both = [near(h) for h in halves]
    block_f = like((tensors, rows_dev, cols), F32)
    block_b = like((tensors, rows_dev, cols), BF16)
    d_q, d_k, d_v, d_g = run(
        attn_back_first,
        [block_b, block_f, block_f, block_b],
        where,
        [docs, d_resid_far, *d_resid_both, proj, attended, attn_out],
        name="attn_back_first",
    )
    got_back_own, d_q = tie(got_back_own, d_q)
    (d_resid,) = run(resid_back, [row_b], None, [back_own, got_back_own, resid, d_out], name="resid_back")
    d_resid_near = near(d_resid)
    give, *d_projected = run(
        attn_back_second,
        [like((pair, width), BF16)] + [block_b] * 4,
        where,
        [docs, d_resid, d_resid_near, proj, attended, attn_out, d_q, d_k, d_v, d_g, attn_in],
        [pltpu.VMEM((tensors, rows_dev, cols), F32)] * 2,
        name="attn_back_second",
    )
    take = near(give)
    (keep,) = run(
        attn_back_keep,
        [like((pair, width), F32)],
        None,
        [*d_projected, attn_in],
        name="attn_back_keep",
    )
    sum_far, sum_own = run(add_near, [row_b, row_b], None, [keep, take], name="add_near")
    got_own = far(sum_far)
    got_far = far(sum_own)
    d_packed, *halves = run(
        packed_back,
        [row_b] + [piece_b] * pieces,
        None,
        [sum_own, got_own, packed, d_resid],
        name="packed_back",
    )

    cot_near = [near(h) for h in halves]
    backs = run(
        functools.partial(back_send, events),
        [like((events * capacity, width), BF16)] * packs,
        None,
        [hot, d_packed],
        name="back_send",
    )
    over_pack = [backs[0]] + [crossed(backs[b], b) for b in range(1, packs)]
    part_f = like((width, cols), F32)
    part1, part0 = run(
        enc_grads_first,
        [part_f, part_f],
        where,
        [d_packed, *cot_near, mine, mine_near, act_a, pre_a, enc_weight],
        name="enc_grads_first",
    )
    got_far, part1, part0, *over_pack = tie(got_far, part1, part0, *over_pack)
    (cot_far,) = run(
        packed_back, [row_b], None, [sum_far, got_far, packed_far, d_resid_far], name="packed_back_far"
    )
    cot_both = near(cot_far)
    back_own, *back_sends = run(
        lambda *refs: back_turn(*refs, events),
        [like((packs * capacity, width), BF16)] * events,
        None,
        over_pack,
        name="back_turn",
    )
    over_event = [back_own] + [crossed(v, (a + 1) * packs) for a, v in enumerate(back_sends)]

    cot_far, hidden_far = tie(cot_far, hidden_far)
    (out_far,) = run(
        ffn_out_far, [row_b], None, [hidden_far, ffn_out, ffn_out_near], name="ffn_out_far"
    )
    got_out = far(out_far)
    (packed_out,) = run(
        ffn_out_own, [row_b], None, [hidden_own, ffn_out, ffn_out_near, resid, got_out], name="ffn_out_own"
    )

    bits = list(range(groups.bit_length() - 1))
    pack_bits = bits[: packs.bit_length() - 1]
    event_bits = bits[len(pack_bits) :]
    size = width // groups
    total = [pltpu.VMEM((width, cols), F32)]

    def halves(remaining):
        shape = (2 ** (len(remaining) - 1), size, cols)
        return [like(shape, F32), like(shape, BF16)]

    def reduce_over(stages, start, name):
        nonlocal over_event
        remaining = list(bits)
        kept, send = start((tuple(remaining), stages[0]))
        got = crossed(send, 1 << stages[0])
        if stages[0] in event_bits:
            got, *over_event = tie(got, *over_event)
        remaining.remove(stages[0])
        for bit in stages[1:]:
            kept, send = run(
                functools.partial(halve_again, tuple(remaining), bit),
                halves(remaining),
                where,
                [kept, got],
                name=name + str(bit),
            )
            got = crossed(send, 1 << bit)
            remaining.remove(bit)
        return kept, got

    def start1(setting):
        return run(
            functools.partial(enc_grad1_second, *setting),
            halves(bits),
            where,
            [cot_far, cot_both, act_b, part1],
            total,
            name="enc_grad1_second",
        )

    def start0(setting):
        return run(
            functools.partial(enc_grad0_second, *setting),
            halves(bits),
            where,
            [cot_far, cot_both, mine_far, mine_both, pre_b, enc_weight, part0],
            total,
            name="enc_grad0_second",
        )

    kept1, got1 = reduce_over(event_bits + pack_bits, start1, "halve1_")
    kept0, got0 = reduce_over(pack_bits[:1] + event_bits + pack_bits[1:], start0, "halve0_")
    (row_grad,) = run(
        back_recv,
        [row_b],
        None,
        [place] + over_event,
        name="back_recv",
    )
    (enc_grad,) = run(finish, [like((2, size, cols), F32)], None, [kept0, got0, kept1, got1], name="finish")
    return (packed_out[None], row_grad, enc_grad)


def solution(mesh):
    placed = (
        P(("event", "pack", "tensor"), None),
        P(("event", "pack", "tensor")),
        P(("event", "pack", "tensor")),
        P(("event", "pack"), None),
        P(),
        P(None, None, "tensor"),
        P("tensor", None),
        P(None, None, "tensor"),
        P("tensor", None),
        P(("event", "pack"), "tensor", None),
    )
    return jax.shard_map(
        shards,
        mesh=mesh,
        in_specs=placed,
        out_specs=(
            P(("event", "pack"), "tensor", None),
            P(("event", "pack", "tensor"), None),
            P(None, ("event", "pack"), "tensor"),
        ),
        check_vma=False,
    )
```

```python
import functools

import jax
import jax.numpy as jnp
from jax import lax
from jax.experimental import pallas as pl
from jax.experimental.pallas import tpu as pltpu
from jax.sharding import PartitionSpec as P

D = 1024
HEADS = 16
HEAD = D // HEADS
EPS = 1e-06
F32 = jnp.float32
BF16 = jnp.bfloat16
MIB = 1 << 20
CHUNK = 256


def dot(left, right, dims=((1,), (0,))):
    return lax.dot_general(left, right, (dims, ((), ())), preferred_element_type=F32)


NT = ((1,), (1,))
TN = ((0,), (0,))


def bf16(value):
    return value.astype(BF16)


def silu_grad(value, sigma):
    return sigma * (1.0 + value * (1.0 - sigma))


def norm_factor(wide):
    return lax.rsqrt(jnp.mean(wide * wide, axis=-1, keepdims=True) + EPS)


def norm_back(grad, normed, factor):
    return factor * (grad - normed * jnp.mean(grad * normed, axis=-1, keepdims=True))


def turned(row, rows):
    return jnp.broadcast_to(row.astype(F32), (rows, rows)).T


def like(shape, dtype):
    return jax.ShapeDtypeStruct(shape, dtype)


def run(body, outs, args, scratch=(), flops=0, name=None):
    return pl.pallas_call(
        body,
        out_shape=list(outs),
        in_specs=[pl.BlockSpec(memory_space=pltpu.VMEM)] * len(args),
        out_specs=[pl.BlockSpec(memory_space=pltpu.VMEM)] * len(outs),
        scratch_shapes=list(scratch),
        compiler_params=pltpu.CompilerParams(vmem_limit_bytes=16 * MIB),
        cost_estimate=pl.CostEstimate(flops=flops, bytes_accessed=0, transcendentals=0),
        name=name,
    )(*args)


def group_index():
    return lax.axis_index("event") * lax.axis_size("pack") + lax.axis_index("pack")


def tensor_index():
    return lax.axis_index("tensor")


def tie(*values):
    return lax.optimization_barrier(values)


def route_send(capacity, order, code, features, *outs):
    sends, place_ref = outs[:-1], outs[-1]
    groups = len(sends)
    rows, width = features.shape
    shift = rows.bit_length() - 1
    o_row = code[...] >> shift
    slot = code[...] & (rows - 1)
    o_col = turned(o_row, rows)
    i = lax.broadcasted_iota(jnp.int32, (rows, rows), 0)
    j = lax.broadcasted_iota(jnp.int32, (rows, rows), 1)
    earlier = jnp.where((o_col == o_row.astype(F32)) & (i < j), 1.0, 0.0)
    rank = jnp.sum(earlier, axis=0, keepdims=True).astype(jnp.int32)
    place_ref[...] = o_row * capacity + rank
    place = (o_row ^ group_index()) * capacity + rank
    spots = lax.broadcasted_iota(jnp.int32, (groups * capacity, rows), 0)
    hot = jnp.where(spots == place, 1.0, 0.0).astype(BF16)
    big = dot(hot, features[...])
    tags = dot(hot, bf16(turned(slot + 1, rows)))
    for k, send in zip(order, sends):
        part = slice(k * capacity, (k + 1) * capacity)
        send[:, :width] = bf16(big[part])
        send[:, width:] = bf16(tags[part])


def route_recv(*refs):
    gots, (rows_ref, hot_ref) = refs[:-2], refs[-2:]
    rows, width = rows_ref.shape
    got = jnp.concatenate([g[...].astype(F32) for g in gots], axis=0)
    lanes = lax.broadcasted_iota(jnp.int32, (got.shape[0], rows), 1) + 1
    hot = jnp.where(got[:, width:] == lanes.astype(F32), 1.0, 0.0).astype(BF16)
    hot_ref[...] = hot
    rows_ref[...] = bf16(dot(hot, bf16(got[:, :width]), TN))


def back_send(order, hot, d_packed, out):
    capacity = out.shape[1]
    big = dot(hot[...], d_packed[...])
    for n, k in enumerate(order):
        out[group_index() ^ k] = bf16(big[n * capacity : (n + 1) * capacity])


def back_recv(place, got_ref, out):
    got = jnp.concatenate([got_ref[k].astype(F32) for k in range(got_ref.shape[0])], axis=0)
    spots = lax.broadcasted_iota(jnp.int32, (got.shape[0], out.shape[0]), 0)
    hot = jnp.where(spots == place[...], 1.0, 0.0).astype(BF16)
    out[...] = bf16(dot(hot, bf16(got), TN))


def encode(rows, enc, w_in, pre_all, pre_ref, act_ref, packed_ref, store):
    width = rows.shape[1]
    cols = pre_ref.shape[1]
    for n in range(width // CHUNK):
        part = slice(n * CHUNK, (n + 1) * CHUNK)
        pre = dot(rows, enc[0, :, part])
        pre_all[:, part] = pre
        act_ref[:, part] = bf16(pre * jax.nn.sigmoid(pre))
    pre_ref[...] = pre_all[:, pl.ds(pl.multiple_of(tensor_index() * cols, cols), cols)]
    packed = bf16(dot(act_ref[...], enc[1]))
    packed_ref[...] = packed[: packed_ref.shape[0]]
    wide = packed.astype(F32)
    normed = bf16(wide * norm_factor(wide))
    for c in range(w_in.shape[0]):
        store(c, bf16(dot(normed, w_in[c])))


def encode_first(first, second, enc, w_in, pre_ref, act_ref, packed_ref, proj_ref, pre_all):
    rows = jnp.concatenate([first[...], second[...]], axis=0)
    half = first.shape[0]

    def store(c, value):
        proj_ref[c, 0] = value[:half]
        proj_ref[c, 1] = value[half:]

    encode(rows, enc, w_in, pre_all, pre_ref, act_ref, packed_ref, store)


def window(docs, r, rows):
    t = tensor_index()
    b = t ^ r
    ahead = jnp.where(b > 0, (b - 1) ^ t, r)
    doc_q = turned(docs[b], rows)
    doc_own = docs[b].astype(F32)
    doc_ahead = docs[jnp.maximum(b - 1, 0)].astype(F32)
    i = lax.broadcasted_iota(jnp.int32, (rows, rows), 0)
    j = lax.broadcasted_iota(jnp.int32, (rows, rows), 1)
    own = jnp.where((doc_q == doc_own) & (j <= i), 1.0, 0.0)
    prior = jnp.where(doc_q == doc_ahead, 1.0, 0.0) * jnp.where(b > 0, 1.0, 0.0)
    allowed = jnp.concatenate([prior, own], axis=1)
    root_inv = lax.rsqrt(jnp.sum(allowed, axis=1, keepdims=True))
    return ahead, allowed, root_inv


def head_masks(cols):
    lane = lax.broadcasted_iota(jnp.int32, (1, cols), 1) // HEAD
    return [jnp.where(lane == h, 1.0, 0.0) for h in range(cols // HEAD)]


def spread(value, masks):
    return jnp.concatenate([value * bf16(m) for m in masks], axis=0)


def collect(value, masks):
    rows = value.shape[0] // len(masks)
    total = None
    for h, m in enumerate(masks):
        part = value[h * rows : (h + 1) * rows] * m
        total = part if total is None else total + part
    return total


def attend_first(
    docs, third, fourth, proj_a, enc, w_in,
    pre_ref, act_ref, packed_ref, proj_ref, att_ref, give_ref, keep_ref, pre_all,
):
    rows = jnp.concatenate([third[...], fourth[...]], axis=0)
    half = third.shape[0]
    cols = proj_a.shape[-1]
    proj_ref[:, 0:2] = proj_a[...]

    def store(c, value):
        proj_ref[c, 2] = value[:half]
        proj_ref[c, 3] = value[half:]

    encode(rows, enc, w_in, pre_all, pre_ref, act_ref, packed_ref, store)
    masks = head_masks(cols)
    for r, (target, place) in enumerate(((keep_ref, 1), (give_ref, 1), (keep_ref, 0), (give_ref, 0))):
        ahead, allowed, root_inv = window(docs, r, half)
        keys = jnp.concatenate([proj_ref[1, ahead], proj_ref[1, r]], axis=0)
        values = jnp.concatenate([proj_ref[2, ahead], proj_ref[2, r]], axis=0)
        many = jnp.concatenate([allowed] * len(masks), axis=0)
        scores = dot(spread(proj_ref[0, r], masks), keys, NT) * HEAD ** (-0.5)
        weights = bf16(scores * jax.nn.sigmoid(scores) * many)
        attended = collect(dot(weights, values), masks) * root_inv
        gate = proj_ref[3, r].astype(F32)
        att_ref[r] = attended
        target[place * half : (place + 1) * half, :] = bf16(attended * gate * jax.nn.sigmoid(gate))


def attn_out_part(index, keep, take, w_own, w_near, out):
    rows = out.shape[0]
    part = slice(index * rows, (index + 1) * rows)
    out[...] = bf16(dot(keep[part, :], w_own[...]) + dot(take[part, :], w_near[...]))


def residual(packed, part, got, resid_ref, normed_ref):
    resid = bf16(packed[...].astype(F32) + (part[...].astype(F32) + got[...].astype(F32)))
    resid_ref[...] = resid
    wide = resid.astype(F32)
    normed_ref[...] = bf16(wide * norm_factor(wide))


def ffn(rows_ref, d_out_ref, in_a, in_b, out_a, out_b, hidden_ref, back_ref):
    rows = rows_ref[...]
    cotangent = d_out_ref[...]
    units = out_a.shape[0]
    back = None
    for index, (w_in, w_out) in enumerate(((in_a, out_a), (in_b, out_b))):
        for n in range(units // CHUNK):
            part = slice(n * CHUNK, (n + 1) * CHUNK)
            d_hidden = dot(cotangent, w_out[part, :], NT)
            gate = dot(rows, w_in[0, :, part])
            upper = dot(rows, w_in[1, :, part])
            sigma = jax.nn.sigmoid(gate)
            silu = gate * sigma
            hidden_ref[:, index * units + n * CHUNK : index * units + (n + 1) * CHUNK] = bf16(silu * upper)
            d_gate = bf16(d_hidden * upper * silu_grad(gate, sigma))
            d_upper = bf16(d_hidden * silu)
            term = dot(d_gate, w_in[0, :, part], NT) + dot(d_upper, w_in[1, :, part], NT)
            back = term if back is None else back + term
    back_ref[...] = back.astype(back_ref.dtype)


def ffn_out_far(hidden, w_a, w_b, out):
    units = w_a.shape[0]
    out[...] = bf16(dot(hidden[:, :units], w_a[...]) + dot(hidden[:, units:], w_b[...]))


def ffn_out_own(hidden, w_a, w_b, resid, got, out):
    units = w_a.shape[0]
    total = dot(hidden[:, :units], w_a[...]) + dot(hidden[:, units:], w_b[...])
    out[...] = bf16(resid[...].astype(F32) + total + got[...].astype(F32))


def store_halves(value, out, halves):
    out[...] = value
    rows = value.shape[0] // max(len(halves), 1)
    for n, target in enumerate(halves):
        target[...] = value[n * rows : (n + 1) * rows]


def resid_back(back, got, resid, d_out, out, *halves):
    wide = resid[...].astype(F32)
    factor = norm_factor(wide)
    grad = back[...].astype(F32) + got[...].astype(F32)
    store_halves(bf16(d_out[...].astype(F32) + norm_back(grad, wide * factor, factor)), out, halves)


def attend_back(docs, d_resid, r, proj_ref, att_ref, w_out, masks, d_q, d_k, d_v, d_g):
    half = d_resid.shape[0]
    scale = HEAD ** (-0.5)
    ahead, allowed, root_inv = window(docs, r, half)
    gate = proj_ref[3, r].astype(F32)
    sigma_g = jax.nn.sigmoid(gate)
    d_gated = dot(d_resid, w_out, NT)
    d_att = bf16(d_gated * (gate * sigma_g) * root_inv)
    d_g[r] = bf16(d_gated * att_ref[r] * silu_grad(gate, sigma_g))
    keys = jnp.concatenate([proj_ref[1, ahead], proj_ref[1, r]], axis=0)
    values = jnp.concatenate([proj_ref[2, ahead], proj_ref[2, r]], axis=0)
    many = jnp.concatenate([allowed] * len(masks), axis=0)
    query = spread(proj_ref[0, r], masks)
    d_att_m = spread(d_att, masks)
    scores = dot(query, keys, NT) * scale
    sigma = jax.nn.sigmoid(scores)
    weights = bf16(scores * sigma * many)
    d_weights = dot(d_att_m, values, NT)
    d_scores = bf16(d_weights * silu_grad(scores, sigma) * many)
    d_q[r] = bf16(collect(dot(d_scores, keys), masks) * scale)
    d_keys = dot(d_scores, query, TN) * scale
    d_values = dot(weights, d_att_m, TN)
    d_k[ahead] += d_keys[:half]
    d_k[r] += d_keys[half:]
    d_v[ahead] += d_values[:half]
    d_v[r] += d_values[half:]


def joined(refs):
    return jnp.concatenate([r[...] for r in refs], axis=0)


def attn_back_first(docs, third, fourth_a, fourth_b, proj, att, w_out, d_q, d_k, d_v, d_g):
    masks = head_masks(w_out.shape[0])
    d_k[...] = jnp.zeros_like(d_k)
    d_v[...] = jnp.zeros_like(d_v)
    for r, rows in ((2, [third]), (3, [fourth_a, fourth_b])):
        attend_back(docs, joined(rows), r, proj, att, w_out[...], masks, d_q, d_k, d_v, d_g)


def back_norm(grads, w_in, first, second):
    total = None
    for c, grad in enumerate(grads):
        left = jnp.concatenate([grad[first], grad[second]], axis=0)
        term = dot(left, w_in[c], NT)
        total = term if total is None else total + term
    return total


def attn_back_second(
    docs, first, second, proj, att, w_out, d_q_far, d_k_far, d_v_far, d_g_far, w_in,
    give_ref, d_q, d_k, d_v, d_g, sum_k, sum_v,
):
    masks = head_masks(w_out.shape[0])
    d_q[2:4] = d_q_far[2:4]
    d_g[2:4] = d_g_far[2:4]
    sum_k[...] = d_k_far[...]
    sum_v[...] = d_v_far[...]
    for r, rows in ((0, first), (1, second)):
        attend_back(docs, rows[...], r, proj, att, w_out[...], masks, d_q, sum_k, sum_v, d_g)
    d_k[...] = bf16(sum_k[...])
    d_v[...] = bf16(sum_v[...])
    give_ref[...] = bf16(back_norm((d_q, d_k, d_v, d_g), w_in, 3, 1))


def attn_back_keep(d_q, d_k, d_v, d_g, w_in, keep_ref):
    keep_ref[...] = back_norm((d_q, d_k, d_v, d_g), w_in, 2, 0)


def add_near(keep, take, out_far, out_own):
    half = out_far.shape[0]
    out_far[...] = bf16(keep[:half, :] + take[:half, :].astype(F32))
    out_own[...] = bf16(keep[half:, :] + take[half:, :].astype(F32))


def packed_back(part, got, packed, d_resid, out, *halves):
    wide = packed[...].astype(F32)
    factor = norm_factor(wide)
    grad = part[...].astype(F32) + got[...].astype(F32)
    store_halves(bf16(d_resid[...].astype(F32) + norm_back(grad, wide * factor, factor)), out, halves)


def column_of(ref, index, cols):
    return ref[:, pl.ds(pl.multiple_of(index * cols, cols), cols)]


def rows_term(act_refs, cot):
    return dot(jnp.concatenate([a[...] for a in act_refs], axis=0), cot, TN)


def first_cot(cots, pre, enc):
    cols = pre.shape[1]
    cot = joined(cots)
    value = pre[...]
    w1_rows = enc[1, pl.ds(pl.multiple_of(tensor_index() * cols, cols), cols), :]
    return bf16(dot(cot, w1_rows, NT) * silu_grad(value, jax.nn.sigmoid(value)))


def cot_columns(cots, cols):
    return jnp.concatenate([column_of(c, tensor_index(), cols) for c in cots], axis=0)


def enc_grads_first(*refs):
    cots, (act0_a, act0_b, act1, pre, enc, part1, part0) = refs[:-7], refs[-7:]
    cols = pre.shape[1]
    part1[...] = rows_term([act1], cot_columns(cots, cols))
    part0[...] = rows_term([act0_a, act0_b], first_cot(cots, pre, enc))


def halve(bits, bit, total, keep, send):
    place = bits.index(bit)
    count, size, _ = keep.shape
    mine = (group_index() >> bit) & 1
    for j in range(count):
        low = j & ((1 << place) - 1)
        base = ((j >> place) << (place + 1)) | low
        for target, value in ((keep, mine), (send, 1 - mine)):
            index = base + (value << place)
            rows = total[pl.ds(pl.multiple_of(index * size, size), size), :]
            target[j] = rows.astype(target.dtype)


def enc_grad1_second(bits, bit, *refs):
    cots, (act1, part1, keep, send, total) = refs[:-5], refs[-5:]
    total[...] = rows_term([act1], cot_columns(cots, part1.shape[1])) + part1[...]
    halve(bits, bit, total, keep, send)


def enc_grad0_second(bits, bit, *refs):
    cots, (act0_a, act0_b, pre, enc, part0, keep, send, total) = refs[:-8], refs[-8:]
    total[...] = rows_term([act0_a, act0_b], first_cot(cots, pre, enc)) + part0[...]
    halve(bits, bit, total, keep, send)


def halve_again(bits, bit, kept, got, keep, send):
    place = bits.index(bit)
    mine = (group_index() >> bit) & 1
    for j in range(keep.shape[0]):
        low = j & ((1 << place) - 1)
        base = ((j >> place) << (place + 1)) | low
        for target, value in ((keep, mine), (send, 1 - mine)):
            index = base + (value << place)
            target[j] = (kept[index] + got[index].astype(F32)).astype(target.dtype)


def finish(kept0, got0, kept1, got1, out):
    out[0] = kept0[0] + got0[0].astype(F32)
    out[1] = kept1[0] + got1[0].astype(F32)


def shards(
    features,
    dest_owner,
    dest_slot,
    doc_ids,
    enc_weight,
    attn_in,
    attn_out,
    ffn_in,
    ffn_out,
    out_grad,
):
    rows_dev, width = features.shape
    group_axes = ("event", "pack")
    groups = lax.axis_size(group_axes)
    packs = lax.axis_size("pack")
    tensors = lax.axis_size("tensor")
    cols = attn_in.shape[2]
    comps = attn_in.shape[0]
    units = ffn_out.shape[0]
    d_out = out_grad[0]
    docs = doc_ids.reshape(tensors, 1, rows_dev)

    def near(value):
        return lax.ppermute(value, "tensor", [(i, i ^ 1) for i in range(tensors)])

    def far(value):
        return lax.ppermute(value, "tensor", [(i, i ^ 2) for i in range(tensors)])

    def crossed(value, k):
        return lax.ppermute(value, group_axes, [(i, i ^ k) for i in range(groups)])

    row_b = like((rows_dev, width), BF16)
    row_f = like((rows_dev, width), F32)

    mean_load = rows_dev // groups
    capacity = -(-(mean_load + mean_load // 2) // 8) * 8
    code = (dest_owner * rows_dev + dest_slot).reshape(1, rows_dev)
    order = [0] + sorted(
        range(1, groups), key=lambda k: (-((2 * (k % packs)) // packs), k % packs, k)
    )
    *sends, place = run(
        functools.partial(route_send, capacity, order),
        [like((capacity, width + rows_dev), BF16)] * groups + [like((1, rows_dev), jnp.int32)],
        [code, features],
        flops=4 * 10**9,
        name="route_send",
    )
    ffn_in_near, ffn_out_near = near(ffn_in), near(ffn_out)
    early = [crossed(sends[n], order[n]) for n in (1, 2)]
    ffn_in_near, ffn_out_near, *sends = tie(ffn_in_near, ffn_out_near, *sends)
    gots = [sends[0], *early] + [crossed(sends[n], order[n]) for n in range(3, groups)]
    mine, hot = run(
        route_recv,
        [row_b, like((groups * capacity, rows_dev), BF16)],
        gots,
        name="route_recv",
    )

    mine_far = far(mine)
    mine_near = near(mine)

    pair = 2 * rows_dev
    pre_a, act_a, packed, proj_a = run(
        encode_first,
        [
            like((pair, cols), F32),
            like((pair, width), BF16),
            row_b,
            like((comps, 2, rows_dev, cols), BF16),
        ],
        [mine, mine_near, enc_weight, attn_in],
        [pltpu.VMEM((pair, width), F32)],
        name="encode_first",
    )
    mine_far, proj_a = tie(mine_far, proj_a)
    mine_far, attn_out_late, d_out_late = tie(mine_far, attn_out, d_out)
    mine_both = near(mine_far)
    attn_out_near = near(attn_out_late)
    d_out_far = far(d_out_late)
    pre_b, act_b, packed_far, proj, attended, give, keep = run(
        attend_first,
        [
            like((pair, cols), F32),
            like((pair, width), BF16),
            row_b,
            like((comps, tensors, rows_dev, cols), BF16),
            like((tensors, rows_dev, cols), F32),
            like((pair, cols), BF16),
            like((pair, cols), BF16),
        ],
        [docs, mine_far, mine_both, proj_a, enc_weight, attn_in],
        [pltpu.VMEM((pair, width), F32)],
        name="attend_first",
    )
    take = near(give)
    take, d_out_far = tie(take, d_out_far)


    def out_part(index, name):
        return run(
            functools.partial(attn_out_part, index),
            [row_b],
            [keep, take, attn_out, attn_out_near],
            name=name,
        )[0]

    part_far = out_part(0, "attn_out_far")
    got_own = far(part_far)
    part_own = out_part(1, "attn_out_own")
    got_far = far(part_own)

    def feed(rows, cotangent, name):
        return run(
            ffn,
            [like((rows_dev, 2 * units), BF16), row_b],
            [rows, cotangent, ffn_in, ffn_in_near, ffn_out, ffn_out_near],
            name=name,
        )

    resid, normed2 = run(residual, [row_b, row_b], [packed, part_own, got_own], name="residual")
    hidden_own, back_own = feed(normed2, d_out, "ffn_own")
    got_far, back_own = tie(got_far, back_own)
    got_back_far = far(back_own)
    resid_far, normed2_far = run(
        residual, [row_b, row_b], [packed_far, part_far, got_far], name="residual_far"
    )
    hidden_far, back_far = feed(normed2_far, d_out_far, "ffn_far")
    got_back_own = far(back_far)

    pieces = 2
    piece_b = like((rows_dev // pieces, width), BF16)
    d_resid_far, *halves = run(
        resid_back,
        [row_b] + [piece_b] * pieces,
        [back_far, got_back_far, resid_far, d_out_far],
        name="resid_back_far",
    )
    d_resid_both = [near(h) for h in halves]
    block_f = like((tensors, rows_dev, cols), F32)
    block_b = like((tensors, rows_dev, cols), BF16)
    d_q, d_k, d_v, d_g = run(
        attn_back_first,
        [block_b, block_f, block_f, block_b],
        [docs, d_resid_far, *d_resid_both, proj, attended, attn_out],
        name="attn_back_first",
    )
    got_back_own, d_q = tie(got_back_own, d_q)
    (d_resid,) = run(resid_back, [row_b], [back_own, got_back_own, resid, d_out], name="resid_back")
    d_resid_near = near(d_resid)
    give, *d_projected = run(
        attn_back_second,
        [like((pair, width), BF16)] + [block_b] * 4,
        [docs, d_resid, d_resid_near, proj, attended, attn_out, d_q, d_k, d_v, d_g, attn_in],
        [pltpu.VMEM((tensors, rows_dev, cols), F32)] * 2,
        name="attn_back_second",
    )
    take = near(give)
    (keep,) = run(
        attn_back_keep,
        [like((pair, width), F32)],
        [*d_projected, attn_in],
        name="attn_back_keep",
    )
    sum_far, sum_own = run(add_near, [row_b, row_b], [keep, take], name="add_near")
    got_own = far(sum_far)
    got_far = far(sum_own)
    d_packed, *halves = run(
        packed_back,
        [row_b] + [piece_b] * pieces,
        [sum_own, got_own, packed, d_resid],
        name="packed_back",
    )

    cot_near = [near(h) for h in halves]
    (backs,) = run(
        functools.partial(back_send, order),
        [like((groups, capacity, width), BF16)],
        [hot, d_packed],
        name="back_send",
    )
    returned = lax.all_to_all(backs, group_axes, split_axis=0, concat_axis=0, tiled=True)

    part_f = like((width, cols), F32)
    part1, part0 = run(
        enc_grads_first,
        [part_f, part_f],
        [d_packed, *cot_near, mine, mine_near, act_a, pre_a, enc_weight],
        name="enc_grads_first",
    )
    got_far, part1, part0 = tie(got_far, part1, part0)
    (cot_far,) = run(
        packed_back, [row_b], [sum_far, got_far, packed_far, d_resid_far], name="packed_back_far"
    )
    cot_both = near(cot_far)
    cot_far, hidden_far = tie(cot_far, hidden_far)
    (out_far,) = run(
        ffn_out_far, [row_b], [hidden_far, ffn_out, ffn_out_near], name="ffn_out_far"
    )
    bits = list(range(groups.bit_length() - 1))
    pack_bits = bits[: packs.bit_length() - 1]
    event_bits = bits[len(pack_bits) :]
    size = width // groups
    total = [pltpu.VMEM((width, cols), F32)]

    def halves(remaining):
        shape = (2 ** (len(remaining) - 1), size, cols)
        return [like(shape, F32), like(shape, BF16)]

    def reduce_over(stages, start, held, name):
        remaining = list(bits)
        kept, send = start((tuple(remaining), stages[0]))
        got = crossed(send, 1 << stages[0])
        got, held = tie(got, held)
        remaining.remove(stages[0])
        for bit in stages[1:]:
            kept, send = run(
                functools.partial(halve_again, tuple(remaining), bit),
                halves(remaining),
                [kept, got],
                name=name + str(bit),
            )
            got = crossed(send, 1 << bit)
            remaining.remove(bit)
        return kept, got, held

    def start1(setting):
        return run(
            functools.partial(enc_grad1_second, *setting),
            halves(bits),
            [cot_far, cot_both, act_b, part1],
            total,
            name="enc_grad1_second",
        )

    def start0(setting):
        return run(
            functools.partial(enc_grad0_second, *setting),
            halves(bits),
            [cot_far, cot_both, mine_far, mine_both, pre_b, enc_weight, part0],
            total,
            name="enc_grad0_second",
        )

    kept1, got1, returned = reduce_over(event_bits + pack_bits, start1, returned, "halve1_")
    kept0, got0, out_far = reduce_over(
        pack_bits[:1] + event_bits + pack_bits[1:], start0, out_far, "halve0_"
    )
    got_out = far(out_far)
    (packed_out,) = run(
        ffn_out_own, [row_b], [hidden_own, ffn_out, ffn_out_near, resid, got_out], name="ffn_out_own"
    )
    (row_grad,) = run(
        back_recv,
        [row_b],
        [place, returned],
        name="back_recv",
    )
    got1, got0, packed_out, row_grad = tie(got1, got0, packed_out, row_grad)
    (enc_grad,) = run(finish, [like((2, size, cols), F32)], [kept0, got0, kept1, got1], name="finish")
    return (packed_out[None], row_grad, enc_grad)


def solution(mesh):
    placed = (
        P(("event", "pack", "tensor"), None),
        P(("event", "pack", "tensor")),
        P(("event", "pack", "tensor")),
        P(("event", "pack"), None),
        P(),
        P(None, None, "tensor"),
        P("tensor", None),
        P(None, None, "tensor"),
        P("tensor", None),
        P(("event", "pack"), "tensor", None),
    )
    return jax.shard_map(
        shards,
        mesh=mesh,
        in_specs=placed,
        out_specs=(
            P(("event", "pack"), "tensor", None),
            P(("event", "pack", "tensor"), None),
            P(None, ("event", "pack"), "tensor"),
        ),
        check_vma=False,
    )
```

```python
import functools

import jax
import jax.numpy as jnp
from jax import lax
from jax.experimental import pallas as pl
from jax.experimental.pallas import tpu as pltpu
from jax.sharding import PartitionSpec as P

D = 1024
HEADS = 16
HEAD = D // HEADS
EPS = 1e-06
F32 = jnp.float32
BF16 = jnp.bfloat16
MIB = 1 << 20
CHUNK = 256


def dot(left, right, dims=((1,), (0,))):
    return lax.dot_general(left, right, (dims, ((), ())), preferred_element_type=F32)


NT = ((1,), (1,))
TN = ((0,), (0,))


def bf16(value):
    return value.astype(BF16)


def silu_grad(value, sigma):
    return sigma * (1.0 + value * (1.0 - sigma))


def norm_factor(wide):
    return lax.rsqrt(jnp.mean(wide * wide, axis=-1, keepdims=True) + EPS)


def norm_back(grad, normed, factor):
    return factor * (grad - normed * jnp.mean(grad * normed, axis=-1, keepdims=True))


def turned(row, rows):
    return jnp.broadcast_to(row.astype(F32), (rows, rows)).T


def like(shape, dtype):
    return jax.ShapeDtypeStruct(shape, dtype)


def run(body, outs, args, scratch=(), flops=0, name=None):
    return pl.pallas_call(
        body,
        out_shape=list(outs),
        in_specs=[pl.BlockSpec(memory_space=pltpu.VMEM)] * len(args),
        out_specs=[pl.BlockSpec(memory_space=pltpu.VMEM)] * len(outs),
        scratch_shapes=list(scratch),
        compiler_params=pltpu.CompilerParams(vmem_limit_bytes=16 * MIB),
        cost_estimate=pl.CostEstimate(flops=flops, bytes_accessed=0, transcendentals=0),
        name=name,
    )(*args)


def group_index():
    return lax.axis_index("event") * lax.axis_size("pack") + lax.axis_index("pack")


def tensor_index():
    return lax.axis_index("tensor")


def tie(*values):
    return lax.optimization_barrier(values)


def route_send(capacity, order, packs, code, features, *outs):
    sends, place_ref = outs[:-1], outs[-1]
    groups = len(sends)
    rows, width = features.shape
    shift = rows.bit_length() - 1
    o_row = code[...] >> shift
    slot = code[...] & (rows - 1)
    o_col = turned(o_row, rows)
    i = lax.broadcasted_iota(jnp.int32, (rows, rows), 0)
    j = lax.broadcasted_iota(jnp.int32, (rows, rows), 1)
    earlier = jnp.where((o_col == o_row.astype(F32)) & (i < j), 1.0, 0.0)
    rank = jnp.sum(earlier, axis=0, keepdims=True).astype(jnp.int32)
    offset = o_row ^ group_index()
    place = offset * capacity + rank
    turn = packs.bit_length() - 1
    events = groups // packs
    place_ref[...] = ((offset & (packs - 1)) * events + (offset >> turn)) * capacity + rank
    spots = lax.broadcasted_iota(jnp.int32, (groups * capacity, rows), 0)
    hot = jnp.where(spots == place, 1.0, 0.0).astype(BF16)
    big = dot(hot, features[...])
    tags = dot(hot, bf16(turned(slot + 1, rows)))
    for k, send in zip(order, sends):
        part = slice(k * capacity, (k + 1) * capacity)
        send[:, :width] = bf16(big[part])
        send[:, width:] = bf16(tags[part])


def route_recv(*refs):
    gots, (rows_ref, hot_ref) = refs[:-2], refs[-2:]
    rows, width = rows_ref.shape
    got = jnp.concatenate([g[...].astype(F32) for g in gots], axis=0)
    lanes = lax.broadcasted_iota(jnp.int32, (got.shape[0], rows), 1) + 1
    hot = jnp.where(got[:, width:] == lanes.astype(F32), 1.0, 0.0).astype(BF16)
    hot_ref[...] = hot
    rows_ref[...] = bf16(dot(hot, bf16(got[:, :width]), TN))


def back_send(order, packs, hot, d_packed, own, *sends):
    events = len(order) // packs
    capacity = hot.shape[0] // len(order)
    big = dot(hot[...], d_packed[...])
    at = {k: n for n, k in enumerate(order)}
    for a in range(events):
        parts = [at[a * packs + b] * capacity for b in range(packs)]
        rows = jnp.concatenate([big[p : p + capacity] for p in parts], axis=0)
        (own, *sends)[a][...] = bf16(rows)


def back_turn(events, *refs):
    packs = len(refs) - events
    own, gots, outs = refs[0], refs[1 : -packs], refs[-packs:]
    rows = jnp.concatenate([r[...].astype(F32) for r in (own, *gots)], axis=0)
    capacity = outs[0].shape[0] // events
    for b, out in enumerate(outs):
        parts = [
            rows[(a * packs + b) * capacity : (a * packs + b + 1) * capacity] for a in range(events)
        ]
        out[...] = bf16(jnp.concatenate(parts, axis=0))


def back_recv(place, *refs):
    gots, out = refs[:-1], refs[-1]
    got = bf16(jnp.concatenate([g[...].astype(F32) for g in gots], axis=0))
    spots = lax.broadcasted_iota(jnp.int32, (got.shape[0], out.shape[0]), 0)
    hot = jnp.where(spots == place[...], 1.0, 0.0).astype(BF16)
    out[...] = bf16(dot(hot, got, TN))


def encode(rows, enc, w_in, pre_all, pre_ref, act_ref, packed_ref, store):
    width = rows.shape[1]
    cols = pre_ref.shape[1]
    for n in range(width // CHUNK):
        part = slice(n * CHUNK, (n + 1) * CHUNK)
        pre = dot(rows, enc[0, :, part])
        pre_all[:, part] = pre
        act_ref[:, part] = bf16(pre * jax.nn.sigmoid(pre))
    pre_ref[...] = pre_all[:, pl.ds(pl.multiple_of(tensor_index() * cols, cols), cols)]
    packed = bf16(dot(act_ref[...], enc[1]))
    packed_ref[...] = packed[: packed_ref.shape[0]]
    wide = packed.astype(F32)
    normed = bf16(wide * norm_factor(wide))
    for c in range(w_in.shape[0]):
        store(c, bf16(dot(normed, w_in[c])))


def encode_first(first, second, enc, w_in, pre_ref, act_ref, packed_ref, proj_ref, pre_all):
    rows = jnp.concatenate([first[...], second[...]], axis=0)
    half = first.shape[0]

    def store(c, value):
        proj_ref[c, 0] = value[:half]
        proj_ref[c, 1] = value[half:]

    encode(rows, enc, w_in, pre_all, pre_ref, act_ref, packed_ref, store)


def window(docs, r, rows):
    t = tensor_index()
    b = t ^ r
    ahead = jnp.where(b > 0, (b - 1) ^ t, r)
    doc_q = turned(docs[b], rows)
    doc_own = docs[b].astype(F32)
    doc_ahead = docs[jnp.maximum(b - 1, 0)].astype(F32)
    i = lax.broadcasted_iota(jnp.int32, (rows, rows), 0)
    j = lax.broadcasted_iota(jnp.int32, (rows, rows), 1)
    own = jnp.where((doc_q == doc_own) & (j <= i), 1.0, 0.0)
    prior = jnp.where(doc_q == doc_ahead, 1.0, 0.0) * jnp.where(b > 0, 1.0, 0.0)
    allowed = jnp.concatenate([prior, own], axis=1)
    root_inv = lax.rsqrt(jnp.sum(allowed, axis=1, keepdims=True))
    return ahead, allowed, root_inv


def head_masks(cols):
    lane = lax.broadcasted_iota(jnp.int32, (1, cols), 1) // HEAD
    return [jnp.where(lane == h, 1.0, 0.0) for h in range(cols // HEAD)]


def spread(value, masks):
    return jnp.concatenate([value * bf16(m) for m in masks], axis=0)


def collect(value, masks):
    rows = value.shape[0] // len(masks)
    total = None
    for h, m in enumerate(masks):
        part = value[h * rows : (h + 1) * rows] * m
        total = part if total is None else total + part
    return total


def attend_first(
    docs, third, fourth, proj_a, enc, w_in,
    pre_ref, act_ref, packed_ref, proj_ref, att_ref, give_ref, keep_ref, pre_all,
):
    rows = jnp.concatenate([third[...], fourth[...]], axis=0)
    half = third.shape[0]
    cols = proj_a.shape[-1]
    proj_ref[:, 0:2] = proj_a[...]

    def store(c, value):
        proj_ref[c, 2] = value[:half]
        proj_ref[c, 3] = value[half:]

    encode(rows, enc, w_in, pre_all, pre_ref, act_ref, packed_ref, store)
    masks = head_masks(cols)
    for r, (target, place) in enumerate(((keep_ref, 1), (give_ref, 1), (keep_ref, 0), (give_ref, 0))):
        ahead, allowed, root_inv = window(docs, r, half)
        keys = jnp.concatenate([proj_ref[1, ahead], proj_ref[1, r]], axis=0)
        values = jnp.concatenate([proj_ref[2, ahead], proj_ref[2, r]], axis=0)
        many = jnp.concatenate([allowed] * len(masks), axis=0)
        scores = dot(spread(proj_ref[0, r], masks), keys, NT) * HEAD ** (-0.5)
        weights = bf16(scores * jax.nn.sigmoid(scores) * many)
        attended = collect(dot(weights, values), masks) * root_inv
        gate = proj_ref[3, r].astype(F32)
        att_ref[r] = attended
        target[place * half : (place + 1) * half, :] = bf16(attended * gate * jax.nn.sigmoid(gate))


def attn_out_part(index, keep, take, w_own, w_near, out):
    rows = out.shape[0]
    part = slice(index * rows, (index + 1) * rows)
    out[...] = bf16(dot(keep[part, :], w_own[...]) + dot(take[part, :], w_near[...]))


def residual(packed, part, got, resid_ref, normed_ref):
    resid = bf16(packed[...].astype(F32) + (part[...].astype(F32) + got[...].astype(F32)))
    resid_ref[...] = resid
    wide = resid.astype(F32)
    normed_ref[...] = bf16(wide * norm_factor(wide))


def ffn(rows_ref, d_out_ref, in_a, in_b, out_a, out_b, hidden_ref, back_ref):
    rows = rows_ref[...]
    cotangent = d_out_ref[...]
    units = out_a.shape[0]
    back = None
    for index, (w_in, w_out) in enumerate(((in_a, out_a), (in_b, out_b))):
        for n in range(units // CHUNK):
            part = slice(n * CHUNK, (n + 1) * CHUNK)
            d_hidden = dot(cotangent, w_out[part, :], NT)
            gate = dot(rows, w_in[0, :, part])
            upper = dot(rows, w_in[1, :, part])
            sigma = jax.nn.sigmoid(gate)
            silu = gate * sigma
            hidden_ref[:, index * units + n * CHUNK : index * units + (n + 1) * CHUNK] = bf16(silu * upper)
            d_gate = bf16(d_hidden * upper * silu_grad(gate, sigma))
            d_upper = bf16(d_hidden * silu)
            term = dot(d_gate, w_in[0, :, part], NT) + dot(d_upper, w_in[1, :, part], NT)
            back = term if back is None else back + term
    back_ref[...] = back.astype(back_ref.dtype)


def ffn_out_far(hidden, w_a, w_b, out):
    units = w_a.shape[0]
    out[...] = bf16(dot(hidden[:, :units], w_a[...]) + dot(hidden[:, units:], w_b[...]))


def ffn_out_own(hidden, w_a, w_b, resid, got, out):
    units = w_a.shape[0]
    total = dot(hidden[:, :units], w_a[...]) + dot(hidden[:, units:], w_b[...])
    out[...] = bf16(resid[...].astype(F32) + total + got[...].astype(F32))


def store_halves(value, out, halves):
    out[...] = value
    rows = value.shape[0] // max(len(halves), 1)
    for n, target in enumerate(halves):
        target[...] = value[n * rows : (n + 1) * rows]


def resid_back(back, got, resid, d_out, out, *halves):
    wide = resid[...].astype(F32)
    factor = norm_factor(wide)
    grad = back[...].astype(F32) + got[...].astype(F32)
    store_halves(bf16(d_out[...].astype(F32) + norm_back(grad, wide * factor, factor)), out, halves)


def attend_back(docs, d_resid, r, proj_ref, att_ref, w_out, masks, d_q, d_k, d_v, d_g):
    half = d_resid.shape[0]
    scale = HEAD ** (-0.5)
    ahead, allowed, root_inv = window(docs, r, half)
    gate = proj_ref[3, r].astype(F32)
    sigma_g = jax.nn.sigmoid(gate)
    d_gated = dot(d_resid, w_out, NT)
    d_att = bf16(d_gated * (gate * sigma_g) * root_inv)
    d_g[r] = bf16(d_gated * att_ref[r] * silu_grad(gate, sigma_g))
    keys = jnp.concatenate([proj_ref[1, ahead], proj_ref[1, r]], axis=0)
    values = jnp.concatenate([proj_ref[2, ahead], proj_ref[2, r]], axis=0)
    many = jnp.concatenate([allowed] * len(masks), axis=0)
    query = spread(proj_ref[0, r], masks)
    d_att_m = spread(d_att, masks)
    scores = dot(query, keys, NT) * scale
    sigma = jax.nn.sigmoid(scores)
    weights = bf16(scores * sigma * many)
    d_weights = dot(d_att_m, values, NT)
    d_scores = bf16(d_weights * silu_grad(scores, sigma) * many)
    d_q[r] = bf16(collect(dot(d_scores, keys), masks) * scale)
    d_keys = dot(d_scores, query, TN) * scale
    d_values = dot(weights, d_att_m, TN)
    d_k[ahead] += d_keys[:half]
    d_k[r] += d_keys[half:]
    d_v[ahead] += d_values[:half]
    d_v[r] += d_values[half:]


def joined(refs):
    return jnp.concatenate([r[...] for r in refs], axis=0)


def attn_back_first(docs, third, fourth_a, fourth_b, proj, att, w_out, d_q, d_k, d_v, d_g):
    masks = head_masks(w_out.shape[0])
    d_k[...] = jnp.zeros_like(d_k)
    d_v[...] = jnp.zeros_like(d_v)
    for r, rows in ((2, [third]), (3, [fourth_a, fourth_b])):
        attend_back(docs, joined(rows), r, proj, att, w_out[...], masks, d_q, d_k, d_v, d_g)


def back_norm(grads, w_in, first, second):
    total = None
    for c, grad in enumerate(grads):
        left = jnp.concatenate([grad[first], grad[second]], axis=0)
        term = dot(left, w_in[c], NT)
        total = term if total is None else total + term
    return total


def attn_back_second(
    docs, first, second, proj, att, w_out, d_q_far, d_k_far, d_v_far, d_g_far, w_in,
    give_ref, d_q, d_k, d_v, d_g, sum_k, sum_v,
):
    masks = head_masks(w_out.shape[0])
    d_q[2:4] = d_q_far[2:4]
    d_g[2:4] = d_g_far[2:4]
    sum_k[...] = d_k_far[...]
    sum_v[...] = d_v_far[...]
    for r, rows in ((0, first), (1, second)):
        attend_back(docs, rows[...], r, proj, att, w_out[...], masks, d_q, sum_k, sum_v, d_g)
    d_k[...] = bf16(sum_k[...])
    d_v[...] = bf16(sum_v[...])
    give_ref[...] = bf16(back_norm((d_q, d_k, d_v, d_g), w_in, 3, 1))


def attn_back_keep(d_q, d_k, d_v, d_g, w_in, keep_ref):
    keep_ref[...] = back_norm((d_q, d_k, d_v, d_g), w_in, 2, 0)


def add_near(keep, take, out_far, out_own):
    half = out_far.shape[0]
    out_far[...] = bf16(keep[:half, :] + take[:half, :].astype(F32))
    out_own[...] = bf16(keep[half:, :] + take[half:, :].astype(F32))


def packed_back(part, got, packed, d_resid, out, *halves):
    wide = packed[...].astype(F32)
    factor = norm_factor(wide)
    grad = part[...].astype(F32) + got[...].astype(F32)
    store_halves(bf16(d_resid[...].astype(F32) + norm_back(grad, wide * factor, factor)), out, halves)


def column_of(ref, index, cols):
    return ref[:, pl.ds(pl.multiple_of(index * cols, cols), cols)]


def rows_term(act_refs, cot):
    return dot(jnp.concatenate([a[...] for a in act_refs], axis=0), cot, TN)


def first_cot(cots, pre, enc):
    cols = pre.shape[1]
    cot = joined(cots)
    value = pre[...]
    w1_rows = enc[1, pl.ds(pl.multiple_of(tensor_index() * cols, cols), cols), :]
    return bf16(dot(cot, w1_rows, NT) * silu_grad(value, jax.nn.sigmoid(value)))


def cot_columns(cots, cols):
    return jnp.concatenate([column_of(c, tensor_index(), cols) for c in cots], axis=0)


def enc_grads_first(*refs):
    cots, (act0_a, act0_b, act1, pre, enc, part1, part0) = refs[:-7], refs[-7:]
    cols = pre.shape[1]
    part1[...] = rows_term([act1], cot_columns(cots, cols))
    part0[...] = rows_term([act0_a, act0_b], first_cot(cots, pre, enc))


def halve(bits, bit, total, keep, send):
    place = bits.index(bit)
    count, size, _ = keep.shape
    mine = (group_index() >> bit) & 1
    for j in range(count):
        low = j & ((1 << place) - 1)
        base = ((j >> place) << (place + 1)) | low
        for target, value in ((keep, mine), (send, 1 - mine)):
            index = base + (value << place)
            rows = total[pl.ds(pl.multiple_of(index * size, size), size), :]
            target[j] = rows.astype(target.dtype)


def enc_grad1_second(bits, bit, *refs):
    cots, (act1, part1, keep, send, total) = refs[:-5], refs[-5:]
    total[...] = rows_term([act1], cot_columns(cots, part1.shape[1])) + part1[...]
    halve(bits, bit, total, keep, send)


def enc_grad0_second(bits, bit, *refs):
    cots, (act0_a, act0_b, pre, enc, part0, keep, send, total) = refs[:-8], refs[-8:]
    total[...] = rows_term([act0_a, act0_b], first_cot(cots, pre, enc)) + part0[...]
    halve(bits, bit, total, keep, send)


def halve_again(bits, bit, kept, got, keep, send):
    place = bits.index(bit)
    mine = (group_index() >> bit) & 1
    for j in range(keep.shape[0]):
        low = j & ((1 << place) - 1)
        base = ((j >> place) << (place + 1)) | low
        for target, value in ((keep, mine), (send, 1 - mine)):
            index = base + (value << place)
            target[j] = (kept[index] + got[index].astype(F32)).astype(target.dtype)


def finish(kept0, got0, kept1, got1, out):
    out[0] = kept0[0] + got0[0].astype(F32)
    out[1] = kept1[0] + got1[0].astype(F32)


def shards(
    features,
    dest_owner,
    dest_slot,
    doc_ids,
    enc_weight,
    attn_in,
    attn_out,
    ffn_in,
    ffn_out,
    out_grad,
):
    rows_dev, width = features.shape
    group_axes = ("event", "pack")
    groups = lax.axis_size(group_axes)
    packs = lax.axis_size("pack")
    tensors = lax.axis_size("tensor")
    cols = attn_in.shape[2]
    comps = attn_in.shape[0]
    units = ffn_out.shape[0]
    d_out = out_grad[0]
    docs = doc_ids.reshape(tensors, 1, rows_dev)

    def near(value):
        return lax.ppermute(value, "tensor", [(i, i ^ 1) for i in range(tensors)])

    def far(value):
        return lax.ppermute(value, "tensor", [(i, i ^ 2) for i in range(tensors)])

    def crossed(value, k):
        return lax.ppermute(value, group_axes, [(i, i ^ k) for i in range(groups)])

    row_b = like((rows_dev, width), BF16)
    row_f = like((rows_dev, width), F32)

    mean_load = rows_dev // groups
    capacity = -(-(mean_load + mean_load // 2) // 8) * 8
    code = (dest_owner * rows_dev + dest_slot).reshape(1, rows_dev)
    order = [0] + sorted(
        range(1, groups), key=lambda k: (-((2 * (k % packs)) // packs), k % packs, k)
    )
    *sends, place = run(
        functools.partial(route_send, capacity, order, packs),
        [like((capacity, width + rows_dev), BF16)] * groups + [like((1, rows_dev), jnp.int32)],
        [code, features],
        flops=4 * 10**9,
        name="route_send",
    )
    ffn_in_near, ffn_out_near = near(ffn_in), near(ffn_out)
    early = [crossed(sends[n], order[n]) for n in (1, 2)]
    ffn_in_near, ffn_out_near, *sends = tie(ffn_in_near, ffn_out_near, *sends)
    gots = [sends[0], *early] + [crossed(sends[n], order[n]) for n in range(3, groups)]
    mine, hot = run(
        route_recv,
        [row_b, like((groups * capacity, rows_dev), BF16)],
        gots,
        name="route_recv",
    )

    mine_far = far(mine)
    mine_near = near(mine)

    pair = 2 * rows_dev
    pre_a, act_a, packed, proj_a = run(
        encode_first,
        [
            like((pair, cols), F32),
            like((pair, width), BF16),
            row_b,
            like((comps, 2, rows_dev, cols), BF16),
        ],
        [mine, mine_near, enc_weight, attn_in],
        [pltpu.VMEM((pair, width), F32)],
        name="encode_first",
    )
    mine_far, proj_a = tie(mine_far, proj_a)
    mine_far, attn_out_late, d_out_late = tie(mine_far, attn_out, d_out)
    mine_both = near(mine_far)
    attn_out_near = near(attn_out_late)
    d_out_far = far(d_out_late)
    pre_b, act_b, packed_far, proj, attended, give, keep = run(
        attend_first,
        [
            like((pair, cols), F32),
            like((pair, width), BF16),
            row_b,
            like((comps, tensors, rows_dev, cols), BF16),
            like((tensors, rows_dev, cols), F32),
            like((pair, cols), BF16),
            like((pair, cols), BF16),
        ],
        [docs, mine_far, mine_both, proj_a, enc_weight, attn_in],
        [pltpu.VMEM((pair, width), F32)],
        name="attend_first",
    )
    take = near(give)
    take, d_out_far = tie(take, d_out_far)


    def out_part(index, name):
        return run(
            functools.partial(attn_out_part, index),
            [row_b],
            [keep, take, attn_out, attn_out_near],
            name=name,
        )[0]

    part_far = out_part(0, "attn_out_far")
    got_own = far(part_far)
    part_own = out_part(1, "attn_out_own")
    got_far = far(part_own)

    def feed(rows, cotangent, name):
        return run(
            ffn,
            [like((rows_dev, 2 * units), BF16), row_b],
            [rows, cotangent, ffn_in, ffn_in_near, ffn_out, ffn_out_near],
            name=name,
        )

    resid, normed2 = run(residual, [row_b, row_b], [packed, part_own, got_own], name="residual")
    hidden_own, back_own = feed(normed2, d_out, "ffn_own")
    got_far, back_own = tie(got_far, back_own)
    got_back_far = far(back_own)
    resid_far, normed2_far = run(
        residual, [row_b, row_b], [packed_far, part_far, got_far], name="residual_far"
    )
    hidden_far, back_far = feed(normed2_far, d_out_far, "ffn_far")
    got_back_own = far(back_far)

    pieces = 2
    piece_b = like((rows_dev // pieces, width), BF16)
    d_resid_far, *halves = run(
        resid_back,
        [row_b] + [piece_b] * pieces,
        [back_far, got_back_far, resid_far, d_out_far],
        name="resid_back_far",
    )
    d_resid_both = [near(h) for h in halves]
    block_f = like((tensors, rows_dev, cols), F32)
    block_b = like((tensors, rows_dev, cols), BF16)
    d_q, d_k, d_v, d_g = run(
        attn_back_first,
        [block_b, block_f, block_f, block_b],
        [docs, d_resid_far, *d_resid_both, proj, attended, attn_out],
        name="attn_back_first",
    )
    got_back_own, d_q = tie(got_back_own, d_q)
    (d_resid,) = run(resid_back, [row_b], [back_own, got_back_own, resid, d_out], name="resid_back")
    d_resid_near = near(d_resid)
    give, *d_projected = run(
        attn_back_second,
        [like((pair, width), BF16)] + [block_b] * 4,
        [docs, d_resid, d_resid_near, proj, attended, attn_out, d_q, d_k, d_v, d_g, attn_in],
        [pltpu.VMEM((tensors, rows_dev, cols), F32)] * 2,
        name="attn_back_second",
    )
    take = near(give)
    (keep,) = run(
        attn_back_keep,
        [like((pair, width), F32)],
        [*d_projected, attn_in],
        name="attn_back_keep",
    )
    sum_far, sum_own = run(add_near, [row_b, row_b], [keep, take], name="add_near")
    got_own = far(sum_far)
    got_far = far(sum_own)
    d_packed, *halves = run(
        packed_back,
        [row_b] + [piece_b] * pieces,
        [sum_own, got_own, packed, d_resid],
        name="packed_back",
    )

    cot_near = [near(h) for h in halves]
    events = groups // packs
    back_own, *backs = run(
        functools.partial(back_send, order, packs),
        [like((packs * capacity, width), BF16)] * events,
        [hot, d_packed],
        name="back_send",
    )
    over_event = [crossed(v, (n + 1) * packs) for n, v in enumerate(backs)]

    part_f = like((width, cols), F32)
    part1, part0 = run(
        enc_grads_first,
        [part_f, part_f],
        [d_packed, *cot_near, mine, mine_near, act_a, pre_a, enc_weight],
        name="enc_grads_first",
    )
    got_far, part1, part0 = tie(got_far, part1, part0)
    cot_far, *cot_pieces = run(
        packed_back,
        [row_b] + [piece_b] * pieces,
        [sum_far, got_far, packed_far, d_resid_far],
        name="packed_back_far",
    )
    cot_both = [near(piece) for piece in cot_pieces]
    *cot_both, over_event = tie(*cot_both, over_event)
    back_own, *turned_rows = run(
        functools.partial(back_turn, events),
        [like((events * capacity, width), BF16)] * packs,
        [back_own, *over_event],
        name="back_turn",
    )
    returned = [back_own] + [crossed(v, b + 1) for b, v in enumerate(turned_rows)]

    cot_far, hidden_far = tie(cot_far, hidden_far)
    (out_far,) = run(
        ffn_out_far, [row_b], [hidden_far, ffn_out, ffn_out_near], name="ffn_out_far"
    )
    bits = list(range(groups.bit_length() - 1))
    pack_bits = bits[: packs.bit_length() - 1]
    event_bits = bits[len(pack_bits) :]
    size = width // groups
    total = [pltpu.VMEM((width, cols), F32)]

    def halves(remaining):
        shape = (2 ** (len(remaining) - 1), size, cols)
        return [like(shape, F32), like(shape, BF16)]

    def reduce_over(stages, start, held, name):
        remaining = list(bits)
        kept, send = start((tuple(remaining), stages[0]))
        got = crossed(send, 1 << stages[0])
        got, *held = tie(got, *held)
        remaining.remove(stages[0])
        for bit in stages[1:]:
            kept, send = run(
                functools.partial(halve_again, tuple(remaining), bit),
                halves(remaining),
                [kept, got],
                name=name + str(bit),
            )
            got = crossed(send, 1 << bit)
            remaining.remove(bit)
        return kept, got, held

    def start1(setting):
        return run(
            functools.partial(enc_grad1_second, *setting),
            halves(bits),
            [cot_far, *cot_both, act_b, part1],
            total,
            name="enc_grad1_second",
        )

    def start0(setting):
        return run(
            functools.partial(enc_grad0_second, *setting),
            halves(bits),
            [cot_far, *cot_both, mine_far, mine_both, pre_b, enc_weight, part0],
            total,
            name="enc_grad0_second",
        )

    kept1, got1, returned = reduce_over(event_bits + pack_bits, start1, returned, "halve1_")
    kept0, got0, (out_far,) = reduce_over(
        pack_bits[:1] + event_bits + pack_bits[1:], start0, [out_far], "halve0_"
    )
    got_out = far(out_far)
    (packed_out,) = run(
        ffn_out_own, [row_b], [hidden_own, ffn_out, ffn_out_near, resid, got_out], name="ffn_out_own"
    )
    (row_grad,) = run(
        back_recv,
        [row_b],
        [place, *returned],
        name="back_recv",
    )
    got1, got0, packed_out, row_grad = tie(got1, got0, packed_out, row_grad)
    (enc_grad,) = run(finish, [like((2, size, cols), F32)], [kept0, got0, kept1, got1], name="finish")
    return (packed_out[None], row_grad, enc_grad)


def solution(mesh):
    placed = (
        P(("event", "pack", "tensor"), None),
        P(("event", "pack", "tensor")),
        P(("event", "pack", "tensor")),
        P(("event", "pack"), None),
        P(),
        P(None, None, "tensor"),
        P("tensor", None),
        P(None, None, "tensor"),
        P("tensor", None),
        P(("event", "pack"), "tensor", None),
    )
    return jax.shard_map(
        shards,
        mesh=mesh,
        in_specs=placed,
        out_specs=(
            P(("event", "pack"), "tensor", None),
            P(("event", "pack", "tensor"), None),
            P(None, ("event", "pack"), "tensor"),
        ),
        check_vma=False,
    )
```

```python
import functools

import jax
import jax.numpy as jnp
from jax import lax
from jax.experimental import pallas as pl
from jax.experimental.pallas import tpu as pltpu
from jax.sharding import PartitionSpec as P

D = 1024
HEADS = 16
HEAD = D // HEADS
EPS = 1e-06
F32 = jnp.float32
BF16 = jnp.bfloat16
MIB = 1 << 20
CHUNK = 256


def dot(left, right, dims=((1,), (0,))):
    return lax.dot_general(left, right, (dims, ((), ())), preferred_element_type=F32)


NT = ((1,), (1,))
TN = ((0,), (0,))


def bf16(value):
    return value.astype(BF16)


def silu_grad(value, sigma):
    return sigma * (1.0 + value * (1.0 - sigma))


def norm_factor(wide):
    return lax.rsqrt(jnp.mean(wide * wide, axis=-1, keepdims=True) + EPS)


def norm_back(grad, normed, factor):
    return factor * (grad - normed * jnp.mean(grad * normed, axis=-1, keepdims=True))


def joined(refs):
    return jnp.concatenate([r[...] for r in refs], axis=0)


def turned(row, rows):
    return jnp.broadcast_to(row.astype(F32), (rows, rows)).T


def like(shape, dtype):
    return jax.ShapeDtypeStruct(shape, dtype)


def run(body, outs, args, scratch=(), flops=0, name=None):
    return pl.pallas_call(
        body,
        out_shape=list(outs),
        in_specs=[pl.BlockSpec(memory_space=pltpu.VMEM)] * len(args),
        out_specs=[pl.BlockSpec(memory_space=pltpu.VMEM)] * len(outs),
        scratch_shapes=list(scratch),
        compiler_params=pltpu.CompilerParams(vmem_limit_bytes=16 * MIB),
        cost_estimate=pl.CostEstimate(flops=flops, bytes_accessed=0, transcendentals=0),
        name=name,
    )(*args)


def group_index():
    return lax.axis_index("event") * lax.axis_size("pack") + lax.axis_index("pack")


def tensor_index():
    return lax.axis_index("tensor")


def tie(*values):
    return lax.optimization_barrier(values)


def route_send(capacity, order, code, features, *outs):
    sends, place_ref = outs[:-1], outs[-1]
    groups = len(sends)
    rows, width = features.shape
    shift = rows.bit_length() - 1
    o_row = code[...] >> shift
    slot = code[...] & (rows - 1)
    o_col = turned(o_row, rows)
    i = lax.broadcasted_iota(jnp.int32, (rows, rows), 0)
    j = lax.broadcasted_iota(jnp.int32, (rows, rows), 1)
    earlier = jnp.where((o_col == o_row.astype(F32)) & (i < j), 1.0, 0.0)
    rank = jnp.sum(earlier, axis=0, keepdims=True).astype(jnp.int32)
    place = (o_row ^ group_index()) * capacity + rank
    place_ref[...] = place
    spots = lax.broadcasted_iota(jnp.int32, (groups * capacity, rows), 0)
    hot = jnp.where(spots == place, 1.0, 0.0).astype(BF16)
    big = dot(hot, features[...])
    tags = dot(hot, bf16(turned(slot + 1, rows)))
    for k, send in zip(order, sends):
        part = slice(k * capacity, (k + 1) * capacity)
        send[:, :width] = bf16(big[part])
        send[:, width:] = bf16(tags[part])


def route_recv(*refs):
    gots, (rows_ref, hot_ref) = refs[:-2], refs[-2:]
    rows, width = rows_ref.shape
    got = jnp.concatenate([g[...].astype(F32) for g in gots], axis=0)
    lanes = lax.broadcasted_iota(jnp.int32, (got.shape[0], rows), 1) + 1
    hot = jnp.where(got[:, width:] == lanes.astype(F32), 1.0, 0.0).astype(BF16)
    hot_ref[...] = hot
    rows_ref[...] = bf16(dot(hot, bf16(got[:, :width]), TN))


def back_send(order, hot, d_packed, keep, send):
    groups = len(order)
    capacity = hot.shape[0] // groups
    big = dot(hot[...], d_packed[...])
    at = {k: n * capacity for n, k in enumerate(order)}
    for target, first in ((keep, 0), (send, groups // 2)):
        parts = [big[at[first + k] : at[first + k] + capacity] for k in range(groups // 2)]
        target[...] = bf16(jnp.concatenate(parts, axis=0))


def picked(places, capacity, refs):
    wide = [r[...].astype(F32) for r in refs]
    parts = [wide[n][p * capacity : (p + 1) * capacity] for n, p in places]
    return bf16(jnp.concatenate(parts, axis=0))


def back_pick(places, capacity, *refs):
    refs[-1][...] = picked(places, capacity, refs[:-1])


def back_recv(places, capacity, place, *refs):
    got, out = picked(places, capacity, refs[:-1]), refs[-1]
    spots = lax.broadcasted_iota(jnp.int32, (got.shape[0], out.shape[0]), 0)
    hot = jnp.where(spots == place[...], 1.0, 0.0).astype(BF16)
    out[...] = bf16(dot(hot, got, TN))


def encode(rows, enc, w_in, pre_all, pre_ref, act_ref, store):
    width = rows.shape[1]
    cols = pre_ref.shape[1]
    for n in range(width // CHUNK):
        part = slice(n * CHUNK, (n + 1) * CHUNK)
        pre = dot(rows, enc[0, :, part])
        pre_all[:, part] = pre
        act_ref[:, part] = bf16(pre * jax.nn.sigmoid(pre))
    pre_ref[...] = pre_all[:, pl.ds(pl.multiple_of(tensor_index() * cols, cols), cols)]
    packed = bf16(dot(act_ref[...], enc[1]))
    wide = packed.astype(F32)
    normed = bf16(wide * norm_factor(wide))
    for c in range(w_in.shape[0]):
        store(c, bf16(dot(normed, w_in[c])))
    return packed


def encode_blocks(*refs):
    blocks, (enc, w_in, pre_ref, act_ref, packed_ref, proj_ref, pre_all) = refs[:-7], refs[-7:]
    rows = joined(blocks)
    size = blocks[0].shape[0]

    def store(c, value):
        for n in range(len(blocks)):
            proj_ref[c, n] = value[n * size : (n + 1) * size]

    packed = encode(rows, enc, w_in, pre_all, pre_ref, act_ref, store)
    packed_ref[...] = packed[:size]


def window(docs, r, rows):
    t = tensor_index()
    b = t ^ r
    ahead = jnp.where(b > 0, (b - 1) ^ t, r)
    doc_q = turned(docs[b], rows)
    doc_own = docs[b].astype(F32)
    doc_ahead = docs[jnp.maximum(b - 1, 0)].astype(F32)
    i = lax.broadcasted_iota(jnp.int32, (rows, rows), 0)
    j = lax.broadcasted_iota(jnp.int32, (rows, rows), 1)
    own = jnp.where((doc_q == doc_own) & (j <= i), 1.0, 0.0)
    prior = jnp.where(doc_q == doc_ahead, 1.0, 0.0) * jnp.where(b > 0, 1.0, 0.0)
    allowed = jnp.concatenate([prior, own], axis=1)
    root_inv = lax.rsqrt(jnp.sum(allowed, axis=1, keepdims=True))
    return ahead, allowed, root_inv


def head_masks(cols):
    lane = lax.broadcasted_iota(jnp.int32, (1, cols), 1) // HEAD
    return [jnp.where(lane == h, 1.0, 0.0) for h in range(cols // HEAD)]


def spread(value, masks):
    return jnp.concatenate([value * bf16(m) for m in masks], axis=0)


def collect(value, masks):
    rows = value.shape[0] // len(masks)
    total = None
    for h, m in enumerate(masks):
        part = value[h * rows : (h + 1) * rows] * m
        total = part if total is None else total + part
    return total


def attend_first(
    docs, fourth, pre_c, act_c, proj_a, proj_c, enc, w_in,
    pre_ref, act_ref, proj_ref, att_ref, give_ref, keep_ref, pre_all,
):
    half = fourth.shape[0]
    cols = proj_a.shape[-1]
    proj_ref[:, 0:2] = proj_a[...]
    proj_ref[:, 2:3] = proj_c[...]
    pre_ref[:half, :] = pre_c[...]
    act_ref[:half, :] = act_c[...]

    def store(c, value):
        proj_ref[c, 3] = value

    encode(
        fourth[...], enc, w_in, pre_all, pre_ref.at[half : 2 * half], act_ref.at[half : 2 * half], store
    )
    masks = head_masks(cols)
    for r, (target, place) in enumerate(((keep_ref, 1), (give_ref, 1), (keep_ref, 0), (give_ref, 0))):
        ahead, allowed, root_inv = window(docs, r, half)
        keys = jnp.concatenate([proj_ref[1, ahead], proj_ref[1, r]], axis=0)
        values = jnp.concatenate([proj_ref[2, ahead], proj_ref[2, r]], axis=0)
        many = jnp.concatenate([allowed] * len(masks), axis=0)
        scores = dot(spread(proj_ref[0, r], masks), keys, NT) * HEAD ** (-0.5)
        weights = bf16(scores * jax.nn.sigmoid(scores) * many)
        attended = collect(dot(weights, values), masks) * root_inv
        gate = proj_ref[3, r].astype(F32)
        att_ref[r] = attended
        target[place * half : (place + 1) * half, :] = bf16(attended * gate * jax.nn.sigmoid(gate))


def attn_out_part(index, keep, take, w_own, w_near, out):
    rows = out.shape[0]
    part = slice(index * rows, (index + 1) * rows)
    out[...] = bf16(dot(keep[part, :], w_own[...]) + dot(take[part, :], w_near[...]))


def residual(packed, part, got, resid_ref, normed_ref):
    resid = bf16(packed[...].astype(F32) + (part[...].astype(F32) + got[...].astype(F32)))
    resid_ref[...] = resid
    wide = resid.astype(F32)
    normed_ref[...] = bf16(wide * norm_factor(wide))


def ffn(rows_ref, d_out_ref, in_a, in_b, out_a, out_b, hidden_ref, back_ref):
    rows = rows_ref[...]
    cotangent = d_out_ref[...]
    units = out_a.shape[0]
    back = None
    for index, (w_in, w_out) in enumerate(((in_a, out_a), (in_b, out_b))):
        for n in range(units // CHUNK):
            part = slice(n * CHUNK, (n + 1) * CHUNK)
            d_hidden = dot(cotangent, w_out[part, :], NT)
            gate = dot(rows, w_in[0, :, part])
            upper = dot(rows, w_in[1, :, part])
            sigma = jax.nn.sigmoid(gate)
            silu = gate * sigma
            hidden_ref[:, index * units + n * CHUNK : index * units + (n + 1) * CHUNK] = bf16(silu * upper)
            d_gate = bf16(d_hidden * upper * silu_grad(gate, sigma))
            d_upper = bf16(d_hidden * silu)
            term = dot(d_gate, w_in[0, :, part], NT) + dot(d_upper, w_in[1, :, part], NT)
            back = term if back is None else back + term
    back_ref[...] = back.astype(back_ref.dtype)


def ffn_out_far(hidden, w_a, w_b, out):
    units = w_a.shape[0]
    out[...] = bf16(dot(hidden[:, :units], w_a[...]) + dot(hidden[:, units:], w_b[...]))


def ffn_out_own(hidden, w_a, w_b, resid, got, out):
    units = w_a.shape[0]
    total = dot(hidden[:, :units], w_a[...]) + dot(hidden[:, units:], w_b[...])
    out[...] = bf16(resid[...].astype(F32) + total + got[...].astype(F32))


def store_halves(value, out, halves):
    out[...] = value
    rows = value.shape[0] // max(len(halves), 1)
    for n, target in enumerate(halves):
        target[...] = value[n * rows : (n + 1) * rows]


def resid_back(back, got, resid, d_out, out, *halves):
    wide = resid[...].astype(F32)
    factor = norm_factor(wide)
    grad = back[...].astype(F32) + got[...].astype(F32)
    store_halves(bf16(d_out[...].astype(F32) + norm_back(grad, wide * factor, factor)), out, halves)


def attend_back(docs, d_resid, r, proj_ref, att_ref, w_out, masks, d_q, d_k, d_v, d_g):
    half = d_resid.shape[0]
    scale = HEAD ** (-0.5)
    ahead, allowed, root_inv = window(docs, r, half)
    gate = proj_ref[3, r].astype(F32)
    sigma_g = jax.nn.sigmoid(gate)
    d_gated = dot(d_resid, w_out, NT)
    d_att = bf16(d_gated * (gate * sigma_g) * root_inv)
    d_g[r] = bf16(d_gated * att_ref[r] * silu_grad(gate, sigma_g))
    keys = jnp.concatenate([proj_ref[1, ahead], proj_ref[1, r]], axis=0)
    values = jnp.concatenate([proj_ref[2, ahead], proj_ref[2, r]], axis=0)
    many = jnp.concatenate([allowed] * len(masks), axis=0)
    query = spread(proj_ref[0, r], masks)
    d_att_m = spread(d_att, masks)
    scores = dot(query, keys, NT) * scale
    sigma = jax.nn.sigmoid(scores)
    weights = bf16(scores * sigma * many)
    d_weights = dot(d_att_m, values, NT)
    d_scores = bf16(d_weights * silu_grad(scores, sigma) * many)
    d_q[r] = bf16(collect(dot(d_scores, keys), masks) * scale)
    d_keys = dot(d_scores, query, TN) * scale
    d_values = dot(weights, d_att_m, TN)
    d_k[ahead] += d_keys[:half]
    d_k[r] += d_keys[half:]
    d_v[ahead] += d_values[:half]
    d_v[r] += d_values[half:]


def attn_back_first(docs, third, fourth_a, fourth_b, proj, att, w_out, d_q, d_k, d_v, d_g):
    masks = head_masks(w_out.shape[0])
    d_k[...] = jnp.zeros_like(d_k)
    d_v[...] = jnp.zeros_like(d_v)
    for r, rows in ((2, [third]), (3, [fourth_a, fourth_b])):
        attend_back(docs, joined(rows), r, proj, att, w_out[...], masks, d_q, d_k, d_v, d_g)


def back_norm(grads, w_in, first, second):
    total = None
    for c, grad in enumerate(grads):
        left = jnp.concatenate([grad[first], grad[second]], axis=0)
        term = dot(left, w_in[c], NT)
        total = term if total is None else total + term
    return total


def attn_back_own(docs, first, proj, att, w_out, d_k_far, d_v_far, d_q, d_k, d_v, d_g):
    masks = head_masks(w_out.shape[0])
    d_k[...] = d_k_far[...]
    d_v[...] = d_v_far[...]
    attend_back(docs, first[...], 0, proj, att, w_out[...], masks, d_q, d_k, d_v, d_g)


def attn_back_second(
    docs, second, proj, att, w_out, d_q_far, d_g_far, d_q_own, d_k_own, d_v_own, d_g_own, w_in,
    give_ref, d_q, d_k, d_v, d_g, sum_k, sum_v,
):
    masks = head_masks(w_out.shape[0])
    d_q[2:4] = d_q_far[2:4]
    d_g[2:4] = d_g_far[2:4]
    d_q[0] = d_q_own[0]
    d_g[0] = d_g_own[0]
    sum_k[...] = d_k_own[...]
    sum_v[...] = d_v_own[...]
    attend_back(docs, second[...], 1, proj, att, w_out[...], masks, d_q, sum_k, sum_v, d_g)
    d_k[...] = bf16(sum_k[...])
    d_v[...] = bf16(sum_v[...])
    give_ref[...] = bf16(back_norm((d_q, d_k, d_v, d_g), w_in, 3, 1))


def attn_back_keep(d_q, d_k, d_v, d_g, w_in, keep_ref):
    keep_ref[...] = back_norm((d_q, d_k, d_v, d_g), w_in, 2, 0)


def add_near(keep, take, out_far, out_own):
    half = out_far.shape[0]
    out_far[...] = bf16(keep[:half, :] + take[:half, :].astype(F32))
    out_own[...] = bf16(keep[half:, :] + take[half:, :].astype(F32))


def packed_back(part, got, packed, d_resid, out, *halves):
    wide = packed[...].astype(F32)
    factor = norm_factor(wide)
    grad = part[...].astype(F32) + got[...].astype(F32)
    store_halves(bf16(d_resid[...].astype(F32) + norm_back(grad, wide * factor, factor)), out, halves)


def column_of(ref, index, cols):
    return ref[:, pl.ds(pl.multiple_of(index * cols, cols), cols)]


def rows_term(act_refs, cot):
    return dot(jnp.concatenate([a[...] for a in act_refs], axis=0), cot, TN)


def first_cot(cots, pre, enc):
    cols = pre.shape[1]
    cot = joined(cots)
    value = pre[...]
    w1_rows = enc[1, pl.ds(pl.multiple_of(tensor_index() * cols, cols), cols), :]
    return bf16(dot(cot, w1_rows, NT) * silu_grad(value, jax.nn.sigmoid(value)))


def cot_columns(cots, cols):
    return jnp.concatenate([column_of(c, tensor_index(), cols) for c in cots], axis=0)


def enc_grads_first(*refs):
    cots, (act0_a, act0_b, act1, pre, enc, part1, part0) = refs[:-7], refs[-7:]
    cols = pre.shape[1]
    part1[...] = rows_term([act1], cot_columns(cots, cols))
    part0[...] = rows_term([act0_a, act0_b], first_cot(cots, pre, enc))


def halve(bits, bit, total, keep, send):
    place = bits.index(bit)
    count, size, _ = keep.shape
    mine = (group_index() >> bit) & 1
    for j in range(count):
        low = j & ((1 << place) - 1)
        base = ((j >> place) << (place + 1)) | low
        for target, value in ((keep, mine), (send, 1 - mine)):
            index = base + (value << place)
            rows = total[pl.ds(pl.multiple_of(index * size, size), size), :]
            target[j] = rows.astype(target.dtype)


def enc_grad1_second(bits, bit, *refs):
    cots, (act1, part1, keep, send, total) = refs[:-5], refs[-5:]
    total[...] = rows_term([act1], cot_columns(cots, part1.shape[1])) + part1[...]
    halve(bits, bit, total, keep, send)


def enc_grad0_second(bits, bit, *refs):
    cots, (act0_a, act0_b, pre, enc, part0, keep, send, total) = refs[:-8], refs[-8:]
    total[...] = rows_term([act0_a, act0_b], first_cot(cots, pre, enc)) + part0[...]
    halve(bits, bit, total, keep, send)


def halve_again(bits, bit, kept, got, keep, send):
    place = bits.index(bit)
    mine = (group_index() >> bit) & 1
    for j in range(keep.shape[0]):
        low = j & ((1 << place) - 1)
        base = ((j >> place) << (place + 1)) | low
        for target, value in ((keep, mine), (send, 1 - mine)):
            index = base + (value << place)
            target[j] = (kept[index] + got[index].astype(F32)).astype(target.dtype)


def finish(kept0, got0, kept1, got1, out):
    out[0] = kept0[0] + got0[0].astype(F32)
    out[1] = kept1[0] + got1[0].astype(F32)


def shards(
    features,
    dest_owner,
    dest_slot,
    doc_ids,
    enc_weight,
    attn_in,
    attn_out,
    ffn_in,
    ffn_out,
    out_grad,
):
    rows_dev, width = features.shape
    group_axes = ("event", "pack")
    groups = lax.axis_size(group_axes)
    packs = lax.axis_size("pack")
    tensors = lax.axis_size("tensor")
    cols = attn_in.shape[2]
    comps = attn_in.shape[0]
    units = ffn_out.shape[0]
    d_out = out_grad[0]
    docs = doc_ids.reshape(tensors, 1, rows_dev)

    def near(value):
        return lax.ppermute(value, "tensor", [(i, i ^ 1) for i in range(tensors)])

    def far(value):
        return lax.ppermute(value, "tensor", [(i, i ^ 2) for i in range(tensors)])

    def crossed(value, k):
        return lax.ppermute(value, group_axes, [(i, i ^ k) for i in range(groups)])

    row_b = like((rows_dev, width), BF16)
    row_f = like((rows_dev, width), F32)

    mean_load = rows_dev // groups
    capacity = -(-(mean_load + mean_load // 2) // 8) * 8
    code = (dest_owner * rows_dev + dest_slot).reshape(1, rows_dev)
    order = [0] + sorted(
        range(1, groups), key=lambda k: (-((2 * (k % packs)) // packs), k % packs, k)
    )
    *sends, place = run(
        functools.partial(route_send, capacity, order),
        [like((capacity, width + rows_dev), BF16)] * groups + [like((1, rows_dev), jnp.int32)],
        [code, features],
        flops=4 * 10**9,
        name="route_send",
    )
    ffn_in_near, ffn_out_near = near(ffn_in), near(ffn_out)
    early = [crossed(sends[n], order[n]) for n in (1, 2)]
    ffn_in_near, ffn_out_near, *sends = tie(ffn_in_near, ffn_out_near, *sends)
    gots = [sends[0], *early] + [crossed(sends[n], order[n]) for n in range(3, groups)]
    mine, hot = run(
        route_recv,
        [row_b, like((groups * capacity, rows_dev), BF16)],
        gots,
        name="route_recv",
    )

    mine_far = far(mine)
    mine_near = near(mine)

    pair = 2 * rows_dev
    pre_a, act_a, packed, proj_a = run(
        encode_blocks,
        [
            like((pair, cols), F32),
            like((pair, width), BF16),
            row_b,
            like((comps, 2, rows_dev, cols), BF16),
        ],
        [mine, mine_near, enc_weight, attn_in],
        [pltpu.VMEM((pair, width), F32)],
        name="encode_first",
    )
    mine_far, proj_a = tie(mine_far, proj_a)
    mine_far, attn_out_late, d_out_late = tie(mine_far, attn_out, d_out)
    mine_both = near(mine_far)
    attn_out_near = near(attn_out_late)
    d_out_far = far(d_out_late)
    pre_c, act_c, packed_far, proj_c = run(
        encode_blocks,
        [like((rows_dev, cols), F32), row_b, row_b, like((comps, 1, rows_dev, cols), BF16)],
        [mine_far, enc_weight, attn_in],
        [pltpu.VMEM((rows_dev, width), F32)],
        name="encode_third",
    )
    pre_b, act_b, proj, attended, give, keep = run(
        attend_first,
        [
            like((pair, cols), F32),
            like((pair, width), BF16),
            like((comps, tensors, rows_dev, cols), BF16),
            like((tensors, rows_dev, cols), F32),
            like((pair, cols), BF16),
            like((pair, cols), BF16),
        ],
        [docs, mine_both, pre_c, act_c, proj_a, proj_c, enc_weight, attn_in],
        [pltpu.VMEM((rows_dev, width), F32)],
        name="attend_first",
    )
    take = near(give)


    def out_part(index, name):
        return run(
            functools.partial(attn_out_part, index),
            [row_b],
            [keep, take, attn_out, attn_out_near],
            name=name,
        )[0]

    part_far = out_part(0, "attn_out_far")
    got_own = far(part_far)
    part_own = out_part(1, "attn_out_own")
    part_own, d_out_far = tie(part_own, d_out_far)
    got_far = far(part_own)

    def feed(rows, cotangent, name):
        return run(
            ffn,
            [like((rows_dev, 2 * units), BF16), row_b],
            [rows, cotangent, ffn_in, ffn_in_near, ffn_out, ffn_out_near],
            name=name,
        )

    resid, normed2 = run(residual, [row_b, row_b], [packed, part_own, got_own], name="residual")
    hidden_own, back_own = feed(normed2, d_out, "ffn_own")
    got_far, back_own = tie(got_far, back_own)
    got_back_far = far(back_own)
    resid_far, normed2_far = run(
        residual, [row_b, row_b], [packed_far, part_far, got_far], name="residual_far"
    )
    hidden_far, back_far = feed(normed2_far, d_out_far, "ffn_far")
    got_back_own = far(back_far)

    pieces = 2
    piece_b = like((rows_dev // pieces, width), BF16)
    d_resid_far, *halves = run(
        resid_back,
        [row_b] + [piece_b] * pieces,
        [back_far, got_back_far, resid_far, d_out_far],
        name="resid_back_far",
    )
    d_resid_both = [near(h) for h in halves]
    block_f = like((tensors, rows_dev, cols), F32)
    block_b = like((tensors, rows_dev, cols), BF16)
    d_q, d_k, d_v, d_g = run(
        attn_back_first,
        [block_b, block_f, block_f, block_b],
        [docs, d_resid_far, *d_resid_both, proj, attended, attn_out],
        name="attn_back_first",
    )
    got_back_own, d_q = tie(got_back_own, d_q)
    (d_resid,) = run(resid_back, [row_b], [back_own, got_back_own, resid, d_out], name="resid_back")
    d_resid_near = near(d_resid)
    own_grads = run(
        attn_back_own,
        [block_b, block_f, block_f, block_b],
        [docs, d_resid, proj, attended, attn_out, d_k, d_v],
        name="attn_back_own",
    )
    give, *d_projected = run(
        attn_back_second,
        [like((pair, width), BF16)] + [block_b] * 4,
        [docs, d_resid_near, proj, attended, attn_out, d_q, d_g, *own_grads, attn_in],
        [pltpu.VMEM((tensors, rows_dev, cols), F32)] * 2,
        name="attn_back_second",
    )
    take = near(give)
    (keep,) = run(
        attn_back_keep,
        [like((pair, width), F32)],
        [*d_projected, attn_in],
        name="attn_back_keep",
    )
    sum_far, sum_own = run(add_near, [row_b, row_b], [keep, take], name="add_near")
    got_own = far(sum_far)
    got_far = far(sum_own)
    d_packed, *halves = run(
        packed_back,
        [row_b] + [piece_b] * pieces,
        [sum_own, got_own, packed, d_resid],
        name="packed_back",
    )

    cot_near = [near(h) for h in halves]
    half_rows = like((groups * capacity // 2, width), BF16)
    kept, back = run(
        functools.partial(back_send, order), [half_rows] * 2, [hot, d_packed], name="back_send"
    )
    back_got = crossed(back, groups // 2)

    part_f = like((width, cols), F32)
    part1, part0 = run(
        enc_grads_first,
        [part_f, part_f],
        [d_packed, *cot_near, mine, mine_near, act_a, pre_a, enc_weight],
        name="enc_grads_first",
    )
    got_far, part1, part0 = tie(got_far, part1, part0)
    cot_far, *cot_pieces = run(
        packed_back,
        [row_b] + [piece_b] * pieces,
        [sum_far, got_far, packed_far, d_resid_far],
        name="packed_back_far",
    )
    cot_both = [near(piece) for piece in cot_pieces]
    *cot_both, back_got = tie(*cot_both, back_got)
    arrays = [kept, back_got]
    held = {k: divmod(k, groups // 2) for k in range(groups)}

    def send_back(bit):
        moved = [k for k in range(groups) if k & bit]
        (back,) = run(
            functools.partial(back_pick, [held[k] for k in moved], capacity),
            [half_rows],
            arrays,
            name="back_pick",
        )
        held.update({k: (len(arrays), n) for n, k in enumerate(moved)})
        arrays.append(crossed(back, bit))

    bit = groups // 4
    while bit > 1:
        send_back(bit)
        bit //= 2

    cot_far, hidden_far = tie(cot_far, hidden_far)
    (out_far,) = run(
        ffn_out_far, [row_b], [hidden_far, ffn_out, ffn_out_near], name="ffn_out_far"
    )
    bits = list(range(groups.bit_length() - 1))
    pack_bits = bits[: packs.bit_length() - 1]
    event_bits = bits[len(pack_bits) :]
    size = width // groups
    total = [pltpu.VMEM((width, cols), F32)]

    def halves(remaining):
        shape = (2 ** (len(remaining) - 1), size, cols)
        return [like(shape, F32), like(shape, BF16)]

    def reduce_over(stages, start, name, beside=None):
        remaining = list(bits)
        kept, send = start((tuple(remaining), stages[0]))
        got = crossed(send, 1 << stages[0])
        remaining.remove(stages[0])
        for bit in stages[1:]:
            kept, send = run(
                functools.partial(halve_again, tuple(remaining), bit),
                halves(remaining),
                [kept, got],
                name=name + str(bit),
            )
            got = crossed(send, 1 << bit)
            remaining.remove(bit)
            if beside is not None and bit == stages[1]:
                got, beside[-1] = tie(got, beside[-1])
        return kept, got

    def start1(setting):
        return run(
            functools.partial(enc_grad1_second, *setting),
            halves(bits),
            [cot_far, *cot_both, act_b, part1],
            total,
            name="enc_grad1_second",
        )

    def start0(setting):
        return run(
            functools.partial(enc_grad0_second, *setting),
            halves(bits),
            [cot_far, *cot_both, mine_far, mine_both, pre_b, enc_weight, part0],
            total,
            name="enc_grad0_second",
        )

    kept1, got1 = reduce_over(event_bits + pack_bits, start1, "halve1_", arrays)
    kept0, got0 = reduce_over(pack_bits[:1] + event_bits + pack_bits[1:], start0, "halve0_")
    send_back(1)
    back_places = [held[k] for k in range(groups)]
    got_out = far(out_far)
    (packed_out,) = run(
        ffn_out_own, [row_b], [hidden_own, ffn_out, ffn_out_near, resid, got_out], name="ffn_out_own"
    )
    (row_grad,) = run(
        functools.partial(back_recv, back_places, capacity),
        [row_b],
        [place, *arrays],
        name="back_recv",
    )
    got1, got0, packed_out, row_grad = tie(got1, got0, packed_out, row_grad)
    (enc_grad,) = run(finish, [like((2, size, cols), F32)], [kept0, got0, kept1, got1], name="finish")
    return (packed_out[None], row_grad, enc_grad)


def solution(mesh):
    placed = (
        P(("event", "pack", "tensor"), None),
        P(("event", "pack", "tensor")),
        P(("event", "pack", "tensor")),
        P(("event", "pack"), None),
        P(),
        P(None, None, "tensor"),
        P("tensor", None),
        P(None, None, "tensor"),
        P("tensor", None),
        P(("event", "pack"), "tensor", None),
    )
    return jax.shard_map(
        shards,
        mesh=mesh,
        in_specs=placed,
        out_specs=(
            P(("event", "pack"), "tensor", None),
            P(("event", "pack", "tensor"), None),
            P(None, ("event", "pack"), "tensor"),
        ),
        check_vma=False,
    )
```

```python
import functools

import jax
import jax.numpy as jnp
from jax import lax
from jax.experimental import pallas as pl
from jax.experimental.pallas import tpu as pltpu
from jax.sharding import PartitionSpec as P

D = 1024
HEADS = 16
HEAD = D // HEADS
EPS = 1e-06
F32 = jnp.float32
BF16 = jnp.bfloat16
MIB = 1 << 20
CHUNK = 256


def dot(left, right, dims=((1,), (0,))):
    return lax.dot_general(left, right, (dims, ((), ())), preferred_element_type=F32)


NT = ((1,), (1,))
TN = ((0,), (0,))


def bf16(value):
    return value.astype(BF16)


def silu_grad(value, sigma):
    return sigma * (1.0 + value * (1.0 - sigma))


def norm_factor(wide):
    return lax.rsqrt(jnp.mean(wide * wide, axis=-1, keepdims=True) + EPS)


def norm_back(grad, normed, factor):
    return factor * (grad - normed * jnp.mean(grad * normed, axis=-1, keepdims=True))


def joined(refs):
    return jnp.concatenate([r[...] for r in refs], axis=0)


def store_halves(value, out, halves):
    out[...] = value
    rows = value.shape[0] // max(len(halves), 1)
    for n, target in enumerate(halves):
        target[...] = value[n * rows : (n + 1) * rows]


def turned(row, rows):
    return jnp.broadcast_to(row.astype(F32), (rows, rows)).T


def like(shape, dtype):
    return jax.ShapeDtypeStruct(shape, dtype)


def run(body, outs, args, scratch=(), flops=0, name=None):
    return pl.pallas_call(
        body,
        out_shape=list(outs),
        in_specs=[pl.BlockSpec(memory_space=pltpu.VMEM)] * len(args),
        out_specs=[pl.BlockSpec(memory_space=pltpu.VMEM)] * len(outs),
        scratch_shapes=list(scratch),
        compiler_params=pltpu.CompilerParams(vmem_limit_bytes=16 * MIB),
        cost_estimate=pl.CostEstimate(flops=flops, bytes_accessed=0, transcendentals=0),
        name=name,
    )(*args)


def group_index():
    return lax.axis_index("event") * lax.axis_size("pack") + lax.axis_index("pack")


def tensor_index():
    return lax.axis_index("tensor")


def tie(*values):
    return lax.optimization_barrier(values)


def route_send(capacity, order, code, features, *outs):
    sends, place_ref = outs[:-1], outs[-1]
    groups = len(sends)
    rows, width = features.shape
    shift = rows.bit_length() - 1
    o_row = code[...] >> shift
    slot = code[...] & (rows - 1)
    o_col = turned(o_row, rows)
    i = lax.broadcasted_iota(jnp.int32, (rows, rows), 0)
    j = lax.broadcasted_iota(jnp.int32, (rows, rows), 1)
    earlier = jnp.where((o_col == o_row.astype(F32)) & (i < j), 1.0, 0.0)
    rank = jnp.sum(earlier, axis=0, keepdims=True).astype(jnp.int32)
    place = (o_row ^ group_index()) * capacity + rank
    place_ref[...] = place
    spots = lax.broadcasted_iota(jnp.int32, (groups * capacity, rows), 0)
    hot = jnp.where(spots == place, 1.0, 0.0).astype(BF16)
    big = dot(hot, features[...])
    tags = dot(hot, bf16(turned(slot + 1, rows)))
    for k, send in zip(order, sends):
        part = slice(k * capacity, (k + 1) * capacity)
        send[:, :width] = bf16(big[part])
        send[:, width:] = bf16(tags[part])


def route_recv(*refs):
    gots, (rows_ref, hot_ref, *halves) = refs[:-4], refs[-4:]
    rows, width = rows_ref.shape
    got = jnp.concatenate([g[...].astype(F32) for g in gots], axis=0)
    lanes = lax.broadcasted_iota(jnp.int32, (got.shape[0], rows), 1) + 1
    hot = jnp.where(got[:, width:] == lanes.astype(F32), 1.0, 0.0).astype(BF16)
    hot_ref[...] = hot
    store_halves(bf16(dot(hot, bf16(got[:, :width]), TN)), rows_ref, halves)


def back_send(order, bit, hot, d_packed, keep, send):
    groups = len(order)
    capacity = hot.shape[0] // groups
    big = dot(hot[...], d_packed[...])
    at = {k: n * capacity for n, k in enumerate(order)}
    for target, value in ((keep, 0), (send, bit)):
        chosen = [k for k in range(groups) if k & bit == value]
        parts = [big[at[k] : at[k] + capacity] for k in chosen]
        target[...] = bf16(jnp.concatenate(parts, axis=0))


def picked(places, capacity, refs):
    wide = [r[...].astype(F32) for r in refs]
    parts = [wide[n][p * capacity : (p + 1) * capacity] for n, p in places]
    return bf16(jnp.concatenate(parts, axis=0))


def back_pick(places, capacity, *refs):
    refs[-1][...] = picked(places, capacity, refs[:-1])


def back_recv(places, capacity, place, *refs):
    got, out = picked(places, capacity, refs[:-1]), refs[-1]
    spots = lax.broadcasted_iota(jnp.int32, (got.shape[0], out.shape[0]), 0)
    hot = jnp.where(spots == place[...], 1.0, 0.0).astype(BF16)
    out[...] = bf16(dot(hot, got, TN))


def encode(rows, enc, w_in, pre_all, pre_ref, act_ref, store):
    width = rows.shape[1]
    cols = pre_ref.shape[1]
    for n in range(width // CHUNK):
        part = slice(n * CHUNK, (n + 1) * CHUNK)
        pre = dot(rows, enc[0, :, part])
        pre_all[:, part] = pre
        act_ref[:, part] = bf16(pre * jax.nn.sigmoid(pre))
    pre_ref[...] = pre_all[:, pl.ds(pl.multiple_of(tensor_index() * cols, cols), cols)]
    packed = bf16(dot(act_ref[...], enc[1]))
    wide = packed.astype(F32)
    normed = bf16(wide * norm_factor(wide))
    for c in range(w_in.shape[0]):
        store(c, bf16(dot(normed, w_in[c])))
    return packed


def encode_blocks(*refs):
    blocks, (enc, w_in, pre_ref, act_ref, packed_ref, proj_ref, pre_all) = refs[:-7], refs[-7:]
    rows = joined(blocks)
    count, size = proj_ref.shape[1:3]

    def store(c, value):
        for n in range(count):
            proj_ref[c, n] = value[n * size : (n + 1) * size]

    packed = encode(rows, enc, w_in, pre_all, pre_ref, act_ref, store)
    packed_ref[...] = packed[:size]


def window(docs, r, rows):
    t = tensor_index()
    b = t ^ r
    ahead = jnp.where(b > 0, (b - 1) ^ t, r)
    doc_q = turned(docs[b], rows)
    doc_own = docs[b].astype(F32)
    doc_ahead = docs[jnp.maximum(b - 1, 0)].astype(F32)
    i = lax.broadcasted_iota(jnp.int32, (rows, rows), 0)
    j = lax.broadcasted_iota(jnp.int32, (rows, rows), 1)
    own = jnp.where((doc_q == doc_own) & (j <= i), 1.0, 0.0)
    prior = jnp.where(doc_q == doc_ahead, 1.0, 0.0) * jnp.where(b > 0, 1.0, 0.0)
    allowed = jnp.concatenate([prior, own], axis=1)
    root_inv = lax.rsqrt(jnp.sum(allowed, axis=1, keepdims=True))
    return ahead, allowed, root_inv


def head_masks(cols):
    lane = lax.broadcasted_iota(jnp.int32, (1, cols), 1) // HEAD
    return [jnp.where(lane == h, 1.0, 0.0) for h in range(cols // HEAD)]


def spread(value, masks):
    return jnp.concatenate([value * bf16(m) for m in masks], axis=0)


def collect(value, masks):
    rows = value.shape[0] // len(masks)
    total = None
    for h, m in enumerate(masks):
        part = value[h * rows : (h + 1) * rows] * m
        total = part if total is None else total + part
    return total


def attend_first(
    docs, fourth, pre_c, act_c, proj_a, proj_c, enc, w_in,
    pre_ref, act_ref, proj_ref, att_ref, give_ref, keep_ref, pre_all,
):
    half = fourth.shape[0]
    cols = proj_a.shape[-1]
    proj_ref[:, 0:2] = proj_a[...]
    proj_ref[:, 2:3] = proj_c[...]
    pre_ref[:half, :] = pre_c[...]
    act_ref[:half, :] = act_c[...]

    def store(c, value):
        proj_ref[c, 3] = value

    encode(
        fourth[...], enc, w_in, pre_all, pre_ref.at[half : 2 * half], act_ref.at[half : 2 * half], store
    )
    masks = head_masks(cols)
    for r, (target, place) in enumerate(((keep_ref, 1), (give_ref, 1), (keep_ref, 0), (give_ref, 0))):
        ahead, allowed, root_inv = window(docs, r, half)
        keys = jnp.concatenate([proj_ref[1, ahead], proj_ref[1, r]], axis=0)
        values = jnp.concatenate([proj_ref[2, ahead], proj_ref[2, r]], axis=0)
        many = jnp.concatenate([allowed] * len(masks), axis=0)
        scores = dot(spread(proj_ref[0, r], masks), keys, NT) * HEAD ** (-0.5)
        weights = bf16(scores * jax.nn.sigmoid(scores) * many)
        attended = collect(dot(weights, values), masks) * root_inv
        gate = proj_ref[3, r].astype(F32)
        att_ref[r] = attended
        target[place * half : (place + 1) * half, :] = bf16(attended * gate * jax.nn.sigmoid(gate))


def attn_out_part(index, keep, take, w_own, w_near, out):
    rows = out.shape[0]
    part = slice(index * rows, (index + 1) * rows)
    out[...] = bf16(dot(keep[part, :], w_own[...]) + dot(take[part, :], w_near[...]))


def residual(packed, part, got, resid_ref, normed_ref):
    resid = bf16(packed[...].astype(F32) + (part[...].astype(F32) + got[...].astype(F32)))
    resid_ref[...] = resid
    wide = resid.astype(F32)
    normed_ref[...] = bf16(wide * norm_factor(wide))


def ffn(rows_ref, d_out_ref, in_a, in_b, out_a, out_b, hidden_ref, back_ref):
    rows = rows_ref[...]
    cotangent = d_out_ref[...]
    units = out_a.shape[0]
    back = None
    for index, (w_in, w_out) in enumerate(((in_a, out_a), (in_b, out_b))):
        for n in range(units // CHUNK):
            part = slice(n * CHUNK, (n + 1) * CHUNK)
            d_hidden = dot(cotangent, w_out[part, :], NT)
            gate = dot(rows, w_in[0, :, part])
            upper = dot(rows, w_in[1, :, part])
            sigma = jax.nn.sigmoid(gate)
            silu = gate * sigma
            hidden_ref[:, index * units + n * CHUNK : index * units + (n + 1) * CHUNK] = bf16(silu * upper)
            d_gate = bf16(d_hidden * upper * silu_grad(gate, sigma))
            d_upper = bf16(d_hidden * silu)
            term = dot(d_gate, w_in[0, :, part], NT) + dot(d_upper, w_in[1, :, part], NT)
            back = term if back is None else back + term
    back_ref[...] = back.astype(back_ref.dtype)


def ffn_out_far(hidden, w_a, w_b, out):
    units = w_a.shape[0]
    out[...] = bf16(dot(hidden[:, :units], w_a[...]) + dot(hidden[:, units:], w_b[...]))


def ffn_out_own(hidden, w_a, w_b, resid, got, out):
    units = w_a.shape[0]
    total = dot(hidden[:, :units], w_a[...]) + dot(hidden[:, units:], w_b[...])
    out[...] = bf16(resid[...].astype(F32) + total + got[...].astype(F32))


def resid_back(back, got, resid, d_out, out, *halves):
    wide = resid[...].astype(F32)
    factor = norm_factor(wide)
    grad = back[...].astype(F32) + got[...].astype(F32)
    store_halves(bf16(d_out[...].astype(F32) + norm_back(grad, wide * factor, factor)), out, halves)


def attend_back(docs, d_resid, r, proj_ref, att_ref, w_out, masks, d_q, d_k, d_v, d_g):
    half = d_resid.shape[0]
    scale = HEAD ** (-0.5)
    ahead, allowed, root_inv = window(docs, r, half)
    gate = proj_ref[3, r].astype(F32)
    sigma_g = jax.nn.sigmoid(gate)
    d_gated = dot(d_resid, w_out, NT)
    d_att = bf16(d_gated * (gate * sigma_g) * root_inv)
    d_g[r] = bf16(d_gated * att_ref[r] * silu_grad(gate, sigma_g))
    keys = jnp.concatenate([proj_ref[1, ahead], proj_ref[1, r]], axis=0)
    values = jnp.concatenate([proj_ref[2, ahead], proj_ref[2, r]], axis=0)
    many = jnp.concatenate([allowed] * len(masks), axis=0)
    query = spread(proj_ref[0, r], masks)
    d_att_m = spread(d_att, masks)
    scores = dot(query, keys, NT) * scale
    sigma = jax.nn.sigmoid(scores)
    weights = bf16(scores * sigma * many)
    d_weights = dot(d_att_m, values, NT)
    d_scores = bf16(d_weights * silu_grad(scores, sigma) * many)
    d_q[r] = bf16(collect(dot(d_scores, keys), masks) * scale)
    d_keys = dot(d_scores, query, TN) * scale
    d_values = dot(weights, d_att_m, TN)
    d_k[ahead] += d_keys[:half]
    d_k[r] += d_keys[half:]
    d_v[ahead] += d_values[:half]
    d_v[r] += d_values[half:]


def attn_back_first(docs, third, fourth_a, fourth_b, proj, att, w_out, d_q, d_k, d_v, d_g):
    masks = head_masks(w_out.shape[0])
    d_k[...] = jnp.zeros_like(d_k)
    d_v[...] = jnp.zeros_like(d_v)
    for r, rows in ((2, [third]), (3, [fourth_a, fourth_b])):
        attend_back(docs, joined(rows), r, proj, att, w_out[...], masks, d_q, d_k, d_v, d_g)


def back_norm(grads, w_in, first, second):
    total = None
    for c, grad in enumerate(grads):
        left = jnp.concatenate([grad[first], grad[second]], axis=0)
        term = dot(left, w_in[c], NT)
        total = term if total is None else total + term
    return total


def attn_back_own(docs, first, proj, att, w_out, d_k_far, d_v_far, d_q, d_k, d_v, d_g):
    masks = head_masks(w_out.shape[0])
    d_k[...] = d_k_far[...]
    d_v[...] = d_v_far[...]
    attend_back(docs, first[...], 0, proj, att, w_out[...], masks, d_q, d_k, d_v, d_g)


def attn_back_second(
    docs, second, proj, att, w_out, d_q_far, d_g_far, d_q_own, d_k_own, d_v_own, d_g_own, w_in,
    give_ref, d_q, d_k, d_v, d_g, sum_k, sum_v,
):
    masks = head_masks(w_out.shape[0])
    d_q[2:4] = d_q_far[2:4]
    d_g[2:4] = d_g_far[2:4]
    d_q[0] = d_q_own[0]
    d_g[0] = d_g_own[0]
    sum_k[...] = d_k_own[...]
    sum_v[...] = d_v_own[...]
    attend_back(docs, second[...], 1, proj, att, w_out[...], masks, d_q, sum_k, sum_v, d_g)
    d_k[...] = bf16(sum_k[...])
    d_v[...] = bf16(sum_v[...])
    give_ref[...] = bf16(back_norm((d_q, d_k, d_v, d_g), w_in, 3, 1))


def attn_back_keep(d_q, d_k, d_v, d_g, w_in, keep_ref):
    keep_ref[...] = back_norm((d_q, d_k, d_v, d_g), w_in, 2, 0)


def add_near(keep, take, out_far, out_own):
    half = out_far.shape[0]
    out_far[...] = bf16(keep[:half, :] + take[:half, :].astype(F32))
    out_own[...] = bf16(keep[half:, :] + take[half:, :].astype(F32))


def packed_back(part, got, packed, d_resid, out, *halves):
    wide = packed[...].astype(F32)
    factor = norm_factor(wide)
    grad = part[...].astype(F32) + got[...].astype(F32)
    store_halves(bf16(d_resid[...].astype(F32) + norm_back(grad, wide * factor, factor)), out, halves)


def column_of(ref, index, cols):
    return ref[:, pl.ds(pl.multiple_of(index * cols, cols), cols)]


def rows_term(act_refs, cot):
    return dot(jnp.concatenate([a[...] for a in act_refs], axis=0), cot, TN)


def first_cot(cots, pre, enc):
    cols = pre.shape[1]
    cot = joined(cots)
    value = pre[...]
    w1_rows = enc[1, pl.ds(pl.multiple_of(tensor_index() * cols, cols), cols), :]
    return bf16(dot(cot, w1_rows, NT) * silu_grad(value, jax.nn.sigmoid(value)))


def cot_columns(cots, cols):
    return jnp.concatenate([column_of(c, tensor_index(), cols) for c in cots], axis=0)


def enc_grads_first(*refs):
    rows, (act1, pre, enc, part1, part0) = refs[:-5], refs[-5:]
    cots, act0 = rows[: len(rows) // 2], rows[len(rows) // 2 :]
    cols = pre.shape[1]
    part1[...] = rows_term([act1], cot_columns(cots, cols))
    part0[...] = rows_term(act0, first_cot(cots, pre, enc))


def halve(bits, bit, total, keep, send):
    place = bits.index(bit)
    count, size, _ = keep.shape
    mine = (group_index() >> bit) & 1
    for j in range(count):
        low = j & ((1 << place) - 1)
        base = ((j >> place) << (place + 1)) | low
        for target, value in ((keep, mine), (send, 1 - mine)):
            index = base + (value << place)
            rows = total[pl.ds(pl.multiple_of(index * size, size), size), :]
            target[j] = rows.astype(target.dtype)


def enc_grad1_second(bits, bit, *refs):
    cots, (act1, part1, keep, send, total) = refs[:-5], refs[-5:]
    total[...] = rows_term([act1], cot_columns(cots, part1.shape[1])) + part1[...]
    halve(bits, bit, total, keep, send)


def enc_grad0_second(bits, bit, *refs):
    cots, (act0_a, act0_b, pre, enc, part0, keep, send, total) = refs[:-8], refs[-8:]
    total[...] = rows_term([act0_a, act0_b], first_cot(cots, pre, enc)) + part0[...]
    halve(bits, bit, total, keep, send)


def halve_again(bits, bit, kept, got, keep, send):
    place = bits.index(bit)
    mine = (group_index() >> bit) & 1
    for j in range(keep.shape[0]):
        low = j & ((1 << place) - 1)
        base = ((j >> place) << (place + 1)) | low
        for target, value in ((keep, mine), (send, 1 - mine)):
            index = base + (value << place)
            target[j] = (kept[index] + got[index].astype(F32)).astype(target.dtype)


def finish(kept0, got0, kept1, got1, out):
    out[0] = kept0[0] + got0[0].astype(F32)
    out[1] = kept1[0] + got1[0].astype(F32)


def shards(
    features,
    dest_owner,
    dest_slot,
    doc_ids,
    enc_weight,
    attn_in,
    attn_out,
    ffn_in,
    ffn_out,
    out_grad,
):
    rows_dev, width = features.shape
    group_axes = ("event", "pack")
    groups = lax.axis_size(group_axes)
    packs = lax.axis_size("pack")
    tensors = lax.axis_size("tensor")
    cols = attn_in.shape[2]
    comps = attn_in.shape[0]
    units = ffn_out.shape[0]
    d_out = out_grad[0]
    docs = doc_ids.reshape(tensors, 1, rows_dev)

    def near(value):
        return lax.ppermute(value, "tensor", [(i, i ^ 1) for i in range(tensors)])

    def far(value):
        return lax.ppermute(value, "tensor", [(i, i ^ 2) for i in range(tensors)])

    def crossed(value, k):
        return lax.ppermute(value, group_axes, [(i, i ^ k) for i in range(groups)])

    row_b = like((rows_dev, width), BF16)
    row_f = like((rows_dev, width), F32)

    mean_load = rows_dev // groups
    capacity = -(-(mean_load + mean_load // 2) // 8) * 8
    code = (dest_owner * rows_dev + dest_slot).reshape(1, rows_dev)
    order = [0] + sorted(
        range(1, groups), key=lambda k: (-((2 * (k % packs)) // packs), k % packs, k)
    )
    *sends, place = run(
        functools.partial(route_send, capacity, order),
        [like((capacity, width + rows_dev), BF16)] * groups + [like((1, rows_dev), jnp.int32)],
        [code, features],
        flops=4 * 10**9,
        name="route_send",
    )
    ffn_in_near, ffn_out_near = near(ffn_in), near(ffn_out)
    early = [crossed(sends[n], order[n]) for n in (1, 2)]
    ffn_in_near, ffn_out_near, *sends = tie(ffn_in_near, ffn_out_near, *sends)
    gots = [sends[0], *early] + [crossed(sends[n], order[n]) for n in range(3, groups)]
    pieces = 2
    piece_b = like((rows_dev // pieces, width), BF16)
    mine, hot, *halves = run(
        route_recv,
        [row_b, like((groups * capacity, rows_dev), BF16)] + [piece_b] * pieces,
        gots,
        name="route_recv",
    )

    mine_far = far(mine)
    mine_near = [near(h) for h in halves]

    pair = 2 * rows_dev
    pre_a, act_a, packed, proj_a = run(
        encode_blocks,
        [
            like((pair, cols), F32),
            like((pair, width), BF16),
            row_b,
            like((comps, 2, rows_dev, cols), BF16),
        ],
        [mine, *mine_near, enc_weight, attn_in],
        [pltpu.VMEM((pair, width), F32)],
        name="encode_first",
    )
    mine_far, proj_a = tie(mine_far, proj_a)
    mine_far, attn_out_late, d_out_late = tie(mine_far, attn_out, d_out)
    mine_both = near(mine_far)
    attn_out_near = near(attn_out_late)
    d_out_far = far(d_out_late)
    pre_c, act_c, packed_far, proj_c = run(
        encode_blocks,
        [like((rows_dev, cols), F32), row_b, row_b, like((comps, 1, rows_dev, cols), BF16)],
        [mine_far, enc_weight, attn_in],
        [pltpu.VMEM((rows_dev, width), F32)],
        name="encode_third",
    )
    pre_b, act_b, proj, attended, give, keep = run(
        attend_first,
        [
            like((pair, cols), F32),
            like((pair, width), BF16),
            like((comps, tensors, rows_dev, cols), BF16),
            like((tensors, rows_dev, cols), F32),
            like((pair, cols), BF16),
            like((pair, cols), BF16),
        ],
        [docs, mine_both, pre_c, act_c, proj_a, proj_c, enc_weight, attn_in],
        [pltpu.VMEM((rows_dev, width), F32)],
        name="attend_first",
    )
    take = near(give)


    def out_part(index, name):
        return run(
            functools.partial(attn_out_part, index),
            [row_b],
            [keep, take, attn_out, attn_out_near],
            name=name,
        )[0]

    part_far = out_part(0, "attn_out_far")
    got_own = far(part_far)
    part_own = out_part(1, "attn_out_own")
    part_own, d_out_far = tie(part_own, d_out_far)
    got_far = far(part_own)

    def feed(rows, cotangent, name):
        return run(
            ffn,
            [like((rows_dev, 2 * units), BF16), row_b],
            [rows, cotangent, ffn_in, ffn_in_near, ffn_out, ffn_out_near],
            name=name,
        )

    resid, normed2 = run(residual, [row_b, row_b], [packed, part_own, got_own], name="residual")
    hidden_own, back_own = feed(normed2, d_out, "ffn_own")
    got_far, back_own = tie(got_far, back_own)
    got_back_far = far(back_own)
    resid_far, normed2_far = run(
        residual, [row_b, row_b], [packed_far, part_far, got_far], name="residual_far"
    )
    hidden_far, back_far = feed(normed2_far, d_out_far, "ffn_far")
    got_back_own = far(back_far)

    d_resid_far, *halves = run(
        resid_back,
        [row_b] + [piece_b] * pieces,
        [back_far, got_back_far, resid_far, d_out_far],
        name="resid_back_far",
    )
    d_resid_both = [near(h) for h in halves]
    block_f = like((tensors, rows_dev, cols), F32)
    block_b = like((tensors, rows_dev, cols), BF16)
    d_q, d_k, d_v, d_g = run(
        attn_back_first,
        [block_b, block_f, block_f, block_b],
        [docs, d_resid_far, *d_resid_both, proj, attended, attn_out],
        name="attn_back_first",
    )
    got_back_own, d_q = tie(got_back_own, d_q)
    (d_resid,) = run(resid_back, [row_b], [back_own, got_back_own, resid, d_out], name="resid_back")
    d_resid_near = near(d_resid)
    own_grads = run(
        attn_back_own,
        [block_b, block_f, block_f, block_b],
        [docs, d_resid, proj, attended, attn_out, d_k, d_v],
        name="attn_back_own",
    )
    give, *d_projected = run(
        attn_back_second,
        [like((pair, width), BF16)] + [block_b] * 4,
        [docs, d_resid_near, proj, attended, attn_out, d_q, d_g, *own_grads, attn_in],
        [pltpu.VMEM((tensors, rows_dev, cols), F32)] * 2,
        name="attn_back_second",
    )
    take = near(give)
    (keep,) = run(
        attn_back_keep,
        [like((pair, width), F32)],
        [*d_projected, attn_in],
        name="attn_back_keep",
    )
    sum_far, sum_own = run(add_near, [row_b, row_b], [keep, take], name="add_near")
    got_own = far(sum_far)
    got_far = far(sum_own)
    d_packed, *halves = run(
        packed_back,
        [row_b] + [piece_b] * pieces,
        [sum_own, got_own, packed, d_resid],
        name="packed_back",
    )

    cot_near = [near(h) for h in halves]
    half_rows = like((groups * capacity // 2, width), BF16)
    group_bits = [1 << b for b in range(groups.bit_length() - 1)]
    near_bit, pack_far, event_far = group_bits[0], group_bits[1 : packs.bit_length() - 1], group_bits[packs.bit_length() - 1 :]
    back_bits = pack_far[::-1] + event_far[::-1] + [near_bit]
    kept, back = run(
        functools.partial(back_send, order, back_bits[0]), [half_rows] * 2, [hot, d_packed], name="back_send"
    )
    back_got = crossed(back, back_bits[0])

    part_f = like((width, cols), F32)
    part1, part0 = run(
        enc_grads_first,
        [part_f, part_f],
        [d_packed, *cot_near, mine, *mine_near, act_a, pre_a, enc_weight],
        name="enc_grads_first",
    )
    got_far, part1, part0 = tie(got_far, part1, part0)
    cot_far, *cot_pieces = run(
        packed_back,
        [row_b] + [like((rows_dev // 4, width), BF16)] * 4,
        [sum_far, got_far, packed_far, d_resid_far],
        name="packed_back_far",
    )
    cot_both = [near(piece) for piece in cot_pieces]
    cot_far, hidden_far = tie(cot_far, hidden_far)
    (out_far,) = run(
        ffn_out_far, [row_b], [hidden_far, ffn_out, ffn_out_near], name="ffn_out_far"
    )
    bits = list(range(groups.bit_length() - 1))
    pack_bits = bits[: packs.bit_length() - 1]
    event_bits = bits[len(pack_bits) :]
    size = width // groups
    total = [pltpu.VMEM((width, cols), F32)]

    def halves(remaining):
        shape = (2 ** (len(remaining) - 1), size, cols)
        return [like(shape, F32), like(shape, BF16)]

    def reduce_over(stages, kept, send, name, beside=False):
        remaining = list(bits)
        got = crossed(send, 1 << stages[0])
        remaining.remove(stages[0])
        for bit in stages[1:]:
            kept, send = run(
                functools.partial(halve_again, tuple(remaining), bit),
                halves(remaining),
                [kept, got],
                name=name + str(bit),
            )
            got = crossed(send, 1 << bit)
            remaining.remove(bit)
            if beside and bit == stages[1]:
                got, arrays[-1] = tie(got, arrays[-1])
        return kept, got

    def start1(setting):
        return run(
            functools.partial(enc_grad1_second, *setting),
            halves(bits),
            [cot_far, *cot_both, act_b, part1],
            total,
            name="enc_grad1_second",
        )

    def start0(setting):
        return run(
            functools.partial(enc_grad0_second, *setting),
            halves(bits),
            [cot_far, *cot_both, mine_far, mine_both, pre_b, enc_weight, part0],
            total,
            name="enc_grad0_second",
        )

    kept1, send1 = start1((tuple(bits), event_bits[0]))
    send1, part0 = tie(send1, part0)
    part0, back_got = tie(part0, back_got)
    kept0, send0 = start0((tuple(bits), pack_bits[0]))
    arrays = [kept, back_got]
    held = {}
    for n, value in enumerate((0, back_bits[0])):
        chosen = [k for k in range(groups) if k & back_bits[0] == value]
        held.update({k: (n, at) for at, k in enumerate(chosen)})

    def send_back(bit):
        moved = [k for k in range(groups) if k & bit]
        (back,) = run(
            functools.partial(back_pick, [held[k] for k in moved], capacity),
            [half_rows],
            arrays,
            name="back_pick",
        )
        held.update({k: (len(arrays), n) for n, k in enumerate(moved)})
        arrays.append(crossed(back, bit))

    for bit in back_bits[1:-1]:
        send_back(bit)
    kept1, got1 = reduce_over(event_bits + pack_bits, kept1, send1, "halve1_", True)
    kept0, got0 = reduce_over(
        pack_bits[:1] + event_bits + pack_bits[1:], kept0, send0, "halve0_"
    )
    send_back(back_bits[-1])
    back_places = [held[k] for k in range(groups)]
    got_out = far(out_far)
    (packed_out,) = run(
        ffn_out_own, [row_b], [hidden_own, ffn_out, ffn_out_near, resid, got_out], name="ffn_out_own"
    )
    (row_grad,) = run(
        functools.partial(back_recv, back_places, capacity),
        [row_b],
        [place, *arrays],
        name="back_recv",
    )
    got1, got0, packed_out, row_grad = tie(got1, got0, packed_out, row_grad)
    (enc_grad,) = run(finish, [like((2, size, cols), F32)], [kept0, got0, kept1, got1], name="finish")
    return (packed_out[None], row_grad, enc_grad)


def solution(mesh):
    placed = (
        P(("event", "pack", "tensor"), None),
        P(("event", "pack", "tensor")),
        P(("event", "pack", "tensor")),
        P(("event", "pack"), None),
        P(),
        P(None, None, "tensor"),
        P("tensor", None),
        P(None, None, "tensor"),
        P("tensor", None),
        P(("event", "pack"), "tensor", None),
    )
    return jax.shard_map(
        shards,
        mesh=mesh,
        in_specs=placed,
        out_specs=(
            P(("event", "pack"), "tensor", None),
            P(("event", "pack", "tensor"), None),
            P(None, ("event", "pack"), "tensor"),
        ),
        check_vma=False,
    )
```

```python
import functools

import jax
import jax.numpy as jnp
from jax import lax
from jax.experimental import pallas as pl
from jax.experimental.pallas import tpu as pltpu
from jax.sharding import PartitionSpec as P

D = 1024
HEADS = 16
HEAD = D // HEADS
EPS = 1e-06
F32 = jnp.float32
BF16 = jnp.bfloat16
MIB = 1 << 20
CHUNK = 256


def dot(left, right, dims=((1,), (0,))):
    return lax.dot_general(left, right, (dims, ((), ())), preferred_element_type=F32)


NT = ((1,), (1,))
TN = ((0,), (0,))


def bf16(value):
    return value.astype(BF16)


def silu_grad(value, sigma):
    return sigma * (1.0 + value * (1.0 - sigma))


def norm_factor(wide):
    return lax.rsqrt(jnp.mean(wide * wide, axis=-1, keepdims=True) + EPS)


def norm_back(grad, normed, factor):
    return factor * (grad - normed * jnp.mean(grad * normed, axis=-1, keepdims=True))


def joined(refs):
    return jnp.concatenate([r[...] for r in refs], axis=0)


def store_halves(value, out, halves):
    out[...] = value
    rows = value.shape[0] // max(len(halves), 1)
    for n, target in enumerate(halves):
        target[...] = value[n * rows : (n + 1) * rows]


def turned(row, rows):
    return jnp.broadcast_to(row.astype(F32), (rows, rows)).T


def like(shape, dtype):
    return jax.ShapeDtypeStruct(shape, dtype)


def run(body, outs, args, scratch=(), flops=0, name=None):
    return pl.pallas_call(
        body,
        out_shape=list(outs),
        in_specs=[pl.BlockSpec(memory_space=pltpu.VMEM)] * len(args),
        out_specs=[pl.BlockSpec(memory_space=pltpu.VMEM)] * len(outs),
        scratch_shapes=list(scratch),
        compiler_params=pltpu.CompilerParams(vmem_limit_bytes=16 * MIB),
        cost_estimate=pl.CostEstimate(flops=flops, bytes_accessed=0, transcendentals=0),
        name=name,
    )(*args)


def group_index():
    return lax.axis_index("event") * lax.axis_size("pack") + lax.axis_index("pack")


def tensor_index():
    return lax.axis_index("tensor")


def tie(*values):
    return lax.optimization_barrier(values)


def route_send(capacity, order, code, features, *outs):
    sends, place_ref = outs[:-1], outs[-1]
    groups = len(sends)
    rows, width = features.shape
    shift = rows.bit_length() - 1
    o_row = code[...] >> shift
    slot = code[...] & (rows - 1)
    o_col = turned(o_row, rows)
    i = lax.broadcasted_iota(jnp.int32, (rows, rows), 0)
    j = lax.broadcasted_iota(jnp.int32, (rows, rows), 1)
    earlier = jnp.where((o_col == o_row.astype(F32)) & (i < j), 1.0, 0.0)
    rank = jnp.sum(earlier, axis=0, keepdims=True).astype(jnp.int32)
    place = (o_row ^ group_index()) * capacity + rank
    place_ref[...] = place
    spots = lax.broadcasted_iota(jnp.int32, (groups * capacity, rows), 0)
    hot = jnp.where(spots == place, 1.0, 0.0).astype(BF16)
    big = dot(hot, features[...])
    tags = dot(hot, bf16(turned(slot + 1, rows)))
    for k, send in zip(order, sends):
        part = slice(k * capacity, (k + 1) * capacity)
        send[:, :width] = bf16(big[part])
        send[:, width:] = bf16(tags[part])


def route_recv(*refs):
    gots, (rows_ref, hot_ref, *halves) = refs[:-4], refs[-4:]
    rows, width = rows_ref.shape
    got = jnp.concatenate([g[...].astype(F32) for g in gots], axis=0)
    lanes = lax.broadcasted_iota(jnp.int32, (got.shape[0], rows), 1) + 1
    hot = jnp.where(got[:, width:] == lanes.astype(F32), 1.0, 0.0).astype(BF16)
    hot_ref[...] = hot
    store_halves(bf16(dot(hot, bf16(got[:, :width]), TN)), rows_ref, halves)


def back_send(order, bit, hot, d_packed, keep, send):
    groups = len(order)
    capacity = hot.shape[0] // groups
    big = dot(hot[...], d_packed[...])
    at = {k: n * capacity for n, k in enumerate(order)}
    for target, value in ((keep, 0), (send, bit)):
        chosen = [k for k in range(groups) if k & bit == value]
        parts = [big[at[k] : at[k] + capacity] for k in chosen]
        target[...] = bf16(jnp.concatenate(parts, axis=0))


def picked(places, capacity, refs):
    wide = [r[...].astype(F32) for r in refs]
    parts = [wide[n][p * capacity : (p + 1) * capacity] for n, p in places]
    return bf16(jnp.concatenate(parts, axis=0))


def back_pick(places, capacity, *refs):
    refs[-1][...] = picked(places, capacity, refs[:-1])


def back_recv(places, capacity, place, *refs):
    got, out = picked(places, capacity, refs[:-1]), refs[-1]
    spots = lax.broadcasted_iota(jnp.int32, (got.shape[0], out.shape[0]), 0)
    hot = jnp.where(spots == place[...], 1.0, 0.0).astype(BF16)
    out[...] = bf16(dot(hot, got, TN))


def encode(rows, enc, w_in, pre_all, pre_ref, act_ref, store):
    width = rows.shape[1]
    cols = pre_ref.shape[1]
    for n in range(width // CHUNK):
        part = slice(n * CHUNK, (n + 1) * CHUNK)
        pre = dot(rows, enc[0, :, part])
        pre_all[:, part] = pre
        act_ref[:, part] = bf16(pre * jax.nn.sigmoid(pre))
    pre_ref[...] = pre_all[:, pl.ds(pl.multiple_of(tensor_index() * cols, cols), cols)]
    packed = bf16(dot(act_ref[...], enc[1]))
    wide = packed.astype(F32)
    normed = bf16(wide * norm_factor(wide))
    for c in range(w_in.shape[0]):
        store(c, bf16(dot(normed, w_in[c])))
    return packed


def encode_blocks(*refs):
    blocks, (enc, w_in, pre_ref, act_ref, packed_ref, proj_ref, pre_all) = refs[:-7], refs[-7:]
    rows = joined(blocks)
    count, size = proj_ref.shape[1:3]

    def store(c, value):
        for n in range(count):
            proj_ref[c, n] = value[n * size : (n + 1) * size]

    packed = encode(rows, enc, w_in, pre_all, pre_ref, act_ref, store)
    packed_ref[...] = packed[:size]


def window(docs, r, rows):
    t = tensor_index()
    b = t ^ r
    ahead = jnp.where(b > 0, (b - 1) ^ t, r)
    doc_q = turned(docs[b], rows)
    doc_own = docs[b].astype(F32)
    doc_ahead = docs[jnp.maximum(b - 1, 0)].astype(F32)
    i = lax.broadcasted_iota(jnp.int32, (rows, rows), 0)
    j = lax.broadcasted_iota(jnp.int32, (rows, rows), 1)
    own = jnp.where((doc_q == doc_own) & (j <= i), 1.0, 0.0)
    prior = jnp.where(doc_q == doc_ahead, 1.0, 0.0) * jnp.where(b > 0, 1.0, 0.0)
    allowed = jnp.concatenate([prior, own], axis=1)
    root_inv = lax.rsqrt(jnp.sum(allowed, axis=1, keepdims=True))
    return ahead, allowed, root_inv


def head_masks(cols):
    lane = lax.broadcasted_iota(jnp.int32, (1, cols), 1) // HEAD
    return [jnp.where(lane == h, 1.0, 0.0) for h in range(cols // HEAD)]


def spread(value, masks):
    return jnp.concatenate([value * bf16(m) for m in masks], axis=0)


def collect(value, masks):
    rows = value.shape[0] // len(masks)
    total = None
    for h, m in enumerate(masks):
        part = value[h * rows : (h + 1) * rows] * m
        total = part if total is None else total + part
    return total


def attend_first(
    docs, fourth, pre_c, act_c, proj_a, proj_c, enc, w_in,
    pre_ref, act_ref, proj_ref, att_ref, give_ref, keep_ref, pre_all,
):
    half = fourth.shape[0]
    cols = proj_a.shape[-1]
    proj_ref[:, 0:2] = proj_a[...]
    proj_ref[:, 2:3] = proj_c[...]
    pre_ref[:half, :] = pre_c[...]
    act_ref[:half, :] = act_c[...]

    def store(c, value):
        proj_ref[c, 3] = value

    encode(
        fourth[...], enc, w_in, pre_all, pre_ref.at[half : 2 * half], act_ref.at[half : 2 * half], store
    )
    masks = head_masks(cols)
    for r, (target, place) in enumerate(((keep_ref, 1), (give_ref, 1), (keep_ref, 0), (give_ref, 0))):
        ahead, allowed, root_inv = window(docs, r, half)
        keys = jnp.concatenate([proj_ref[1, ahead], proj_ref[1, r]], axis=0)
        values = jnp.concatenate([proj_ref[2, ahead], proj_ref[2, r]], axis=0)
        many = jnp.concatenate([allowed] * len(masks), axis=0)
        scores = dot(spread(proj_ref[0, r], masks), keys, NT) * HEAD ** (-0.5)
        weights = bf16(scores * jax.nn.sigmoid(scores) * many)
        attended = collect(dot(weights, values), masks) * root_inv
        gate = proj_ref[3, r].astype(F32)
        att_ref[r] = attended
        target[place * half : (place + 1) * half, :] = bf16(attended * gate * jax.nn.sigmoid(gate))


def attn_out_part(index, keep, take, w_own, w_near, out):
    rows = out.shape[0]
    part = slice(index * rows, (index + 1) * rows)
    out[...] = bf16(dot(keep[part, :], w_own[...]) + dot(take[part, :], w_near[...]))


def residual(packed, part, got, resid_ref, normed_ref):
    resid = bf16(packed[...].astype(F32) + (part[...].astype(F32) + got[...].astype(F32)))
    resid_ref[...] = resid
    wide = resid.astype(F32)
    normed_ref[...] = bf16(wide * norm_factor(wide))


def ffn(rows_ref, d_out_ref, in_a, in_b, out_a, out_b, hidden_ref, back_ref):
    rows = rows_ref[...]
    cotangent = d_out_ref[...]
    units = out_a.shape[0]
    back = None
    for index, (w_in, w_out) in enumerate(((in_a, out_a), (in_b, out_b))):
        for n in range(units // CHUNK):
            part = slice(n * CHUNK, (n + 1) * CHUNK)
            d_hidden = dot(cotangent, w_out[part, :], NT)
            gate = dot(rows, w_in[0, :, part])
            upper = dot(rows, w_in[1, :, part])
            sigma = jax.nn.sigmoid(gate)
            silu = gate * sigma
            hidden_ref[:, index * units + n * CHUNK : index * units + (n + 1) * CHUNK] = bf16(silu * upper)
            d_gate = bf16(d_hidden * upper * silu_grad(gate, sigma))
            d_upper = bf16(d_hidden * silu)
            term = dot(d_gate, w_in[0, :, part], NT) + dot(d_upper, w_in[1, :, part], NT)
            back = term if back is None else back + term
    back_ref[...] = back.astype(back_ref.dtype)


def ffn_out_far(hidden, w_a, w_b, out):
    units = w_a.shape[0]
    out[...] = bf16(dot(hidden[:, :units], w_a[...]) + dot(hidden[:, units:], w_b[...]))


def ffn_out_own(hidden, w_a, w_b, resid, got, out):
    units = w_a.shape[0]
    total = dot(hidden[:, :units], w_a[...]) + dot(hidden[:, units:], w_b[...])
    out[...] = bf16(resid[...].astype(F32) + total + got[...].astype(F32))


def resid_back(back, got, resid, d_out, out, *halves):
    wide = resid[...].astype(F32)
    factor = norm_factor(wide)
    grad = back[...].astype(F32) + got[...].astype(F32)
    store_halves(bf16(d_out[...].astype(F32) + norm_back(grad, wide * factor, factor)), out, halves)


def attend_back(docs, d_resid, r, proj_ref, att_ref, w_out, masks, d_q, d_k, d_v, d_g):
    half = d_resid.shape[0]
    scale = HEAD ** (-0.5)
    ahead, allowed, root_inv = window(docs, r, half)
    gate = proj_ref[3, r].astype(F32)
    sigma_g = jax.nn.sigmoid(gate)
    d_gated = dot(d_resid, w_out, NT)
    d_att = bf16(d_gated * (gate * sigma_g) * root_inv)
    d_g[r] = bf16(d_gated * att_ref[r] * silu_grad(gate, sigma_g))
    keys = jnp.concatenate([proj_ref[1, ahead], proj_ref[1, r]], axis=0)
    values = jnp.concatenate([proj_ref[2, ahead], proj_ref[2, r]], axis=0)
    many = jnp.concatenate([allowed] * len(masks), axis=0)
    query = spread(proj_ref[0, r], masks)
    d_att_m = spread(d_att, masks)
    scores = dot(query, keys, NT) * scale
    sigma = jax.nn.sigmoid(scores)
    weights = bf16(scores * sigma * many)
    d_weights = dot(d_att_m, values, NT)
    d_scores = bf16(d_weights * silu_grad(scores, sigma) * many)
    d_q[r] = bf16(collect(dot(d_scores, keys), masks) * scale)
    d_keys = dot(d_scores, query, TN) * scale
    d_values = dot(weights, d_att_m, TN)
    d_k[ahead] += d_keys[:half]
    d_k[r] += d_keys[half:]
    d_v[ahead] += d_values[:half]
    d_v[r] += d_values[half:]


def attn_back_first(docs, third, fourth_a, fourth_b, proj, att, w_out, d_q, d_k, d_v, d_g):
    masks = head_masks(w_out.shape[0])
    d_k[...] = jnp.zeros_like(d_k)
    d_v[...] = jnp.zeros_like(d_v)
    for r, rows in ((2, [third]), (3, [fourth_a, fourth_b])):
        attend_back(docs, joined(rows), r, proj, att, w_out[...], masks, d_q, d_k, d_v, d_g)


def attn_back_own(
    docs, first, proj, att, w_out, d_q_far, d_k_far, d_v_far, d_g_far, w_in, give_ref, d_q, d_k, d_v, d_g
):
    masks = head_masks(w_out.shape[0])
    d_q[...] = d_q_far[...]
    d_g[...] = d_g_far[...]
    d_k[...] = d_k_far[...]
    d_v[...] = d_v_far[...]
    attend_back(docs, first[...], 0, proj, att, w_out[...], masks, d_q, d_k, d_v, d_g)
    give_ref[...] = bf16(back_norm((d_q, d_k, d_v, d_g), w_in, 3))


def attn_back_second(
    docs, second, proj, att, w_out, d_q_own, d_k_own, d_v_own, d_g_own, d_q, d_k, d_v, d_g, sum_k, sum_v
):
    masks = head_masks(w_out.shape[0])
    d_q[...] = d_q_own[...]
    d_g[...] = d_g_own[...]
    sum_k[...] = d_k_own[...]
    sum_v[...] = d_v_own[...]
    attend_back(docs, second[...], 1, proj, att, w_out[...], masks, d_q, sum_k, sum_v, d_g)
    d_k[...] = bf16(sum_k[...])
    d_v[...] = bf16(sum_v[...])


def back_norm(grads, w_in, block):
    total = None
    for c, grad in enumerate(grads):
        term = dot(bf16(grad[block]), w_in[c], NT)
        total = term if total is None else total + term
    return total


def back_give(block, d_q, d_k, d_v, d_g, w_in, out):
    out[...] = bf16(back_norm((d_q, d_k, d_v, d_g), w_in, block))


def back_sum(block, d_q, d_k, d_v, d_g, w_in, take, out):
    out[...] = bf16(back_norm((d_q, d_k, d_v, d_g), w_in, block) + take[...].astype(F32))


def packed_back(part, got, packed, d_resid, out, *halves):
    wide = packed[...].astype(F32)
    factor = norm_factor(wide)
    grad = part[...].astype(F32) + got[...].astype(F32)
    store_halves(bf16(d_resid[...].astype(F32) + norm_back(grad, wide * factor, factor)), out, halves)


def column_of(ref, index, cols):
    return ref[:, pl.ds(pl.multiple_of(index * cols, cols), cols)]


def rows_term(act_refs, cot):
    return dot(jnp.concatenate([a[...] for a in act_refs], axis=0), cot, TN)


def first_cot(cots, pre, enc):
    cols = pre.shape[1]
    cot = joined(cots)
    value = pre[...]
    w1_rows = enc[1, pl.ds(pl.multiple_of(tensor_index() * cols, cols), cols), :]
    return bf16(dot(cot, w1_rows, NT) * silu_grad(value, jax.nn.sigmoid(value)))


def cot_columns(cots, cols):
    return jnp.concatenate([column_of(c, tensor_index(), cols) for c in cots], axis=0)


def enc_grads_first(*refs):
    rows, (act1, pre, enc, part1, part0) = refs[:-5], refs[-5:]
    cots, act0 = rows[: len(rows) // 2], rows[len(rows) // 2 :]
    cols = pre.shape[1]
    part1[...] = rows_term([act1], cot_columns(cots, cols))
    part0[...] = rows_term(act0, first_cot(cots, pre, enc))


def halve(bits, bit, total, keep, send):
    place = bits.index(bit)
    count, size, _ = keep.shape
    mine = (group_index() >> bit) & 1
    for j in range(count):
        low = j & ((1 << place) - 1)
        base = ((j >> place) << (place + 1)) | low
        for target, value in ((keep, mine), (send, 1 - mine)):
            index = base + (value << place)
            rows = total[pl.ds(pl.multiple_of(index * size, size), size), :]
            target[j] = rows.astype(target.dtype)


def enc_grad1_second(bits, bit, *refs):
    cots, (act1, part1, keep, send, total) = refs[:-5], refs[-5:]
    total[...] = rows_term([act1], cot_columns(cots, part1.shape[1])) + part1[...]
    halve(bits, bit, total, keep, send)


def enc_grad0_second(bits, bit, *refs):
    cots, (act0_a, act0_b, pre, enc, part0, keep, send, total) = refs[:-8], refs[-8:]
    total[...] = rows_term([act0_a, act0_b], first_cot(cots, pre, enc)) + part0[...]
    halve(bits, bit, total, keep, send)


def halve_again(bits, bit, kept, got, keep, send):
    place = bits.index(bit)
    mine = (group_index() >> bit) & 1
    for j in range(keep.shape[0]):
        low = j & ((1 << place) - 1)
        base = ((j >> place) << (place + 1)) | low
        for target, value in ((keep, mine), (send, 1 - mine)):
            index = base + (value << place)
            target[j] = (kept[index] + got[index].astype(F32)).astype(target.dtype)


def finish(kept0, got0, kept1, got1, out):
    out[0] = kept0[0] + got0[0].astype(F32)
    out[1] = kept1[0] + got1[0].astype(F32)


def shards(
    features,
    dest_owner,
    dest_slot,
    doc_ids,
    enc_weight,
    attn_in,
    attn_out,
    ffn_in,
    ffn_out,
    out_grad,
):
    rows_dev, width = features.shape
    group_axes = ("event", "pack")
    groups = lax.axis_size(group_axes)
    packs = lax.axis_size("pack")
    tensors = lax.axis_size("tensor")
    cols = attn_in.shape[2]
    comps = attn_in.shape[0]
    units = ffn_out.shape[0]
    d_out = out_grad[0]
    docs = doc_ids.reshape(tensors, 1, rows_dev)

    def near(value):
        return lax.ppermute(value, "tensor", [(i, i ^ 1) for i in range(tensors)])

    def far(value):
        return lax.ppermute(value, "tensor", [(i, i ^ 2) for i in range(tensors)])

    def crossed(value, k):
        return lax.ppermute(value, group_axes, [(i, i ^ k) for i in range(groups)])

    row_b = like((rows_dev, width), BF16)
    row_f = like((rows_dev, width), F32)

    mean_load = rows_dev // groups
    capacity = -(-(mean_load + mean_load // 2) // 8) * 8
    code = (dest_owner * rows_dev + dest_slot).reshape(1, rows_dev)
    order = [0] + sorted(
        range(1, groups), key=lambda k: (-((2 * (k % packs)) // packs), k % packs, k)
    )
    *sends, place = run(
        functools.partial(route_send, capacity, order),
        [like((capacity, width + rows_dev), BF16)] * groups + [like((1, rows_dev), jnp.int32)],
        [code, features],
        flops=4 * 10**9,
        name="route_send",
    )
    ffn_in_near, ffn_out_near = near(ffn_in), near(ffn_out)
    early = [crossed(sends[n], order[n]) for n in (1, 2)]
    ffn_in_near, ffn_out_near, *sends = tie(ffn_in_near, ffn_out_near, *sends)
    gots = [sends[0], *early] + [crossed(sends[n], order[n]) for n in range(3, groups)]
    pieces = 2
    piece_b = like((rows_dev // pieces, width), BF16)
    mine, hot, *halves = run(
        route_recv,
        [row_b, like((groups * capacity, rows_dev), BF16)] + [piece_b] * pieces,
        gots,
        name="route_recv",
    )

    mine_far = far(mine)
    mine_near = [near(h) for h in halves]

    pair = 2 * rows_dev
    pre_a, act_a, packed, proj_a = run(
        encode_blocks,
        [
            like((pair, cols), F32),
            like((pair, width), BF16),
            row_b,
            like((comps, 2, rows_dev, cols), BF16),
        ],
        [mine, *mine_near, enc_weight, attn_in],
        [pltpu.VMEM((pair, width), F32)],
        name="encode_first",
    )
    mine_far, proj_a = tie(mine_far, proj_a)
    mine_far, attn_out_late, d_out_late = tie(mine_far, attn_out, d_out)
    mine_both = near(mine_far)
    attn_out_near = near(attn_out_late)
    d_out_far = far(d_out_late)
    pre_c, act_c, packed_far, proj_c = run(
        encode_blocks,
        [like((rows_dev, cols), F32), row_b, row_b, like((comps, 1, rows_dev, cols), BF16)],
        [mine_far, enc_weight, attn_in],
        [pltpu.VMEM((rows_dev, width), F32)],
        name="encode_third",
    )
    pre_b, act_b, proj, attended, give, keep = run(
        attend_first,
        [
            like((pair, cols), F32),
            like((pair, width), BF16),
            like((comps, tensors, rows_dev, cols), BF16),
            like((tensors, rows_dev, cols), F32),
            like((pair, cols), BF16),
            like((pair, cols), BF16),
        ],
        [docs, mine_both, pre_c, act_c, proj_a, proj_c, enc_weight, attn_in],
        [pltpu.VMEM((rows_dev, width), F32)],
        name="attend_first",
    )
    take = near(give)


    def out_part(index, name):
        return run(
            functools.partial(attn_out_part, index),
            [row_b],
            [keep, take, attn_out, attn_out_near],
            name=name,
        )[0]

    part_far = out_part(0, "attn_out_far")
    got_own = far(part_far)
    part_own = out_part(1, "attn_out_own")
    part_own, d_out_far = tie(part_own, d_out_far)
    got_far = far(part_own)

    def feed(rows, cotangent, name):
        return run(
            ffn,
            [like((rows_dev, 2 * units), BF16), row_b],
            [rows, cotangent, ffn_in, ffn_in_near, ffn_out, ffn_out_near],
            name=name,
        )

    resid, normed2 = run(residual, [row_b, row_b], [packed, part_own, got_own], name="residual")
    hidden_own, back_own = feed(normed2, d_out, "ffn_own")
    got_far, back_own = tie(got_far, back_own)
    got_back_far = far(back_own)
    resid_far, normed2_far = run(
        residual, [row_b, row_b], [packed_far, part_far, got_far], name="residual_far"
    )
    hidden_far, back_far = feed(normed2_far, d_out_far, "ffn_far")
    got_back_own = far(back_far)

    d_resid_far, *halves = run(
        resid_back,
        [row_b] + [piece_b] * pieces,
        [back_far, got_back_far, resid_far, d_out_far],
        name="resid_back_far",
    )
    d_resid_both = [near(h) for h in halves]
    block_f = like((tensors, rows_dev, cols), F32)
    block_b = like((tensors, rows_dev, cols), BF16)
    d_q, d_k, d_v, d_g = run(
        attn_back_first,
        [block_b, block_f, block_f, block_b],
        [docs, d_resid_far, *d_resid_both, proj, attended, attn_out],
        name="attn_back_first",
    )
    got_back_own, d_q = tie(got_back_own, d_q)
    (d_resid,) = run(resid_back, [row_b], [back_own, got_back_own, resid, d_out], name="resid_back")
    d_resid_near = near(d_resid)
    give, *own_grads = run(
        attn_back_own,
        [row_b, block_b, block_f, block_f, block_b],
        [docs, d_resid, proj, attended, attn_out, d_q, d_k, d_v, d_g, attn_in],
        name="attn_back_own",
    )
    take = near(give)
    d_projected = run(
        attn_back_second,
        [block_b] * 4,
        [docs, d_resid_near, proj, attended, attn_out, *own_grads],
        [pltpu.VMEM((tensors, rows_dev, cols), F32)] * 2,
        name="attn_back_second",
    )

    def back_part(body, block, more, name):
        return run(functools.partial(body, block), [row_b], [*d_projected, attn_in, *more], name=name)[0]

    sum_far = back_part(back_sum, 2, [take], "back_sum_far")
    take = near(back_part(back_give, 1, [], "back_give"))
    sum_own = back_part(back_sum, 0, [take], "back_sum_own")
    got_own = far(sum_far)
    got_far = far(sum_own)
    d_packed, *halves = run(
        packed_back,
        [row_b] + [piece_b] * pieces,
        [sum_own, got_own, packed, d_resid],
        name="packed_back",
    )

    cot_near = [near(h) for h in halves]
    half_rows = like((groups * capacity // 2, width), BF16)
    group_bits = [1 << b for b in range(groups.bit_length() - 1)]
    near_bit, pack_far, event_far = group_bits[0], group_bits[1 : packs.bit_length() - 1], group_bits[packs.bit_length() - 1 :]
    back_bits = pack_far[::-1] + [near_bit] + event_far[::-1]
    kept, back = run(
        functools.partial(back_send, order, back_bits[0]), [half_rows] * 2, [hot, d_packed], name="back_send"
    )
    back_got = crossed(back, back_bits[0])

    part_f = like((width, cols), F32)
    part1, part0 = run(
        enc_grads_first,
        [part_f, part_f],
        [d_packed, *cot_near, mine, *mine_near, act_a, pre_a, enc_weight],
        name="enc_grads_first",
    )
    got_far, part1, part0 = tie(got_far, part1, part0)
    cot_far, *cot_pieces = run(
        packed_back,
        [row_b] + [like((rows_dev // 4, width), BF16)] * 4,
        [sum_far, got_far, packed_far, d_resid_far],
        name="packed_back_far",
    )
    cot_both = [near(piece) for piece in cot_pieces]
    cot_far, hidden_far = tie(cot_far, hidden_far)
    (out_far,) = run(
        ffn_out_far, [row_b], [hidden_far, ffn_out, ffn_out_near], name="ffn_out_far"
    )
    bits = list(range(groups.bit_length() - 1))
    pack_bits = bits[: packs.bit_length() - 1]
    event_bits = bits[len(pack_bits) :]
    size = width // groups
    total = [pltpu.VMEM((width, cols), F32)]

    def halves(remaining):
        shape = (2 ** (len(remaining) - 1), size, cols)
        return [like(shape, F32), like(shape, BF16)]

    def reduce_over(stages, kept, send, name, beside=False):
        remaining = list(bits)
        got = crossed(send, 1 << stages[0])
        remaining.remove(stages[0])
        for bit in stages[1:]:
            kept, send = run(
                functools.partial(halve_again, tuple(remaining), bit),
                halves(remaining),
                [kept, got],
                name=name + str(bit),
            )
            got = crossed(send, 1 << bit)
            remaining.remove(bit)
            if beside and bit == stages[1]:
                got, arrays[-1] = tie(got, arrays[-1])
        return kept, got

    def start1(setting):
        return run(
            functools.partial(enc_grad1_second, *setting),
            halves(bits),
            [cot_far, *cot_both, act_b, part1],
            total,
            name="enc_grad1_second",
        )

    def start0(setting):
        return run(
            functools.partial(enc_grad0_second, *setting),
            halves(bits),
            [cot_far, *cot_both, mine_far, mine_both, pre_b, enc_weight, part0],
            total,
            name="enc_grad0_second",
        )

    kept1, send1 = start1((tuple(bits), event_bits[0]))
    send1, part0 = tie(send1, part0)
    part0, back_got = tie(part0, back_got)
    kept0, send0 = start0((tuple(bits), event_bits[0]))
    arrays = [kept, back_got]
    held = {}
    for n, value in enumerate((0, back_bits[0])):
        chosen = [k for k in range(groups) if k & back_bits[0] == value]
        held.update({k: (n, at) for at, k in enumerate(chosen)})

    def send_back(bit):
        moved = [k for k in range(groups) if k & bit]
        (back,) = run(
            functools.partial(back_pick, [held[k] for k in moved], capacity),
            [half_rows],
            arrays,
            name="back_pick",
        )
        held.update({k: (len(arrays), n) for n, k in enumerate(moved)})
        arrays.append(crossed(back, bit))

    for bit in back_bits[1:-1]:
        send_back(bit)
    kept1, got1 = reduce_over(event_bits + pack_bits, kept1, send1, "halve1_", True)
    kept0, got0 = reduce_over(event_bits + pack_bits, kept0, send0, "halve0_")
    got1, hidden_own, place = tie(got1, hidden_own, place)
    send_back(back_bits[-1])
    back_places = [held[k] for k in range(groups)]
    got_out = far(out_far)
    (packed_out,) = run(
        ffn_out_own, [row_b], [hidden_own, ffn_out, ffn_out_near, resid, got_out], name="ffn_out_own"
    )
    (row_grad,) = run(
        functools.partial(back_recv, back_places, capacity),
        [row_b],
        [place, *arrays],
        name="back_recv",
    )
    got1, got0, packed_out, row_grad = tie(got1, got0, packed_out, row_grad)
    (enc_grad,) = run(finish, [like((2, size, cols), F32)], [kept0, got0, kept1, got1], name="finish")
    return (packed_out[None], row_grad, enc_grad)


def solution(mesh):
    placed = (
        P(("event", "pack", "tensor"), None),
        P(("event", "pack", "tensor")),
        P(("event", "pack", "tensor")),
        P(("event", "pack"), None),
        P(),
        P(None, None, "tensor"),
        P("tensor", None),
        P(None, None, "tensor"),
        P("tensor", None),
        P(("event", "pack"), "tensor", None),
    )
    return jax.shard_map(
        shards,
        mesh=mesh,
        in_specs=placed,
        out_specs=(
            P(("event", "pack"), "tensor", None),
            P(("event", "pack", "tensor"), None),
            P(None, ("event", "pack"), "tensor"),
        ),
        check_vma=False,
    )
```

```python
import functools

import jax
import jax.numpy as jnp
from jax import lax
from jax.experimental import pallas as pl
from jax.experimental.pallas import tpu as pltpu
from jax.sharding import PartitionSpec as P

D = 1024
HEADS = 16
HEAD = D // HEADS
EPS = 1e-06
F32 = jnp.float32
BF16 = jnp.bfloat16
MIB = 1 << 20
CHUNK = 256


def dot(left, right, dims=((1,), (0,))):
    return lax.dot_general(left, right, (dims, ((), ())), preferred_element_type=F32)


NT = ((1,), (1,))
TN = ((0,), (0,))


def bf16(value):
    return value.astype(BF16)


def silu_grad(value, sigma):
    return sigma * (1.0 + value * (1.0 - sigma))


def norm_factor(wide):
    return lax.rsqrt(jnp.mean(wide * wide, axis=-1, keepdims=True) + EPS)


def norm_back(grad, normed, factor):
    return factor * (grad - normed * jnp.mean(grad * normed, axis=-1, keepdims=True))


def joined(refs):
    return jnp.concatenate([r[...] for r in refs], axis=0)


def store_halves(value, out, halves):
    out[...] = value
    rows = value.shape[0] // max(len(halves), 1)
    for n, target in enumerate(halves):
        target[...] = value[n * rows : (n + 1) * rows]


def turned(row, rows):
    return jnp.broadcast_to(row.astype(F32), (rows, rows)).T


def like(shape, dtype):
    return jax.ShapeDtypeStruct(shape, dtype)


def run(body, outs, args, scratch=(), flops=0, name=None, aliases=None):
    return pl.pallas_call(
        body,
        out_shape=list(outs),
        in_specs=[pl.BlockSpec(memory_space=pltpu.VMEM)] * len(args),
        out_specs=[pl.BlockSpec(memory_space=pltpu.VMEM)] * len(outs),
        scratch_shapes=list(scratch),
        input_output_aliases=aliases or {},
        compiler_params=pltpu.CompilerParams(vmem_limit_bytes=16 * MIB),
        cost_estimate=pl.CostEstimate(flops=flops, bytes_accessed=0, transcendentals=0),
        name=name,
    )(*args)


def group_index():
    return lax.axis_index("event") * lax.axis_size("pack") + lax.axis_index("pack")


def tensor_index():
    return lax.axis_index("tensor")


def tie(*values):
    return lax.optimization_barrier(values)


def route_send(capacity, order, code, features, *outs):
    sends, place_ref = outs[:-1], outs[-1]
    groups = len(sends)
    rows, width = features.shape
    shift = rows.bit_length() - 1
    o_row = code[...] >> shift
    slot = code[...] & (rows - 1)
    o_col = turned(o_row, rows)
    i = lax.broadcasted_iota(jnp.int32, (rows, rows), 0)
    j = lax.broadcasted_iota(jnp.int32, (rows, rows), 1)
    earlier = jnp.where((o_col == o_row.astype(F32)) & (i < j), 1.0, 0.0)
    rank = jnp.sum(earlier, axis=0, keepdims=True).astype(jnp.int32)
    place = (o_row ^ group_index()) * capacity + rank
    place_ref[...] = place
    spots = lax.broadcasted_iota(jnp.int32, (groups * capacity, rows), 0)
    hot = jnp.where(spots == place, 1.0, 0.0).astype(BF16)
    big = dot(hot, features[...])
    tags = dot(hot, bf16(turned(slot + 1, rows)))
    for k, send in zip(order, sends):
        part = slice(k * capacity, (k + 1) * capacity)
        send[:, :width] = bf16(big[part])
        send[:, width:] = bf16(tags[part])


def route_recv(*refs):
    gots, (rows_ref, hot_ref, *halves) = refs[:-4], refs[-4:]
    rows, width = rows_ref.shape
    got = jnp.concatenate([g[...].astype(F32) for g in gots], axis=0)
    lanes = lax.broadcasted_iota(jnp.int32, (got.shape[0], rows), 1) + 1
    hot = jnp.where(got[:, width:] == lanes.astype(F32), 1.0, 0.0).astype(BF16)
    hot_ref[...] = hot
    store_halves(bf16(dot(hot, bf16(got[:, :width]), TN)), rows_ref, halves)


def back_send(order, bit, hot, d_packed, keep, send):
    groups = len(order)
    capacity = hot.shape[0] // groups
    big = dot(hot[...], d_packed[...])
    at = {k: n * capacity for n, k in enumerate(order)}
    for target, value in ((keep, 0), (send, bit)):
        chosen = [k for k in range(groups) if k & bit == value]
        parts = [big[at[k] : at[k] + capacity] for k in chosen]
        target[...] = bf16(jnp.concatenate(parts, axis=0))


def picked(places, capacity, refs):
    wide = [r[...].astype(F32) for r in refs]
    parts = [wide[n][p * capacity : (p + 1) * capacity] for n, p in places]
    return bf16(jnp.concatenate(parts, axis=0))


def back_pick(places, capacity, *refs):
    refs[-1][...] = picked(places, capacity, refs[:-1])


def back_recv(places, capacity, place, *refs):
    got, out = picked(places, capacity, refs[:-1]), refs[-1]
    spots = lax.broadcasted_iota(jnp.int32, (got.shape[0], out.shape[0]), 0)
    hot = jnp.where(spots == place[...], 1.0, 0.0).astype(BF16)
    out[...] = bf16(dot(hot, got, TN))


def encode(rows, enc, w_in, pre_all, pre_ref, act_ref, store):
    width = rows.shape[1]
    cols = pre_ref.shape[1]
    for n in range(width // CHUNK):
        part = slice(n * CHUNK, (n + 1) * CHUNK)
        pre = dot(rows, enc[0, :, part])
        pre_all[:, part] = pre
        act_ref[:, part] = bf16(pre * jax.nn.sigmoid(pre))
    pre_ref[...] = pre_all[:, pl.ds(pl.multiple_of(tensor_index() * cols, cols), cols)]
    packed = bf16(dot(act_ref[...], enc[1]))
    wide = packed.astype(F32)
    normed = bf16(wide * norm_factor(wide))
    for c in range(w_in.shape[0]):
        store(c, bf16(dot(normed, w_in[c])))
    return packed


def encode_blocks(*refs):
    blocks, (enc, w_in, pre_ref, act_ref, packed_ref, proj_ref, pre_all) = refs[:-7], refs[-7:]
    rows = joined(blocks)
    count, size = proj_ref.shape[1:3]

    def store(c, value):
        for n in range(count):
            proj_ref[c, n] = value[n * size : (n + 1) * size]

    packed = encode(rows, enc, w_in, pre_all, pre_ref, act_ref, store)
    packed_ref[...] = packed[:size]


def turn(attn_in, attn_out, in_ref, out_ref):
    for c in range(attn_in.shape[0]):
        in_ref[c] = attn_in[c].T
    out_ref[...] = attn_out[...].T


def window(docs, r, rows):
    t = tensor_index()
    b = t ^ r
    ahead = jnp.where(b > 0, (b - 1) ^ t, r)
    doc_q = turned(docs[b], rows)
    doc_own = docs[b].astype(F32)
    doc_ahead = docs[jnp.maximum(b - 1, 0)].astype(F32)
    i = lax.broadcasted_iota(jnp.int32, (rows, rows), 0)
    j = lax.broadcasted_iota(jnp.int32, (rows, rows), 1)
    own = jnp.where((doc_q == doc_own) & (j <= i), 1.0, 0.0)
    prior = jnp.where(doc_q == doc_ahead, 1.0, 0.0) * jnp.where(b > 0, 1.0, 0.0)
    allowed = jnp.concatenate([prior, own], axis=1)
    root_inv = lax.rsqrt(jnp.sum(allowed, axis=1, keepdims=True))
    return ahead, allowed, root_inv


def head_masks(cols):
    lane = lax.broadcasted_iota(jnp.int32, (1, cols), 1) // HEAD
    return [jnp.where(lane == h, 1.0, 0.0) for h in range(cols // HEAD)]


def spread(value, masks):
    return jnp.concatenate([value * bf16(m) for m in masks], axis=0)


def collect(value, masks):
    rows = value.shape[0] // len(masks)
    total = None
    for h, m in enumerate(masks):
        part = value[h * rows : (h + 1) * rows] * m
        total = part if total is None else total + part
    return total


def attend_first(
    docs, fourth, pre_c, act_c, proj_a, proj_c, enc, w_in,
    pre_ref, act_ref, proj_ref, att_ref, give_ref, keep_ref, pre_all,
):
    half = fourth.shape[0]
    cols = proj_a.shape[-1]
    proj_ref[:, 0:2] = proj_a[...]
    proj_ref[:, 2:3] = proj_c[...]
    pre_ref[:half, :] = pre_c[...]
    act_ref[:half, :] = act_c[...]

    def store(c, value):
        proj_ref[c, 3] = value

    encode(
        fourth[...], enc, w_in, pre_all, pre_ref.at[half : 2 * half], act_ref.at[half : 2 * half], store
    )
    masks = head_masks(cols)
    for r, (target, place) in enumerate(((keep_ref, 1), (give_ref, 1), (keep_ref, 0), (give_ref, 0))):
        ahead, allowed, root_inv = window(docs, r, half)
        keys = jnp.concatenate([proj_ref[1, ahead], proj_ref[1, r]], axis=0)
        values = jnp.concatenate([proj_ref[2, ahead], proj_ref[2, r]], axis=0)
        many = jnp.concatenate([allowed] * len(masks), axis=0)
        scores = dot(spread(proj_ref[0, r], masks), keys, NT) * HEAD ** (-0.5)
        weights = bf16(scores * jax.nn.sigmoid(scores) * many)
        attended = collect(dot(weights, values), masks) * root_inv
        gate = proj_ref[3, r].astype(F32)
        att_ref[r] = attended
        target[place * half : (place + 1) * half, :] = bf16(attended * gate * jax.nn.sigmoid(gate))


def attn_out_part(index, keep, take, w_own, w_near, out):
    rows = out.shape[0]
    part = slice(index * rows, (index + 1) * rows)
    out[...] = bf16(dot(keep[part, :], w_own[...]) + dot(take[part, :], w_near[...]))


def residual(packed, part, got, resid_ref, normed_ref):
    resid = bf16(packed[...].astype(F32) + (part[...].astype(F32) + got[...].astype(F32)))
    resid_ref[...] = resid
    wide = resid.astype(F32)
    normed_ref[...] = bf16(wide * norm_factor(wide))


def ffn(rows_ref, d_out_ref, in_a, in_b, out_a, out_b, hidden_ref, back_ref):
    rows = rows_ref[...]
    cotangent = d_out_ref[...]
    units = out_a.shape[0]
    back = None
    for index, (w_in, w_out) in enumerate(((in_a, out_a), (in_b, out_b))):
        for n in range(units // CHUNK):
            part = slice(n * CHUNK, (n + 1) * CHUNK)
            d_hidden = dot(cotangent, w_out[part, :], NT)
            gate = dot(rows, w_in[0, :, part])
            upper = dot(rows, w_in[1, :, part])
            sigma = jax.nn.sigmoid(gate)
            silu = gate * sigma
            hidden_ref[:, index * units + n * CHUNK : index * units + (n + 1) * CHUNK] = bf16(silu * upper)
            d_gate = bf16(d_hidden * upper * silu_grad(gate, sigma))
            d_upper = bf16(d_hidden * silu)
            term = dot(d_gate, w_in[0, :, part], NT) + dot(d_upper, w_in[1, :, part], NT)
            back = term if back is None else back + term
    back_ref[...] = back.astype(back_ref.dtype)


def ffn_out_far(hidden, w_a, w_b, out):
    units = w_a.shape[0]
    out[...] = bf16(dot(hidden[:, :units], w_a[...]) + dot(hidden[:, units:], w_b[...]))


def ffn_out_own(hidden, w_a, w_b, resid, got, out):
    units = w_a.shape[0]
    total = dot(hidden[:, :units], w_a[...]) + dot(hidden[:, units:], w_b[...])
    out[...] = bf16(resid[...].astype(F32) + total + got[...].astype(F32))


def resid_back(back, got, resid, d_out, out, *halves):
    wide = resid[...].astype(F32)
    factor = norm_factor(wide)
    grad = back[...].astype(F32) + got[...].astype(F32)
    store_halves(bf16(d_out[...].astype(F32) + norm_back(grad, wide * factor, factor)), out, halves)


def attend_back(docs, d_resid, r, proj_ref, att_ref, w_out, masks, d_q, d_k, d_v, d_g):
    half = d_resid.shape[0]
    scale = HEAD ** (-0.5)
    ahead, allowed, root_inv = window(docs, r, half)
    gate = proj_ref[3, r].astype(F32)
    sigma_g = jax.nn.sigmoid(gate)
    d_gated = dot(d_resid, w_out)
    d_att = bf16(d_gated * (gate * sigma_g) * root_inv)
    d_g[r] = bf16(d_gated * att_ref[r] * silu_grad(gate, sigma_g))
    keys = jnp.concatenate([proj_ref[1, ahead], proj_ref[1, r]], axis=0)
    values = jnp.concatenate([proj_ref[2, ahead], proj_ref[2, r]], axis=0)
    many = jnp.concatenate([allowed] * len(masks), axis=0)
    query = spread(proj_ref[0, r], masks)
    d_att_m = spread(d_att, masks)
    scores = dot(query, keys, NT) * scale
    sigma = jax.nn.sigmoid(scores)
    weights = bf16(scores * sigma * many)
    d_weights = dot(d_att_m, values, NT)
    d_scores = bf16(d_weights * silu_grad(scores, sigma) * many)
    d_q[r] = bf16(collect(dot(d_scores, keys), masks) * scale)
    d_keys = dot(d_scores, query, TN) * scale
    d_values = dot(weights, d_att_m, TN)
    d_k[ahead] += d_keys[:half]
    d_k[r] += d_keys[half:]
    d_v[ahead] += d_values[:half]
    d_v[r] += d_values[half:]


def attn_back_first(docs, third, fourth_a, fourth_b, proj, att, w_out, d_q, d_k, d_v, d_g):
    masks = head_masks(w_out.shape[1])
    d_k[...] = jnp.zeros_like(d_k)
    d_v[...] = jnp.zeros_like(d_v)
    for r, rows in ((2, [third]), (3, [fourth_a, fourth_b])):
        attend_back(docs, joined(rows), r, proj, att, w_out[...], masks, d_q, d_k, d_v, d_g)


def attn_back_own(
    docs, first, proj, att, w_out, _q, _k, _v, _g, w_in, give_ref, d_q, d_k, d_v, d_g
):
    masks = head_masks(w_out.shape[1])
    attend_back(docs, first[...], 0, proj, att, w_out[...], masks, d_q, d_k, d_v, d_g)
    give_ref[...] = bf16(back_norm((d_q, d_k, d_v, d_g), w_in, 3))


def attn_back_second(
    docs, second, proj, att, w_out, _q, _k, _v, _g, d_q, d_k, d_v, d_g
):
    masks = head_masks(w_out.shape[1])
    attend_back(docs, second[...], 1, proj, att, w_out[...], masks, d_q, d_k, d_v, d_g)


def back_norm(grads, w_in, block):
    total = None
    for c, grad in enumerate(grads):
        term = dot(bf16(grad[block]), w_in[c])
        total = term if total is None else total + term
    return total


def back_give(block, d_q, d_k, d_v, d_g, w_in, *outs):
    value = bf16(back_norm((d_q, d_k, d_v, d_g), w_in, block))
    rows = value.shape[0] // len(outs)
    for n, out in enumerate(outs):
        out[...] = value[n * rows : (n + 1) * rows]


def back_sum(block, d_q, d_k, d_v, d_g, w_in, *refs):
    takes, out = refs[:-1], refs[-1]
    out[...] = bf16(back_norm((d_q, d_k, d_v, d_g), w_in, block) + joined(takes).astype(F32))


def packed_back(part, got, packed, d_resid, out, *halves):
    wide = packed[...].astype(F32)
    factor = norm_factor(wide)
    grad = part[...].astype(F32) + got[...].astype(F32)
    store_halves(bf16(d_resid[...].astype(F32) + norm_back(grad, wide * factor, factor)), out, halves)


def column_of(ref, index, cols):
    return ref[:, pl.ds(pl.multiple_of(index * cols, cols), cols)]


def rows_term(act_refs, cot):
    return dot(jnp.concatenate([a[...] for a in act_refs], axis=0), cot, TN)


def first_cot(cots, pre, enc):
    cols = pre.shape[1]
    cot = joined(cots)
    value = pre[...]
    w1_rows = enc[1, pl.ds(pl.multiple_of(tensor_index() * cols, cols), cols), :]
    return bf16(dot(cot, w1_rows, NT) * silu_grad(value, jax.nn.sigmoid(value)))


def cot_columns(cots, cols):
    return jnp.concatenate([column_of(c, tensor_index(), cols) for c in cots], axis=0)


def enc_grads_first(*refs):
    rows, (act1, pre, enc, part1, part0) = refs[:-5], refs[-5:]
    cots, act0 = rows[: len(rows) // 2], rows[len(rows) // 2 :]
    cols = pre.shape[1]
    part1[...] = rows_term([act1], cot_columns(cots, cols))
    part0[...] = rows_term(act0, first_cot(cots, pre, enc))


def halve(bits, bit, total, keep, send):
    place = bits.index(bit)
    count, size, _ = keep.shape
    mine = (group_index() >> bit) & 1
    for j in range(count):
        low = j & ((1 << place) - 1)
        base = ((j >> place) << (place + 1)) | low
        for target, value in ((keep, mine), (send, 1 - mine)):
            index = base + (value << place)
            rows = total[pl.ds(pl.multiple_of(index * size, size), size), :]
            target[j] = rows.astype(target.dtype)


def enc_grad1_second(bits, bit, *refs):
    cots, (act1, part1, keep, send, total) = refs[:-5], refs[-5:]
    total[...] = rows_term([act1], cot_columns(cots, part1.shape[1])) + part1[...]
    halve(bits, bit, total, keep, send)


def enc_grad0_second(bits, bit, *refs):
    cots, (act0_a, act0_b, pre, enc, part0, keep, send, total) = refs[:-8], refs[-8:]
    total[...] = rows_term([act0_a, act0_b], first_cot(cots, pre, enc)) + part0[...]
    halve(bits, bit, total, keep, send)


def halve_again(bits, bit, kept, got, keep, send):
    place = bits.index(bit)
    mine = (group_index() >> bit) & 1
    for j in range(keep.shape[0]):
        low = j & ((1 << place) - 1)
        base = ((j >> place) << (place + 1)) | low
        for target, value in ((keep, mine), (send, 1 - mine)):
            index = base + (value << place)
            target[j] = (kept[index] + got[index].astype(F32)).astype(target.dtype)


def finish(kept1, got1, kept0, got0, out):
    out[0] = kept0[0] + got0[0].astype(F32)
    out[1] = kept1[0] + got1[0].astype(F32)


def shards(
    features,
    dest_owner,
    dest_slot,
    doc_ids,
    enc_weight,
    attn_in,
    attn_out,
    ffn_in,
    ffn_out,
    out_grad,
):
    rows_dev, width = features.shape
    group_axes = ("event", "pack")
    groups = lax.axis_size(group_axes)
    packs = lax.axis_size("pack")
    tensors = lax.axis_size("tensor")
    cols = attn_in.shape[2]
    comps = attn_in.shape[0]
    units = ffn_out.shape[0]
    d_out = out_grad[0]
    docs = doc_ids.reshape(tensors, 1, rows_dev)

    def near(value):
        return lax.ppermute(value, "tensor", [(i, i ^ 1) for i in range(tensors)])

    def far(value):
        return lax.ppermute(value, "tensor", [(i, i ^ 2) for i in range(tensors)])

    def crossed(value, k):
        return lax.ppermute(value, group_axes, [(i, i ^ k) for i in range(groups)])

    row_b = like((rows_dev, width), BF16)
    row_f = like((rows_dev, width), F32)

    mean_load = rows_dev // groups
    capacity = -(-(mean_load + mean_load // 2) // 8) * 8
    code = (dest_owner * rows_dev + dest_slot).reshape(1, rows_dev)
    order = [0] + sorted(
        range(1, groups), key=lambda k: (-((2 * (k % packs)) // packs), k % packs, k)
    )
    *sends, place = run(
        functools.partial(route_send, capacity, order),
        [like((capacity, width + rows_dev), BF16)] * groups + [like((1, rows_dev), jnp.int32)],
        [code, features],
        flops=4 * 10**9,
        name="route_send",
    )
    ffn_in_near, ffn_out_near = near(ffn_in), near(ffn_out)
    early = [crossed(sends[n], order[n]) for n in (1, 2)]
    ffn_in_near, ffn_out_near, *sends = tie(ffn_in_near, ffn_out_near, *sends)
    gots = [sends[0], *early] + [crossed(sends[n], order[n]) for n in range(3, groups)]
    pieces = 2
    piece_b = like((rows_dev // pieces, width), BF16)
    in_turned, out_turned = run(
        turn,
        [like((comps, cols, width), BF16), like((width, cols), BF16)],
        [attn_in, attn_out],
        name="turn",
    )
    in_turned, *gots = tie(in_turned, *gots)
    mine, hot, *halves = run(
        route_recv,
        [row_b, like((groups * capacity, rows_dev), BF16)] + [piece_b] * pieces,
        gots,
        name="route_recv",
    )

    mine_far = far(mine)
    mine_near = [near(h) for h in halves]

    pair = 2 * rows_dev
    pre_a, act_a, packed, proj_a = run(
        encode_blocks,
        [
            like((pair, cols), F32),
            like((pair, width), BF16),
            row_b,
            like((comps, 2, rows_dev, cols), BF16),
        ],
        [mine, *mine_near, enc_weight, attn_in],
        [pltpu.VMEM((pair, width), F32)],
        name="encode_first",
    )
    mine_far, proj_a = tie(mine_far, proj_a)
    mine_far, attn_out_late, d_out_late = tie(mine_far, attn_out, d_out)
    mine_both = near(mine_far)
    attn_out_near = near(attn_out_late)
    d_out_far = far(d_out_late)
    pre_c, act_c, packed_far, proj_c = run(
        encode_blocks,
        [like((rows_dev, cols), F32), row_b, row_b, like((comps, 1, rows_dev, cols), BF16)],
        [mine_far, enc_weight, attn_in],
        [pltpu.VMEM((rows_dev, width), F32)],
        name="encode_third",
    )
    pre_b, act_b, proj, attended, give, keep = run(
        attend_first,
        [
            like((pair, cols), F32),
            like((pair, width), BF16),
            like((comps, tensors, rows_dev, cols), BF16),
            like((tensors, rows_dev, cols), F32),
            like((pair, cols), BF16),
            like((pair, cols), BF16),
        ],
        [docs, mine_both, pre_c, act_c, proj_a, proj_c, enc_weight, attn_in],
        [pltpu.VMEM((rows_dev, width), F32)],
        name="attend_first",
    )
    take = near(give)


    def out_part(index, name):
        return run(
            functools.partial(attn_out_part, index),
            [row_b],
            [keep, take, attn_out, attn_out_near],
            name=name,
        )[0]

    part_far = out_part(0, "attn_out_far")
    got_own = far(part_far)
    part_own = out_part(1, "attn_out_own")
    part_own, d_out_far = tie(part_own, d_out_far)
    got_far = far(part_own)

    def feed(rows, cotangent, name):
        return run(
            ffn,
            [like((rows_dev, 2 * units), BF16), row_b],
            [rows, cotangent, ffn_in, ffn_in_near, ffn_out, ffn_out_near],
            name=name,
        )

    resid, normed2 = run(residual, [row_b, row_b], [packed, part_own, got_own], name="residual")
    hidden_own, back_own = feed(normed2, d_out, "ffn_own")
    got_far, back_own = tie(got_far, back_own)
    got_back_far = far(back_own)
    resid_far, normed2_far = run(
        residual, [row_b, row_b], [packed_far, part_far, got_far], name="residual_far"
    )
    hidden_far, back_far = feed(normed2_far, d_out_far, "ffn_far")
    got_back_own = far(back_far)

    d_resid_far, *halves = run(
        resid_back,
        [row_b] + [piece_b] * pieces,
        [back_far, got_back_far, resid_far, d_out_far],
        name="resid_back_far",
    )
    d_resid_both = [near(h) for h in halves]
    block_f = like((tensors, rows_dev, cols), F32)
    block_b = like((tensors, rows_dev, cols), BF16)
    d_q, d_k, d_v, d_g = run(
        attn_back_first,
        [block_b, block_f, block_f, block_b],
        [docs, d_resid_far, *d_resid_both, proj, attended, out_turned],
        name="attn_back_first",
    )
    got_back_own, d_q = tie(got_back_own, d_q)
    (d_resid,) = run(resid_back, [row_b], [back_own, got_back_own, resid, d_out], name="resid_back")
    d_resid_near = near(d_resid)
    give, *own_grads = run(
        attn_back_own,
        [row_b, block_b, block_f, block_f, block_b],
        [docs, d_resid, proj, attended, out_turned, d_q, d_k, d_v, d_g, in_turned],
        aliases={5: 1, 6: 2, 7: 3, 8: 4},
        name="attn_back_own",
    )
    take = near(give)
    d_projected = run(
        attn_back_second,
        [block_b, block_f, block_f, block_b],
        [docs, d_resid_near, proj, attended, out_turned, *own_grads],
        aliases={5: 0, 6: 1, 7: 2, 8: 3},
        name="attn_back_second",
    )

    def back_part(body, block, outs, more, name):
        return run(functools.partial(body, block), outs, [*d_projected, in_turned, *more], name=name)

    (sum_far,) = back_part(back_sum, 2, [row_b], [take], "back_sum_far")
    sum_far, *d_projected = tie(sum_far, *d_projected)
    takes = [near(h) for h in back_part(back_give, 1, [piece_b] * pieces, [], "back_give")]
    (sum_own,) = back_part(back_sum, 0, [row_b], takes, "back_sum_own")
    got_own = far(sum_far)
    got_far = far(sum_own)
    d_packed, *halves = run(
        packed_back,
        [row_b] + [piece_b] * pieces,
        [sum_own, got_own, packed, d_resid],
        name="packed_back",
    )

    cot_near = [near(h) for h in halves]
    half_rows = like((groups * capacity // 2, width), BF16)
    group_bits = [1 << b for b in range(groups.bit_length() - 1)]
    near_bit, pack_far, event_far = group_bits[0], group_bits[1 : packs.bit_length() - 1], group_bits[packs.bit_length() - 1 :]
    back_bits = event_far[::-1] + pack_far[::-1] + [near_bit]
    kept, back = run(
        functools.partial(back_send, order, back_bits[0]), [half_rows] * 2, [hot, d_packed], name="back_send"
    )
    back_got = crossed(back, back_bits[0])

    part_f = like((width, cols), F32)
    part1, part0 = run(
        enc_grads_first,
        [part_f, part_f],
        [d_packed, *cot_near, mine, *mine_near, act_a, pre_a, enc_weight],
        name="enc_grads_first",
    )
    got_far, part1, part0 = tie(got_far, part1, part0)
    cot_far, *cot_pieces = run(
        packed_back,
        [row_b] + [like((rows_dev // 4, width), BF16)] * 4,
        [sum_far, got_far, packed_far, d_resid_far],
        name="packed_back_far",
    )
    cot_both = [near(piece) for piece in cot_pieces]
    cot_far, hidden_far = tie(cot_far, hidden_far)
    (out_far,) = run(
        ffn_out_far, [row_b], [hidden_far, ffn_out, ffn_out_near], name="ffn_out_far"
    )
    bits = list(range(groups.bit_length() - 1))
    pack_bits = bits[: packs.bit_length() - 1]
    event_bits = bits[len(pack_bits) :]
    size = width // groups
    total = [pltpu.VMEM((width, cols), F32)]

    def halves(remaining):
        shape = (2 ** (len(remaining) - 1), size, cols)
        return [like(shape, F32), like(shape, BF16)]

    def reduce_over(stages, kept, send, name, beside=False):
        remaining = list(bits)
        got = crossed(send, 1 << stages[0])
        remaining.remove(stages[0])
        for bit in stages[1:]:
            kept, send = run(
                functools.partial(halve_again, tuple(remaining), bit),
                halves(remaining),
                [kept, got],
                name=name + str(bit),
            )
            got = crossed(send, 1 << bit)
            remaining.remove(bit)
            if beside and bit == stages[1]:
                got, arrays[-1] = tie(got, arrays[-1])
        return kept, got

    def start1(setting):
        return run(
            functools.partial(enc_grad1_second, *setting),
            halves(bits),
            [cot_far, *cot_both, act_b, part1],
            total,
            name="enc_grad1_second",
        )

    def start0(setting):
        return run(
            functools.partial(enc_grad0_second, *setting),
            halves(bits),
            [cot_far, *cot_both, mine_far, mine_both, pre_b, enc_weight, part0],
            total,
            name="enc_grad0_second",
        )

    kept1, send1 = start1((tuple(bits), event_bits[0]))
    send1, part0 = tie(send1, part0)
    part0, back_got = tie(part0, back_got)
    kept0, send0 = start0((tuple(bits), event_bits[0]))
    arrays = [kept, back_got]
    held = {}
    for n, value in enumerate((0, back_bits[0])):
        chosen = [k for k in range(groups) if k & back_bits[0] == value]
        held.update({k: (n, at) for at, k in enumerate(chosen)})

    def send_back(bit):
        moved = [k for k in range(groups) if k & bit]
        (back,) = run(
            functools.partial(back_pick, [held[k] for k in moved], capacity),
            [half_rows],
            arrays,
            name="back_pick",
        )
        held.update({k: (len(arrays), n) for n, k in enumerate(moved)})
        arrays.append(crossed(back, bit))

    for bit in back_bits[1:-1]:
        send_back(bit)
    kept1, got1 = reduce_over(event_bits + pack_bits, kept1, send1, "halve1_", True)
    kept0, got0 = reduce_over(event_bits + pack_bits, kept0, send0, "halve0_")
    got1, place = tie(got1, place)
    send_back(back_bits[-1])
    back_places = [held[k] for k in range(groups)]
    got_out = far(out_far)
    (packed_out,) = run(
        ffn_out_own, [row_b], [hidden_own, ffn_out, ffn_out_near, resid, got_out], name="ffn_out_own"
    )
    (row_grad,) = run(
        functools.partial(back_recv, back_places, capacity),
        [row_b],
        [place, *arrays],
        name="back_recv",
    )
    got1, got0, packed_out, row_grad = tie(got1, got0, packed_out, row_grad)
    (enc_grad,) = run(finish, [like((2, size, cols), F32)], [kept1, got1, kept0, got0], name="finish")
    return (packed_out[None], row_grad, enc_grad)


def solution(mesh):
    placed = (
        P(("event", "pack", "tensor"), None),
        P(("event", "pack", "tensor")),
        P(("event", "pack", "tensor")),
        P(("event", "pack"), None),
        P(),
        P(None, None, "tensor"),
        P("tensor", None),
        P(None, None, "tensor"),
        P("tensor", None),
        P(("event", "pack"), "tensor", None),
    )
    return jax.shard_map(
        shards,
        mesh=mesh,
        in_specs=placed,
        out_specs=(
            P(("event", "pack"), "tensor", None),
            P(("event", "pack", "tensor"), None),
            P(None, ("event", "pack"), "tensor"),
        ),
        check_vma=False,
    )
```

```python
import functools

import jax
import jax.numpy as jnp
from jax import lax
from jax.experimental import pallas as pl
from jax.experimental.pallas import tpu as pltpu
from jax.sharding import PartitionSpec as P

D = 1024
HEADS = 16
HEAD = D // HEADS
EPS = 1e-06
F32 = jnp.float32
BF16 = jnp.bfloat16
MIB = 1 << 20
CHUNK = 256


def dot(left, right, dims=((1,), (0,))):
    return lax.dot_general(left, right, (dims, ((), ())), preferred_element_type=F32)


NT = ((1,), (1,))
TN = ((0,), (0,))


def bf16(value):
    return value.astype(BF16)


def silu_grad(value, sigma):
    return sigma * (1.0 + value * (1.0 - sigma))


def norm_factor(wide):
    return lax.rsqrt(jnp.mean(wide * wide, axis=-1, keepdims=True) + EPS)


def norm_back(grad, normed, factor):
    return factor * (grad - normed * jnp.mean(grad * normed, axis=-1, keepdims=True))


def joined(refs):
    return jnp.concatenate([r[...] for r in refs], axis=0)


def store_halves(value, out, halves):
    out[...] = value
    rows = value.shape[0] // max(len(halves), 1)
    for n, target in enumerate(halves):
        target[...] = value[n * rows : (n + 1) * rows]


def turned(row, rows):
    return jnp.broadcast_to(row.astype(F32), (rows, rows)).T


def like(shape, dtype):
    return jax.ShapeDtypeStruct(shape, dtype)


def run(body, outs, args, scratch=(), flops=0, name=None, aliases=None):
    return pl.pallas_call(
        body,
        out_shape=list(outs),
        in_specs=[pl.BlockSpec(memory_space=pltpu.VMEM)] * len(args),
        out_specs=[pl.BlockSpec(memory_space=pltpu.VMEM)] * len(outs),
        scratch_shapes=list(scratch),
        input_output_aliases=aliases or {},
        compiler_params=pltpu.CompilerParams(vmem_limit_bytes=16 * MIB),
        cost_estimate=pl.CostEstimate(flops=flops, bytes_accessed=0, transcendentals=0),
        name=name,
    )(*args)


def group_index():
    return lax.axis_index("event") * lax.axis_size("pack") + lax.axis_index("pack")


def tensor_index():
    return lax.axis_index("tensor")


def tie(*values):
    return lax.optimization_barrier(values)


def route_send(capacity, order, code, features, *outs):
    sends, place_ref = outs[:-1], outs[-1]
    groups = len(sends)
    rows, width = features.shape
    shift = rows.bit_length() - 1
    o_row = code[...] >> shift
    slot = code[...] & (rows - 1)
    o_col = turned(o_row, rows)
    i = lax.broadcasted_iota(jnp.int32, (rows, rows), 0)
    j = lax.broadcasted_iota(jnp.int32, (rows, rows), 1)
    earlier = jnp.where((o_col == o_row.astype(F32)) & (i < j), 1.0, 0.0)
    rank = jnp.sum(earlier, axis=0, keepdims=True).astype(jnp.int32)
    place = (o_row ^ group_index()) * capacity + rank
    place_ref[...] = place
    spots = lax.broadcasted_iota(jnp.int32, (groups * capacity, rows), 0)
    hot = jnp.where(spots == place, 1.0, 0.0).astype(BF16)
    big = dot(hot, features[...])
    tags = dot(hot, bf16(turned(slot + 1, rows)))
    for k, send in zip(order, sends):
        part = slice(k * capacity, (k + 1) * capacity)
        send[:, :width] = bf16(big[part])
        send[:, width:] = bf16(tags[part])


def route_recv(*refs):
    gots, (rows_ref, hot_ref, *halves) = refs[:-4], refs[-4:]
    rows, width = rows_ref.shape
    got = jnp.concatenate([g[...].astype(F32) for g in gots], axis=0)
    lanes = lax.broadcasted_iota(jnp.int32, (got.shape[0], rows), 1) + 1
    hot = jnp.where(got[:, width:] == lanes.astype(F32), 1.0, 0.0).astype(BF16)
    hot_ref[...] = hot
    store_halves(bf16(dot(hot, bf16(got[:, :width]), TN)), rows_ref, halves)


def back_send(order, bit, hot, d_packed, keep, send):
    groups = len(order)
    capacity = hot.shape[0] // groups
    big = dot(hot[...], d_packed[...])
    at = {k: n * capacity for n, k in enumerate(order)}
    for target, value in ((keep, 0), (send, bit)):
        chosen = [k for k in range(groups) if k & bit == value]
        parts = [big[at[k] : at[k] + capacity] for k in chosen]
        target[...] = bf16(jnp.concatenate(parts, axis=0))


def picked(places, capacity, refs):
    wide = [r[...].astype(F32) for r in refs]
    parts = [wide[n][p * capacity : (p + 1) * capacity] for n, p in places]
    return bf16(jnp.concatenate(parts, axis=0))


def back_pick(places, capacity, *refs):
    refs[-1][...] = picked(places, capacity, refs[:-1])


def back_recv(places, capacity, place, *refs):
    got, out = picked(places, capacity, refs[:-1]), refs[-1]
    spots = lax.broadcasted_iota(jnp.int32, (got.shape[0], out.shape[0]), 0)
    hot = jnp.where(spots == place[...], 1.0, 0.0).astype(BF16)
    out[...] = bf16(dot(hot, got, TN))


def encode(rows, enc, w_in, pre_all, pre_ref, act_ref, store):
    width = rows.shape[1]
    cols = pre_ref.shape[1]
    for n in range(width // CHUNK):
        part = slice(n * CHUNK, (n + 1) * CHUNK)
        pre = dot(rows, enc[0, :, part])
        pre_all[:, part] = pre
        act_ref[:, part] = bf16(pre * jax.nn.sigmoid(pre))
    pre_ref[...] = pre_all[:, pl.ds(pl.multiple_of(tensor_index() * cols, cols), cols)]
    packed = bf16(dot(act_ref[...], enc[1]))
    wide = packed.astype(F32)
    normed = bf16(wide * norm_factor(wide))
    for c in range(w_in.shape[0]):
        store(c, bf16(dot(normed, w_in[c])))
    return packed


def encode_blocks(*refs):
    blocks, (enc, w_in, pre_ref, act_ref, packed_ref, proj_ref, pre_all) = refs[:-7], refs[-7:]
    rows = joined(blocks)
    count, size = proj_ref.shape[1:3]

    def store(c, value):
        for n in range(count):
            proj_ref[c, n] = value[n * size : (n + 1) * size]

    packed = encode(rows, enc, w_in, pre_all, pre_ref, act_ref, store)
    packed_ref[...] = packed[:size]


def turn(attn_in, attn_out, in_ref, out_ref):
    for c in range(attn_in.shape[0]):
        in_ref[c] = attn_in[c].T
    out_ref[...] = attn_out[...].T


def window(docs, r, rows):
    t = tensor_index()
    b = t ^ r
    ahead = jnp.where(b > 0, (b - 1) ^ t, r)
    doc_q = turned(docs[b], rows)
    doc_own = docs[b].astype(F32)
    doc_ahead = docs[jnp.maximum(b - 1, 0)].astype(F32)
    i = lax.broadcasted_iota(jnp.int32, (rows, rows), 0)
    j = lax.broadcasted_iota(jnp.int32, (rows, rows), 1)
    own = jnp.where((doc_q == doc_own) & (j <= i), 1.0, 0.0)
    prior = jnp.where(doc_q == doc_ahead, 1.0, 0.0) * jnp.where(b > 0, 1.0, 0.0)
    allowed = jnp.concatenate([prior, own], axis=1)
    root_inv = lax.rsqrt(jnp.sum(allowed, axis=1, keepdims=True))
    return ahead, allowed, root_inv


def head_masks(cols):
    lane = lax.broadcasted_iota(jnp.int32, (1, cols), 1) // HEAD
    return [jnp.where(lane == h, 1.0, 0.0) for h in range(cols // HEAD)]


def spread(value, masks):
    return jnp.concatenate([value * bf16(m) for m in masks], axis=0)


def collect(value, masks):
    rows = value.shape[0] // len(masks)
    total = None
    for h, m in enumerate(masks):
        part = value[h * rows : (h + 1) * rows] * m
        total = part if total is None else total + part
    return total


def attend_first(
    docs, fourth, pre_c, act_c, proj_a, proj_c, enc, w_in,
    pre_ref, act_ref, proj_ref, att_ref, give_ref, keep_ref, pre_all,
):
    half = fourth.shape[0]
    cols = proj_a.shape[-1]
    proj_ref[:, 0:2] = proj_a[...]
    proj_ref[:, 2:3] = proj_c[...]
    pre_ref[:half, :] = pre_c[...]
    act_ref[:half, :] = act_c[...]

    def store(c, value):
        proj_ref[c, 3] = value

    encode(
        fourth[...], enc, w_in, pre_all, pre_ref.at[half : 2 * half], act_ref.at[half : 2 * half], store
    )
    masks = head_masks(cols)
    for r, (target, place) in enumerate(((keep_ref, 1), (give_ref, 1), (keep_ref, 0), (give_ref, 0))):
        ahead, allowed, root_inv = window(docs, r, half)
        keys = jnp.concatenate([proj_ref[1, ahead], proj_ref[1, r]], axis=0)
        values = jnp.concatenate([proj_ref[2, ahead], proj_ref[2, r]], axis=0)
        many = jnp.concatenate([allowed] * len(masks), axis=0)
        scores = dot(spread(proj_ref[0, r], masks), keys, NT) * HEAD ** (-0.5)
        weights = bf16(scores * jax.nn.sigmoid(scores) * many)
        attended = collect(dot(weights, values), masks) * root_inv
        gate = proj_ref[3, r].astype(F32)
        att_ref[r] = attended
        target[place * half : (place + 1) * half, :] = bf16(attended * gate * jax.nn.sigmoid(gate))


def attn_out_part(index, keep, take, w_own, w_near, out):
    rows = out.shape[0]
    part = slice(index * rows, (index + 1) * rows)
    out[...] = bf16(dot(keep[part, :], w_own[...]) + dot(take[part, :], w_near[...]))


def residual(packed, part, got, resid_ref, normed_ref):
    resid = bf16(packed[...].astype(F32) + (part[...].astype(F32) + got[...].astype(F32)))
    resid_ref[...] = resid
    wide = resid.astype(F32)
    normed_ref[...] = bf16(wide * norm_factor(wide))


def ffn(rows_ref, d_out_ref, in_a, in_b, out_a, out_b, hidden_ref, back_ref):
    rows = rows_ref[...]
    cotangent = d_out_ref[...]
    units = out_a.shape[0]
    back = None
    for index, (w_in, w_out) in enumerate(((in_a, out_a), (in_b, out_b))):
        for n in range(units // CHUNK):
            part = slice(n * CHUNK, (n + 1) * CHUNK)
            d_hidden = dot(cotangent, w_out[part, :], NT)
            gate = dot(rows, w_in[0, :, part])
            upper = dot(rows, w_in[1, :, part])
            sigma = jax.nn.sigmoid(gate)
            silu = gate * sigma
            hidden_ref[:, index * units + n * CHUNK : index * units + (n + 1) * CHUNK] = bf16(silu * upper)
            d_gate = bf16(d_hidden * upper * silu_grad(gate, sigma))
            d_upper = bf16(d_hidden * silu)
            term = dot(d_gate, w_in[0, :, part], NT) + dot(d_upper, w_in[1, :, part], NT)
            back = term if back is None else back + term
    back_ref[...] = back.astype(back_ref.dtype)


def ffn_out_far(hidden, w_a, w_b, out):
    units = w_a.shape[0]
    out[...] = bf16(dot(hidden[:, :units], w_a[...]) + dot(hidden[:, units:], w_b[...]))


def ffn_out_own(hidden, w_a, w_b, resid, got, out):
    units = w_a.shape[0]
    total = dot(hidden[:, :units], w_a[...]) + dot(hidden[:, units:], w_b[...])
    out[...] = bf16(resid[...].astype(F32) + total + got[...].astype(F32))


def resid_back(back, got, resid, d_out, out, *halves):
    wide = resid[...].astype(F32)
    factor = norm_factor(wide)
    grad = back[...].astype(F32) + got[...].astype(F32)
    store_halves(bf16(d_out[...].astype(F32) + norm_back(grad, wide * factor, factor)), out, halves)


def attend_back(docs, d_resid, r, proj_ref, att_ref, w_out, masks, d_q, d_k, d_v, d_g):
    half = d_resid.shape[0]
    scale = HEAD ** (-0.5)
    ahead, allowed, root_inv = window(docs, r, half)
    gate = proj_ref[3, r].astype(F32)
    sigma_g = jax.nn.sigmoid(gate)
    d_gated = dot(d_resid, w_out)
    d_att = bf16(d_gated * (gate * sigma_g) * root_inv)
    d_g[r] = bf16(d_gated * att_ref[r] * silu_grad(gate, sigma_g))
    keys = jnp.concatenate([proj_ref[1, ahead], proj_ref[1, r]], axis=0)
    values = jnp.concatenate([proj_ref[2, ahead], proj_ref[2, r]], axis=0)
    many = jnp.concatenate([allowed] * len(masks), axis=0)
    query = spread(proj_ref[0, r], masks)
    d_att_m = spread(d_att, masks)
    scores = dot(query, keys, NT) * scale
    sigma = jax.nn.sigmoid(scores)
    weights = bf16(scores * sigma * many)
    d_weights = dot(d_att_m, values, NT)
    d_scores = bf16(d_weights * silu_grad(scores, sigma) * many)
    d_q[r] = bf16(collect(dot(d_scores, keys), masks) * scale)
    d_keys = dot(d_scores, query, TN) * scale
    d_values = dot(weights, d_att_m, TN)
    d_k[ahead] += d_keys[:half]
    d_k[r] += d_keys[half:]
    d_v[ahead] += d_values[:half]
    d_v[r] += d_values[half:]


def attn_back_first(docs, third, fourth_a, fourth_b, proj, att, w_out, d_q, d_k, d_v, d_g):
    masks = head_masks(w_out.shape[1])
    d_k[...] = jnp.zeros_like(d_k)
    d_v[...] = jnp.zeros_like(d_v)
    for r, rows in ((2, [third]), (3, [fourth_a, fourth_b])):
        attend_back(docs, joined(rows), r, proj, att, w_out[...], masks, d_q, d_k, d_v, d_g)


def attn_back_own(
    docs, first, proj, att, w_out, _q, _k, _v, _g, w_in, give_ref, d_q, d_k, d_v, d_g
):
    masks = head_masks(w_out.shape[1])
    attend_back(docs, first[...], 0, proj, att, w_out[...], masks, d_q, d_k, d_v, d_g)
    give_ref[...] = bf16(back_norm((d_q, d_k, d_v, d_g), w_in, 3))


def attn_back_second(
    docs, second, proj, att, w_out, _q, _k, _v, _g, d_q, d_k, d_v, d_g
):
    masks = head_masks(w_out.shape[1])
    attend_back(docs, second[...], 1, proj, att, w_out[...], masks, d_q, d_k, d_v, d_g)


def back_norm(grads, w_in, block):
    total = None
    for c, grad in enumerate(grads):
        term = dot(bf16(grad[block]), w_in[c])
        total = term if total is None else total + term
    return total


def back_give(block, d_q, d_k, d_v, d_g, w_in, *outs):
    value = bf16(back_norm((d_q, d_k, d_v, d_g), w_in, block))
    rows = value.shape[0] // len(outs)
    for n, out in enumerate(outs):
        out[...] = value[n * rows : (n + 1) * rows]


def back_sum(block, d_q, d_k, d_v, d_g, w_in, *refs):
    takes, out = refs[:-1], refs[-1]
    out[...] = bf16(back_norm((d_q, d_k, d_v, d_g), w_in, block) + joined(takes).astype(F32))


def packed_back(part, got, packed, d_resid, out, *halves):
    wide = packed[...].astype(F32)
    factor = norm_factor(wide)
    grad = part[...].astype(F32) + got[...].astype(F32)
    store_halves(bf16(d_resid[...].astype(F32) + norm_back(grad, wide * factor, factor)), out, halves)


def column_of(ref, index, cols):
    return ref[:, pl.ds(pl.multiple_of(index * cols, cols), cols)]


def rows_term(act_refs, cot):
    return dot(jnp.concatenate([a[...] for a in act_refs], axis=0), cot, TN)


def first_cot(cots, pre, enc):
    cols = pre.shape[1]
    cot = joined(cots)
    value = pre[...]
    w1_rows = enc[1, pl.ds(pl.multiple_of(tensor_index() * cols, cols), cols), :]
    return bf16(dot(cot, w1_rows, NT) * silu_grad(value, jax.nn.sigmoid(value)))


def cot_columns(cots, cols):
    return jnp.concatenate([column_of(c, tensor_index(), cols) for c in cots], axis=0)


def enc_grads_first(*refs):
    rows, (act1, pre, enc, part1, part0) = refs[:-5], refs[-5:]
    cots, act0 = rows[: len(rows) // 2], rows[len(rows) // 2 :]
    cols = pre.shape[1]
    part1[...] = rows_term([act1], cot_columns(cots, cols))
    part0[...] = rows_term(act0, first_cot(cots, pre, enc))


def halve(bits, bit, total, keep, send):
    place = bits.index(bit)
    count, size, _ = keep.shape
    mine = (group_index() >> bit) & 1
    for j in range(count):
        low = j & ((1 << place) - 1)
        base = ((j >> place) << (place + 1)) | low
        for target, value in ((keep, mine), (send, 1 - mine)):
            index = base + (value << place)
            rows = total[pl.ds(pl.multiple_of(index * size, size), size), :]
            target[j] = rows.astype(target.dtype)


def enc_grad1_second(bits, bit, *refs):
    cots, (act1, part1, keep, send, total) = refs[:-5], refs[-5:]
    total[...] = rows_term([act1], cot_columns(cots, part1.shape[1])) + part1[...]
    halve(bits, bit, total, keep, send)


def enc_grad0_second(bits, bit, *refs):
    cots, (act0_a, act0_b, pre, enc, part0, keep, send, total) = refs[:-8], refs[-8:]
    total[...] = rows_term([act0_a, act0_b], first_cot(cots, pre, enc)) + part0[...]
    halve(bits, bit, total, keep, send)


def halve_again(bits, bit, kept, got, keep, send):
    place = bits.index(bit)
    mine = (group_index() >> bit) & 1
    for j in range(keep.shape[0]):
        low = j & ((1 << place) - 1)
        base = ((j >> place) << (place + 1)) | low
        for target, value in ((keep, mine), (send, 1 - mine)):
            index = base + (value << place)
            target[j] = (kept[index] + got[index].astype(F32)).astype(target.dtype)


def finish(kept1, got1, kept0, got0, out):
    out[0] = kept0[0] + got0[0].astype(F32)
    out[1] = kept1[0] + got1[0].astype(F32)


def shards(
    features,
    dest_owner,
    dest_slot,
    doc_ids,
    enc_weight,
    attn_in,
    attn_out,
    ffn_in,
    ffn_out,
    out_grad,
):
    rows_dev, width = features.shape
    group_axes = ("event", "pack")
    groups = lax.axis_size(group_axes)
    packs = lax.axis_size("pack")
    tensors = lax.axis_size("tensor")
    cols = attn_in.shape[2]
    comps = attn_in.shape[0]
    units = ffn_out.shape[0]
    d_out = out_grad[0]
    docs = doc_ids.reshape(tensors, 1, rows_dev)

    def near(value):
        return lax.ppermute(value, "tensor", [(i, i ^ 1) for i in range(tensors)])

    def far(value):
        return lax.ppermute(value, "tensor", [(i, i ^ 2) for i in range(tensors)])

    def crossed(value, k):
        return lax.ppermute(value, group_axes, [(i, i ^ k) for i in range(groups)])

    row_b = like((rows_dev, width), BF16)
    row_f = like((rows_dev, width), F32)

    mean_load = rows_dev // groups
    capacity = -(-(mean_load + mean_load // 2) // 8) * 8
    code = (dest_owner * rows_dev + dest_slot).reshape(1, rows_dev)
    order = [0] + sorted(
        range(1, groups), key=lambda k: (-((2 * (k % packs)) // packs), k % packs, k)
    )
    *sends, place = run(
        functools.partial(route_send, capacity, order),
        [like((capacity, width + rows_dev), BF16)] * groups + [like((1, rows_dev), jnp.int32)],
        [code, features],
        flops=4 * 10**9,
        name="route_send",
    )
    ffn_in_near, ffn_out_near = near(ffn_in), near(ffn_out)
    early = [crossed(sends[n], order[n]) for n in (1, 2)]
    ffn_in_near, ffn_out_near, *sends = tie(ffn_in_near, ffn_out_near, *sends)
    gots = [sends[0], *early] + [crossed(sends[n], order[n]) for n in range(3, groups)]
    pieces = 2
    piece_b = like((rows_dev // pieces, width), BF16)
    in_turned, out_turned = run(
        turn,
        [like((comps, cols, width), BF16), like((width, cols), BF16)],
        [attn_in, attn_out],
        name="turn",
    )
    in_turned, *gots = tie(in_turned, *gots)
    mine, hot, *halves = run(
        route_recv,
        [row_b, like((groups * capacity, rows_dev), BF16)] + [piece_b] * pieces,
        gots,
        name="route_recv",
    )

    mine_far = far(mine)
    mine_near = [near(h) for h in halves]

    pair = 2 * rows_dev
    pre_a, act_a, packed, proj_a = run(
        encode_blocks,
        [
            like((pair, cols), F32),
            like((pair, width), BF16),
            row_b,
            like((comps, 2, rows_dev, cols), BF16),
        ],
        [mine, *mine_near, enc_weight, attn_in],
        [pltpu.VMEM((pair, width), F32)],
        name="encode_first",
    )
    mine_far, proj_a = tie(mine_far, proj_a)
    mine_far, attn_out_late, d_out_late = tie(mine_far, attn_out, d_out)
    mine_both = near(mine_far)
    attn_out_near = near(attn_out_late)
    d_out_far = far(d_out_late)
    pre_c, act_c, packed_far, proj_c = run(
        encode_blocks,
        [like((rows_dev, cols), F32), row_b, row_b, like((comps, 1, rows_dev, cols), BF16)],
        [mine_far, enc_weight, attn_in],
        [pltpu.VMEM((rows_dev, width), F32)],
        name="encode_third",
    )
    pre_b, act_b, proj, attended, give, keep = run(
        attend_first,
        [
            like((pair, cols), F32),
            like((pair, width), BF16),
            like((comps, tensors, rows_dev, cols), BF16),
            like((tensors, rows_dev, cols), F32),
            like((pair, cols), BF16),
            like((pair, cols), BF16),
        ],
        [docs, mine_both, pre_c, act_c, proj_a, proj_c, enc_weight, attn_in],
        [pltpu.VMEM((rows_dev, width), F32)],
        name="attend_first",
    )
    take = near(give)


    def out_part(index, name):
        return run(
            functools.partial(attn_out_part, index),
            [row_b],
            [keep, take, attn_out, attn_out_near],
            name=name,
        )[0]

    part_far = out_part(0, "attn_out_far")
    got_own = far(part_far)
    part_own = out_part(1, "attn_out_own")
    part_own, d_out_far = tie(part_own, d_out_far)
    got_far = far(part_own)

    def feed(rows, cotangent, name):
        return run(
            ffn,
            [like((rows_dev, 2 * units), BF16), row_b],
            [rows, cotangent, ffn_in, ffn_in_near, ffn_out, ffn_out_near],
            name=name,
        )

    resid, normed2 = run(residual, [row_b, row_b], [packed, part_own, got_own], name="residual")
    hidden_own, back_own = feed(normed2, d_out, "ffn_own")
    got_far, back_own = tie(got_far, back_own)
    got_back_far = far(back_own)
    resid_far, normed2_far = run(
        residual, [row_b, row_b], [packed_far, part_far, got_far], name="residual_far"
    )
    hidden_far, back_far = feed(normed2_far, d_out_far, "ffn_far")
    got_back_own = far(back_far)

    d_resid_far, *halves = run(
        resid_back,
        [row_b] + [piece_b] * pieces,
        [back_far, got_back_far, resid_far, d_out_far],
        name="resid_back_far",
    )
    d_resid_both = [near(h) for h in halves]
    block_f = like((tensors, rows_dev, cols), F32)
    block_b = like((tensors, rows_dev, cols), BF16)
    d_q, d_k, d_v, d_g = run(
        attn_back_first,
        [block_b, block_f, block_f, block_b],
        [docs, d_resid_far, *d_resid_both, proj, attended, out_turned],
        name="attn_back_first",
    )
    got_back_own, d_q = tie(got_back_own, d_q)
    (d_resid,) = run(resid_back, [row_b], [back_own, got_back_own, resid, d_out], name="resid_back")
    d_resid_near = near(d_resid)
    give, *own_grads = run(
        attn_back_own,
        [row_b, block_b, block_f, block_f, block_b],
        [docs, d_resid, proj, attended, out_turned, d_q, d_k, d_v, d_g, in_turned],
        aliases={5: 1, 6: 2, 7: 3, 8: 4},
        name="attn_back_own",
    )
    take = near(give)
    d_projected = run(
        attn_back_second,
        [block_b, block_f, block_f, block_b],
        [docs, d_resid_near, proj, attended, out_turned, *own_grads],
        aliases={5: 0, 6: 1, 7: 2, 8: 3},
        name="attn_back_second",
    )

    def back_part(body, block, outs, more, name):
        return run(functools.partial(body, block), outs, [*d_projected, in_turned, *more], name=name)

    (sum_far,) = back_part(back_sum, 2, [row_b], [take], "back_sum_far")
    sum_far, *d_projected = tie(sum_far, *d_projected)
    takes = [near(h) for h in back_part(back_give, 1, [piece_b] * pieces, [], "back_give")]
    (sum_own,) = back_part(back_sum, 0, [row_b], takes, "back_sum_own")
    got_own = far(sum_far)
    got_far = far(sum_own)
    d_packed, *halves = run(
        packed_back,
        [row_b] + [piece_b] * pieces,
        [sum_own, got_own, packed, d_resid],
        name="packed_back",
    )

    cot_near = [near(h) for h in halves]
    half_rows = like((groups * capacity // 2, width), BF16)
    group_bits = [1 << b for b in range(groups.bit_length() - 1)]
    near_bit, pack_far, event_far = group_bits[0], group_bits[1 : packs.bit_length() - 1], group_bits[packs.bit_length() - 1 :]
    back_bits = event_far[::-1] + [near_bit] + pack_far[::-1]
    kept, back = run(
        functools.partial(back_send, order, back_bits[0]), [half_rows] * 2, [hot, d_packed], name="back_send"
    )
    back_got = crossed(back, back_bits[0])

    part_f = like((width, cols), F32)
    part1, part0 = run(
        enc_grads_first,
        [part_f, part_f],
        [d_packed, *cot_near, mine, *mine_near, act_a, pre_a, enc_weight],
        name="enc_grads_first",
    )
    got_far, part1, part0 = tie(got_far, part1, part0)
    cot_far, *cot_pieces = run(
        packed_back,
        [row_b] + [like((rows_dev // 4, width), BF16)] * 4,
        [sum_far, got_far, packed_far, d_resid_far],
        name="packed_back_far",
    )
    cot_both = [near(piece) for piece in cot_pieces]
    cot_far, hidden_far = tie(cot_far, hidden_far)
    (out_far,) = run(
        ffn_out_far, [row_b], [hidden_far, ffn_out, ffn_out_near], name="ffn_out_far"
    )
    bits = list(range(groups.bit_length() - 1))
    pack_bits = bits[: packs.bit_length() - 1]
    event_bits = bits[len(pack_bits) :]
    size = width // groups
    total = [pltpu.VMEM((width, cols), F32)]

    def halves(remaining):
        shape = (2 ** (len(remaining) - 1), size, cols)
        return [like(shape, F32), like(shape, BF16)]

    def reduce_over(stages, kept, send, name, beside):
        remaining = list(bits)
        got = crossed(send, 1 << stages[0])
        if beside == stages[0]:
            got, arrays[-1] = tie(got, arrays[-1])
        remaining.remove(stages[0])
        for bit in stages[1:]:
            kept, send = run(
                functools.partial(halve_again, tuple(remaining), bit),
                halves(remaining),
                [kept, got],
                name=name + str(bit),
            )
            got = crossed(send, 1 << bit)
            remaining.remove(bit)
            if bit == beside:
                got, arrays[-1] = tie(got, arrays[-1])
        return kept, got

    def start1(setting):
        return run(
            functools.partial(enc_grad1_second, *setting),
            halves(bits),
            [cot_far, *cot_both, act_b, part1],
            total,
            name="enc_grad1_second",
        )

    def start0(setting):
        return run(
            functools.partial(enc_grad0_second, *setting),
            halves(bits),
            [cot_far, *cot_both, mine_far, mine_both, pre_b, enc_weight, part0],
            total,
            name="enc_grad0_second",
        )

    kept1, send1 = start1((tuple(bits), event_bits[0]))
    send1, part0 = tie(send1, part0)
    part0, back_got = tie(part0, back_got)
    kept0, send0 = start0((tuple(bits), event_bits[0]))
    arrays = [kept, back_got]
    held = {}
    for n, value in enumerate((0, back_bits[0])):
        chosen = [k for k in range(groups) if k & back_bits[0] == value]
        held.update({k: (n, at) for at, k in enumerate(chosen)})

    def send_back(bit):
        moved = [k for k in range(groups) if k & bit]
        (back,) = run(
            functools.partial(back_pick, [held[k] for k in moved], capacity),
            [half_rows],
            arrays,
            name="back_pick",
        )
        held.update({k: (len(arrays), n) for n, k in enumerate(moved)})
        arrays.append(crossed(back, bit))

    for bit in back_bits[1:-1]:
        send_back(bit)
    kept1, got1 = reduce_over(event_bits + pack_bits, kept1, send1, "halve1_", event_bits[0])
    send_back(back_bits[-1])
    kept0, got0 = reduce_over(event_bits + pack_bits, kept0, send0, "halve0_", pack_bits[0])
    got1, place = tie(got1, place)
    back_places = [held[k] for k in range(groups)]
    got_out = far(out_far)
    (packed_out,) = run(
        ffn_out_own, [row_b], [hidden_own, ffn_out, ffn_out_near, resid, got_out], name="ffn_out_own"
    )
    (row_grad,) = run(
        functools.partial(back_recv, back_places, capacity),
        [row_b],
        [place, *arrays],
        name="back_recv",
    )
    got1, got0, packed_out, row_grad = tie(got1, got0, packed_out, row_grad)
    (enc_grad,) = run(finish, [like((2, size, cols), F32)], [kept1, got1, kept0, got0], name="finish")
    return (packed_out[None], row_grad, enc_grad)


def solution(mesh):
    placed = (
        P(("event", "pack", "tensor"), None),
        P(("event", "pack", "tensor")),
        P(("event", "pack", "tensor")),
        P(("event", "pack"), None),
        P(),
        P(None, None, "tensor"),
        P("tensor", None),
        P(None, None, "tensor"),
        P("tensor", None),
        P(("event", "pack"), "tensor", None),
    )
    return jax.shard_map(
        shards,
        mesh=mesh,
        in_specs=placed,
        out_specs=(
            P(("event", "pack"), "tensor", None),
            P(("event", "pack", "tensor"), None),
            P(None, ("event", "pack"), "tensor"),
        ),
        check_vma=False,
    )
```

```python
import functools

import jax
import jax.numpy as jnp
from jax import lax
from jax.experimental import pallas as pl
from jax.experimental.pallas import tpu as pltpu
from jax.sharding import PartitionSpec as P

D = 1024
HEADS = 16
HEAD = D // HEADS
EPS = 1e-06
F32 = jnp.float32
BF16 = jnp.bfloat16
MIB = 1 << 20
CHUNK = 256


def dot(left, right, dims=((1,), (0,))):
    return lax.dot_general(left, right, (dims, ((), ())), preferred_element_type=F32)


NT = ((1,), (1,))
TN = ((0,), (0,))


def bf16(value):
    return value.astype(BF16)


def silu_grad(value, sigma):
    return sigma * (1.0 + value * (1.0 - sigma))


def norm_factor(wide):
    return lax.rsqrt(jnp.mean(wide * wide, axis=-1, keepdims=True) + EPS)


def norm_back(grad, normed, factor):
    return factor * (grad - normed * jnp.mean(grad * normed, axis=-1, keepdims=True))


def joined(refs):
    return jnp.concatenate([r[...] for r in refs], axis=0)


def store_halves(value, out, halves):
    out[...] = value
    rows = value.shape[0] // max(len(halves), 1)
    for n, target in enumerate(halves):
        target[...] = value[n * rows : (n + 1) * rows]


def turned(row, rows):
    return jnp.broadcast_to(row.astype(F32), (rows, rows)).T


def like(shape, dtype):
    return jax.ShapeDtypeStruct(shape, dtype)


def run(body, outs, args, scratch=(), flops=0, name=None, aliases=None):
    return pl.pallas_call(
        body,
        out_shape=list(outs),
        in_specs=[pl.BlockSpec(memory_space=pltpu.VMEM)] * len(args),
        out_specs=[pl.BlockSpec(memory_space=pltpu.VMEM)] * len(outs),
        scratch_shapes=list(scratch),
        input_output_aliases=aliases or {},
        compiler_params=pltpu.CompilerParams(vmem_limit_bytes=16 * MIB),
        cost_estimate=pl.CostEstimate(flops=flops, bytes_accessed=0, transcendentals=0),
        name=name,
    )(*args)


def group_index():
    return lax.axis_index("event") * lax.axis_size("pack") + lax.axis_index("pack")


def tensor_index():
    return lax.axis_index("tensor")


def tie(*values):
    return lax.optimization_barrier(values)


def route_send(capacity, order, code, features, *outs):
    sends, place_ref = outs[:-1], outs[-1]
    groups = len(sends)
    rows, width = features.shape
    shift = rows.bit_length() - 1
    o_row = code[...] >> shift
    slot = code[...] & (rows - 1)
    o_col = turned(o_row, rows)
    i = lax.broadcasted_iota(jnp.int32, (rows, rows), 0)
    j = lax.broadcasted_iota(jnp.int32, (rows, rows), 1)
    earlier = jnp.where((o_col == o_row.astype(F32)) & (i < j), 1.0, 0.0)
    rank = jnp.sum(earlier, axis=0, keepdims=True).astype(jnp.int32)
    place = (o_row ^ group_index()) * capacity + rank
    place_ref[...] = place
    spots = lax.broadcasted_iota(jnp.int32, (groups * capacity, rows), 0)
    hot = jnp.where(spots == place, 1.0, 0.0).astype(BF16)
    big = dot(hot, features[...])
    tags = dot(hot, bf16(turned(slot + 1, rows)))
    for k, send in zip(order, sends):
        part = slice(k * capacity, (k + 1) * capacity)
        send[:, :width] = bf16(big[part])
        send[:, width:] = bf16(tags[part])


def route_recv(*refs):
    gots, (rows_ref, hot_ref, *halves) = refs[:-4], refs[-4:]
    rows, width = rows_ref.shape
    got = jnp.concatenate([g[...].astype(F32) for g in gots], axis=0)
    lanes = lax.broadcasted_iota(jnp.int32, (got.shape[0], rows), 1) + 1
    hot = jnp.where(got[:, width:] == lanes.astype(F32), 1.0, 0.0).astype(BF16)
    hot_ref[...] = hot
    store_halves(bf16(dot(hot, bf16(got[:, :width]), TN)), rows_ref, halves)


def back_send(order, bit, hot, d_packed, keep, send):
    groups = len(order)
    capacity = hot.shape[0] // groups
    big = dot(hot[...], d_packed[...])
    at = {k: n * capacity for n, k in enumerate(order)}
    for target, value in ((keep, 0), (send, bit)):
        chosen = [k for k in range(groups) if k & bit == value]
        parts = [big[at[k] : at[k] + capacity] for k in chosen]
        target[...] = bf16(jnp.concatenate(parts, axis=0))


def picked(places, capacity, refs):
    wide = [r[...].astype(F32) for r in refs]
    parts = [wide[n][p * capacity : (p + 1) * capacity] for n, p in places]
    return bf16(jnp.concatenate(parts, axis=0))


def back_pick(places, capacity, *refs):
    refs[-1][...] = picked(places, capacity, refs[:-1])


def back_recv(places, capacity, place, *refs):
    got, out = picked(places, capacity, refs[:-1]), refs[-1]
    spots = lax.broadcasted_iota(jnp.int32, (got.shape[0], out.shape[0]), 0)
    hot = jnp.where(spots == place[...], 1.0, 0.0).astype(BF16)
    out[...] = bf16(dot(hot, got, TN))


def encode(rows, enc, w_in, pre_all, pre_ref, act_ref, store):
    width = rows.shape[1]
    cols = pre_ref.shape[1]
    for n in range(width // CHUNK):
        part = slice(n * CHUNK, (n + 1) * CHUNK)
        pre = dot(rows, enc[0, :, part])
        pre_all[:, part] = pre
        act_ref[:, part] = bf16(pre * jax.nn.sigmoid(pre))
    pre_ref[...] = pre_all[:, pl.ds(pl.multiple_of(tensor_index() * cols, cols), cols)]
    packed = bf16(dot(act_ref[...], enc[1]))
    wide = packed.astype(F32)
    normed = bf16(wide * norm_factor(wide))
    for c in range(w_in.shape[0]):
        store(c, bf16(dot(normed, w_in[c])))
    return packed


def encode_blocks(*refs):
    blocks, (enc, w_in, pre_ref, act_ref, packed_ref, proj_ref, pre_all) = refs[:-7], refs[-7:]
    rows = joined(blocks)
    count, size = proj_ref.shape[1:3]

    def store(c, value):
        for n in range(count):
            proj_ref[c, n] = value[n * size : (n + 1) * size]

    packed = encode(rows, enc, w_in, pre_all, pre_ref, act_ref, store)
    packed_ref[...] = packed[:size]


def turn(attn_in, attn_out, in_ref, out_ref):
    for c in range(attn_in.shape[0]):
        in_ref[c] = attn_in[c].T
    out_ref[...] = attn_out[...].T


def window(docs, r, rows):
    t = tensor_index()
    b = t ^ r
    ahead = jnp.where(b > 0, (b - 1) ^ t, r)
    doc_q = turned(docs[b], rows)
    doc_own = docs[b].astype(F32)
    doc_ahead = docs[jnp.maximum(b - 1, 0)].astype(F32)
    i = lax.broadcasted_iota(jnp.int32, (rows, rows), 0)
    j = lax.broadcasted_iota(jnp.int32, (rows, rows), 1)
    own = jnp.where((doc_q == doc_own) & (j <= i), 1.0, 0.0)
    prior = jnp.where(doc_q == doc_ahead, 1.0, 0.0) * jnp.where(b > 0, 1.0, 0.0)
    allowed = jnp.concatenate([prior, own], axis=1)
    root_inv = lax.rsqrt(jnp.sum(allowed, axis=1, keepdims=True))
    return ahead, allowed, root_inv


def head_masks(cols):
    lane = lax.broadcasted_iota(jnp.int32, (1, cols), 1) // HEAD
    return [jnp.where(lane == h, 1.0, 0.0) for h in range(cols // HEAD)]


def spread(value, masks):
    return jnp.concatenate([value * bf16(m) for m in masks], axis=0)


def collect(value, masks):
    rows = value.shape[0] // len(masks)
    total = None
    for h, m in enumerate(masks):
        part = value[h * rows : (h + 1) * rows] * m
        total = part if total is None else total + part
    return total


def attend_first(
    docs, fourth, pre_c, act_c, proj_a, proj_c, enc, w_in,
    pre_ref, act_ref, proj_ref, att_ref, give_ref, keep_ref, pre_all,
):
    half = fourth.shape[0]
    cols = proj_a.shape[-1]
    proj_ref[:, 0:2] = proj_a[...]
    proj_ref[:, 2:3] = proj_c[...]
    pre_ref[:half, :] = pre_c[...]
    act_ref[:half, :] = act_c[...]

    def store(c, value):
        proj_ref[c, 3] = value

    encode(
        fourth[...], enc, w_in, pre_all, pre_ref.at[half : 2 * half], act_ref.at[half : 2 * half], store
    )
    masks = head_masks(cols)
    for r, (target, place) in enumerate(((keep_ref, 1), (give_ref, 1), (keep_ref, 0), (give_ref, 0))):
        ahead, allowed, root_inv = window(docs, r, half)
        keys = jnp.concatenate([proj_ref[1, ahead], proj_ref[1, r]], axis=0)
        values = jnp.concatenate([proj_ref[2, ahead], proj_ref[2, r]], axis=0)
        many = jnp.concatenate([allowed] * len(masks), axis=0)
        scores = dot(spread(proj_ref[0, r], masks), keys, NT) * HEAD ** (-0.5)
        weights = bf16(scores * jax.nn.sigmoid(scores) * many)
        attended = collect(dot(weights, values), masks) * root_inv
        gate = proj_ref[3, r].astype(F32)
        att_ref[r] = attended
        target[place * half : (place + 1) * half, :] = bf16(attended * gate * jax.nn.sigmoid(gate))


def attn_out_part(index, keep, take, w_own, w_near, out):
    rows = out.shape[0]
    part = slice(index * rows, (index + 1) * rows)
    out[...] = bf16(dot(keep[part, :], w_own[...]) + dot(take[part, :], w_near[...]))


def residual(packed, part, got, resid_ref, normed_ref):
    resid = bf16(packed[...].astype(F32) + (part[...].astype(F32) + got[...].astype(F32)))
    resid_ref[...] = resid
    wide = resid.astype(F32)
    normed_ref[...] = bf16(wide * norm_factor(wide))


def ffn(rows_ref, d_out_ref, in_a, in_b, out_a, out_b, hidden_ref, back_ref):
    rows = rows_ref[...]
    cotangent = d_out_ref[...]
    units = out_a.shape[0]
    back = None
    for index, (w_in, w_out) in enumerate(((in_a, out_a), (in_b, out_b))):
        for n in range(units // CHUNK):
            part = slice(n * CHUNK, (n + 1) * CHUNK)
            d_hidden = dot(cotangent, w_out[part, :], NT)
            gate = dot(rows, w_in[0, :, part])
            upper = dot(rows, w_in[1, :, part])
            sigma = jax.nn.sigmoid(gate)
            silu = gate * sigma
            hidden_ref[:, index * units + n * CHUNK : index * units + (n + 1) * CHUNK] = bf16(silu * upper)
            d_gate = bf16(d_hidden * upper * silu_grad(gate, sigma))
            d_upper = bf16(d_hidden * silu)
            term = dot(d_gate, w_in[0, :, part], NT) + dot(d_upper, w_in[1, :, part], NT)
            back = term if back is None else back + term
    back_ref[...] = back.astype(back_ref.dtype)


def ffn_out_far(hidden, w_a, w_b, out):
    units = w_a.shape[0]
    out[...] = bf16(dot(hidden[:, :units], w_a[...]) + dot(hidden[:, units:], w_b[...]))


def ffn_out_own(hidden, w_a, w_b, resid, got, out):
    units = w_a.shape[0]
    total = dot(hidden[:, :units], w_a[...]) + dot(hidden[:, units:], w_b[...])
    out[...] = bf16(resid[...].astype(F32) + total + got[...].astype(F32))


def resid_back(back, got, resid, d_out, out, *halves):
    wide = resid[...].astype(F32)
    factor = norm_factor(wide)
    grad = back[...].astype(F32) + got[...].astype(F32)
    store_halves(bf16(d_out[...].astype(F32) + norm_back(grad, wide * factor, factor)), out, halves)


def attend_back(docs, d_resid, r, proj_ref, att_ref, w_out, masks, d_q, d_k, d_v, d_g):
    half = d_resid.shape[0]
    scale = HEAD ** (-0.5)
    ahead, allowed, root_inv = window(docs, r, half)
    gate = proj_ref[3, r].astype(F32)
    sigma_g = jax.nn.sigmoid(gate)
    d_gated = dot(d_resid, w_out)
    d_att = bf16(d_gated * (gate * sigma_g) * root_inv)
    d_g[r] = bf16(d_gated * att_ref[r] * silu_grad(gate, sigma_g))
    keys = jnp.concatenate([proj_ref[1, ahead], proj_ref[1, r]], axis=0)
    values = jnp.concatenate([proj_ref[2, ahead], proj_ref[2, r]], axis=0)
    many = jnp.concatenate([allowed] * len(masks), axis=0)
    query = spread(proj_ref[0, r], masks)
    d_att_m = spread(d_att, masks)
    scores = dot(query, keys, NT) * scale
    sigma = jax.nn.sigmoid(scores)
    weights = bf16(scores * sigma * many)
    d_weights = dot(d_att_m, values, NT)
    d_scores = bf16(d_weights * silu_grad(scores, sigma) * many)
    d_q[r] = bf16(collect(dot(d_scores, keys), masks) * scale)
    d_keys = dot(d_scores, query, TN) * scale
    d_values = dot(weights, d_att_m, TN)
    d_k[ahead] += d_keys[:half]
    d_k[r] += d_keys[half:]
    d_v[ahead] += d_values[:half]
    d_v[r] += d_values[half:]


def attn_back_first(docs, third, fourth_a, fourth_b, proj, att, w_out, d_q, d_k, d_v, d_g):
    masks = head_masks(w_out.shape[1])
    d_k[...] = jnp.zeros_like(d_k)
    d_v[...] = jnp.zeros_like(d_v)
    for r, rows in ((2, [third]), (3, [fourth_a, fourth_b])):
        attend_back(docs, joined(rows), r, proj, att, w_out[...], masks, d_q, d_k, d_v, d_g)


def attn_back_own(
    docs, first, proj, att, w_out, _q, _k, _v, _g, w_in, give_ref, d_q, d_k, d_v, d_g
):
    masks = head_masks(w_out.shape[1])
    attend_back(docs, first[...], 0, proj, att, w_out[...], masks, d_q, d_k, d_v, d_g)
    give_ref[...] = bf16(back_norm((d_q, d_k, d_v, d_g), w_in, 3))


def attn_back_second(
    docs, second, proj, att, w_out, _q, _k, _v, _g, d_q, d_k, d_v, d_g
):
    masks = head_masks(w_out.shape[1])
    attend_back(docs, second[...], 1, proj, att, w_out[...], masks, d_q, d_k, d_v, d_g)


def back_norm(grads, w_in, block):
    total = None
    for c, grad in enumerate(grads):
        term = dot(bf16(grad[block]), w_in[c])
        total = term if total is None else total + term
    return total


def back_give(block, d_q, d_k, d_v, d_g, w_in, *outs):
    value = bf16(back_norm((d_q, d_k, d_v, d_g), w_in, block))
    rows = value.shape[0] // len(outs)
    for n, out in enumerate(outs):
        out[...] = value[n * rows : (n + 1) * rows]


def back_sum(block, d_q, d_k, d_v, d_g, w_in, *refs):
    takes, out = refs[:-1], refs[-1]
    out[...] = bf16(back_norm((d_q, d_k, d_v, d_g), w_in, block) + joined(takes).astype(F32))


def packed_back(part, got, packed, d_resid, out, *halves):
    wide = packed[...].astype(F32)
    factor = norm_factor(wide)
    grad = part[...].astype(F32) + got[...].astype(F32)
    store_halves(bf16(d_resid[...].astype(F32) + norm_back(grad, wide * factor, factor)), out, halves)


def column_of(ref, index, cols):
    return ref[:, pl.ds(pl.multiple_of(index * cols, cols), cols)]


def rows_term(act_refs, cot):
    return dot(jnp.concatenate([a[...] for a in act_refs], axis=0), cot, TN)


def first_cot(cots, pre, enc):
    cols = pre.shape[1]
    cot = joined(cots)
    value = pre[...]
    w1_rows = enc[1, pl.ds(pl.multiple_of(tensor_index() * cols, cols), cols), :]
    return bf16(dot(cot, w1_rows, NT) * silu_grad(value, jax.nn.sigmoid(value)))


def cot_columns(cots, cols):
    return jnp.concatenate([column_of(c, tensor_index(), cols) for c in cots], axis=0)


def enc_grads_first(*refs):
    rows, (act1, pre, enc, part1, part0) = refs[:-5], refs[-5:]
    cots, act0 = rows[: len(rows) // 2], rows[len(rows) // 2 :]
    cols = pre.shape[1]
    part1[...] = rows_term([act1], cot_columns(cots, cols))
    part0[...] = rows_term(act0, first_cot(cots, pre, enc))


def halve(bits, bit, total, keep, send):
    place = bits.index(bit)
    count, size, _ = keep.shape
    mine = (group_index() >> bit) & 1
    for j in range(count):
        low = j & ((1 << place) - 1)
        base = ((j >> place) << (place + 1)) | low
        for target, value in ((keep, mine), (send, 1 - mine)):
            index = base + (value << place)
            rows = total[pl.ds(pl.multiple_of(index * size, size), size), :]
            target[j] = rows.astype(target.dtype)


def enc_grads_second(bits, bit, *refs):
    rows, refs = refs[:-11], refs[-11:]
    act1, pre, enc, part1, part0, keep1, send1, keep0, send0 = refs[:9]
    total1, total0 = refs[9:]
    cots, act0 = rows[:-2], rows[-2:]
    total1[...] = rows_term([act1], cot_columns(cots, part1.shape[1])) + part1[...]
    halve(bits, bit, total1, keep1, send1)
    total0[...] = rows_term(act0, first_cot(cots, pre, enc)) + part0[...]
    halve(bits, bit, total0, keep0, send0)


def halve_again(bits, bit, kept, got, keep, send):
    place = bits.index(bit)
    mine = (group_index() >> bit) & 1
    for j in range(keep.shape[0]):
        low = j & ((1 << place) - 1)
        base = ((j >> place) << (place + 1)) | low
        for target, value in ((keep, mine), (send, 1 - mine)):
            index = base + (value << place)
            target[j] = (kept[index] + got[index].astype(F32)).astype(target.dtype)


def finish(kept1, got1, kept0, got0, out):
    out[0] = kept0[0] + got0[0].astype(F32)
    out[1] = kept1[0] + got1[0].astype(F32)


def shards(
    features,
    dest_owner,
    dest_slot,
    doc_ids,
    enc_weight,
    attn_in,
    attn_out,
    ffn_in,
    ffn_out,
    out_grad,
):
    rows_dev, width = features.shape
    group_axes = ("event", "pack")
    groups = lax.axis_size(group_axes)
    packs = lax.axis_size("pack")
    tensors = lax.axis_size("tensor")
    cols = attn_in.shape[2]
    comps = attn_in.shape[0]
    units = ffn_out.shape[0]
    d_out = out_grad[0]
    docs = doc_ids.reshape(tensors, 1, rows_dev)

    def near(value):
        return lax.ppermute(value, "tensor", [(i, i ^ 1) for i in range(tensors)])

    def far(value):
        return lax.ppermute(value, "tensor", [(i, i ^ 2) for i in range(tensors)])

    def crossed(value, k):
        return lax.ppermute(value, group_axes, [(i, i ^ k) for i in range(groups)])

    row_b = like((rows_dev, width), BF16)
    row_f = like((rows_dev, width), F32)

    mean_load = rows_dev // groups
    capacity = -(-(mean_load + mean_load // 2) // 8) * 8
    code = (dest_owner * rows_dev + dest_slot).reshape(1, rows_dev)
    order = [0] + sorted(
        range(1, groups), key=lambda k: (-((2 * (k % packs)) // packs), k % packs, k)
    )
    *sends, place = run(
        functools.partial(route_send, capacity, order),
        [like((capacity, width + rows_dev), BF16)] * groups + [like((1, rows_dev), jnp.int32)],
        [code, features],
        flops=4 * 10**9,
        name="route_send",
    )
    ffn_in_near, ffn_out_near = near(ffn_in), near(ffn_out)
    early = [crossed(sends[n], order[n]) for n in (1, 2)]
    ffn_in_near, ffn_out_near, *sends = tie(ffn_in_near, ffn_out_near, *sends)
    gots = [sends[0], *early] + [crossed(sends[n], order[n]) for n in range(3, groups)]
    pieces = 2
    piece_b = like((rows_dev // pieces, width), BF16)
    in_turned, out_turned = run(
        turn,
        [like((comps, cols, width), BF16), like((width, cols), BF16)],
        [attn_in, attn_out],
        name="turn",
    )
    in_turned, *gots = tie(in_turned, *gots)
    mine, hot, *halves = run(
        route_recv,
        [row_b, like((groups * capacity, rows_dev), BF16)] + [piece_b] * pieces,
        gots,
        name="route_recv",
    )

    mine_far = far(mine)
    mine_near = [near(h) for h in halves]

    pair = 2 * rows_dev
    pre_a, act_a, packed, proj_a = run(
        encode_blocks,
        [
            like((pair, cols), F32),
            like((pair, width), BF16),
            row_b,
            like((comps, 2, rows_dev, cols), BF16),
        ],
        [mine, *mine_near, enc_weight, attn_in],
        [pltpu.VMEM((pair, width), F32)],
        name="encode_first",
    )
    mine_far, proj_a = tie(mine_far, proj_a)
    mine_far, attn_out_late, d_out_late = tie(mine_far, attn_out, d_out)
    mine_both = near(mine_far)
    attn_out_near = near(attn_out_late)
    d_out_far = far(d_out_late)
    pre_c, act_c, packed_far, proj_c = run(
        encode_blocks,
        [like((rows_dev, cols), F32), row_b, row_b, like((comps, 1, rows_dev, cols), BF16)],
        [mine_far, enc_weight, attn_in],
        [pltpu.VMEM((rows_dev, width), F32)],
        name="encode_third",
    )
    pre_b, act_b, proj, attended, give, keep = run(
        attend_first,
        [
            like((pair, cols), F32),
            like((pair, width), BF16),
            like((comps, tensors, rows_dev, cols), BF16),
            like((tensors, rows_dev, cols), F32),
            like((pair, cols), BF16),
            like((pair, cols), BF16),
        ],
        [docs, mine_both, pre_c, act_c, proj_a, proj_c, enc_weight, attn_in],
        [pltpu.VMEM((rows_dev, width), F32)],
        name="attend_first",
    )
    take = near(give)


    def out_part(index, name):
        return run(
            functools.partial(attn_out_part, index),
            [row_b],
            [keep, take, attn_out, attn_out_near],
            name=name,
        )[0]

    part_far = out_part(0, "attn_out_far")
    got_own = far(part_far)
    part_own = out_part(1, "attn_out_own")
    part_own, d_out_far = tie(part_own, d_out_far)
    got_far = far(part_own)

    def feed(rows, cotangent, name):
        return run(
            ffn,
            [like((rows_dev, 2 * units), BF16), row_b],
            [rows, cotangent, ffn_in, ffn_in_near, ffn_out, ffn_out_near],
            name=name,
        )

    resid, normed2 = run(residual, [row_b, row_b], [packed, part_own, got_own], name="residual")
    hidden_own, back_own = feed(normed2, d_out, "ffn_own")
    got_far, back_own = tie(got_far, back_own)
    got_back_far = far(back_own)
    resid_far, normed2_far = run(
        residual, [row_b, row_b], [packed_far, part_far, got_far], name="residual_far"
    )
    hidden_far, back_far = feed(normed2_far, d_out_far, "ffn_far")
    got_back_own = far(back_far)

    d_resid_far, *halves = run(
        resid_back,
        [row_b] + [piece_b] * pieces,
        [back_far, got_back_far, resid_far, d_out_far],
        name="resid_back_far",
    )
    d_resid_both = [near(h) for h in halves]
    block_f = like((tensors, rows_dev, cols), F32)
    block_b = like((tensors, rows_dev, cols), BF16)
    d_q, d_k, d_v, d_g = run(
        attn_back_first,
        [block_b, block_f, block_f, block_b],
        [docs, d_resid_far, *d_resid_both, proj, attended, out_turned],
        name="attn_back_first",
    )
    got_back_own, d_q = tie(got_back_own, d_q)
    (d_resid,) = run(resid_back, [row_b], [back_own, got_back_own, resid, d_out], name="resid_back")
    d_resid_near = near(d_resid)
    give, *own_grads = run(
        attn_back_own,
        [row_b, block_b, block_f, block_f, block_b],
        [docs, d_resid, proj, attended, out_turned, d_q, d_k, d_v, d_g, in_turned],
        aliases={5: 1, 6: 2, 7: 3, 8: 4},
        name="attn_back_own",
    )
    take = near(give)
    d_projected = run(
        attn_back_second,
        [block_b, block_f, block_f, block_b],
        [docs, d_resid_near, proj, attended, out_turned, *own_grads],
        aliases={5: 0, 6: 1, 7: 2, 8: 3},
        name="attn_back_second",
    )

    def back_part(body, block, outs, more, name):
        return run(functools.partial(body, block), outs, [*d_projected, in_turned, *more], name=name)

    (sum_far,) = back_part(back_sum, 2, [row_b], [take], "back_sum_far")
    sum_far, *d_projected = tie(sum_far, *d_projected)
    takes = [near(h) for h in back_part(back_give, 1, [piece_b] * pieces, [], "back_give")]
    (sum_own,) = back_part(back_sum, 0, [row_b], takes, "back_sum_own")
    got_own = far(sum_far)
    got_far = far(sum_own)
    d_packed, *halves = run(
        packed_back,
        [row_b] + [piece_b] * pieces,
        [sum_own, got_own, packed, d_resid],
        name="packed_back",
    )

    cot_near = [near(h) for h in halves]
    half_rows = like((groups * capacity // 2, width), BF16)
    group_bits = [1 << b for b in range(groups.bit_length() - 1)]
    near_bit, pack_far, event_far = group_bits[0], group_bits[1 : packs.bit_length() - 1], group_bits[packs.bit_length() - 1 :]
    back_bits = pack_far[::-1] + [near_bit] + event_far[::-1]
    kept, back = run(
        functools.partial(back_send, order, back_bits[0]), [half_rows] * 2, [hot, d_packed], name="back_send"
    )
    back_got = crossed(back, back_bits[0])

    part_f = like((width, cols), F32)
    part1, part0 = run(
        enc_grads_first,
        [part_f, part_f],
        [d_packed, *cot_near, mine, *mine_near, act_a, pre_a, enc_weight],
        name="enc_grads_first",
    )
    got_far, part1, part0 = tie(got_far, part1, part0)
    cot_far, *cot_pieces = run(
        packed_back,
        [row_b] + [like((rows_dev // 4, width), BF16)] * 4,
        [sum_far, got_far, packed_far, d_resid_far],
        name="packed_back_far",
    )
    cot_both = [near(piece) for piece in cot_pieces]
    cot_far, hidden_far = tie(cot_far, hidden_far)
    (out_far,) = run(
        ffn_out_far, [row_b], [hidden_far, ffn_out, ffn_out_near], name="ffn_out_far"
    )
    bits = list(range(groups.bit_length() - 1))
    pack_bits = bits[: packs.bit_length() - 1]
    event_bits = bits[len(pack_bits) :]
    size = width // groups
    total = [pltpu.VMEM((width, cols), F32)]

    def halves(remaining):
        shape = (2 ** (len(remaining) - 1), size, cols)
        return [like(shape, F32), like(shape, BF16)]

    def reduce_over(stages, kept, send, name, beside):
        remaining = list(bits)
        got = crossed(send, 1 << stages[0])
        if beside == stages[0]:
            got, arrays[-1] = tie(got, arrays[-1])
        remaining.remove(stages[0])
        for bit in stages[1:]:
            kept, send = run(
                functools.partial(halve_again, tuple(remaining), bit),
                halves(remaining),
                [kept, got],
                name=name + str(bit),
            )
            got = crossed(send, 1 << bit)
            remaining.remove(bit)
            if bit == beside:
                got, arrays[-1] = tie(got, arrays[-1])
        return kept, got

    kept1, send1, kept0, send0 = run(
        functools.partial(enc_grads_second, tuple(bits), event_bits[0]),
        halves(bits) * 2,
        [cot_far, *cot_both, mine_far, mine_both, act_b, pre_b, enc_weight, part1, part0],
        total * 2,
        name="enc_grads_second",
    )
    arrays = [kept, back_got]
    held = {}
    for n, value in enumerate((0, back_bits[0])):
        chosen = [k for k in range(groups) if k & back_bits[0] == value]
        held.update({k: (n, at) for at, k in enumerate(chosen)})

    def send_back(bit):
        moved = [k for k in range(groups) if k & bit]
        (back,) = run(
            functools.partial(back_pick, [held[k] for k in moved], capacity),
            [half_rows],
            arrays,
            name="back_pick",
        )
        held.update({k: (len(arrays), n) for n, k in enumerate(moved)})
        arrays.append(crossed(back, bit))

    for bit in back_bits[1:-1]:
        send_back(bit)
    kept1, got1 = reduce_over(event_bits + pack_bits, kept1, send1, "halve1_", None)
    kept0, got0 = reduce_over(event_bits + pack_bits, kept0, send0, "halve0_", event_bits[0])
    send_back(back_bits[-1])
    got1, place = tie(got1, place)
    back_places = [held[k] for k in range(groups)]
    got_out = far(out_far)
    (packed_out,) = run(
        ffn_out_own, [row_b], [hidden_own, ffn_out, ffn_out_near, resid, got_out], name="ffn_out_own"
    )
    (row_grad,) = run(
        functools.partial(back_recv, back_places, capacity),
        [row_b],
        [place, *arrays],
        name="back_recv",
    )
    got1, got0, packed_out, row_grad = tie(got1, got0, packed_out, row_grad)
    (enc_grad,) = run(finish, [like((2, size, cols), F32)], [kept1, got1, kept0, got0], name="finish")
    return (packed_out[None], row_grad, enc_grad)


def solution(mesh):
    placed = (
        P(("event", "pack", "tensor"), None),
        P(("event", "pack", "tensor")),
        P(("event", "pack", "tensor")),
        P(("event", "pack"), None),
        P(),
        P(None, None, "tensor"),
        P("tensor", None),
        P(None, None, "tensor"),
        P("tensor", None),
        P(("event", "pack"), "tensor", None),
    )
    return jax.shard_map(
        shards,
        mesh=mesh,
        in_specs=placed,
        out_specs=(
            P(("event", "pack"), "tensor", None),
            P(("event", "pack", "tensor"), None),
            P(None, ("event", "pack"), "tensor"),
        ),
        check_vma=False,
    )
```

```python
import functools

import jax
import jax.numpy as jnp
from jax import lax
from jax.experimental import pallas as pl
from jax.experimental.pallas import tpu as pltpu
from jax.sharding import PartitionSpec as P

D = 1024
HEADS = 16
HEAD = D // HEADS
EPS = 1e-06
F32 = jnp.float32
BF16 = jnp.bfloat16
MIB = 1 << 20
CHUNK = 256


def dot(left, right, dims=((1,), (0,))):
    return lax.dot_general(left, right, (dims, ((), ())), preferred_element_type=F32)


NT = ((1,), (1,))
TN = ((0,), (0,))


def bf16(value):
    return value.astype(BF16)


def silu_grad(value, sigma):
    return sigma * (1.0 + value * (1.0 - sigma))


def norm_factor(wide):
    return lax.rsqrt(jnp.mean(wide * wide, axis=-1, keepdims=True) + EPS)


def norm_back(grad, normed, factor):
    return factor * (grad - normed * jnp.mean(grad * normed, axis=-1, keepdims=True))


def joined(refs):
    return jnp.concatenate([r[...] for r in refs], axis=0)


def store_halves(value, out, halves):
    out[...] = value
    rows = value.shape[0] // max(len(halves), 1)
    for n, target in enumerate(halves):
        target[...] = value[n * rows : (n + 1) * rows]


def turned(row, rows):
    return jnp.broadcast_to(row.astype(F32), (rows, rows)).T


def like(shape, dtype):
    return jax.ShapeDtypeStruct(shape, dtype)


def run(body, outs, args, scratch=(), flops=0, name=None, aliases=None):
    return pl.pallas_call(
        body,
        out_shape=list(outs),
        in_specs=[pl.BlockSpec(memory_space=pltpu.VMEM)] * len(args),
        out_specs=[pl.BlockSpec(memory_space=pltpu.VMEM)] * len(outs),
        scratch_shapes=list(scratch),
        input_output_aliases=aliases or {},
        compiler_params=pltpu.CompilerParams(vmem_limit_bytes=16 * MIB),
        cost_estimate=pl.CostEstimate(flops=flops, bytes_accessed=0, transcendentals=0),
        name=name,
    )(*args)


def group_index():
    return lax.axis_index("event") * lax.axis_size("pack") + lax.axis_index("pack")


def tensor_index():
    return lax.axis_index("tensor")


def tie(*values):
    return lax.optimization_barrier(values)


def route_send(capacity, order, code, features, *outs):
    sends, place_ref = outs[:-1], outs[-1]
    groups = len(sends)
    rows, width = features.shape
    shift = rows.bit_length() - 1
    o_row = code[...] >> shift
    slot = code[...] & (rows - 1)
    o_col = turned(o_row, rows)
    i = lax.broadcasted_iota(jnp.int32, (rows, rows), 0)
    j = lax.broadcasted_iota(jnp.int32, (rows, rows), 1)
    earlier = jnp.where((o_col == o_row.astype(F32)) & (i < j), 1.0, 0.0)
    rank = jnp.sum(earlier, axis=0, keepdims=True).astype(jnp.int32)
    place = (o_row ^ group_index()) * capacity + rank
    place_ref[...] = place
    spots = lax.broadcasted_iota(jnp.int32, (groups * capacity, rows), 0)
    hot = jnp.where(spots == place, 1.0, 0.0).astype(BF16)
    big = dot(hot, features[...])
    tags = dot(hot, bf16(turned(slot + 1, rows)))
    for k, send in zip(order, sends):
        part = slice(k * capacity, (k + 1) * capacity)
        send[:, :width] = bf16(big[part])
        send[:, width:] = bf16(tags[part])


def route_recv(*refs):
    gots, (rows_ref, hot_ref, *halves) = refs[:-4], refs[-4:]
    rows, width = rows_ref.shape
    got = jnp.concatenate([g[...].astype(F32) for g in gots], axis=0)
    lanes = lax.broadcasted_iota(jnp.int32, (got.shape[0], rows), 1) + 1
    hot = jnp.where(got[:, width:] == lanes.astype(F32), 1.0, 0.0).astype(BF16)
    hot_ref[...] = hot
    store_halves(bf16(dot(hot, bf16(got[:, :width]), TN)), rows_ref, halves)


def back_send(order, bit, hot, d_packed, keep, send):
    groups = len(order)
    capacity = hot.shape[0] // groups
    big = dot(hot[...], d_packed[...])
    at = {k: n * capacity for n, k in enumerate(order)}
    for target, value in ((keep, 0), (send, bit)):
        chosen = [k for k in range(groups) if k & bit == value]
        parts = [big[at[k] : at[k] + capacity] for k in chosen]
        target[...] = bf16(jnp.concatenate(parts, axis=0))


def picked(places, capacity, refs):
    wide = [r[...].astype(F32) for r in refs]
    parts = [wide[n][p * capacity : (p + 1) * capacity] for n, p in places]
    return bf16(jnp.concatenate(parts, axis=0))


def back_pick(places, capacity, *refs):
    refs[-1][...] = picked(places, capacity, refs[:-1])


def back_recv(places, capacity, place, *refs):
    got, out = picked(places, capacity, refs[:-1]), refs[-1]
    spots = lax.broadcasted_iota(jnp.int32, (got.shape[0], out.shape[0]), 0)
    hot = jnp.where(spots == place[...], 1.0, 0.0).astype(BF16)
    out[...] = bf16(dot(hot, got, TN))


def encode(rows, enc, w_in, pre_all, pre_ref, act_ref, store):
    width = rows.shape[1]
    cols = pre_ref.shape[1]
    for n in range(width // CHUNK):
        part = slice(n * CHUNK, (n + 1) * CHUNK)
        pre = dot(rows, enc[0, :, part])
        pre_all[:, part] = pre
        act_ref[:, part] = bf16(pre * jax.nn.sigmoid(pre))
    pre_ref[...] = pre_all[:, pl.ds(pl.multiple_of(tensor_index() * cols, cols), cols)]
    packed = bf16(dot(act_ref[...], enc[1]))
    wide = packed.astype(F32)
    normed = bf16(wide * norm_factor(wide))
    for c in range(w_in.shape[0]):
        store(c, bf16(dot(normed, w_in[c])))
    return packed


def encode_blocks(*refs):
    blocks, (enc, w_in, pre_ref, act_ref, packed_ref, proj_ref, pre_all) = refs[:-7], refs[-7:]
    rows = joined(blocks)
    count, size = proj_ref.shape[1:3]

    def store(c, value):
        for n in range(count):
            proj_ref[c, n] = value[n * size : (n + 1) * size]

    packed = encode(rows, enc, w_in, pre_all, pre_ref, act_ref, store)
    packed_ref[...] = packed[:size]


def turn(attn_in, attn_out, in_ref, out_ref):
    for c in range(attn_in.shape[0]):
        in_ref[c] = attn_in[c].T
    out_ref[...] = attn_out[...].T


def window(docs, r, rows):
    t = tensor_index()
    b = t ^ r
    ahead = jnp.where(b > 0, (b - 1) ^ t, r)
    doc_q = turned(docs[b], rows)
    doc_own = docs[b].astype(F32)
    doc_ahead = docs[jnp.maximum(b - 1, 0)].astype(F32)
    i = lax.broadcasted_iota(jnp.int32, (rows, rows), 0)
    j = lax.broadcasted_iota(jnp.int32, (rows, rows), 1)
    own = jnp.where((doc_q == doc_own) & (j <= i), 1.0, 0.0)
    prior = jnp.where(doc_q == doc_ahead, 1.0, 0.0) * jnp.where(b > 0, 1.0, 0.0)
    allowed = jnp.concatenate([prior, own], axis=1)
    root_inv = lax.rsqrt(jnp.sum(allowed, axis=1, keepdims=True))
    return ahead, allowed, root_inv


def head_masks(cols):
    lane = lax.broadcasted_iota(jnp.int32, (1, cols), 1) // HEAD
    return [jnp.where(lane == h, 1.0, 0.0) for h in range(cols // HEAD)]


def spread(value, masks):
    return jnp.concatenate([value * bf16(m) for m in masks], axis=0)


def collect(value, masks):
    rows = value.shape[0] // len(masks)
    total = None
    for h, m in enumerate(masks):
        part = value[h * rows : (h + 1) * rows] * m
        total = part if total is None else total + part
    return total


def attend_first(
    docs, fourth, pre_c, act_c, proj_a, proj_c, enc, w_in,
    pre_ref, act_ref, proj_ref, att_ref, give_ref, keep_ref, pre_all,
):
    half = fourth.shape[0]
    cols = proj_a.shape[-1]
    proj_ref[:, 0:2] = proj_a[...]
    proj_ref[:, 2:3] = proj_c[...]
    pre_ref[:half, :] = pre_c[...]
    act_ref[:half, :] = act_c[...]

    def store(c, value):
        proj_ref[c, 3] = value

    encode(
        fourth[...], enc, w_in, pre_all, pre_ref.at[half : 2 * half], act_ref.at[half : 2 * half], store
    )
    masks = head_masks(cols)
    for r, (target, place) in enumerate(((keep_ref, 1), (give_ref, 1), (keep_ref, 0), (give_ref, 0))):
        ahead, allowed, root_inv = window(docs, r, half)
        keys = jnp.concatenate([proj_ref[1, ahead], proj_ref[1, r]], axis=0)
        values = jnp.concatenate([proj_ref[2, ahead], proj_ref[2, r]], axis=0)
        many = jnp.concatenate([allowed] * len(masks), axis=0)
        scores = dot(spread(proj_ref[0, r], masks), keys, NT) * HEAD ** (-0.5)
        weights = bf16(scores * jax.nn.sigmoid(scores) * many)
        attended = collect(dot(weights, values), masks) * root_inv
        gate = proj_ref[3, r].astype(F32)
        att_ref[r] = attended
        target[place * half : (place + 1) * half, :] = bf16(attended * gate * jax.nn.sigmoid(gate))


def attn_out_part(index, keep, take, w_own, w_near, out):
    rows = out.shape[0]
    part = slice(index * rows, (index + 1) * rows)
    out[...] = bf16(dot(keep[part, :], w_own[...]) + dot(take[part, :], w_near[...]))


def residual(packed, part, got, resid_ref, normed_ref):
    resid = bf16(packed[...].astype(F32) + (part[...].astype(F32) + got[...].astype(F32)))
    resid_ref[...] = resid
    wide = resid.astype(F32)
    normed_ref[...] = bf16(wide * norm_factor(wide))


def ffn(rows_ref, d_out_ref, in_a, in_b, out_a, out_b, hidden_ref, back_ref):
    rows = rows_ref[...]
    cotangent = d_out_ref[...]
    units = out_a.shape[0]
    back = None
    for index, (w_in, w_out) in enumerate(((in_a, out_a), (in_b, out_b))):
        for n in range(units // CHUNK):
            part = slice(n * CHUNK, (n + 1) * CHUNK)
            d_hidden = dot(cotangent, w_out[part, :], NT)
            gate = dot(rows, w_in[0, :, part])
            upper = dot(rows, w_in[1, :, part])
            sigma = jax.nn.sigmoid(gate)
            silu = gate * sigma
            hidden_ref[:, index * units + n * CHUNK : index * units + (n + 1) * CHUNK] = bf16(silu * upper)
            d_gate = bf16(d_hidden * upper * silu_grad(gate, sigma))
            d_upper = bf16(d_hidden * silu)
            term = dot(d_gate, w_in[0, :, part], NT) + dot(d_upper, w_in[1, :, part], NT)
            back = term if back is None else back + term
    back_ref[...] = back.astype(back_ref.dtype)


def ffn_out_far(hidden, w_a, w_b, out):
    units = w_a.shape[0]
    out[...] = bf16(dot(hidden[:, :units], w_a[...]) + dot(hidden[:, units:], w_b[...]))


def ffn_out_own(hidden, w_a, w_b, resid, got, out):
    units = w_a.shape[0]
    total = dot(hidden[:, :units], w_a[...]) + dot(hidden[:, units:], w_b[...])
    out[...] = bf16(resid[...].astype(F32) + total + got[...].astype(F32))


def resid_back(back, got, resid, d_out, out, *halves):
    wide = resid[...].astype(F32)
    factor = norm_factor(wide)
    grad = back[...].astype(F32) + got[...].astype(F32)
    store_halves(bf16(d_out[...].astype(F32) + norm_back(grad, wide * factor, factor)), out, halves)


def attend_back(docs, d_resid, r, proj_ref, att_ref, w_out, masks, d_q, d_k, d_v, d_g):
    half = d_resid.shape[0]
    scale = HEAD ** (-0.5)
    ahead, allowed, root_inv = window(docs, r, half)
    gate = proj_ref[3, r].astype(F32)
    sigma_g = jax.nn.sigmoid(gate)
    d_gated = dot(d_resid, w_out)
    d_att = bf16(d_gated * (gate * sigma_g) * root_inv)
    d_g[r] = bf16(d_gated * att_ref[r] * silu_grad(gate, sigma_g))
    keys = jnp.concatenate([proj_ref[1, ahead], proj_ref[1, r]], axis=0)
    values = jnp.concatenate([proj_ref[2, ahead], proj_ref[2, r]], axis=0)
    many = jnp.concatenate([allowed] * len(masks), axis=0)
    query = spread(proj_ref[0, r], masks)
    d_att_m = spread(d_att, masks)
    scores = dot(query, keys, NT) * scale
    sigma = jax.nn.sigmoid(scores)
    weights = bf16(scores * sigma * many)
    d_weights = dot(d_att_m, values, NT)
    d_scores = bf16(d_weights * silu_grad(scores, sigma) * many)
    d_q[r] = bf16(collect(dot(d_scores, keys), masks) * scale)
    d_keys = dot(d_scores, query, TN) * scale
    d_values = dot(weights, d_att_m, TN)
    d_k[ahead] += d_keys[:half]
    d_k[r] += d_keys[half:]
    d_v[ahead] += d_values[:half]
    d_v[r] += d_values[half:]


def attn_back_first(docs, third, fourth_a, fourth_b, proj, att, w_out, d_q, d_k, d_v, d_g):
    masks = head_masks(w_out.shape[1])
    d_k[...] = jnp.zeros_like(d_k)
    d_v[...] = jnp.zeros_like(d_v)
    for r, rows in ((2, [third]), (3, [fourth_a, fourth_b])):
        attend_back(docs, joined(rows), r, proj, att, w_out[...], masks, d_q, d_k, d_v, d_g)


def attn_back_own(
    docs, first, proj, att, w_out, _q, _k, _v, _g, w_in, give_ref, d_q, d_k, d_v, d_g
):
    masks = head_masks(w_out.shape[1])
    attend_back(docs, first[...], 0, proj, att, w_out[...], masks, d_q, d_k, d_v, d_g)
    give_ref[...] = bf16(back_norm((d_q, d_k, d_v, d_g), w_in, 3))


def attn_back_second(
    docs, second, proj, att, w_out, _q, _k, _v, _g, d_q, d_k, d_v, d_g
):
    masks = head_masks(w_out.shape[1])
    attend_back(docs, second[...], 1, proj, att, w_out[...], masks, d_q, d_k, d_v, d_g)


def back_norm(grads, w_in, block):
    total = None
    for c, grad in enumerate(grads):
        term = dot(bf16(grad[block]), w_in[c])
        total = term if total is None else total + term
    return total


def back_give(block, d_q, d_k, d_v, d_g, w_in, *outs):
    value = bf16(back_norm((d_q, d_k, d_v, d_g), w_in, block))
    rows = value.shape[0] // len(outs)
    for n, out in enumerate(outs):
        out[...] = value[n * rows : (n + 1) * rows]


def back_sum(block, d_q, d_k, d_v, d_g, w_in, *refs):
    takes, out = refs[:-1], refs[-1]
    out[...] = bf16(back_norm((d_q, d_k, d_v, d_g), w_in, block) + joined(takes).astype(F32))


def packed_back(part, got, packed, d_resid, out, *halves):
    wide = packed[...].astype(F32)
    factor = norm_factor(wide)
    grad = part[...].astype(F32) + got[...].astype(F32)
    store_halves(bf16(d_resid[...].astype(F32) + norm_back(grad, wide * factor, factor)), out, halves)


def column_of(ref, index, cols):
    return ref[:, pl.ds(pl.multiple_of(index * cols, cols), cols)]


def rows_term(act_refs, cot):
    return dot(jnp.concatenate([a[...] for a in act_refs], axis=0), cot, TN)


def first_cot(cots, pre, enc):
    cols = pre.shape[1]
    cot = joined(cots)
    value = pre[...]
    w1_rows = enc[1, pl.ds(pl.multiple_of(tensor_index() * cols, cols), cols), :]
    return bf16(dot(cot, w1_rows, NT) * silu_grad(value, jax.nn.sigmoid(value)))


def cot_columns(cots, cols):
    return jnp.concatenate([column_of(c, tensor_index(), cols) for c in cots], axis=0)


def enc_grads_first(*refs):
    rows, (act1, pre, enc, part1, part0) = refs[:-5], refs[-5:]
    cots, act0 = rows[: len(rows) // 2], rows[len(rows) // 2 :]
    cols = pre.shape[1]
    part1[...] = rows_term([act1], cot_columns(cots, cols))
    part0[...] = rows_term(act0, first_cot(cots, pre, enc))


def halve(bits, bit, total, keep, send):
    place = bits.index(bit)
    count, size, _ = keep.shape
    mine = (group_index() >> bit) & 1
    for j in range(count):
        low = j & ((1 << place) - 1)
        base = ((j >> place) << (place + 1)) | low
        for target, value in ((keep, mine), (send, 1 - mine)):
            index = base + (value << place)
            rows = total[pl.ds(pl.multiple_of(index * size, size), size), :]
            target[j] = rows.astype(target.dtype)


def enc_grads_second(bits, bit, *refs):
    rows, refs = refs[:-11], refs[-11:]
    act1, pre, enc, part1, part0, keep1, send1, keep0, send0 = refs[:9]
    total1, total0 = refs[9:]
    cots, act0 = rows[:-2], rows[-2:]
    total1[...] = rows_term([act1], cot_columns(cots, part1.shape[1])) + part1[...]
    halve(bits, bit, total1, keep1, send1)
    total0[...] = rows_term(act0, first_cot(cots, pre, enc)) + part0[...]
    halve(bits, bit, total0, keep0, send0)


def halve_again(bits, bit, kept, got, keep, send):
    place = bits.index(bit)
    mine = (group_index() >> bit) & 1
    for j in range(keep.shape[0]):
        low = j & ((1 << place) - 1)
        base = ((j >> place) << (place + 1)) | low
        for target, value in ((keep, mine), (send, 1 - mine)):
            index = base + (value << place)
            target[j] = (kept[index] + got[index].astype(F32)).astype(target.dtype)


def finish(kept1, got1, kept0, got0, out):
    out[0] = kept0[0] + got0[0].astype(F32)
    out[1] = kept1[0] + got1[0].astype(F32)


def shards(
    features,
    dest_owner,
    dest_slot,
    doc_ids,
    enc_weight,
    attn_in,
    attn_out,
    ffn_in,
    ffn_out,
    out_grad,
):
    rows_dev, width = features.shape
    group_axes = ("event", "pack")
    groups = lax.axis_size(group_axes)
    packs = lax.axis_size("pack")
    tensors = lax.axis_size("tensor")
    cols = attn_in.shape[2]
    comps = attn_in.shape[0]
    units = ffn_out.shape[0]
    d_out = out_grad[0]
    docs = doc_ids.reshape(tensors, 1, rows_dev)

    def near(value):
        return lax.ppermute(value, "tensor", [(i, i ^ 1) for i in range(tensors)])

    def far(value):
        return lax.ppermute(value, "tensor", [(i, i ^ 2) for i in range(tensors)])

    def crossed(value, k):
        return lax.ppermute(value, group_axes, [(i, i ^ k) for i in range(groups)])

    row_b = like((rows_dev, width), BF16)
    row_f = like((rows_dev, width), F32)

    mean_load = rows_dev // groups
    capacity = -(-(mean_load + mean_load // 2) // 8) * 8
    code = (dest_owner * rows_dev + dest_slot).reshape(1, rows_dev)
    offsets = range(1, groups)
    across = sorted((k for k in offsets if 2 * (k % packs) >= packs), key=lambda k: (k % packs, k))
    short = [k for k in offsets if k not in across]
    hops = [k for k in short if k & (k - 1)]
    order = [0] + across[:2] + hops + across[2:] + [k for k in short if k not in hops]
    *sends, place = run(
        functools.partial(route_send, capacity, order),
        [like((capacity, width + rows_dev), BF16)] * groups + [like((1, rows_dev), jnp.int32)],
        [code, features],
        flops=4 * 10**9,
        name="route_send",
    )
    ffn_in_near, ffn_out_near = near(ffn_in), near(ffn_out)
    early = [crossed(sends[n], order[n]) for n in (1, 2)]
    ffn_in_near, ffn_out_near, *sends = tie(ffn_in_near, ffn_out_near, *sends)
    gots = [sends[0], *early] + [crossed(sends[n], order[n]) for n in range(3, groups)]
    pieces = 2
    piece_b = like((rows_dev // pieces, width), BF16)
    in_turned, out_turned = run(
        turn,
        [like((comps, cols, width), BF16), like((width, cols), BF16)],
        [attn_in, attn_out],
        name="turn",
    )
    in_turned, *gots = tie(in_turned, *gots)
    mine, hot, *halves = run(
        route_recv,
        [row_b, like((groups * capacity, rows_dev), BF16)] + [piece_b] * pieces,
        gots,
        name="route_recv",
    )

    mine_far = far(mine)
    mine_near = [near(h) for h in halves]

    pair = 2 * rows_dev
    pre_a, act_a, packed, proj_a = run(
        encode_blocks,
        [
            like((pair, cols), F32),
            like((pair, width), BF16),
            row_b,
            like((comps, 2, rows_dev, cols), BF16),
        ],
        [mine, *mine_near, enc_weight, attn_in],
        [pltpu.VMEM((pair, width), F32)],
        name="encode_first",
    )
    mine_far, proj_a = tie(mine_far, proj_a)
    mine_far, attn_out_late, d_out_late = tie(mine_far, attn_out, d_out)
    mine_both = near(mine_far)
    attn_out_near = near(attn_out_late)
    d_out_far = far(d_out_late)
    pre_c, act_c, packed_far, proj_c = run(
        encode_blocks,
        [like((rows_dev, cols), F32), row_b, row_b, like((comps, 1, rows_dev, cols), BF16)],
        [mine_far, enc_weight, attn_in],
        [pltpu.VMEM((rows_dev, width), F32)],
        name="encode_third",
    )
    pre_b, act_b, proj, attended, give, keep = run(
        attend_first,
        [
            like((pair, cols), F32),
            like((pair, width), BF16),
            like((comps, tensors, rows_dev, cols), BF16),
            like((tensors, rows_dev, cols), F32),
            like((pair, cols), BF16),
            like((pair, cols), BF16),
        ],
        [docs, mine_both, pre_c, act_c, proj_a, proj_c, enc_weight, attn_in],
        [pltpu.VMEM((rows_dev, width), F32)],
        name="attend_first",
    )
    take = near(give)


    def out_part(index, name):
        return run(
            functools.partial(attn_out_part, index),
            [row_b],
            [keep, take, attn_out, attn_out_near],
            name=name,
        )[0]

    part_far = out_part(0, "attn_out_far")
    got_own = far(part_far)
    part_own = out_part(1, "attn_out_own")
    part_own, d_out_far = tie(part_own, d_out_far)
    got_far = far(part_own)

    def feed(rows, cotangent, name):
        return run(
            ffn,
            [like((rows_dev, 2 * units), BF16), row_b],
            [rows, cotangent, ffn_in, ffn_in_near, ffn_out, ffn_out_near],
            name=name,
        )

    resid, normed2 = run(residual, [row_b, row_b], [packed, part_own, got_own], name="residual")
    hidden_own, back_own = feed(normed2, d_out, "ffn_own")
    got_far, back_own = tie(got_far, back_own)
    got_back_far = far(back_own)
    resid_far, normed2_far = run(
        residual, [row_b, row_b], [packed_far, part_far, got_far], name="residual_far"
    )
    hidden_far, back_far = feed(normed2_far, d_out_far, "ffn_far")
    got_back_own = far(back_far)

    d_resid_far, *halves = run(
        resid_back,
        [row_b] + [piece_b] * pieces,
        [back_far, got_back_far, resid_far, d_out_far],
        name="resid_back_far",
    )
    d_resid_both = [near(h) for h in halves]
    block_f = like((tensors, rows_dev, cols), F32)
    block_b = like((tensors, rows_dev, cols), BF16)
    d_q, d_k, d_v, d_g = run(
        attn_back_first,
        [block_b, block_f, block_f, block_b],
        [docs, d_resid_far, *d_resid_both, proj, attended, out_turned],
        name="attn_back_first",
    )
    got_back_own, d_q = tie(got_back_own, d_q)
    (d_resid,) = run(resid_back, [row_b], [back_own, got_back_own, resid, d_out], name="resid_back")
    d_resid_near = near(d_resid)
    give, *own_grads = run(
        attn_back_own,
        [row_b, block_b, block_f, block_f, block_b],
        [docs, d_resid, proj, attended, out_turned, d_q, d_k, d_v, d_g, in_turned],
        aliases={5: 1, 6: 2, 7: 3, 8: 4},
        name="attn_back_own",
    )
    take = near(give)
    d_projected = run(
        attn_back_second,
        [block_b, block_f, block_f, block_b],
        [docs, d_resid_near, proj, attended, out_turned, *own_grads],
        aliases={5: 0, 6: 1, 7: 2, 8: 3},
        name="attn_back_second",
    )

    def back_part(body, block, outs, more, name):
        return run(functools.partial(body, block), outs, [*d_projected, in_turned, *more], name=name)

    (sum_far,) = back_part(back_sum, 2, [row_b], [take], "back_sum_far")
    sum_far, *d_projected = tie(sum_far, *d_projected)
    takes = [near(h) for h in back_part(back_give, 1, [piece_b] * pieces, [], "back_give")]
    (sum_own,) = back_part(back_sum, 0, [row_b], takes, "back_sum_own")
    got_own = far(sum_far)
    got_far = far(sum_own)
    d_packed, *halves = run(
        packed_back,
        [row_b] + [piece_b] * pieces,
        [sum_own, got_own, packed, d_resid],
        name="packed_back",
    )

    cot_near = [near(h) for h in halves]
    half_rows = like((groups * capacity // 2, width), BF16)
    group_bits = [1 << b for b in range(groups.bit_length() - 1)]
    near_bit, pack_far, event_far = group_bits[0], group_bits[1 : packs.bit_length() - 1], group_bits[packs.bit_length() - 1 :]
    back_bits = pack_far[::-1] + [near_bit] + event_far[::-1]
    kept, back = run(
        functools.partial(back_send, order, back_bits[0]), [half_rows] * 2, [hot, d_packed], name="back_send"
    )
    back_got = crossed(back, back_bits[0])

    part_f = like((width, cols), F32)
    part1, part0 = run(
        enc_grads_first,
        [part_f, part_f],
        [d_packed, *cot_near, mine, *mine_near, act_a, pre_a, enc_weight],
        name="enc_grads_first",
    )
    got_far, part1, part0 = tie(got_far, part1, part0)
    cot_far, *cot_pieces = run(
        packed_back,
        [row_b] + [like((rows_dev // 4, width), BF16)] * 4,
        [sum_far, got_far, packed_far, d_resid_far],
        name="packed_back_far",
    )
    cot_both = [near(piece) for piece in cot_pieces]
    cot_far, hidden_far = tie(cot_far, hidden_far)
    (out_far,) = run(
        ffn_out_far, [row_b], [hidden_far, ffn_out, ffn_out_near], name="ffn_out_far"
    )
    bits = list(range(groups.bit_length() - 1))
    pack_bits = bits[: packs.bit_length() - 1]
    event_bits = bits[len(pack_bits) :]
    size = width // groups
    total = [pltpu.VMEM((width, cols), F32)]

    def halves(remaining):
        shape = (2 ** (len(remaining) - 1), size, cols)
        return [like(shape, F32), like(shape, BF16)]

    def reduce_over(stages, kept, send, name, beside):
        remaining = list(bits)
        got = crossed(send, 1 << stages[0])
        if beside == stages[0]:
            got, arrays[-1] = tie(got, arrays[-1])
        remaining.remove(stages[0])
        for bit in stages[1:]:
            kept, send = run(
                functools.partial(halve_again, tuple(remaining), bit),
                halves(remaining),
                [kept, got],
                name=name + str(bit),
            )
            got = crossed(send, 1 << bit)
            remaining.remove(bit)
            if bit == beside:
                got, arrays[-1] = tie(got, arrays[-1])
        return kept, got

    kept1, send1, kept0, send0 = run(
        functools.partial(enc_grads_second, tuple(bits), event_bits[0]),
        halves(bits) * 2,
        [cot_far, *cot_both, mine_far, mine_both, act_b, pre_b, enc_weight, part1, part0],
        total * 2,
        name="enc_grads_second",
    )
    arrays = [kept, back_got]
    held = {}
    for n, value in enumerate((0, back_bits[0])):
        chosen = [k for k in range(groups) if k & back_bits[0] == value]
        held.update({k: (n, at) for at, k in enumerate(chosen)})

    def send_back(bit):
        moved = [k for k in range(groups) if k & bit]
        (back,) = run(
            functools.partial(back_pick, [held[k] for k in moved], capacity),
            [half_rows],
            arrays,
            name="back_pick",
        )
        held.update({k: (len(arrays), n) for n, k in enumerate(moved)})
        arrays.append(crossed(back, bit))

    for bit in back_bits[1:-1]:
        send_back(bit)
    kept1, got1 = reduce_over(event_bits + pack_bits, kept1, send1, "halve1_", None)
    kept0, got0 = reduce_over(event_bits + pack_bits, kept0, send0, "halve0_", event_bits[0])
    send_back(back_bits[-1])
    got1, place = tie(got1, place)
    back_places = [held[k] for k in range(groups)]
    got_out = far(out_far)
    (packed_out,) = run(
        ffn_out_own, [row_b], [hidden_own, ffn_out, ffn_out_near, resid, got_out], name="ffn_out_own"
    )
    (row_grad,) = run(
        functools.partial(back_recv, back_places, capacity),
        [row_b],
        [place, *arrays],
        name="back_recv",
    )
    got1, got0, packed_out, row_grad = tie(got1, got0, packed_out, row_grad)
    (enc_grad,) = run(finish, [like((2, size, cols), F32)], [kept1, got1, kept0, got0], name="finish")
    return (packed_out[None], row_grad, enc_grad)


def solution(mesh):
    placed = (
        P(("event", "pack", "tensor"), None),
        P(("event", "pack", "tensor")),
        P(("event", "pack", "tensor")),
        P(("event", "pack"), None),
        P(),
        P(None, None, "tensor"),
        P("tensor", None),
        P(None, None, "tensor"),
        P("tensor", None),
        P(("event", "pack"), "tensor", None),
    )
    return jax.shard_map(
        shards,
        mesh=mesh,
        in_specs=placed,
        out_specs=(
            P(("event", "pack"), "tensor", None),
            P(("event", "pack", "tensor"), None),
            P(None, ("event", "pack"), "tensor"),
        ),
        check_vma=False,
    )
```

```python
import functools

import jax
import jax.numpy as jnp
from jax import lax
from jax.experimental import pallas as pl
from jax.experimental.pallas import tpu as pltpu
from jax.sharding import PartitionSpec as P

D = 1024
HEADS = 16
HEAD = D // HEADS
EPS = 1e-06
F32 = jnp.float32
BF16 = jnp.bfloat16
MIB = 1 << 20
CHUNK = 256


def dot(left, right, dims=((1,), (0,))):
    return lax.dot_general(left, right, (dims, ((), ())), preferred_element_type=F32)


NT = ((1,), (1,))
TN = ((0,), (0,))


def bf16(value):
    return value.astype(BF16)


def silu_grad(value, sigma):
    return sigma * (1.0 + value * (1.0 - sigma))


def norm_factor(wide):
    return lax.rsqrt(jnp.mean(wide * wide, axis=-1, keepdims=True) + EPS)


def norm_back(grad, normed, factor):
    return factor * (grad - normed * jnp.mean(grad * normed, axis=-1, keepdims=True))


def joined(refs):
    return jnp.concatenate([r[...] for r in refs], axis=0)


def store_halves(value, out, halves):
    out[...] = value
    rows = value.shape[0] // max(len(halves), 1)
    for n, target in enumerate(halves):
        target[...] = value[n * rows : (n + 1) * rows]


def turned(row, rows):
    return jnp.broadcast_to(row.astype(F32), (rows, rows)).T


def like(shape, dtype):
    return jax.ShapeDtypeStruct(shape, dtype)


def run(body, outs, args, scratch=(), flops=0, name=None, aliases=None):
    return pl.pallas_call(
        body,
        out_shape=list(outs),
        in_specs=[pl.BlockSpec(memory_space=pltpu.VMEM)] * len(args),
        out_specs=[pl.BlockSpec(memory_space=pltpu.VMEM)] * len(outs),
        scratch_shapes=list(scratch),
        input_output_aliases=aliases or {},
        compiler_params=pltpu.CompilerParams(vmem_limit_bytes=16 * MIB),
        cost_estimate=pl.CostEstimate(flops=flops, bytes_accessed=0, transcendentals=0),
        name=name,
    )(*args)


def group_index():
    return lax.axis_index("event") * lax.axis_size("pack") + lax.axis_index("pack")


def tensor_index():
    return lax.axis_index("tensor")


def tie(*values):
    return lax.optimization_barrier(values)


def route_send(capacity, order, code, features, *outs):
    sends, place_ref = outs[:-1], outs[-1]
    groups = len(sends)
    rows, width = features.shape
    shift = rows.bit_length() - 1
    o_row = code[...] >> shift
    slot = code[...] & (rows - 1)
    o_col = turned(o_row, rows)
    i = lax.broadcasted_iota(jnp.int32, (rows, rows), 0)
    j = lax.broadcasted_iota(jnp.int32, (rows, rows), 1)
    earlier = jnp.where((o_col == o_row.astype(F32)) & (i < j), 1.0, 0.0)
    rank = jnp.sum(earlier, axis=0, keepdims=True).astype(jnp.int32)
    place = (o_row ^ group_index()) * capacity + rank
    place_ref[...] = place
    spots = lax.broadcasted_iota(jnp.int32, (groups * capacity, rows), 0)
    hot = jnp.where(spots == place, 1.0, 0.0).astype(BF16)
    big = dot(hot, features[...])
    tags = dot(hot, bf16(turned(slot + 1, rows)))
    for k, send in zip(order, sends):
        part = slice(k * capacity, (k + 1) * capacity)
        send[:, :width] = bf16(big[part])
        send[:, width:] = bf16(tags[part])


def route_recv(*refs):
    gots, (rows_ref, hot_ref, *halves) = refs[:-4], refs[-4:]
    rows, width = rows_ref.shape
    got = jnp.concatenate([g[...].astype(F32) for g in gots], axis=0)
    lanes = lax.broadcasted_iota(jnp.int32, (got.shape[0], rows), 1) + 1
    hot = jnp.where(got[:, width:] == lanes.astype(F32), 1.0, 0.0).astype(BF16)
    hot_ref[...] = hot
    store_halves(bf16(dot(hot, bf16(got[:, :width]), TN)), rows_ref, halves)


def back_send(order, bit, hot, d_packed, keep, send):
    groups = len(order)
    capacity = hot.shape[0] // groups
    big = dot(hot[...], d_packed[...])
    at = {k: n * capacity for n, k in enumerate(order)}
    for target, value in ((keep, 0), (send, bit)):
        chosen = [k for k in range(groups) if k & bit == value]
        parts = [big[at[k] : at[k] + capacity] for k in chosen]
        target[...] = bf16(jnp.concatenate(parts, axis=0))


def picked(places, capacity, refs):
    wide = [r[...].astype(F32) for r in refs]
    parts = [wide[n][p * capacity : (p + 1) * capacity] for n, p in places]
    return bf16(jnp.concatenate(parts, axis=0))


def back_pick(places, capacity, *refs):
    refs[-1][...] = picked(places, capacity, refs[:-1])


def back_recv(places, capacity, place, *refs):
    got, out = picked(places, capacity, refs[:-1]), refs[-1]
    spots = lax.broadcasted_iota(jnp.int32, (got.shape[0], out.shape[0]), 0)
    hot = jnp.where(spots == place[...], 1.0, 0.0).astype(BF16)
    out[...] = bf16(dot(hot, got, TN))


def encode(rows, enc, w_in, pre_all, pre_ref, act_ref, store):
    width = rows.shape[1]
    cols = pre_ref.shape[1]
    for n in range(width // CHUNK):
        part = slice(n * CHUNK, (n + 1) * CHUNK)
        pre = dot(rows, enc[0, :, part])
        pre_all[:, part] = pre
        act_ref[:, part] = bf16(pre * jax.nn.sigmoid(pre))
    pre_ref[...] = pre_all[:, pl.ds(pl.multiple_of(tensor_index() * cols, cols), cols)]
    packed = bf16(dot(act_ref[...], enc[1]))
    wide = packed.astype(F32)
    normed = bf16(wide * norm_factor(wide))
    for c in range(w_in.shape[0]):
        store(c, bf16(dot(normed, w_in[c])))
    return packed


def encode_blocks(*refs):
    blocks, (enc, w_in, pre_ref, act_ref, packed_ref, proj_ref, pre_all) = refs[:-7], refs[-7:]
    rows = joined(blocks)
    count, size = proj_ref.shape[1:3]

    def store(c, value):
        for n in range(count):
            proj_ref[c, n] = value[n * size : (n + 1) * size]

    packed = encode(rows, enc, w_in, pre_all, pre_ref, act_ref, store)
    packed_ref[...] = packed[:size]


def turn(attn_in, attn_out, in_ref, out_ref):
    for c in range(attn_in.shape[0]):
        in_ref[c] = attn_in[c].T
    out_ref[...] = attn_out[...].T


def window(docs, r, rows):
    t = tensor_index()
    b = t ^ r
    ahead = jnp.where(b > 0, (b - 1) ^ t, r)
    doc_q = turned(docs[b], rows)
    doc_own = docs[b].astype(F32)
    doc_ahead = docs[jnp.maximum(b - 1, 0)].astype(F32)
    i = lax.broadcasted_iota(jnp.int32, (rows, rows), 0)
    j = lax.broadcasted_iota(jnp.int32, (rows, rows), 1)
    own = jnp.where((doc_q == doc_own) & (j <= i), 1.0, 0.0)
    prior = jnp.where(doc_q == doc_ahead, 1.0, 0.0) * jnp.where(b > 0, 1.0, 0.0)
    allowed = jnp.concatenate([prior, own], axis=1)
    root_inv = lax.rsqrt(jnp.sum(allowed, axis=1, keepdims=True))
    return ahead, allowed, root_inv


def head_masks(cols):
    lane = lax.broadcasted_iota(jnp.int32, (1, cols), 1) // HEAD
    return [jnp.where(lane == h, 1.0, 0.0) for h in range(cols // HEAD)]


def spread(value, masks):
    return jnp.concatenate([value * bf16(m) for m in masks], axis=0)


def collect(value, masks):
    rows = value.shape[0] // len(masks)
    total = None
    for h, m in enumerate(masks):
        part = value[h * rows : (h + 1) * rows] * m
        total = part if total is None else total + part
    return total


def attend_first(
    docs, fourth, pre_c, act_c, proj_a, proj_c, enc, w_in,
    pre_ref, act_ref, proj_ref, att_ref, give_ref, pre_all,
):
    half = fourth.shape[0]
    cols = proj_a.shape[-1]
    proj_ref[:, 0:2] = proj_a[...]
    proj_ref[:, 2:3] = proj_c[...]
    pre_ref[:half, :] = pre_c[...]
    act_ref[:half, :] = act_c[...]

    def store(c, value):
        proj_ref[c, 3] = value

    encode(
        fourth[...], enc, w_in, pre_all, pre_ref.at[half : 2 * half], act_ref.at[half : 2 * half], store
    )
    attend((1, 3), docs, proj_ref, att_ref, give_ref)


def attend_second(docs, proj_ref, _att, att_ref, keep_ref):
    attend((0, 2), docs, proj_ref, att_ref, keep_ref)


def attend(blocks, docs, proj_ref, att_ref, target):
    half, cols = proj_ref.shape[2:]
    masks = head_masks(cols)
    for place, r in enumerate(blocks[::-1]):
        ahead, allowed, root_inv = window(docs, r, half)
        keys = jnp.concatenate([proj_ref[1, ahead], proj_ref[1, r]], axis=0)
        values = jnp.concatenate([proj_ref[2, ahead], proj_ref[2, r]], axis=0)
        many = jnp.concatenate([allowed] * len(masks), axis=0)
        scores = dot(spread(proj_ref[0, r], masks), keys, NT) * HEAD ** (-0.5)
        weights = bf16(scores * jax.nn.sigmoid(scores) * many)
        attended = collect(dot(weights, values), masks) * root_inv
        gate = proj_ref[3, r].astype(F32)
        att_ref[r] = attended
        target[place * half : (place + 1) * half, :] = bf16(attended * gate * jax.nn.sigmoid(gate))


def attn_out_part(index, keep, take, w_own, w_near, out):
    rows = out.shape[0]
    part = slice(index * rows, (index + 1) * rows)
    out[...] = bf16(dot(keep[part, :], w_own[...]) + dot(take[part, :], w_near[...]))


def residual(packed, part, got, resid_ref, normed_ref):
    resid = bf16(packed[...].astype(F32) + (part[...].astype(F32) + got[...].astype(F32)))
    resid_ref[...] = resid
    wide = resid.astype(F32)
    normed_ref[...] = bf16(wide * norm_factor(wide))


def ffn(rows_ref, d_out_ref, in_a, in_b, out_a, out_b, hidden_ref, back_ref):
    rows = rows_ref[...]
    cotangent = d_out_ref[...]
    units = out_a.shape[0]
    back = None
    for index, (w_in, w_out) in enumerate(((in_a, out_a), (in_b, out_b))):
        for n in range(units // CHUNK):
            part = slice(n * CHUNK, (n + 1) * CHUNK)
            d_hidden = dot(cotangent, w_out[part, :], NT)
            gate = dot(rows, w_in[0, :, part])
            upper = dot(rows, w_in[1, :, part])
            sigma = jax.nn.sigmoid(gate)
            silu = gate * sigma
            hidden_ref[:, index * units + n * CHUNK : index * units + (n + 1) * CHUNK] = bf16(silu * upper)
            d_gate = bf16(d_hidden * upper * silu_grad(gate, sigma))
            d_upper = bf16(d_hidden * silu)
            term = dot(d_gate, w_in[0, :, part], NT) + dot(d_upper, w_in[1, :, part], NT)
            back = term if back is None else back + term
    back_ref[...] = back.astype(back_ref.dtype)


def ffn_out_far(hidden, w_a, w_b, out):
    units = w_a.shape[0]
    out[...] = bf16(dot(hidden[:, :units], w_a[...]) + dot(hidden[:, units:], w_b[...]))


def ffn_out_own(hidden, w_a, w_b, resid, got, out):
    units = w_a.shape[0]
    total = dot(hidden[:, :units], w_a[...]) + dot(hidden[:, units:], w_b[...])
    out[...] = bf16(resid[...].astype(F32) + total + got[...].astype(F32))


def resid_back(back, got, resid, d_out, out, *halves):
    wide = resid[...].astype(F32)
    factor = norm_factor(wide)
    grad = back[...].astype(F32) + got[...].astype(F32)
    store_halves(bf16(d_out[...].astype(F32) + norm_back(grad, wide * factor, factor)), out, halves)


def attend_back(docs, d_resid, r, proj_ref, att_ref, w_out, masks, d_q, d_k, d_v, d_g):
    half = d_resid.shape[0]
    scale = HEAD ** (-0.5)
    ahead, allowed, root_inv = window(docs, r, half)
    gate = proj_ref[3, r].astype(F32)
    sigma_g = jax.nn.sigmoid(gate)
    d_gated = dot(d_resid, w_out)
    d_att = bf16(d_gated * (gate * sigma_g) * root_inv)
    d_g[r] = bf16(d_gated * att_ref[r] * silu_grad(gate, sigma_g))
    keys = jnp.concatenate([proj_ref[1, ahead], proj_ref[1, r]], axis=0)
    values = jnp.concatenate([proj_ref[2, ahead], proj_ref[2, r]], axis=0)
    many = jnp.concatenate([allowed] * len(masks), axis=0)
    query = spread(proj_ref[0, r], masks)
    d_att_m = spread(d_att, masks)
    scores = dot(query, keys, NT) * scale
    sigma = jax.nn.sigmoid(scores)
    weights = bf16(scores * sigma * many)
    d_weights = dot(d_att_m, values, NT)
    d_scores = bf16(d_weights * silu_grad(scores, sigma) * many)
    d_q[r] = bf16(collect(dot(d_scores, keys), masks) * scale)
    d_keys = dot(d_scores, query, TN) * scale
    d_values = dot(weights, d_att_m, TN)
    d_k[ahead] += d_keys[:half]
    d_k[r] += d_keys[half:]
    d_v[ahead] += d_values[:half]
    d_v[r] += d_values[half:]


def attn_back_first(docs, third, fourth_a, fourth_b, proj, att, w_out, d_q, d_k, d_v, d_g):
    masks = head_masks(w_out.shape[1])
    d_k[...] = jnp.zeros_like(d_k)
    d_v[...] = jnp.zeros_like(d_v)
    for r, rows in ((2, [third]), (3, [fourth_a, fourth_b])):
        attend_back(docs, joined(rows), r, proj, att, w_out[...], masks, d_q, d_k, d_v, d_g)


def attn_back_own(
    docs, first, proj, att, w_out, _q, _k, _v, _g, w_in, give_ref, d_q, d_k, d_v, d_g
):
    masks = head_masks(w_out.shape[1])
    attend_back(docs, first[...], 0, proj, att, w_out[...], masks, d_q, d_k, d_v, d_g)
    give_ref[...] = bf16(back_norm((d_q, d_k, d_v, d_g), w_in, 3))


def attn_back_second(
    docs, second, proj, att, w_out, _q, _k, _v, _g, d_q, d_k, d_v, d_g
):
    masks = head_masks(w_out.shape[1])
    attend_back(docs, second[...], 1, proj, att, w_out[...], masks, d_q, d_k, d_v, d_g)


def back_norm(grads, w_in, block):
    total = None
    for c, grad in enumerate(grads):
        term = dot(bf16(grad[block]), w_in[c])
        total = term if total is None else total + term
    return total


def back_give(block, d_q, d_k, d_v, d_g, w_in, *outs):
    value = bf16(back_norm((d_q, d_k, d_v, d_g), w_in, block))
    rows = value.shape[0] // len(outs)
    for n, out in enumerate(outs):
        out[...] = value[n * rows : (n + 1) * rows]


def back_sum(block, d_q, d_k, d_v, d_g, w_in, *refs):
    takes, out = refs[:-1], refs[-1]
    out[...] = bf16(back_norm((d_q, d_k, d_v, d_g), w_in, block) + joined(takes).astype(F32))


def packed_back(part, got, packed, d_resid, out, *halves):
    wide = packed[...].astype(F32)
    factor = norm_factor(wide)
    grad = part[...].astype(F32) + got[...].astype(F32)
    store_halves(bf16(d_resid[...].astype(F32) + norm_back(grad, wide * factor, factor)), out, halves)


def column_of(ref, index, cols):
    return ref[:, pl.ds(pl.multiple_of(index * cols, cols), cols)]


def rows_term(act_refs, cot):
    return dot(jnp.concatenate([a[...] for a in act_refs], axis=0), cot, TN)


def first_cot(cots, pre, enc):
    cols = pre.shape[1]
    cot = joined(cots)
    value = pre[...]
    w1_rows = enc[1, pl.ds(pl.multiple_of(tensor_index() * cols, cols), cols), :]
    return bf16(dot(cot, w1_rows, NT) * silu_grad(value, jax.nn.sigmoid(value)))


def cot_columns(cots, cols):
    return jnp.concatenate([column_of(c, tensor_index(), cols) for c in cots], axis=0)


def enc_grads_first(*refs):
    rows, (act1, pre, enc, part1, part0) = refs[:-5], refs[-5:]
    cots, act0 = rows[: len(rows) // 2], rows[len(rows) // 2 :]
    cols = pre.shape[1]
    part1[...] = rows_term([act1], cot_columns(cots, cols))
    part0[...] = rows_term(act0, first_cot(cots, pre, enc))


def halve(bits, bit, total, keep, send):
    place = bits.index(bit)
    count, size, _ = keep.shape
    mine = (group_index() >> bit) & 1
    for j in range(count):
        low = j & ((1 << place) - 1)
        base = ((j >> place) << (place + 1)) | low
        for target, value in ((keep, mine), (send, 1 - mine)):
            index = base + (value << place)
            rows = total[pl.ds(pl.multiple_of(index * size, size), size), :]
            target[j] = rows.astype(target.dtype)


def enc_grads_second(bits, bit, *refs):
    rows, refs = refs[:-11], refs[-11:]
    act1, pre, enc, part1, part0, keep1, send1, keep0, send0 = refs[:9]
    total1, total0 = refs[9:]
    cots, act0 = rows[:-2], rows[-2:]
    total1[...] = rows_term([act1], cot_columns(cots, part1.shape[1])) + part1[...]
    halve(bits, bit, total1, keep1, send1)
    total0[...] = rows_term(act0, first_cot(cots, pre, enc)) + part0[...]
    halve(bits, bit, total0, keep0, send0)


def halve_again(bits, bit, kept, got, keep, send):
    place = bits.index(bit)
    mine = (group_index() >> bit) & 1
    for j in range(keep.shape[0]):
        low = j & ((1 << place) - 1)
        base = ((j >> place) << (place + 1)) | low
        for target, value in ((keep, mine), (send, 1 - mine)):
            index = base + (value << place)
            target[j] = (kept[index] + got[index].astype(F32)).astype(target.dtype)


def finish(kept1, got1, kept0, got0, out):
    out[0] = kept0[0] + got0[0].astype(F32)
    out[1] = kept1[0] + got1[0].astype(F32)


def shards(
    features,
    dest_owner,
    dest_slot,
    doc_ids,
    enc_weight,
    attn_in,
    attn_out,
    ffn_in,
    ffn_out,
    out_grad,
):
    rows_dev, width = features.shape
    group_axes = ("event", "pack")
    groups = lax.axis_size(group_axes)
    packs = lax.axis_size("pack")
    tensors = lax.axis_size("tensor")
    cols = attn_in.shape[2]
    comps = attn_in.shape[0]
    units = ffn_out.shape[0]
    d_out = out_grad[0]
    docs = doc_ids.reshape(tensors, 1, rows_dev)

    def near(value):
        return lax.ppermute(value, "tensor", [(i, i ^ 1) for i in range(tensors)])

    def far(value):
        return lax.ppermute(value, "tensor", [(i, i ^ 2) for i in range(tensors)])

    def crossed(value, k):
        return lax.ppermute(value, group_axes, [(i, i ^ k) for i in range(groups)])

    row_b = like((rows_dev, width), BF16)
    row_f = like((rows_dev, width), F32)

    mean_load = rows_dev // groups
    capacity = -(-(mean_load + mean_load // 2) // 8) * 8
    code = (dest_owner * rows_dev + dest_slot).reshape(1, rows_dev)
    offsets = range(1, groups)
    across = sorted((k for k in offsets if 2 * (k % packs) >= packs), key=lambda k: (k % packs, k))
    short = [k for k in offsets if k not in across]
    hops = [k for k in short if k & (k - 1)]
    order = [0] + across[:2] + hops + across[2:] + [k for k in short if k not in hops]
    *sends, place = run(
        functools.partial(route_send, capacity, order),
        [like((capacity, width + rows_dev), BF16)] * groups + [like((1, rows_dev), jnp.int32)],
        [code, features],
        flops=4 * 10**9,
        name="route_send",
    )
    ffn_in_near, ffn_out_near = near(ffn_in), near(ffn_out)
    early = [crossed(sends[n], order[n]) for n in (1, 2)]
    ffn_in_near, ffn_out_near, *sends = tie(ffn_in_near, ffn_out_near, *sends)
    gots = [sends[0], *early] + [crossed(sends[n], order[n]) for n in range(3, groups)]
    pieces = 2
    piece_b = like((rows_dev // pieces, width), BF16)
    in_turned, out_turned = run(
        turn,
        [like((comps, cols, width), BF16), like((width, cols), BF16)],
        [attn_in, attn_out],
        name="turn",
    )
    in_turned, *gots = tie(in_turned, *gots)
    mine, hot, *halves = run(
        route_recv,
        [row_b, like((groups * capacity, rows_dev), BF16)] + [piece_b] * pieces,
        gots,
        name="route_recv",
    )

    mine_far = far(mine)
    mine_near = [near(h) for h in halves]

    pair = 2 * rows_dev
    pre_a, act_a, packed, proj_a = run(
        encode_blocks,
        [
            like((pair, cols), F32),
            like((pair, width), BF16),
            row_b,
            like((comps, 2, rows_dev, cols), BF16),
        ],
        [mine, *mine_near, enc_weight, attn_in],
        [pltpu.VMEM((pair, width), F32)],
        name="encode_first",
    )
    mine_far, proj_a = tie(mine_far, proj_a)
    mine_far, attn_out_late, d_out_late = tie(mine_far, attn_out, d_out)
    mine_both = near(mine_far)
    attn_out_near = near(attn_out_late)
    d_out_far = far(d_out_late)
    pre_c, act_c, packed_far, proj_c = run(
        encode_blocks,
        [like((rows_dev, cols), F32), row_b, row_b, like((comps, 1, rows_dev, cols), BF16)],
        [mine_far, enc_weight, attn_in],
        [pltpu.VMEM((rows_dev, width), F32)],
        name="encode_third",
    )
    pre_b, act_b, proj, attended, give = run(
        attend_first,
        [
            like((pair, cols), F32),
            like((pair, width), BF16),
            like((comps, tensors, rows_dev, cols), BF16),
            like((tensors, rows_dev, cols), F32),
            like((pair, cols), BF16),
        ],
        [docs, mine_both, pre_c, act_c, proj_a, proj_c, enc_weight, attn_in],
        [pltpu.VMEM((rows_dev, width), F32)],
        name="attend_first",
    )
    take = near(give)
    attended, keep = run(
        attend_second,
        [like((tensors, rows_dev, cols), F32), like((pair, cols), BF16)],
        [docs, proj, attended],
        name="attend_second",
        aliases={2: 0},
    )


    def out_part(index, name):
        return run(
            functools.partial(attn_out_part, index),
            [row_b],
            [keep, take, attn_out, attn_out_near],
            name=name,
        )[0]

    part_far = out_part(0, "attn_out_far")
    got_own = far(part_far)
    part_own = out_part(1, "attn_out_own")
    part_own, d_out_far = tie(part_own, d_out_far)
    got_far = far(part_own)

    def feed(rows, cotangent, name):
        return run(
            ffn,
            [like((rows_dev, 2 * units), BF16), row_b],
            [rows, cotangent, ffn_in, ffn_in_near, ffn_out, ffn_out_near],
            name=name,
        )

    resid, normed2 = run(residual, [row_b, row_b], [packed, part_own, got_own], name="residual")
    hidden_own, back_own = feed(normed2, d_out, "ffn_own")
    got_far, back_own = tie(got_far, back_own)
    got_back_far = far(back_own)
    resid_far, normed2_far = run(
        residual, [row_b, row_b], [packed_far, part_far, got_far], name="residual_far"
    )
    hidden_far, back_far = feed(normed2_far, d_out_far, "ffn_far")
    got_back_own = far(back_far)

    d_resid_far, *halves = run(
        resid_back,
        [row_b] + [piece_b] * pieces,
        [back_far, got_back_far, resid_far, d_out_far],
        name="resid_back_far",
    )
    d_resid_both = [near(h) for h in halves]
    block_f = like((tensors, rows_dev, cols), F32)
    block_b = like((tensors, rows_dev, cols), BF16)
    d_q, d_k, d_v, d_g = run(
        attn_back_first,
        [block_b, block_f, block_f, block_b],
        [docs, d_resid_far, *d_resid_both, proj, attended, out_turned],
        name="attn_back_first",
    )
    got_back_own, d_q = tie(got_back_own, d_q)
    (d_resid,) = run(resid_back, [row_b], [back_own, got_back_own, resid, d_out], name="resid_back")
    d_resid_near = near(d_resid)
    give, *own_grads = run(
        attn_back_own,
        [row_b, block_b, block_f, block_f, block_b],
        [docs, d_resid, proj, attended, out_turned, d_q, d_k, d_v, d_g, in_turned],
        aliases={5: 1, 6: 2, 7: 3, 8: 4},
        name="attn_back_own",
    )
    take = near(give)
    d_projected = run(
        attn_back_second,
        [block_b, block_f, block_f, block_b],
        [docs, d_resid_near, proj, attended, out_turned, *own_grads],
        aliases={5: 0, 6: 1, 7: 2, 8: 3},
        name="attn_back_second",
    )

    def back_part(body, block, outs, more, name):
        return run(functools.partial(body, block), outs, [*d_projected, in_turned, *more], name=name)

    (sum_far,) = back_part(back_sum, 2, [row_b], [take], "back_sum_far")
    sum_far, *d_projected = tie(sum_far, *d_projected)
    takes = [near(h) for h in back_part(back_give, 1, [piece_b] * pieces, [], "back_give")]
    (sum_own,) = back_part(back_sum, 0, [row_b], takes, "back_sum_own")
    got_own = far(sum_far)
    got_far = far(sum_own)
    d_packed, *halves = run(
        packed_back,
        [row_b] + [piece_b] * pieces,
        [sum_own, got_own, packed, d_resid],
        name="packed_back",
    )

    cot_near = [near(h) for h in halves]
    half_rows = like((groups * capacity // 2, width), BF16)
    group_bits = [1 << b for b in range(groups.bit_length() - 1)]
    near_bit, pack_far, event_far = group_bits[0], group_bits[1 : packs.bit_length() - 1], group_bits[packs.bit_length() - 1 :]
    back_bits = pack_far[::-1] + [near_bit] + event_far[::-1]
    kept, back = run(
        functools.partial(back_send, order, back_bits[0]), [half_rows] * 2, [hot, d_packed], name="back_send"
    )
    back_got = crossed(back, back_bits[0])

    part_f = like((width, cols), F32)
    part1, part0 = run(
        enc_grads_first,
        [part_f, part_f],
        [d_packed, *cot_near, mine, *mine_near, act_a, pre_a, enc_weight],
        name="enc_grads_first",
    )
    got_far, part1, part0 = tie(got_far, part1, part0)
    cot_far, *cot_pieces = run(
        packed_back,
        [row_b] + [like((rows_dev // 4, width), BF16)] * 4,
        [sum_far, got_far, packed_far, d_resid_far],
        name="packed_back_far",
    )
    cot_both = [near(piece) for piece in cot_pieces]
    cot_far, hidden_far = tie(cot_far, hidden_far)
    (out_far,) = run(
        ffn_out_far, [row_b], [hidden_far, ffn_out, ffn_out_near], name="ffn_out_far"
    )
    bits = list(range(groups.bit_length() - 1))
    pack_bits = bits[: packs.bit_length() - 1]
    event_bits = bits[len(pack_bits) :]
    size = width // groups
    total = [pltpu.VMEM((width, cols), F32)]

    def halves(remaining):
        shape = (2 ** (len(remaining) - 1), size, cols)
        return [like(shape, F32), like(shape, BF16)]

    def reduce_over(stages, kept, send, name, beside):
        remaining = list(bits)
        got = crossed(send, 1 << stages[0])
        if beside == stages[0]:
            got, arrays[-1] = tie(got, arrays[-1])
        remaining.remove(stages[0])
        for bit in stages[1:]:
            kept, send = run(
                functools.partial(halve_again, tuple(remaining), bit),
                halves(remaining),
                [kept, got],
                name=name + str(bit),
            )
            got = crossed(send, 1 << bit)
            remaining.remove(bit)
            if bit == beside:
                got, arrays[-1] = tie(got, arrays[-1])
        return kept, got

    kept1, send1, kept0, send0 = run(
        functools.partial(enc_grads_second, tuple(bits), event_bits[0]),
        halves(bits) * 2,
        [cot_far, *cot_both, mine_far, mine_both, act_b, pre_b, enc_weight, part1, part0],
        total * 2,
        name="enc_grads_second",
    )
    arrays = [kept, back_got]
    held = {}
    for n, value in enumerate((0, back_bits[0])):
        chosen = [k for k in range(groups) if k & back_bits[0] == value]
        held.update({k: (n, at) for at, k in enumerate(chosen)})

    def send_back(bit):
        moved = [k for k in range(groups) if k & bit]
        (back,) = run(
            functools.partial(back_pick, [held[k] for k in moved], capacity),
            [half_rows],
            arrays,
            name="back_pick",
        )
        held.update({k: (len(arrays), n) for n, k in enumerate(moved)})
        arrays.append(crossed(back, bit))

    for bit in back_bits[1:-1]:
        send_back(bit)
    kept1, got1 = reduce_over(event_bits + pack_bits, kept1, send1, "halve1_", None)
    kept0, got0 = reduce_over(event_bits + pack_bits, kept0, send0, "halve0_", event_bits[0])
    send_back(back_bits[-1])
    got1, place = tie(got1, place)
    back_places = [held[k] for k in range(groups)]
    got_out = far(out_far)
    (packed_out,) = run(
        ffn_out_own, [row_b], [hidden_own, ffn_out, ffn_out_near, resid, got_out], name="ffn_out_own"
    )
    (row_grad,) = run(
        functools.partial(back_recv, back_places, capacity),
        [row_b],
        [place, *arrays],
        name="back_recv",
    )
    got1, got0, packed_out, row_grad = tie(got1, got0, packed_out, row_grad)
    (enc_grad,) = run(finish, [like((2, size, cols), F32)], [kept1, got1, kept0, got0], name="finish")
    return (packed_out[None], row_grad, enc_grad)


def solution(mesh):
    placed = (
        P(("event", "pack", "tensor"), None),
        P(("event", "pack", "tensor")),
        P(("event", "pack", "tensor")),
        P(("event", "pack"), None),
        P(),
        P(None, None, "tensor"),
        P("tensor", None),
        P(None, None, "tensor"),
        P("tensor", None),
        P(("event", "pack"), "tensor", None),
    )
    return jax.shard_map(
        shards,
        mesh=mesh,
        in_specs=placed,
        out_specs=(
            P(("event", "pack"), "tensor", None),
            P(("event", "pack", "tensor"), None),
            P(None, ("event", "pack"), "tensor"),
        ),
        check_vma=False,
    )
```

```python
import functools

import jax
import jax.numpy as jnp
from jax import lax
from jax.experimental import pallas as pl
from jax.experimental.pallas import tpu as pltpu
from jax.sharding import PartitionSpec as P

D = 1024
HEADS = 16
HEAD = D // HEADS
EPS = 1e-06
F32 = jnp.float32
BF16 = jnp.bfloat16
MIB = 1 << 20
CHUNK = 256


def dot(left, right, dims=((1,), (0,))):
    return lax.dot_general(left, right, (dims, ((), ())), preferred_element_type=F32)


NT = ((1,), (1,))
TN = ((0,), (0,))


def bf16(value):
    return value.astype(BF16)


def silu_grad(value, sigma):
    return sigma * (1.0 + value * (1.0 - sigma))


def norm_factor(wide):
    return lax.rsqrt(jnp.mean(wide * wide, axis=-1, keepdims=True) + EPS)


def norm_back(grad, normed, factor):
    return factor * (grad - normed * jnp.mean(grad * normed, axis=-1, keepdims=True))


def joined(refs):
    return jnp.concatenate([r[...] for r in refs], axis=0)


def store_halves(value, out, halves):
    out[...] = value
    rows = value.shape[0] // max(len(halves), 1)
    for n, target in enumerate(halves):
        target[...] = value[n * rows : (n + 1) * rows]


def turned(row, rows):
    return jnp.broadcast_to(row.astype(F32), (rows, rows)).T


def like(shape, dtype):
    return jax.ShapeDtypeStruct(shape, dtype)


def run(body, outs, args, scratch=(), flops=0, name=None, aliases=None):
    return pl.pallas_call(
        body,
        out_shape=list(outs),
        in_specs=[pl.BlockSpec(memory_space=pltpu.VMEM)] * len(args),
        out_specs=[pl.BlockSpec(memory_space=pltpu.VMEM)] * len(outs),
        scratch_shapes=list(scratch),
        input_output_aliases=aliases or {},
        compiler_params=pltpu.CompilerParams(vmem_limit_bytes=16 * MIB),
        cost_estimate=pl.CostEstimate(flops=flops, bytes_accessed=0, transcendentals=0),
        name=name,
    )(*args)


def group_index():
    return lax.axis_index("event") * lax.axis_size("pack") + lax.axis_index("pack")


def tensor_index():
    return lax.axis_index("tensor")


def tie(*values):
    return lax.optimization_barrier(values)


def route_send(capacity, order, code, features, *outs):
    sends, place_ref = outs[:-1], outs[-1]
    groups = len(sends)
    rows, width = features.shape
    shift = rows.bit_length() - 1
    o_row = code[...] >> shift
    slot = code[...] & (rows - 1)
    o_col = turned(o_row, rows)
    i = lax.broadcasted_iota(jnp.int32, (rows, rows), 0)
    j = lax.broadcasted_iota(jnp.int32, (rows, rows), 1)
    earlier = jnp.where((o_col == o_row.astype(F32)) & (i < j), 1.0, 0.0)
    rank = jnp.sum(earlier, axis=0, keepdims=True).astype(jnp.int32)
    place = (o_row ^ group_index()) * capacity + rank
    place_ref[...] = place
    spots = lax.broadcasted_iota(jnp.int32, (groups * capacity, rows), 0)
    hot = jnp.where(spots == place, 1.0, 0.0).astype(BF16)
    big = dot(hot, features[...])
    tags = dot(hot, bf16(turned(slot + 1, rows)))
    for k, send in zip(order, sends):
        part = slice(k * capacity, (k + 1) * capacity)
        send[:, :width] = bf16(big[part])
        send[:, width:] = bf16(tags[part])


def route_recv(*refs):
    gots, (rows_ref, hot_ref, *halves) = refs[:-4], refs[-4:]
    rows, width = rows_ref.shape
    got = jnp.concatenate([g[...].astype(F32) for g in gots], axis=0)
    lanes = lax.broadcasted_iota(jnp.int32, (got.shape[0], rows), 1) + 1
    hot = jnp.where(got[:, width:] == lanes.astype(F32), 1.0, 0.0).astype(BF16)
    hot_ref[...] = hot
    store_halves(bf16(dot(hot, bf16(got[:, :width]), TN)), rows_ref, halves)


def back_send(order, bit, hot, d_packed, keep, send):
    groups = len(order)
    capacity = hot.shape[0] // groups
    big = dot(hot[...], d_packed[...])
    at = {k: n * capacity for n, k in enumerate(order)}
    for target, value in ((keep, 0), (send, bit)):
        chosen = [k for k in range(groups) if k & bit == value]
        parts = [big[at[k] : at[k] + capacity] for k in chosen]
        target[...] = bf16(jnp.concatenate(parts, axis=0))


def picked(places, capacity, refs):
    wide = [r[...].astype(F32) for r in refs]
    parts = [wide[n][p * capacity : (p + 1) * capacity] for n, p in places]
    return bf16(jnp.concatenate(parts, axis=0))


def back_pick(places, capacity, *refs):
    refs[-1][...] = picked(places, capacity, refs[:-1])


def back_recv(places, capacity, place, *refs):
    got, out = picked(places, capacity, refs[:-1]), refs[-1]
    spots = lax.broadcasted_iota(jnp.int32, (got.shape[0], out.shape[0]), 0)
    hot = jnp.where(spots == place[...], 1.0, 0.0).astype(BF16)
    out[...] = bf16(dot(hot, got, TN))


def encode(rows, enc, w_in, pre_all, pre_ref, act_ref, store):
    width = rows.shape[1]
    cols = pre_ref.shape[1]
    for n in range(width // CHUNK):
        part = slice(n * CHUNK, (n + 1) * CHUNK)
        pre = dot(rows, enc[0, :, part])
        pre_all[:, part] = pre
        act_ref[:, part] = bf16(pre * jax.nn.sigmoid(pre))
    pre_ref[...] = pre_all[:, pl.ds(pl.multiple_of(tensor_index() * cols, cols), cols)]
    packed = bf16(dot(act_ref[...], enc[1]))
    wide = packed.astype(F32)
    normed = bf16(wide * norm_factor(wide))
    for c in range(w_in.shape[0]):
        store(c, bf16(dot(normed, w_in[c])))
    return packed


def encode_blocks(*refs):
    blocks, (enc, w_in, pre_ref, act_ref, packed_ref, proj_ref, pre_all) = refs[:-7], refs[-7:]
    rows = joined(blocks)
    count, size = proj_ref.shape[1:3]

    def store(c, value):
        for n in range(count):
            proj_ref[c, n] = value[n * size : (n + 1) * size]

    packed = encode(rows, enc, w_in, pre_all, pre_ref, act_ref, store)
    packed_ref[...] = packed[:size]


def turn(attn_in, attn_out, in_ref, out_ref):
    for c in range(attn_in.shape[0]):
        in_ref[c] = attn_in[c].T
    out_ref[...] = attn_out[...].T


def window(docs, r, rows):
    t = tensor_index()
    b = t ^ r
    ahead = jnp.where(b > 0, (b - 1) ^ t, r)
    doc_q = turned(docs[b], rows)
    doc_own = docs[b].astype(F32)
    doc_ahead = docs[jnp.maximum(b - 1, 0)].astype(F32)
    i = lax.broadcasted_iota(jnp.int32, (rows, rows), 0)
    j = lax.broadcasted_iota(jnp.int32, (rows, rows), 1)
    own = jnp.where((doc_q == doc_own) & (j <= i), 1.0, 0.0)
    prior = jnp.where(doc_q == doc_ahead, 1.0, 0.0) * jnp.where(b > 0, 1.0, 0.0)
    allowed = jnp.concatenate([prior, own], axis=1)
    root_inv = lax.rsqrt(jnp.sum(allowed, axis=1, keepdims=True))
    return ahead, allowed, root_inv


def head_masks(cols):
    lane = lax.broadcasted_iota(jnp.int32, (1, cols), 1) // HEAD
    return [jnp.where(lane == h, 1.0, 0.0) for h in range(cols // HEAD)]


def spread(value, masks):
    return jnp.concatenate([value * bf16(m) for m in masks], axis=0)


def collect(value, masks):
    rows = value.shape[0] // len(masks)
    total = None
    for h, m in enumerate(masks):
        part = value[h * rows : (h + 1) * rows] * m
        total = part if total is None else total + part
    return total


def attend_first(
    docs, fourth, pre_c, act_c, proj_a, proj_c, enc, w_in,
    pre_ref, act_ref, proj_ref, att_ref, give_ref, pre_all,
):
    half = fourth.shape[0]
    cols = proj_a.shape[-1]
    proj_ref[:, 0:2] = proj_a[...]
    proj_ref[:, 2:3] = proj_c[...]
    pre_ref[:half, :] = pre_c[...]
    act_ref[:half, :] = act_c[...]

    def store(c, value):
        proj_ref[c, 3] = value

    encode(
        fourth[...], enc, w_in, pre_all, pre_ref.at[half : 2 * half], act_ref.at[half : 2 * half], store
    )
    attend((1, 3), docs, proj_ref, att_ref, give_ref)


def attend_second(docs, proj_ref, _att, att_ref, keep_ref):
    attend((0, 2), docs, proj_ref, att_ref, keep_ref)


def attend(blocks, docs, proj_ref, att_ref, target):
    half, cols = proj_ref.shape[2:]
    masks = head_masks(cols)
    for place, r in enumerate(blocks[::-1]):
        ahead, allowed, root_inv = window(docs, r, half)
        keys = jnp.concatenate([proj_ref[1, ahead], proj_ref[1, r]], axis=0)
        values = jnp.concatenate([proj_ref[2, ahead], proj_ref[2, r]], axis=0)
        many = jnp.concatenate([allowed] * len(masks), axis=0)
        scores = dot(spread(proj_ref[0, r], masks), keys, NT) * HEAD ** (-0.5)
        weights = bf16(scores * jax.nn.sigmoid(scores) * many)
        attended = collect(dot(weights, values), masks) * root_inv
        gate = proj_ref[3, r].astype(F32)
        att_ref[r] = attended
        target[place * half : (place + 1) * half, :] = bf16(attended * gate * jax.nn.sigmoid(gate))


def attn_out_part(index, keep, take, w_own, w_near, out):
    rows = out.shape[0]
    part = slice(index * rows, (index + 1) * rows)
    out[...] = bf16(dot(keep[part, :], w_own[...]) + dot(take[part, :], w_near[...]))


def residual(packed, part, got, resid_ref, normed_ref):
    resid = bf16(packed[...].astype(F32) + (part[...].astype(F32) + got[...].astype(F32)))
    resid_ref[...] = resid
    wide = resid.astype(F32)
    normed_ref[...] = bf16(wide * norm_factor(wide))


def ffn(rows_ref, d_out_ref, in_a, in_b, out_a, out_b, hidden_ref, back_ref):
    rows = rows_ref[...]
    cotangent = d_out_ref[...]
    units = out_a.shape[0]
    back = None
    for index, (w_in, w_out) in enumerate(((in_a, out_a), (in_b, out_b))):
        for n in range(units // CHUNK):
            part = slice(n * CHUNK, (n + 1) * CHUNK)
            d_hidden = dot(cotangent, w_out[part, :], NT)
            gate = dot(rows, w_in[0, :, part])
            upper = dot(rows, w_in[1, :, part])
            sigma = jax.nn.sigmoid(gate)
            silu = gate * sigma
            hidden_ref[:, index * units + n * CHUNK : index * units + (n + 1) * CHUNK] = bf16(silu * upper)
            d_gate = bf16(d_hidden * upper * silu_grad(gate, sigma))
            d_upper = bf16(d_hidden * silu)
            term = dot(d_gate, w_in[0, :, part], NT) + dot(d_upper, w_in[1, :, part], NT)
            back = term if back is None else back + term
    back_ref[...] = back.astype(back_ref.dtype)


def ffn_out_far(hidden, w_a, w_b, out):
    units = w_a.shape[0]
    out[...] = bf16(dot(hidden[:, :units], w_a[...]) + dot(hidden[:, units:], w_b[...]))


def ffn_out_own(hidden, w_a, w_b, resid, got, out):
    units = w_a.shape[0]
    total = dot(hidden[:, :units], w_a[...]) + dot(hidden[:, units:], w_b[...])
    out[...] = bf16(resid[...].astype(F32) + total + got[...].astype(F32))


def resid_back(back, got, resid, d_out, out, *halves):
    wide = resid[...].astype(F32)
    factor = norm_factor(wide)
    grad = back[...].astype(F32) + got[...].astype(F32)
    store_halves(bf16(d_out[...].astype(F32) + norm_back(grad, wide * factor, factor)), out, halves)


def attend_back(docs, d_resid, r, proj_ref, att_ref, w_out, masks, d_q, d_k, d_v, d_g):
    half = d_resid.shape[0]
    scale = HEAD ** (-0.5)
    ahead, allowed, root_inv = window(docs, r, half)
    gate = proj_ref[3, r].astype(F32)
    sigma_g = jax.nn.sigmoid(gate)
    d_gated = dot(d_resid, w_out)
    d_att = bf16(d_gated * (gate * sigma_g) * root_inv)
    d_g[r] = bf16(d_gated * att_ref[r] * silu_grad(gate, sigma_g))
    keys = jnp.concatenate([proj_ref[1, ahead], proj_ref[1, r]], axis=0)
    values = jnp.concatenate([proj_ref[2, ahead], proj_ref[2, r]], axis=0)
    many = jnp.concatenate([allowed] * len(masks), axis=0)
    query = spread(proj_ref[0, r], masks)
    d_att_m = spread(d_att, masks)
    scores = dot(query, keys, NT) * scale
    sigma = jax.nn.sigmoid(scores)
    weights = bf16(scores * sigma * many)
    d_weights = dot(d_att_m, values, NT)
    d_scores = bf16(d_weights * silu_grad(scores, sigma) * many)
    d_q[r] = bf16(collect(dot(d_scores, keys), masks) * scale)
    d_keys = dot(d_scores, query, TN) * scale
    d_values = dot(weights, d_att_m, TN)
    d_k[ahead] += d_keys[:half]
    d_k[r] += d_keys[half:]
    d_v[ahead] += d_values[:half]
    d_v[r] += d_values[half:]


def attn_back_first(docs, third, fourth_a, fourth_b, proj, att, w_out, d_q, d_k, d_v, d_g):
    masks = head_masks(w_out.shape[1])
    d_k[...] = jnp.zeros_like(d_k)
    d_v[...] = jnp.zeros_like(d_v)
    for r, rows in ((2, [third]), (3, [fourth_a, fourth_b])):
        attend_back(docs, joined(rows), r, proj, att, w_out[...], masks, d_q, d_k, d_v, d_g)


def attn_back_own(
    docs, first, proj, att, w_out, _q, _k, _v, _g, w_in, give_ref, d_q, d_k, d_v, d_g
):
    masks = head_masks(w_out.shape[1])
    attend_back(docs, first[...], 0, proj, att, w_out[...], masks, d_q, d_k, d_v, d_g)
    give_ref[...] = bf16(back_norm((d_q, d_k, d_v, d_g), w_in, 3))


def attn_back_second(
    docs, second, proj, att, w_out, _q, _k, _v, _g, d_q, d_k, d_v, d_g
):
    masks = head_masks(w_out.shape[1])
    attend_back(docs, second[...], 1, proj, att, w_out[...], masks, d_q, d_k, d_v, d_g)


def back_norm(grads, w_in, block):
    total = None
    for c, grad in enumerate(grads):
        term = dot(bf16(grad[block]), w_in[c])
        total = term if total is None else total + term
    return total


def back_give(block, d_q, d_k, d_v, d_g, w_in, *outs):
    value = bf16(back_norm((d_q, d_k, d_v, d_g), w_in, block))
    rows = value.shape[0] // len(outs)
    for n, out in enumerate(outs):
        out[...] = value[n * rows : (n + 1) * rows]


def back_sum(block, d_q, d_k, d_v, d_g, w_in, *refs):
    takes, out = refs[:-1], refs[-1]
    out[...] = bf16(back_norm((d_q, d_k, d_v, d_g), w_in, block) + joined(takes).astype(F32))


def packed_back(part, got, packed, d_resid, out, *halves):
    wide = packed[...].astype(F32)
    factor = norm_factor(wide)
    grad = part[...].astype(F32) + got[...].astype(F32)
    store_halves(bf16(d_resid[...].astype(F32) + norm_back(grad, wide * factor, factor)), out, halves)


def column_of(ref, index, cols):
    return ref[:, pl.ds(pl.multiple_of(index * cols, cols), cols)]


def rows_term(act_refs, cot):
    return dot(jnp.concatenate([a[...] for a in act_refs], axis=0), cot, TN)


def first_cot(cots, pre, enc):
    cols = pre.shape[1]
    cot = joined(cots)
    value = pre[...]
    w1_rows = enc[1, pl.ds(pl.multiple_of(tensor_index() * cols, cols), cols), :]
    return bf16(dot(cot, w1_rows, NT) * silu_grad(value, jax.nn.sigmoid(value)))


def cot_columns(cots, cols):
    return jnp.concatenate([column_of(c, tensor_index(), cols) for c in cots], axis=0)


def enc_grads_first(*refs):
    rows, (act1, pre, enc, part1, part0) = refs[:-5], refs[-5:]
    cots, act0 = rows[: len(rows) // 2], rows[len(rows) // 2 :]
    cols = pre.shape[1]
    part1[...] = rows_term([act1], cot_columns(cots, cols))
    part0[...] = rows_term(act0, first_cot(cots, pre, enc))


def halve(bits, bit, total, keep, send):
    place = bits.index(bit)
    count, size, _ = keep.shape
    mine = (group_index() >> bit) & 1
    for j in range(count):
        low = j & ((1 << place) - 1)
        base = ((j >> place) << (place + 1)) | low
        for target, value in ((keep, mine), (send, 1 - mine)):
            index = base + (value << place)
            rows = total[pl.ds(pl.multiple_of(index * size, size), size), :]
            target[j] = rows.astype(target.dtype)


def enc_grads_second(bits, bit1, bit0, *refs):
    rows, refs = refs[:-11], refs[-11:]
    act1, pre, enc, part1, part0, keep1, send1, keep0, send0 = refs[:9]
    total1, total0 = refs[9:]
    cots, act0 = rows[:-2], rows[-2:]
    total1[...] = rows_term([act1], cot_columns(cots, part1.shape[1])) + part1[...]
    halve(bits, bit1, total1, keep1, send1)
    total0[...] = rows_term(act0, first_cot(cots, pre, enc)) + part0[...]
    halve(bits, bit0, total0, keep0, send0)


def halve_again(bits, bit, kept, got, keep, send):
    place = bits.index(bit)
    mine = (group_index() >> bit) & 1
    for j in range(keep.shape[0]):
        low = j & ((1 << place) - 1)
        base = ((j >> place) << (place + 1)) | low
        for target, value in ((keep, mine), (send, 1 - mine)):
            index = base + (value << place)
            target[j] = (kept[index] + got[index].astype(F32)).astype(target.dtype)


def finish(kept1, got1, kept0, got0, out):
    out[0] = kept0[0] + got0[0].astype(F32)
    out[1] = kept1[0] + got1[0].astype(F32)


def shards(
    features,
    dest_owner,
    dest_slot,
    doc_ids,
    enc_weight,
    attn_in,
    attn_out,
    ffn_in,
    ffn_out,
    out_grad,
):
    rows_dev, width = features.shape
    group_axes = ("event", "pack")
    groups = lax.axis_size(group_axes)
    packs = lax.axis_size("pack")
    tensors = lax.axis_size("tensor")
    cols = attn_in.shape[2]
    comps = attn_in.shape[0]
    units = ffn_out.shape[0]
    d_out = out_grad[0]
    docs = doc_ids.reshape(tensors, 1, rows_dev)

    def near(value):
        return lax.ppermute(value, "tensor", [(i, i ^ 1) for i in range(tensors)])

    def far(value):
        return lax.ppermute(value, "tensor", [(i, i ^ 2) for i in range(tensors)])

    def crossed(value, k):
        return lax.ppermute(value, group_axes, [(i, i ^ k) for i in range(groups)])

    row_b = like((rows_dev, width), BF16)
    row_f = like((rows_dev, width), F32)

    mean_load = rows_dev // groups
    capacity = -(-(mean_load + mean_load // 2) // 8) * 8
    code = (dest_owner * rows_dev + dest_slot).reshape(1, rows_dev)
    offsets = range(1, groups)
    across = sorted((k for k in offsets if 2 * (k % packs) >= packs), key=lambda k: (k % packs, k))
    short = [k for k in offsets if k not in across]
    hops = [k for k in short if k & (k - 1)]
    order = [0] + across[:2] + hops + across[2:] + [k for k in short if k not in hops]
    *sends, place = run(
        functools.partial(route_send, capacity, order),
        [like((capacity, width + rows_dev), BF16)] * groups + [like((1, rows_dev), jnp.int32)],
        [code, features],
        flops=4 * 10**9,
        name="route_send",
    )
    ffn_in_near, ffn_out_near = near(ffn_in), near(ffn_out)
    early = [crossed(sends[n], order[n]) for n in (1, 2)]
    ffn_in_near, ffn_out_near, *sends = tie(ffn_in_near, ffn_out_near, *sends)
    gots = [sends[0], *early] + [crossed(sends[n], order[n]) for n in range(3, groups)]
    pieces = 2
    piece_b = like((rows_dev // pieces, width), BF16)
    in_turned, out_turned = run(
        turn,
        [like((comps, cols, width), BF16), like((width, cols), BF16)],
        [attn_in, attn_out],
        name="turn",
    )
    in_turned, *gots = tie(in_turned, *gots)
    mine, hot, *halves = run(
        route_recv,
        [row_b, like((groups * capacity, rows_dev), BF16)] + [piece_b] * pieces,
        gots,
        name="route_recv",
    )

    mine_far = far(mine)
    mine_near = [near(h) for h in halves]

    pair = 2 * rows_dev
    pre_a, act_a, packed, proj_a = run(
        encode_blocks,
        [
            like((pair, cols), F32),
            like((pair, width), BF16),
            row_b,
            like((comps, 2, rows_dev, cols), BF16),
        ],
        [mine, *mine_near, enc_weight, attn_in],
        [pltpu.VMEM((pair, width), F32)],
        name="encode_first",
    )
    mine_far, proj_a = tie(mine_far, proj_a)
    mine_far, attn_out_late, d_out_late = tie(mine_far, attn_out, d_out)
    mine_both = near(mine_far)
    attn_out_near = near(attn_out_late)
    d_out_far = far(d_out_late)
    pre_c, act_c, packed_far, proj_c = run(
        encode_blocks,
        [like((rows_dev, cols), F32), row_b, row_b, like((comps, 1, rows_dev, cols), BF16)],
        [mine_far, enc_weight, attn_in],
        [pltpu.VMEM((rows_dev, width), F32)],
        name="encode_third",
    )
    pre_b, act_b, proj, attended, give = run(
        attend_first,
        [
            like((pair, cols), F32),
            like((pair, width), BF16),
            like((comps, tensors, rows_dev, cols), BF16),
            like((tensors, rows_dev, cols), F32),
            like((pair, cols), BF16),
        ],
        [docs, mine_both, pre_c, act_c, proj_a, proj_c, enc_weight, attn_in],
        [pltpu.VMEM((rows_dev, width), F32)],
        name="attend_first",
    )
    take = near(give)
    attended, keep = run(
        attend_second,
        [like((tensors, rows_dev, cols), F32), like((pair, cols), BF16)],
        [docs, proj, attended],
        name="attend_second",
        aliases={2: 0},
    )


    def out_part(index, name):
        return run(
            functools.partial(attn_out_part, index),
            [row_b],
            [keep, take, attn_out, attn_out_near],
            name=name,
        )[0]

    part_far = out_part(0, "attn_out_far")
    got_own = far(part_far)
    part_own = out_part(1, "attn_out_own")
    part_own, d_out_far = tie(part_own, d_out_far)
    got_far = far(part_own)

    def feed(rows, cotangent, name):
        return run(
            ffn,
            [like((rows_dev, 2 * units), BF16), row_b],
            [rows, cotangent, ffn_in, ffn_in_near, ffn_out, ffn_out_near],
            name=name,
        )

    resid, normed2 = run(residual, [row_b, row_b], [packed, part_own, got_own], name="residual")
    hidden_own, back_own = feed(normed2, d_out, "ffn_own")
    got_far, back_own = tie(got_far, back_own)
    got_back_far = far(back_own)
    resid_far, normed2_far = run(
        residual, [row_b, row_b], [packed_far, part_far, got_far], name="residual_far"
    )
    hidden_far, back_far = feed(normed2_far, d_out_far, "ffn_far")
    got_back_own = far(back_far)

    d_resid_far, *halves = run(
        resid_back,
        [row_b] + [piece_b] * pieces,
        [back_far, got_back_far, resid_far, d_out_far],
        name="resid_back_far",
    )
    d_resid_both = [near(h) for h in halves]
    block_f = like((tensors, rows_dev, cols), F32)
    block_b = like((tensors, rows_dev, cols), BF16)
    d_q, d_k, d_v, d_g = run(
        attn_back_first,
        [block_b, block_f, block_f, block_b],
        [docs, d_resid_far, *d_resid_both, proj, attended, out_turned],
        name="attn_back_first",
    )
    got_back_own, d_q = tie(got_back_own, d_q)
    (d_resid,) = run(resid_back, [row_b], [back_own, got_back_own, resid, d_out], name="resid_back")
    d_resid_near = near(d_resid)
    give, *own_grads = run(
        attn_back_own,
        [row_b, block_b, block_f, block_f, block_b],
        [docs, d_resid, proj, attended, out_turned, d_q, d_k, d_v, d_g, in_turned],
        aliases={5: 1, 6: 2, 7: 3, 8: 4},
        name="attn_back_own",
    )
    take = near(give)
    d_projected = run(
        attn_back_second,
        [block_b, block_f, block_f, block_b],
        [docs, d_resid_near, proj, attended, out_turned, *own_grads],
        aliases={5: 0, 6: 1, 7: 2, 8: 3},
        name="attn_back_second",
    )

    def back_part(body, block, outs, more, name):
        return run(functools.partial(body, block), outs, [*d_projected, in_turned, *more], name=name)

    (sum_far,) = back_part(back_sum, 2, [row_b], [take], "back_sum_far")
    sum_far, *d_projected = tie(sum_far, *d_projected)
    takes = [near(h) for h in back_part(back_give, 1, [piece_b] * pieces, [], "back_give")]
    (sum_own,) = back_part(back_sum, 0, [row_b], takes, "back_sum_own")
    got_own = far(sum_far)
    got_far = far(sum_own)
    d_packed, *halves = run(
        packed_back,
        [row_b] + [piece_b] * pieces,
        [sum_own, got_own, packed, d_resid],
        name="packed_back",
    )

    cot_near = [near(h) for h in halves]
    half_rows = like((groups * capacity // 2, width), BF16)
    group_bits = [1 << b for b in range(groups.bit_length() - 1)]
    near_bit, pack_far, event_far = group_bits[0], group_bits[1 : packs.bit_length() - 1], group_bits[packs.bit_length() - 1 :]
    back_bits = pack_far[::-1] + [near_bit] + event_far[::-1]
    kept, back = run(
        functools.partial(back_send, order, back_bits[0]), [half_rows] * 2, [hot, d_packed], name="back_send"
    )
    back_got = crossed(back, back_bits[0])

    part_f = like((width, cols), F32)
    part1, part0 = run(
        enc_grads_first,
        [part_f, part_f],
        [d_packed, *cot_near, mine, *mine_near, act_a, pre_a, enc_weight],
        name="enc_grads_first",
    )
    got_far, part1, part0 = tie(got_far, part1, part0)
    cot_far, *cot_pieces = run(
        packed_back,
        [row_b] + [like((rows_dev // 4, width), BF16)] * 4,
        [sum_far, got_far, packed_far, d_resid_far],
        name="packed_back_far",
    )
    cot_both = [near(piece) for piece in cot_pieces]
    cot_far, hidden_far = tie(cot_far, hidden_far)
    (out_far,) = run(
        ffn_out_far, [row_b], [hidden_far, ffn_out, ffn_out_near], name="ffn_out_far"
    )
    bits = list(range(groups.bit_length() - 1))
    pack_bits = bits[: packs.bit_length() - 1]
    event_bits = bits[len(pack_bits) :]
    size = width // groups
    total = [pltpu.VMEM((width, cols), F32)]

    def halves(remaining):
        shape = (2 ** (len(remaining) - 1), size, cols)
        return [like(shape, F32), like(shape, BF16)]

    def reduce_over(stages, kept, send, name, beside):
        remaining = list(bits)
        got = crossed(send, 1 << stages[0])
        if beside == stages[0]:
            got, arrays[-1] = tie(got, arrays[-1])
        remaining.remove(stages[0])
        for bit in stages[1:]:
            kept, send = run(
                functools.partial(halve_again, tuple(remaining), bit),
                halves(remaining),
                [kept, got],
                name=name + str(bit),
            )
            got = crossed(send, 1 << bit)
            remaining.remove(bit)
            if bit == beside:
                got, arrays[-1] = tie(got, arrays[-1])
        return kept, got

    kept1, send1, kept0, send0 = run(
        functools.partial(enc_grads_second, tuple(bits), event_bits[0], pack_bits[0]),
        halves(bits) * 2,
        [cot_far, *cot_both, mine_far, mine_both, act_b, pre_b, enc_weight, part1, part0],
        total * 2,
        name="enc_grads_second",
    )
    arrays = [kept, back_got]
    held = {}
    for n, value in enumerate((0, back_bits[0])):
        chosen = [k for k in range(groups) if k & back_bits[0] == value]
        held.update({k: (n, at) for at, k in enumerate(chosen)})

    def send_back(bit):
        moved = [k for k in range(groups) if k & bit]
        (back,) = run(
            functools.partial(back_pick, [held[k] for k in moved], capacity),
            [half_rows],
            arrays,
            name="back_pick",
        )
        held.update({k: (len(arrays), n) for n, k in enumerate(moved)})
        arrays.append(crossed(back, bit))

    for bit in back_bits[1:-1]:
        send_back(bit)
    kept1, got1 = reduce_over(event_bits + pack_bits, kept1, send1, "halve1_", None)
    kept0, got0 = reduce_over(
        pack_bits[:1] + event_bits + pack_bits[1:], kept0, send0, "halve0_", pack_bits[0]
    )
    send_back(back_bits[-1])
    got1, place = tie(got1, place)
    back_places = [held[k] for k in range(groups)]
    got_out = far(out_far)
    (packed_out,) = run(
        ffn_out_own, [row_b], [hidden_own, ffn_out, ffn_out_near, resid, got_out], name="ffn_out_own"
    )
    (row_grad,) = run(
        functools.partial(back_recv, back_places, capacity),
        [row_b],
        [place, *arrays],
        name="back_recv",
    )
    got1, got0, packed_out, row_grad = tie(got1, got0, packed_out, row_grad)
    (enc_grad,) = run(finish, [like((2, size, cols), F32)], [kept1, got1, kept0, got0], name="finish")
    return (packed_out[None], row_grad, enc_grad)


def solution(mesh):
    placed = (
        P(("event", "pack", "tensor"), None),
        P(("event", "pack", "tensor")),
        P(("event", "pack", "tensor")),
        P(("event", "pack"), None),
        P(),
        P(None, None, "tensor"),
        P("tensor", None),
        P(None, None, "tensor"),
        P("tensor", None),
        P(("event", "pack"), "tensor", None),
    )
    return jax.shard_map(
        shards,
        mesh=mesh,
        in_specs=placed,
        out_specs=(
            P(("event", "pack"), "tensor", None),
            P(("event", "pack", "tensor"), None),
            P(None, ("event", "pack"), "tensor"),
        ),
        check_vma=False,
    )
```

```python
import functools

import jax
import jax.numpy as jnp
from jax import lax
from jax.experimental import pallas as pl
from jax.experimental.pallas import tpu as pltpu
from jax.sharding import PartitionSpec as P

D = 1024
HEADS = 16
HEAD = D // HEADS
EPS = 1e-06
F32 = jnp.float32
BF16 = jnp.bfloat16
MIB = 1 << 20
CHUNK = 256


def dot(left, right, dims=((1,), (0,))):
    return lax.dot_general(left, right, (dims, ((), ())), preferred_element_type=F32)


NT = ((1,), (1,))
TN = ((0,), (0,))


def bf16(value):
    return value.astype(BF16)


def silu_grad(value, sigma):
    return sigma * (1.0 + value * (1.0 - sigma))


def norm_factor(wide):
    return lax.rsqrt(jnp.mean(wide * wide, axis=-1, keepdims=True) + EPS)


def norm_back(grad, normed, factor):
    return factor * (grad - normed * jnp.mean(grad * normed, axis=-1, keepdims=True))


def joined(refs):
    return jnp.concatenate([r[...] for r in refs], axis=0)


def store_halves(value, out, halves):
    out[...] = value
    first = 0
    for target in halves:
        target[...] = value[first : first + target.shape[0]]
        first += target.shape[0]


def turned(row, rows):
    return jnp.broadcast_to(row.astype(F32), (rows, rows)).T


def like(shape, dtype):
    return jax.ShapeDtypeStruct(shape, dtype)


def run(body, outs, args, scratch=(), flops=0, name=None, aliases=None):
    return pl.pallas_call(
        body,
        out_shape=list(outs),
        in_specs=[pl.BlockSpec(memory_space=pltpu.VMEM)] * len(args),
        out_specs=[pl.BlockSpec(memory_space=pltpu.VMEM)] * len(outs),
        scratch_shapes=list(scratch),
        input_output_aliases=aliases or {},
        compiler_params=pltpu.CompilerParams(vmem_limit_bytes=16 * MIB),
        cost_estimate=pl.CostEstimate(flops=flops, bytes_accessed=0, transcendentals=0),
        name=name,
    )(*args)


def group_index():
    return lax.axis_index("event") * lax.axis_size("pack") + lax.axis_index("pack")


def tensor_index():
    return lax.axis_index("tensor")


def tie(*values):
    return lax.optimization_barrier(values)


def route_send(capacity, order, code, features, *outs):
    sends, place_ref = outs[:-1], outs[-1]
    groups = len(sends)
    rows, width = features.shape
    shift = rows.bit_length() - 1
    o_row = code[...] >> shift
    slot = code[...] & (rows - 1)
    o_col = turned(o_row, rows)
    i = lax.broadcasted_iota(jnp.int32, (rows, rows), 0)
    j = lax.broadcasted_iota(jnp.int32, (rows, rows), 1)
    earlier = jnp.where((o_col == o_row.astype(F32)) & (i < j), 1.0, 0.0)
    rank = jnp.sum(earlier, axis=0, keepdims=True).astype(jnp.int32)
    place = (o_row ^ group_index()) * capacity + rank
    place_ref[...] = place
    spots = lax.broadcasted_iota(jnp.int32, (groups * capacity, rows), 0)
    hot = jnp.where(spots == place, 1.0, 0.0).astype(BF16)
    big = dot(hot, features[...])
    tags = dot(hot, bf16(turned(slot + 1, rows)))
    for k, send in zip(order, sends):
        part = slice(k * capacity, (k + 1) * capacity)
        send[:, :width] = bf16(big[part])
        send[:, width:] = bf16(tags[part])


def route_recv(*refs):
    gots, (rows_ref, hot_ref, *halves) = refs[:-4], refs[-4:]
    rows, width = rows_ref.shape
    got = jnp.concatenate([g[...].astype(F32) for g in gots], axis=0)
    lanes = lax.broadcasted_iota(jnp.int32, (got.shape[0], rows), 1) + 1
    hot = jnp.where(got[:, width:] == lanes.astype(F32), 1.0, 0.0).astype(BF16)
    hot_ref[...] = hot
    store_halves(bf16(dot(hot, bf16(got[:, :width]), TN)), rows_ref, halves)


def back_send(order, bit, hot, d_packed, keep, send):
    groups = len(order)
    capacity = hot.shape[0] // groups
    big = dot(hot[...], d_packed[...])
    at = {k: n * capacity for n, k in enumerate(order)}
    for target, value in ((keep, 0), (send, bit)):
        chosen = [k for k in range(groups) if k & bit == value]
        parts = [big[at[k] : at[k] + capacity] for k in chosen]
        target[...] = bf16(jnp.concatenate(parts, axis=0))


def picked(places, capacity, refs):
    wide = [r[...].astype(F32) for r in refs]
    parts = [wide[n][p * capacity : (p + 1) * capacity] for n, p in places]
    return bf16(jnp.concatenate(parts, axis=0))


def back_pick(places, capacity, *refs):
    refs[-1][...] = picked(places, capacity, refs[:-1])


def back_recv(places, capacity, place, *refs):
    got, out = picked(places, capacity, refs[:-1]), refs[-1]
    spots = lax.broadcasted_iota(jnp.int32, (got.shape[0], out.shape[0]), 0)
    hot = jnp.where(spots == place[...], 1.0, 0.0).astype(BF16)
    out[...] = bf16(dot(hot, got, TN))


def encode(rows, enc, w_in, pre_all, pre_ref, act_ref, store):
    width = rows.shape[1]
    cols = pre_ref.shape[1]
    for n in range(width // CHUNK):
        part = slice(n * CHUNK, (n + 1) * CHUNK)
        pre = dot(rows, enc[0, :, part])
        pre_all[:, part] = pre
        act_ref[:, part] = bf16(pre * jax.nn.sigmoid(pre))
    pre_ref[...] = pre_all[:, pl.ds(pl.multiple_of(tensor_index() * cols, cols), cols)]
    packed = bf16(dot(act_ref[...], enc[1]))
    wide = packed.astype(F32)
    normed = bf16(wide * norm_factor(wide))
    for c in range(w_in.shape[0]):
        store(c, bf16(dot(normed, w_in[c])))
    return packed


def encode_blocks(*refs):
    blocks, (enc, w_in, pre_ref, act_ref, packed_ref, proj_ref, pre_all) = refs[:-7], refs[-7:]
    rows = joined(blocks)
    count, size = proj_ref.shape[1:3]

    def store(c, value):
        for n in range(count):
            proj_ref[c, n] = value[n * size : (n + 1) * size]

    packed = encode(rows, enc, w_in, pre_all, pre_ref, act_ref, store)
    packed_ref[...] = packed[:size]


def turn(attn_in, attn_out, in_ref, out_ref):
    for c in range(attn_in.shape[0]):
        in_ref[c] = attn_in[c].T
    out_ref[...] = attn_out[...].T


def window(docs, r, rows):
    t = tensor_index()
    b = t ^ r
    ahead = jnp.where(b > 0, (b - 1) ^ t, r)
    doc_q = turned(docs[b], rows)
    doc_own = docs[b].astype(F32)
    doc_ahead = docs[jnp.maximum(b - 1, 0)].astype(F32)
    i = lax.broadcasted_iota(jnp.int32, (rows, rows), 0)
    j = lax.broadcasted_iota(jnp.int32, (rows, rows), 1)
    own = jnp.where((doc_q == doc_own) & (j <= i), 1.0, 0.0)
    prior = jnp.where(doc_q == doc_ahead, 1.0, 0.0) * jnp.where(b > 0, 1.0, 0.0)
    allowed = jnp.concatenate([prior, own], axis=1)
    root_inv = lax.rsqrt(jnp.sum(allowed, axis=1, keepdims=True))
    return ahead, allowed, root_inv


def head_masks(cols):
    lane = lax.broadcasted_iota(jnp.int32, (1, cols), 1) // HEAD
    return [jnp.where(lane == h, 1.0, 0.0) for h in range(cols // HEAD)]


def spread(value, masks):
    return jnp.concatenate([value * bf16(m) for m in masks], axis=0)


def collect(value, masks):
    rows = value.shape[0] // len(masks)
    total = None
    for h, m in enumerate(masks):
        part = value[h * rows : (h + 1) * rows] * m
        total = part if total is None else total + part
    return total


def attend_first(
    docs, fourth, pre_c, act_c, proj_a, proj_c, enc, w_in,
    pre_ref, act_ref, proj_ref, att_ref, give_ref, pre_all,
):
    half = fourth.shape[0]
    cols = proj_a.shape[-1]
    proj_ref[:, 0:2] = proj_a[...]
    proj_ref[:, 2:3] = proj_c[...]
    pre_ref[:half, :] = pre_c[...]
    act_ref[:half, :] = act_c[...]

    def store(c, value):
        proj_ref[c, 3] = value

    encode(
        fourth[...], enc, w_in, pre_all, pre_ref.at[half : 2 * half], act_ref.at[half : 2 * half], store
    )
    attend((1, 3), docs, proj_ref, att_ref, give_ref)


def attend_second(docs, proj_ref, _att, att_ref, keep_ref):
    attend((0, 2), docs, proj_ref, att_ref, keep_ref)


def attend(blocks, docs, proj_ref, att_ref, target):
    half, cols = proj_ref.shape[2:]
    masks = head_masks(cols)
    for place, r in enumerate(blocks[::-1]):
        ahead, allowed, root_inv = window(docs, r, half)
        keys = jnp.concatenate([proj_ref[1, ahead], proj_ref[1, r]], axis=0)
        values = jnp.concatenate([proj_ref[2, ahead], proj_ref[2, r]], axis=0)
        many = jnp.concatenate([allowed] * len(masks), axis=0)
        scores = dot(spread(proj_ref[0, r], masks), keys, NT) * HEAD ** (-0.5)
        weights = bf16(scores * jax.nn.sigmoid(scores) * many)
        attended = collect(dot(weights, values), masks) * root_inv
        gate = proj_ref[3, r].astype(F32)
        att_ref[r] = attended
        target[place * half : (place + 1) * half, :] = bf16(attended * gate * jax.nn.sigmoid(gate))


def attn_out_part(index, keep, take, w_own, w_near, out):
    rows = out.shape[0]
    part = slice(index * rows, (index + 1) * rows)
    out[...] = bf16(dot(keep[part, :], w_own[...]) + dot(take[part, :], w_near[...]))


def residual(packed, part, got, resid_ref, normed_ref):
    resid = bf16(packed[...].astype(F32) + (part[...].astype(F32) + got[...].astype(F32)))
    resid_ref[...] = resid
    wide = resid.astype(F32)
    normed_ref[...] = bf16(wide * norm_factor(wide))


def ffn(rows_ref, d_out_ref, in_a, in_b, out_a, out_b, hidden_ref, back_ref):
    rows = rows_ref[...]
    cotangent = d_out_ref[...]
    units = out_a.shape[0]
    back = None
    for index, (w_in, w_out) in enumerate(((in_a, out_a), (in_b, out_b))):
        for n in range(units // CHUNK):
            part = slice(n * CHUNK, (n + 1) * CHUNK)
            d_hidden = dot(cotangent, w_out[part, :], NT)
            gate = dot(rows, w_in[0, :, part])
            upper = dot(rows, w_in[1, :, part])
            sigma = jax.nn.sigmoid(gate)
            silu = gate * sigma
            hidden_ref[:, index * units + n * CHUNK : index * units + (n + 1) * CHUNK] = bf16(silu * upper)
            d_gate = bf16(d_hidden * upper * silu_grad(gate, sigma))
            d_upper = bf16(d_hidden * silu)
            term = dot(d_gate, w_in[0, :, part], NT) + dot(d_upper, w_in[1, :, part], NT)
            back = term if back is None else back + term
    back_ref[...] = back.astype(back_ref.dtype)


def ffn_out_far(hidden, w_a, w_b, out):
    units = w_a.shape[0]
    out[...] = bf16(dot(hidden[:, :units], w_a[...]) + dot(hidden[:, units:], w_b[...]))


def ffn_out_own(hidden, w_a, w_b, resid, got, out):
    units = w_a.shape[0]
    total = dot(hidden[:, :units], w_a[...]) + dot(hidden[:, units:], w_b[...])
    out[...] = bf16(resid[...].astype(F32) + total + got[...].astype(F32))


def resid_back(back, got, resid, d_out, out, *halves):
    wide = resid[...].astype(F32)
    factor = norm_factor(wide)
    grad = back[...].astype(F32) + got[...].astype(F32)
    store_halves(bf16(d_out[...].astype(F32) + norm_back(grad, wide * factor, factor)), out, halves)


def attend_back(docs, d_resid, r, proj_ref, att_ref, w_out, masks, d_q, d_k, d_v, d_g):
    half = d_resid.shape[0]
    scale = HEAD ** (-0.5)
    ahead, allowed, root_inv = window(docs, r, half)
    gate = proj_ref[3, r].astype(F32)
    sigma_g = jax.nn.sigmoid(gate)
    d_gated = dot(d_resid, w_out)
    d_att = bf16(d_gated * (gate * sigma_g) * root_inv)
    d_g[r] = bf16(d_gated * att_ref[r] * silu_grad(gate, sigma_g))
    keys = jnp.concatenate([proj_ref[1, ahead], proj_ref[1, r]], axis=0)
    values = jnp.concatenate([proj_ref[2, ahead], proj_ref[2, r]], axis=0)
    many = jnp.concatenate([allowed] * len(masks), axis=0)
    query = spread(proj_ref[0, r], masks)
    d_att_m = spread(d_att, masks)
    scores = dot(query, keys, NT) * scale
    sigma = jax.nn.sigmoid(scores)
    weights = bf16(scores * sigma * many)
    d_weights = dot(d_att_m, values, NT)
    d_scores = bf16(d_weights * silu_grad(scores, sigma) * many)
    d_q[r] = bf16(collect(dot(d_scores, keys), masks) * scale)
    d_keys = dot(d_scores, query, TN) * scale
    d_values = dot(weights, d_att_m, TN)
    d_k[ahead] += d_keys[:half]
    d_k[r] += d_keys[half:]
    d_v[ahead] += d_values[:half]
    d_v[r] += d_values[half:]


def attn_back_first(docs, third, fourth_a, fourth_b, proj, att, w_out, d_q, d_k, d_v, d_g):
    masks = head_masks(w_out.shape[1])
    d_k[...] = jnp.zeros_like(d_k)
    d_v[...] = jnp.zeros_like(d_v)
    for r, rows in ((2, [third]), (3, [fourth_a, fourth_b])):
        attend_back(docs, joined(rows), r, proj, att, w_out[...], masks, d_q, d_k, d_v, d_g)


def attn_back_own(
    docs, first, proj, att, w_out, _q, _k, _v, _g, w_in, give_ref, d_q, d_k, d_v, d_g
):
    masks = head_masks(w_out.shape[1])
    attend_back(docs, first[...], 0, proj, att, w_out[...], masks, d_q, d_k, d_v, d_g)
    give_ref[...] = bf16(back_norm((d_q, d_k, d_v, d_g), w_in, 3))


def attn_back_second(
    docs, second, proj, att, w_out, _q, _k, _v, _g, d_q, d_k, d_v, d_g
):
    masks = head_masks(w_out.shape[1])
    attend_back(docs, second[...], 1, proj, att, w_out[...], masks, d_q, d_k, d_v, d_g)


def back_norm(grads, w_in, block):
    total = None
    for c, grad in enumerate(grads):
        term = dot(bf16(grad[block]), w_in[c])
        total = term if total is None else total + term
    return total


def back_give(block, d_q, d_k, d_v, d_g, w_in, *outs):
    value = bf16(back_norm((d_q, d_k, d_v, d_g), w_in, block))
    rows = value.shape[0] // len(outs)
    for n, out in enumerate(outs):
        out[...] = value[n * rows : (n + 1) * rows]


def back_sum(block, d_q, d_k, d_v, d_g, w_in, *refs):
    takes, out = refs[:-1], refs[-1]
    out[...] = bf16(back_norm((d_q, d_k, d_v, d_g), w_in, block) + joined(takes).astype(F32))


def packed_back(part, got, packed, d_resid, out, *halves):
    wide = packed[...].astype(F32)
    factor = norm_factor(wide)
    grad = part[...].astype(F32) + got[...].astype(F32)
    store_halves(bf16(d_resid[...].astype(F32) + norm_back(grad, wide * factor, factor)), out, halves)


def column_of(ref, index, cols):
    return ref[:, pl.ds(pl.multiple_of(index * cols, cols), cols)]


def rows_term(act_refs, cot):
    return dot(jnp.concatenate([a[...] for a in act_refs], axis=0), cot, TN)


def first_cot(cots, pre, enc):
    cols = pre.shape[1]
    cot = joined(cots)
    value = pre[...]
    w1_rows = enc[1, pl.ds(pl.multiple_of(tensor_index() * cols, cols), cols), :]
    return bf16(dot(cot, w1_rows, NT) * silu_grad(value, jax.nn.sigmoid(value)))


def cot_columns(cots, cols):
    return jnp.concatenate([column_of(c, tensor_index(), cols) for c in cots], axis=0)


def enc_grads_first(*refs):
    rows, (act1, pre, enc, part1, part0) = refs[:-5], refs[-5:]
    cots, act0 = rows[: len(rows) // 2], rows[len(rows) // 2 :]
    cols = pre.shape[1]
    part1[...] = rows_term([act1], cot_columns(cots, cols))
    part0[...] = rows_term(act0, first_cot(cots, pre, enc))


def halve(bits, bit, total, keep, send):
    place = bits.index(bit)
    count, size, _ = keep.shape
    mine = (group_index() >> bit) & 1
    for j in range(count):
        low = j & ((1 << place) - 1)
        base = ((j >> place) << (place + 1)) | low
        for target, value in ((keep, mine), (send, 1 - mine)):
            index = base + (value << place)
            rows = total[pl.ds(pl.multiple_of(index * size, size), size), :]
            target[j] = rows.astype(target.dtype)


def enc_grads_second(bits, bit, *refs):
    rows, refs = refs[:-11], refs[-11:]
    act1, pre, enc, part1, part0, keep1, send1, keep0, send0 = refs[:9]
    total1, total0 = refs[9:]
    cots, act0 = rows[:-2], rows[-2:]
    total1[...] = rows_term([act1], cot_columns(cots, part1.shape[1])) + part1[...]
    halve(bits, bit, total1, keep1, send1)
    total0[...] = rows_term(act0, first_cot(cots, pre, enc)) + part0[...]
    halve(bits, bit, total0, keep0, send0)


def halve_again(bits, bit, kept, got, keep, send):
    place = bits.index(bit)
    mine = (group_index() >> bit) & 1
    for j in range(keep.shape[0]):
        low = j & ((1 << place) - 1)
        base = ((j >> place) << (place + 1)) | low
        for target, value in ((keep, mine), (send, 1 - mine)):
            index = base + (value << place)
            target[j] = (kept[index] + got[index].astype(F32)).astype(target.dtype)


def finish(kept1, got1, kept0, got0, out):
    out[0] = kept0[0] + got0[0].astype(F32)
    out[1] = kept1[0] + got1[0].astype(F32)


def shards(
    features,
    dest_owner,
    dest_slot,
    doc_ids,
    enc_weight,
    attn_in,
    attn_out,
    ffn_in,
    ffn_out,
    out_grad,
):
    rows_dev, width = features.shape
    group_axes = ("event", "pack")
    groups = lax.axis_size(group_axes)
    packs = lax.axis_size("pack")
    tensors = lax.axis_size("tensor")
    cols = attn_in.shape[2]
    comps = attn_in.shape[0]
    units = ffn_out.shape[0]
    d_out = out_grad[0]
    docs = doc_ids.reshape(tensors, 1, rows_dev)

    def near(value):
        return lax.ppermute(value, "tensor", [(i, i ^ 1) for i in range(tensors)])

    def far(value):
        return lax.ppermute(value, "tensor", [(i, i ^ 2) for i in range(tensors)])

    def crossed(value, k):
        return lax.ppermute(value, group_axes, [(i, i ^ k) for i in range(groups)])

    row_b = like((rows_dev, width), BF16)
    row_f = like((rows_dev, width), F32)

    mean_load = rows_dev // groups
    capacity = -(-(mean_load + mean_load // 2) // 8) * 8
    code = (dest_owner * rows_dev + dest_slot).reshape(1, rows_dev)
    offsets = range(1, groups)
    across = sorted((k for k in offsets if 2 * (k % packs) >= packs), key=lambda k: (k % packs, k))
    short = [k for k in offsets if k not in across]
    hops = [k for k in short if k & (k - 1)]
    order = [0] + across[:2] + hops + across[2:] + [k for k in short if k not in hops]
    *sends, place = run(
        functools.partial(route_send, capacity, order),
        [like((capacity, width + rows_dev), BF16)] * groups + [like((1, rows_dev), jnp.int32)],
        [code, features],
        flops=4 * 10**9,
        name="route_send",
    )
    ffn_in_near, ffn_out_near = near(ffn_in), near(ffn_out)
    early = [crossed(sends[n], order[n]) for n in (1, 2)]
    ffn_in_near, ffn_out_near, *sends = tie(ffn_in_near, ffn_out_near, *sends)
    gots = [sends[0], *early] + [crossed(sends[n], order[n]) for n in range(3, groups)]
    pieces = 2
    piece_b = like((rows_dev // pieces, width), BF16)
    in_turned, out_turned = run(
        turn,
        [like((comps, cols, width), BF16), like((width, cols), BF16)],
        [attn_in, attn_out],
        name="turn",
    )
    in_turned, *gots = tie(in_turned, *gots)
    mine, hot, *halves = run(
        route_recv,
        [row_b, like((groups * capacity, rows_dev), BF16)] + [piece_b] * pieces,
        gots,
        name="route_recv",
    )

    mine_far = far(mine)
    mine_near = [near(h) for h in halves]

    pair = 2 * rows_dev
    pre_a, act_a, packed, proj_a = run(
        encode_blocks,
        [
            like((pair, cols), F32),
            like((pair, width), BF16),
            row_b,
            like((comps, 2, rows_dev, cols), BF16),
        ],
        [mine, *mine_near, enc_weight, attn_in],
        [pltpu.VMEM((pair, width), F32)],
        name="encode_first",
    )
    mine_far, proj_a = tie(mine_far, proj_a)
    mine_far, attn_out_late, d_out_late = tie(mine_far, attn_out, d_out)
    mine_both = near(mine_far)
    attn_out_near = near(attn_out_late)
    d_out_far = far(d_out_late)
    pre_c, act_c, packed_far, proj_c = run(
        encode_blocks,
        [like((rows_dev, cols), F32), row_b, row_b, like((comps, 1, rows_dev, cols), BF16)],
        [mine_far, enc_weight, attn_in],
        [pltpu.VMEM((rows_dev, width), F32)],
        name="encode_third",
    )
    pre_b, act_b, proj, attended, give = run(
        attend_first,
        [
            like((pair, cols), F32),
            like((pair, width), BF16),
            like((comps, tensors, rows_dev, cols), BF16),
            like((tensors, rows_dev, cols), F32),
            like((pair, cols), BF16),
        ],
        [docs, mine_both, pre_c, act_c, proj_a, proj_c, enc_weight, attn_in],
        [pltpu.VMEM((rows_dev, width), F32)],
        name="attend_first",
    )
    take = near(give)
    attended, keep = run(
        attend_second,
        [like((tensors, rows_dev, cols), F32), like((pair, cols), BF16)],
        [docs, proj, attended],
        name="attend_second",
        aliases={2: 0},
    )


    def out_part(index, name):
        return run(
            functools.partial(attn_out_part, index),
            [row_b],
            [keep, take, attn_out, attn_out_near],
            name=name,
        )[0]

    part_far = out_part(0, "attn_out_far")
    got_own = far(part_far)
    part_own = out_part(1, "attn_out_own")
    part_own, d_out_far = tie(part_own, d_out_far)
    got_far = far(part_own)

    def feed(rows, cotangent, name):
        return run(
            ffn,
            [like((rows_dev, 2 * units), BF16), row_b],
            [rows, cotangent, ffn_in, ffn_in_near, ffn_out, ffn_out_near],
            name=name,
        )

    resid, normed2 = run(residual, [row_b, row_b], [packed, part_own, got_own], name="residual")
    hidden_own, back_own = feed(normed2, d_out, "ffn_own")
    got_far, back_own = tie(got_far, back_own)
    got_back_far = far(back_own)
    resid_far, normed2_far = run(
        residual, [row_b, row_b], [packed_far, part_far, got_far], name="residual_far"
    )
    hidden_far, back_far = feed(normed2_far, d_out_far, "ffn_far")
    got_back_own = far(back_far)

    d_resid_far, *halves = run(
        resid_back,
        [row_b] + [piece_b] * pieces,
        [back_far, got_back_far, resid_far, d_out_far],
        name="resid_back_far",
    )
    d_resid_both = [near(h) for h in halves]
    block_f = like((tensors, rows_dev, cols), F32)
    block_b = like((tensors, rows_dev, cols), BF16)
    d_q, d_k, d_v, d_g = run(
        attn_back_first,
        [block_b, block_f, block_f, block_b],
        [docs, d_resid_far, *d_resid_both, proj, attended, out_turned],
        name="attn_back_first",
    )
    got_back_own, d_q = tie(got_back_own, d_q)
    (d_resid,) = run(resid_back, [row_b], [back_own, got_back_own, resid, d_out], name="resid_back")
    d_resid_near = near(d_resid)
    give, *own_grads = run(
        attn_back_own,
        [row_b, block_b, block_f, block_f, block_b],
        [docs, d_resid, proj, attended, out_turned, d_q, d_k, d_v, d_g, in_turned],
        aliases={5: 1, 6: 2, 7: 3, 8: 4},
        name="attn_back_own",
    )
    take = near(give)
    d_projected = run(
        attn_back_second,
        [block_b, block_f, block_f, block_b],
        [docs, d_resid_near, proj, attended, out_turned, *own_grads],
        aliases={5: 0, 6: 1, 7: 2, 8: 3},
        name="attn_back_second",
    )

    def back_part(body, block, outs, more, name):
        return run(functools.partial(body, block), outs, [*d_projected, in_turned, *more], name=name)

    (sum_far,) = back_part(back_sum, 2, [row_b], [take], "back_sum_far")
    sum_far, *d_projected = tie(sum_far, *d_projected)
    takes = [near(h) for h in back_part(back_give, 1, [piece_b] * pieces, [], "back_give")]
    (sum_own,) = back_part(back_sum, 0, [row_b], takes, "back_sum_own")
    got_own = far(sum_far)
    got_far = far(sum_own)
    d_packed, *halves = run(
        packed_back,
        [row_b] + [piece_b] * pieces,
        [sum_own, got_own, packed, d_resid],
        name="packed_back",
    )

    cot_near = [near(h) for h in halves]
    half_rows = like((groups * capacity // 2, width), BF16)
    group_bits = [1 << b for b in range(groups.bit_length() - 1)]
    near_bit, pack_far, event_far = group_bits[0], group_bits[1 : packs.bit_length() - 1], group_bits[packs.bit_length() - 1 :]
    back_bits = pack_far[::-1] + [near_bit] + event_far[::-1]
    kept, back = run(
        functools.partial(back_send, order, back_bits[0]), [half_rows] * 2, [hot, d_packed], name="back_send"
    )
    back_got = crossed(back, back_bits[0])

    part_f = like((width, cols), F32)
    part1, part0 = run(
        enc_grads_first,
        [part_f, part_f],
        [d_packed, *cot_near, mine, *mine_near, act_a, pre_a, enc_weight],
        name="enc_grads_first",
    )
    got_far, part1, part0 = tie(got_far, part1, part0)
    cot_far, *cot_pieces = run(
        packed_back,
        [row_b] + [like((rows_dev * part // 8, width), BF16) for part in (3, 3, 2)],
        [sum_far, got_far, packed_far, d_resid_far],
        name="packed_back_far",
    )
    cot_both = [near(piece) for piece in cot_pieces]
    cot_far, hidden_far = tie(cot_far, hidden_far)
    (out_far,) = run(
        ffn_out_far, [row_b], [hidden_far, ffn_out, ffn_out_near], name="ffn_out_far"
    )
    bits = list(range(groups.bit_length() - 1))
    pack_bits = bits[: packs.bit_length() - 1]
    event_bits = bits[len(pack_bits) :]
    size = width // groups
    total = [pltpu.VMEM((width, cols), F32)]

    def halves(remaining):
        shape = (2 ** (len(remaining) - 1), size, cols)
        return [like(shape, F32), like(shape, BF16)]

    def reduce_over(stages, kept, send, name, beside):
        remaining = list(bits)
        got = crossed(send, 1 << stages[0])
        if beside == stages[0]:
            got, arrays[-1] = tie(got, arrays[-1])
        remaining.remove(stages[0])
        for bit in stages[1:]:
            kept, send = run(
                functools.partial(halve_again, tuple(remaining), bit),
                halves(remaining),
                [kept, got],
                name=name + str(bit),
            )
            got = crossed(send, 1 << bit)
            remaining.remove(bit)
            if bit == beside:
                got, arrays[-1] = tie(got, arrays[-1])
        return kept, got

    kept1, send1, kept0, send0 = run(
        functools.partial(enc_grads_second, tuple(bits), event_bits[0]),
        halves(bits) * 2,
        [cot_far, *cot_both, mine_far, mine_both, act_b, pre_b, enc_weight, part1, part0],
        total * 2,
        name="enc_grads_second",
    )
    arrays = [kept, back_got]
    held = {}
    for n, value in enumerate((0, back_bits[0])):
        chosen = [k for k in range(groups) if k & back_bits[0] == value]
        held.update({k: (n, at) for at, k in enumerate(chosen)})

    def send_back(bit):
        moved = [k for k in range(groups) if k & bit]
        (back,) = run(
            functools.partial(back_pick, [held[k] for k in moved], capacity),
            [half_rows],
            arrays,
            name="back_pick",
        )
        held.update({k: (len(arrays), n) for n, k in enumerate(moved)})
        arrays.append(crossed(back, bit))

    for bit in back_bits[1:-1]:
        send_back(bit)
    kept1, got1 = reduce_over(event_bits + pack_bits, kept1, send1, "halve1_", None)
    kept0, got0 = reduce_over(event_bits + pack_bits, kept0, send0, "halve0_", event_bits[0])
    send_back(back_bits[-1])
    got1, place = tie(got1, place)
    back_places = [held[k] for k in range(groups)]
    got_out = far(out_far)
    (packed_out,) = run(
        ffn_out_own, [row_b], [hidden_own, ffn_out, ffn_out_near, resid, got_out], name="ffn_out_own"
    )
    (row_grad,) = run(
        functools.partial(back_recv, back_places, capacity),
        [row_b],
        [place, *arrays],
        name="back_recv",
    )
    got1, got0, packed_out, row_grad = tie(got1, got0, packed_out, row_grad)
    (enc_grad,) = run(finish, [like((2, size, cols), F32)], [kept1, got1, kept0, got0], name="finish")
    return (packed_out[None], row_grad, enc_grad)


def solution(mesh):
    placed = (
        P(("event", "pack", "tensor"), None),
        P(("event", "pack", "tensor")),
        P(("event", "pack", "tensor")),
        P(("event", "pack"), None),
        P(),
        P(None, None, "tensor"),
        P("tensor", None),
        P(None, None, "tensor"),
        P("tensor", None),
        P(("event", "pack"), "tensor", None),
    )
    return jax.shard_map(
        shards,
        mesh=mesh,
        in_specs=placed,
        out_specs=(
            P(("event", "pack"), "tensor", None),
            P(("event", "pack", "tensor"), None),
            P(None, ("event", "pack"), "tensor"),
        ),
        check_vma=False,
    )
```
